32 devices in a mesh: dp: 8 (over y, x, core), chan: 4 (over z).
Axes of the slice: x: 2, y: 2, z: 4, core: 2. Of those that a mesh axis runs over, the one named last changes fastest.
Arguments:
- features: bfloat16 [25088, 512], P('dp', 'chan'), may hold values from -6 to 6
- cotangent: float32 [25088, 512], P('dp', 'chan'), may hold values from -6 to 6
- clip_frames: int32 [128], P('dp'), may hold values from 8 to 32, as said below
- spatial_master: float32 [2, 4608, 1152], P(None, 'dp', 'chan'), may hold values from -0.09375 to 0.09375
- spatial_first: float32 [2, 4608, 1152], P(None, 'dp', 'chan'), may hold values from -32 to 32
- spatial_second: float32 [2, 4608, 1152], P(None, 'dp', 'chan'), may hold values from 125.44 to 501.76
- temporal_master: float32 [2, 3, 1152, 512], P(None, None, 'chan', 'dp'), may hold values from -0.109375 to 0.109375
- temporal_first: float32 [2, 3, 1152, 512], P(None, None, 'chan', 'dp'), may hold values from -32 to 32
- temporal_second: float32 [2, 3, 1152, 512], P(None, None, 'chan', 'dp'), may hold values from 125.44 to 501.76
- mid_norm: float32 [4, 1152], P(None, 'chan'), may hold values from 0.5 to 1.5
- mid_first: float32 [4, 1152], P(None, 'chan'), may hold values from -32 to 32
- mid_second: float32 [4, 1152], P(None, 'chan'), may hold values from 125.44 to 501.76
- out_norm: float32 [4, 512], P(None, 'chan'), may hold values from 0.5 to 1.5
- out_first: float32 [4, 512], P(None, 'chan'), may hold values from -32 to 32
- out_second: float32 [4, 512], P(None, 'chan'), may hold values from 125.44 to 501.76
Outputs:
- block_out: float32 [25088, 512], P('dp', 'chan')
- clip_pool: float32 [128, 512], P('dp', 'chan')
- input_grad: float32 [25088, 512], P('dp', 'chan')
- spatial_new: float32 [2, 4608, 1152], P(None, 'dp', 'chan')
- spatial_first_new: float32 [2, 4608, 1152], P(None, 'dp', 'chan')
- spatial_second_new: float32 [2, 4608, 1152], P(None, 'dp', 'chan')
- temporal_new: float32 [2, 3, 1152, 512], P(None, None, 'chan', 'dp')
- temporal_first_new: float32 [2, 3, 1152, 512], P(None, None, 'chan', 'dp')
- temporal_second_new: float32 [2, 3, 1152, 512], P(None, None, 'chan', 'dp')
- mid_norm_new: float32 [4, 1152], P(None, 'chan')
- mid_first_new: float32 [4, 1152], P(None, 'chan')
- mid_second_new: float32 [4, 1152], P(None, 'chan')
- out_norm_new: float32 [4, 512], P(None, 'chan')
- out_first_new: float32 [4, 512], P(None, 'chan')
- out_second_new: float32 [4, 512], P(None, 'chan')
The draws below stay inside these ranges and needn't reach their ends.
Inputs may be any that keep to these rules, and one draw needn't show every extreme that they name: Each entry is 8, 16 or 32; a clip keeps its first clip_frames // 8 of 4 frame slots; every draw holds both 8 and 32.
All inputs are finite; a program needn't handle non-finite values.
Results may differ from the reference program's by a relative error of at most 0.025.
Values may be sent and summed in bfloat16 or wider, within the bound.
A program may use at most 320 MiB of HBM per device.

```python
import math
import jax
import jax.numpy as jnp
from jax import lax

C = 512
MID = 1152
FRAMES = 4
SIDE = 7
STEP = 10
HW = 49
CLIPS = 128
PIXELS = 25088


def draw_clip_frames(key, part):
    key = jax.random.fold_in(key, 7)
    levels = jax.random.randint(key, (CLIPS,), 0, 3)
    levels = levels.at[0].set(2).at[CLIPS - 1].set(0)
    return jnp.array([8, 16, 32], dtype=jnp.int32)[levels]


def steps_of(key, shape, split, low, high):
    gain = 1.0
    for dim, parts in split:
        heights = jax.random.uniform(jax.random.fold_in(jax.random.fold_in(key, 6), dim), (parts,), jnp.float32, low / len(split), high / len(split))
        gain = gain * jnp.repeat(jnp.exp(heights), shape[dim] // parts).reshape((-1,) + (1,) * (len(shape) - 1 - dim))
    return gain


def centred(rng, shape, width, limit, split=(), kind=jnp.bfloat16):
    values = width * jax.random.normal(rng, shape, jnp.float32)
    if split:
        values = values * steps_of(rng, shape, split, -0.22, 0.18)
    return jnp.clip(values, -limit, limit).astype(kind)


def setup_inputs(seed: int = 0) -> dict:
    splits = jax.random.split(jax.random.key(seed), 16)
    features = centred(splits[0], (PIXELS, C), 1.0, 6.0, ((0, 8), (1, 4)))
    cotangent = centred(splits[1], (PIXELS, C), 1.0, 6.0, ((0, 8), (1, 4)), jnp.float32)
    clip_frames = draw_clip_frames(jax.random.fold_in(splits[15], 71), 0)
    spatial_master = centred(splits[3], (2, 9 * C, MID), (9 * C) ** -0.5, 0.09375, ((1, 8), (2, 4)), jnp.float32)
    spatial_first = centred(splits[4], (2, 9 * C, MID), (0.035 * PIXELS ** 0.5), 32.0, ((1, 8), (2, 4)), jnp.float32)
    spatial_second = jnp.clip(jnp.exp(math.log(501.76) - 1.3862944 * jax.random.uniform(splits[5], (2, 9 * C, MID), jnp.float32) ** steps_of(splits[5], (2, 9 * C, MID), ((1, 8), (2, 4)), -0.2, 0.2)), 125.44, 501.76)
    temporal_master = centred(splits[6], (2, 3, MID, C), (3 * MID) ** -0.5, 0.109375, ((2, 4), (3, 8)), jnp.float32)
    temporal_first = centred(splits[7], (2, 3, MID, C), (0.035 * PIXELS ** 0.5), 32.0, ((2, 4), (3, 8)), jnp.float32)
    temporal_second = jnp.clip(jnp.exp(math.log(501.76) - 1.3862944 * jax.random.uniform(splits[8], (2, 3, MID, C), jnp.float32) ** steps_of(splits[8], (2, 3, MID, C), ((2, 4), (3, 8)), -0.2, 0.2)), 125.44, 501.76)
    mid_norm = jnp.clip(0.5 + 1.0 * jax.random.uniform(splits[9], (4, MID), jnp.float32) ** steps_of(splits[9], (4, MID), ((1, 4),), -0.2, 0.2), 0.5, 1.5)
    mid_first = centred(splits[10], (4, MID), (0.035 * PIXELS ** 0.5), 32.0, ((1, 4),), jnp.float32)
    mid_second = jnp.clip(jnp.exp(math.log(501.76) - 1.3862944 * jax.random.uniform(splits[11], (4, MID), jnp.float32) ** steps_of(splits[11], (4, MID), ((1, 4),), -0.2, 0.2)), 125.44, 501.76)
    out_norm = jnp.clip(0.5 + 1.0 * jax.random.uniform(splits[12], (4, C), jnp.float32) ** steps_of(splits[12], (4, C), ((1, 4),), -0.2, 0.2), 0.5, 1.5)
    out_first = centred(splits[13], (4, C), (0.035 * PIXELS ** 0.5), 32.0, ((1, 4),), jnp.float32)
    out_second = jnp.clip(jnp.exp(math.log(501.76) - 1.3862944 * jax.random.uniform(splits[14], (4, C), jnp.float32) ** steps_of(splits[14], (4, C), ((1, 4),), -0.2, 0.2)), 125.44, 501.76)
    return {"features": features, "cotangent": cotangent, "clip_frames": clip_frames, "spatial_master": spatial_master, "spatial_first": spatial_first, "spatial_second": spatial_second, "temporal_master": temporal_master, "temporal_first": temporal_first, "temporal_second": temporal_second, "mid_norm": mid_norm, "mid_first": mid_first, "mid_second": mid_second, "out_norm": out_norm, "out_first": out_first, "out_second": out_second}


@jax.custom_vjp
def low(v):
    return lax.optimization_barrier(v.astype(jnp.bfloat16)).astype(jnp.float32)

@jax.custom_vjp
def low_back(v):
    return v

def low_keep(v):
    return (low(v), None)

def low_pass(kept, grad):
    return (grad,)

def back_keep(v):
    return (v, None)

def back_low(kept, grad):
    return (low(grad),)
low.defvjp(low_keep, low_pass)
low_back.defvjp(back_keep, back_low)
EPS_NORM = 1e-05
EPS_ADAM = 1e-08
BETA_ONE = 0.9
BETA_TWO = 0.95
RATE_CONV = 0.01
RATE_NORM = 0.8
DECAY_CONV = 0.05
PRECISE = lax.Precision.HIGHEST

def frame_mask(clip_frames):
    kept_frames = clip_frames // 8
    frame_ids = jnp.arange(FRAMES, dtype=jnp.int32)
    frame_grid = (frame_ids[None, :] < kept_frames[:, None]).astype(jnp.float32)
    return jnp.broadcast_to(frame_grid[:, :, None], (kept_frames.shape[0], FRAMES, HW)).reshape(-1, 1)

def spatial(inputs, weight):
    tap_weights = weight.reshape(9, -1, weight.shape[1])
    padded = jnp.pad(inputs.reshape(-1, SIDE, SIDE, inputs.shape[1]), ((0, 0), (1, 1), (1, 1), (0, 0)))
    summed = jnp.zeros((padded.shape[0], SIDE, SIDE, weight.shape[1]), jnp.float32)
    for tap_index in range(9):
        row_off, col_off = (tap_index // 3, tap_index % 3)
        window = padded[:, row_off:row_off + SIDE, col_off:col_off + SIDE]
        summed = summed + jnp.einsum('nijc,cm->nijm', window, tap_weights[tap_index], precision=PRECISE)
    return summed.reshape(inputs.shape[0], -1)

def temporal(inputs, weight):
    frame_seq = inputs.reshape(-1, FRAMES, HW, inputs.shape[1])
    padded = jnp.pad(frame_seq, ((0, 0), (1, 1), (0, 0), (0, 0)))
    summed = jnp.zeros(frame_seq.shape[:3] + (weight.shape[2],), jnp.float32)
    for frame_off in range(3):
        summed = summed + jnp.einsum('nfpm,mc->nfpc', padded[:, frame_off:frame_off + FRAMES], weight[frame_off], precision=PRECISE)
    return summed.reshape(inputs.shape[0], -1)

def normalize(values, validity, total_valid, gain_row, bias_row):
    average = lax.optimization_barrier(jnp.sum(values * validity, axis=0)) / total_valid
    centered = values - average
    variance = lax.optimization_barrier(jnp.sum(validity * centered * centered, axis=0)) / total_valid
    return centered * lax.rsqrt(variance + EPS_NORM) * gain_row + bias_row

def forward(features, spatial_master, temporal_master, mid_norm, out_norm, validity):
    total_valid = jnp.sum(validity)
    hidden = features
    for unit_index in range(2):
        spatial_in = low(hidden)
        spatial_out = low_back(spatial(spatial_in, low(spatial_master[unit_index])))
        mid_normed = normalize(spatial_out, validity, total_valid, mid_norm[2 * unit_index], mid_norm[2 * unit_index + 1])
        temporal_in = low(jax.nn.silu(mid_normed) * validity)
        temporal_out = low_back(temporal(temporal_in, low(temporal_master[unit_index])))
        out_normed = normalize(temporal_out, validity, total_valid, out_norm[2 * unit_index], out_norm[2 * unit_index + 1])
        if unit_index == 0:
            hidden = jax.nn.silu(out_normed) * validity
        else:
            hidden = jax.nn.silu(out_normed + features) * validity
    return hidden

def adam_update(weight, moment_one, moment_two, grad_value, rate, decay):
    fresh_one = BETA_ONE * moment_one + (1.0 - BETA_ONE) * grad_value
    fresh_two = BETA_TWO * moment_two + (1.0 - BETA_TWO) * grad_value * grad_value
    scaled = fresh_one / (1.0 - BETA_ONE ** STEP) / (jnp.sqrt(fresh_two / (1.0 - BETA_TWO ** STEP)) + EPS_ADAM)
    return (weight - rate * (scaled + decay * weight), fresh_one, fresh_two)

def reference(features, cotangent, clip_frames, spatial_master, spatial_first, spatial_second, temporal_master, temporal_first, temporal_second, mid_norm, mid_first, mid_second, out_norm, out_first, out_second):
    validity = frame_mask(clip_frames)
    block_input = features.astype(jnp.float32)

    def closed(inputs, spatial_part, temporal_part, mid_part, out_part):
        return forward(inputs, spatial_part, temporal_part, mid_part, out_part, validity)
    block_out, pullback = jax.vjp(closed, block_input, spatial_master, temporal_master, mid_norm, out_norm)
    input_grad, spatial_grad, temporal_grad, mid_grad, out_grad = pullback(cotangent)
    kept_frames = (clip_frames // 8).astype(jnp.float32)
    clip_pool = lax.optimization_barrier(jnp.sum(block_out.reshape(-1, FRAMES * HW, block_out.shape[1]), axis=1)) / (HW * kept_frames)[:, None]
    spatial_new, spatial_one, spatial_two = adam_update(spatial_master, spatial_first, spatial_second, spatial_grad, RATE_CONV, DECAY_CONV)
    temporal_new, temporal_one, temporal_two = adam_update(temporal_master, temporal_first, temporal_second, temporal_grad, RATE_CONV, DECAY_CONV)
    mid_new, mid_one, mid_two = adam_update(mid_norm, mid_first, mid_second, mid_grad, RATE_NORM, 0.0)
    out_new, out_one, out_two = adam_update(out_norm, out_first, out_second, out_grad, RATE_NORM, 0.0)
    return (block_out, clip_pool, input_grad, spatial_new, spatial_one, spatial_two, temporal_new, temporal_one, temporal_two, mid_new, mid_one, mid_two, out_new, out_one, out_two)
```

```python
import jax
import jax.numpy as jnp
import numpy as np
from jax import lax
from jax.experimental import pallas as pl
from jax.experimental.pallas import tpu as pltpu
from jax.sharding import PartitionSpec as P

FRAMES = 4
SIDE = 7
STEP = 10
HW = 49


EPS_NORM = 1e-05
EPS_ADAM = 1e-08
BETA_ONE = 0.9
BETA_TWO = 0.95
RATE_CONV = 0.01
RATE_NORM = 0.8
DECAY_CONV = 0.05


def frame_mask(clip_frames):
    kept_frames = clip_frames // 8
    frame_ids = jnp.arange(FRAMES, dtype=jnp.int32)
    frame_grid = (frame_ids[None, :] < kept_frames[:, None]).astype(jnp.float32)
    return jnp.broadcast_to(frame_grid[:, :, None], (kept_frames.shape[0], FRAMES, HW)).reshape(
        -1, 1
    )


def silu_slope(values):
    sigmoid = jax.nn.sigmoid(values)
    return sigmoid * (1.0 + values * (1.0 - sigmoid))


def spatial_apply(inputs, tap_weights):
    channels = inputs.shape[1]
    padded = jnp.pad(inputs.reshape(-1, SIDE, SIDE, channels), ((0, 0), (1, 1), (1, 1), (0, 0)))
    summed = jnp.zeros((inputs.shape[0], tap_weights.shape[2]), jnp.float32)
    for tap_index in range(9):
        row_off, col_off = (tap_index // 3, tap_index % 3)
        window = padded[:, row_off : row_off + SIDE, col_off : col_off + SIDE].reshape(-1, channels)
        summed = summed + jnp.dot(
            window, tap_weights[tap_index], preferred_element_type=jnp.float32
        )
    return (summed, padded)


def spatial_grads(padded, tap_weights, grad_out):
    channels = padded.shape[3]
    weight_terms = []
    input_sum = jnp.zeros((padded.shape[0], SIDE, SIDE, channels), jnp.float32)
    for tap_index in range(9):
        row_off, col_off = (tap_index // 3, tap_index % 3)
        window = padded[:, row_off : row_off + SIDE, col_off : col_off + SIDE].reshape(-1, channels)
        weight_terms.append(
            lax.dot_general(
                window, grad_out, (((0,), (0,)), ((), ())), preferred_element_type=jnp.float32
            )
        )
        pulled = lax.dot_general(
            grad_out,
            tap_weights[tap_index],
            (((1,), (1,)), ((), ())),
            preferred_element_type=jnp.float32,
        )
        pulled = jnp.pad(pulled.reshape(-1, SIDE, SIDE, channels), ((0, 0), (1, 1), (1, 1), (0, 0)))
        input_sum = (
            input_sum
            + pulled[:, 2 - row_off : 2 - row_off + SIDE, 2 - col_off : 2 - col_off + SIDE]
        )
    return (jnp.stack(weight_terms).reshape(-1, grad_out.shape[1]), input_sum.reshape(-1, channels))


def temporal_apply(inputs, weight):
    frame_seq = inputs.reshape(-1, FRAMES, HW, inputs.shape[1])
    padded = jnp.pad(frame_seq, ((0, 0), (1, 1), (0, 0), (0, 0)))
    summed = jnp.zeros(frame_seq.shape[:3] + (weight.shape[2],), jnp.float32)
    for frame_off in range(3):
        summed = summed + jnp.einsum(
            "nfpm,mc->nfpc",
            padded[:, frame_off : frame_off + FRAMES],
            weight[frame_off],
            preferred_element_type=jnp.float32,
        )
    return (summed.reshape(inputs.shape[0], -1), padded)


def temporal_grads(padded, weight, grad_full):
    grad_seq = grad_full.reshape(-1, FRAMES, HW, grad_full.shape[1])
    grad_pad = jnp.pad(grad_seq, ((0, 0), (1, 1), (0, 0), (0, 0)))
    weight_terms = []
    input_sum = jnp.zeros(padded.shape[:1] + (FRAMES, HW, padded.shape[3]), jnp.float32)
    for frame_off in range(3):
        weight_terms.append(
            jnp.einsum(
                "nfpm,nfpc->mc",
                padded[:, frame_off : frame_off + FRAMES],
                grad_seq,
                preferred_element_type=jnp.float32,
            )
        )
        input_sum = input_sum + jnp.einsum(
            "nfpc,mc->nfpm",
            grad_pad[:, 2 - frame_off : 2 - frame_off + FRAMES],
            weight[frame_off],
            preferred_element_type=jnp.float32,
        )
    return (jnp.stack(weight_terms), input_sum.reshape(grad_full.shape[0], -1))


def normalize(values, validity, gain_row, bias_row):
    local_valid = jnp.sum(validity)
    total_valid, value_sums = lax.psum((local_valid, jnp.sum(values * validity, axis=0)), "dp")
    average = value_sums / total_valid
    centered = values - average
    variance = lax.psum(jnp.sum(validity * centered * centered, axis=0), "dp") / total_valid
    inverse = lax.rsqrt(variance + EPS_NORM)
    standard = centered * inverse
    return (standard * gain_row + bias_row, standard, inverse, total_valid)


def normalize_back(grad_normed, standard, inverse, gain_row, total_valid, validity):
    grad_bias, grad_gain = lax.psum(
        (
            jnp.sum(grad_normed * validity, axis=0),
            jnp.sum(grad_normed * standard * validity, axis=0),
        ),
        "dp",
    )
    grad_values = (
        validity
        * gain_row
        * inverse
        * (grad_normed - grad_bias / total_valid - standard * grad_gain / total_valid)
    )
    return (grad_values, grad_gain, grad_bias)


def adam_update(weight, moment_one, moment_two, grad_value, rate, decay):
    fresh_one = BETA_ONE * moment_one + (1.0 - BETA_ONE) * grad_value
    fresh_two = BETA_TWO * moment_two + (1.0 - BETA_TWO) * grad_value * grad_value
    scaled = (
        fresh_one
        / (1.0 - BETA_ONE**STEP)
        / (jnp.sqrt(fresh_two / (1.0 - BETA_TWO**STEP)) + EPS_ADAM)
    )
    return (weight - rate * (scaled + decay * weight), fresh_one, fresh_two)


def on_device(
    features,
    cotangent,
    clip_frames,
    spatial_master,
    spatial_first,
    spatial_second,
    temporal_master,
    temporal_first,
    temporal_second,
    mid_norm,
    mid_first,
    mid_second,
    out_norm,
    out_first,
    out_second,
):
    validity = frame_mask(clip_frames)
    spatial_all, temporal_all = (
        lax.all_gather(spatial_master.astype(jnp.bfloat16), "dp", axis=1, tiled=True),
        lax.all_gather(temporal_master.astype(jnp.bfloat16), "dp", axis=3, tiled=True),
    )
    channels = temporal_all.shape[3]
    spatial_taps = spatial_all.reshape(2, 9, channels, spatial_all.shape[2])
    residual = features.astype(jnp.float32)
    outgoing = features
    kept_state = []
    for unit_index in range(2):
        gathered = lax.all_gather(outgoing, "chan", axis=1, tiled=True)
        spatial_out, padded = spatial_apply(gathered, spatial_taps[unit_index])
        mid_normed, mid_standard, mid_inverse, total_valid = normalize(
            spatial_out, validity, mid_norm[2 * unit_index], mid_norm[2 * unit_index + 1]
        )
        temporal_in = (jax.nn.silu(mid_normed) * validity).astype(jnp.bfloat16)
        partial_value, frames_padded = temporal_apply(temporal_in, temporal_all[unit_index])
        temporal_out = lax.psum_scatter(
            partial_value.astype(jnp.bfloat16), "chan", scatter_dimension=1, tiled=True
        ).astype(jnp.float32)
        out_normed, out_standard, out_inverse, total_valid = normalize(
            temporal_out, validity, out_norm[2 * unit_index], out_norm[2 * unit_index + 1]
        )
        if unit_index == 0:
            pre_act = out_normed
            outgoing = (jax.nn.silu(pre_act) * validity).astype(jnp.bfloat16)
        else:
            pre_act = out_normed + residual
            block_out = jax.nn.silu(pre_act) * validity
        kept_state.append(
            (
                padded,
                mid_normed,
                mid_standard,
                mid_inverse,
                frames_padded,
                pre_act,
                out_standard,
                out_inverse,
            )
        )
    kept_frames = (clip_frames // 8).astype(jnp.float32)
    clip_pool = (
        jnp.sum(block_out.reshape(-1, FRAMES * HW, block_out.shape[1]), axis=1)
        / (HW * kept_frames)[:, None]
    )
    skip_grad = cotangent * validity * silu_slope(kept_state[1][5])
    grad_pre = skip_grad
    spatial_list = [None, None]
    temporal_list = [None, None]
    mid_rows = [None, None]
    out_rows = [None, None]
    grad_hidden = skip_grad
    for unit_index in (1, 0):
        (
            padded,
            mid_normed,
            mid_standard,
            mid_inverse,
            frames_padded,
            pre_act,
            out_standard,
            out_inverse,
        ) = kept_state[unit_index]
        if unit_index == 0:
            grad_pre = grad_hidden * validity * silu_slope(pre_act)
        grad_temporal, out_gain_grad, out_bias_grad = normalize_back(
            grad_pre, out_standard, out_inverse, out_norm[2 * unit_index], total_valid, validity
        )
        grad_full = lax.all_gather(grad_temporal.astype(jnp.bfloat16), "chan", axis=1, tiled=True)
        temporal_grad, grad_mid = temporal_grads(frames_padded, temporal_all[unit_index], grad_full)
        grad_mid_normed = grad_mid * validity * silu_slope(mid_normed)
        grad_spatial, mid_gain_grad, mid_bias_grad = normalize_back(
            grad_mid_normed,
            mid_standard,
            mid_inverse,
            mid_norm[2 * unit_index],
            total_valid,
            validity,
        )
        spatial_grad, grad_in_part = spatial_grads(
            padded, spatial_taps[unit_index], grad_spatial.astype(jnp.bfloat16)
        )
        grad_hidden = lax.psum_scatter(
            grad_in_part.astype(jnp.bfloat16), "chan", scatter_dimension=1, tiled=True
        ).astype(jnp.float32)
        spatial_list[unit_index] = spatial_grad
        temporal_list[unit_index] = temporal_grad
        mid_rows[unit_index] = (mid_gain_grad, mid_bias_grad)
        out_rows[unit_index] = (out_gain_grad, out_bias_grad)
    input_grad = grad_hidden + skip_grad
    spatial_sum, temporal_sum = (
        lax.psum_scatter(jnp.stack(spatial_list), "dp", scatter_dimension=1, tiled=True),
        lax.psum_scatter(jnp.stack(temporal_list), "dp", scatter_dimension=3, tiled=True),
    )
    mid_grad = jnp.stack([mid_rows[0][0], mid_rows[0][1], mid_rows[1][0], mid_rows[1][1]])
    out_grad = jnp.stack([out_rows[0][0], out_rows[0][1], out_rows[1][0], out_rows[1][1]])
    spatial_new, spatial_one, spatial_two = adam_update(
        spatial_master, spatial_first, spatial_second, spatial_sum, RATE_CONV, DECAY_CONV
    )
    temporal_new, temporal_one, temporal_two = adam_update(
        temporal_master, temporal_first, temporal_second, temporal_sum, RATE_CONV, DECAY_CONV
    )
    mid_new, mid_one, mid_two = adam_update(
        mid_norm, mid_first, mid_second, mid_grad, RATE_NORM, 0.0
    )
    out_new, out_one, out_two = adam_update(
        out_norm, out_first, out_second, out_grad, RATE_NORM, 0.0
    )
    return (
        block_out,
        clip_pool,
        input_grad,
        spatial_new,
        spatial_one,
        spatial_two,
        temporal_new,
        temporal_one,
        temporal_two,
        mid_new,
        mid_one,
        mid_two,
        out_new,
        out_one,
        out_two,
    )


F32 = jnp.float32
BF16 = jnp.bfloat16
MESH = pl.DeviceIdType.MESH
VMEM = pltpu.VMEM
NN = (((1,), (0,)), ((), ()))
NT = (((1,), (1,)), ((), ()))
TN = (((0,), (0,)), ((), ()))
BLOCK_C = 512
MID_C = 1152
ROWS = 784
SLOTS = 16
HALF = 144
TAPS_C = 9 * BLOCK_C
CHIP_S = TAPS_C // 4
CHIP_T = BLOCK_C // 4
PARTS = (("s", 0), ("t", 0), ("s", 1), ("t", 1))
GRANT = 62 * 1024 * 1024


def place():
    dp = lax.axis_index("dp")
    line = lax.axis_index("chan")
    core = lax.rem(dp, 2)
    chip = lax.div(dp, 2)
    x_bit = lax.rem(chip, 2)
    y_bit = lax.div(chip, 2)
    return dict(
        dp=dp,
        line=line,
        core=core,
        chip=chip,
        chip_x=chip + 1 - 2 * x_bit,
        chip_y=chip + 2 - 4 * y_bit,
        chip_d=3 - chip,
        pair=(dp + 1 - 2 * core, line),
        x=(dp + 2 - 4 * x_bit, line),
        y=(dp + 4 - 8 * y_bit, line),
    )


def remote(source, target, send, recv, device):
    return pltpu.make_async_remote_copy(
        src_ref=source,
        dst_ref=target,
        send_sem=send,
        recv_sem=recv,
        device_id=device,
        device_id_type=MESH,
    )


def greet(devices):
    barrier = pltpu.get_barrier_semaphore()
    for device in devices:
        pl.semaphore_signal(barrier, inc=1, device_id=device, device_id_type=MESH)
    pl.semaphore_wait(barrier, len(devices))


def line_peer(at, step):
    return (at["dp"], lax.rem(at["line"] + step, 4))


def gather_kernel(
    ws_in,
    wt_in,
    feat_in,
    cot_in,
    par_in,
    ws_out,
    wt_out,
    feat_out,
    cot_out,
    par_out,
    pair_s,
    pair_t,
    stage_s,
    stage_t,
    pair_send,
    pair_recv,
    act_send,
    act_recv,
    line_send,
    line_recv,
    plane_send,
    plane_recv,
    diag_send,
    diag_recv,
    core_send,
    core_recv,
    own_sem,
):
    at = place()
    line, core, chip = at["line"], at["core"], at["chip"]
    greet([at["pair"], at["x"], at["y"]] + [line_peer(at, step) for step in (1, 2, 3)])

    def area(part, owner_core, owner_chip, first, count):
        kind, unit = part
        lines = pl.ds(first, count)
        if kind == "s":
            lanes = pl.ds(pl.multiple_of(owner_chip * CHIP_S, 128), CHIP_S)
            return ws_out.at[unit, lines, owner_core, :, lanes]
        lanes = pl.ds(pl.multiple_of(owner_chip * CHIP_T, 128), CHIP_T)
        return wt_out.at[unit, :, lines, owner_core, :, lanes]

    started = []

    def send(copy):
        copy.start()
        started.append(copy)

    for index, (kind, unit) in enumerate(PARTS):
        theirs = pl.ds(pl.multiple_of((1 - core) * HALF, 16), HALF)
        source, landing = (ws_in, pair_s) if kind == "s" else (wt_in, pair_t)
        send(
            remote(
                source.at[unit, theirs],
                landing.at[unit],
                pair_send.at[index],
                pair_recv.at[index],
                at["pair"],
            )
        )

    def acts(row, source, target, count):
        def cut(owner):
            return source.at[pl.ds(pl.multiple_of(owner * count, 16), count)]

        lanes = pl.ds(pl.multiple_of(line * 128, 128), 128)
        for step in (1, 2, 3):
            peer = line_peer(at, step)
            send(
                remote(
                    cut(peer[1]),
                    target.at[:, lanes],
                    act_send.at[row, step - 1],
                    act_recv.at[row, step - 1],
                    peer,
                )
            )
        own = pltpu.make_async_copy(cut(line), target.at[:, lanes], own_sem.at[row])
        own.start()
        return own

    def acts_wait(row, source, target, count):
        for step in (1, 2, 3):
            origin = lax.rem(line + 4 - step, 4)
            lanes = pl.ds(pl.multiple_of(origin * 128, 128), 128)
            remote(
                source.at[pl.ds(0, count)],
                target.at[:, lanes],
                act_send.at[row, step - 1],
                act_recv.at[row, step - 1],
                line_peer(at, step),
            ).wait_recv()

    mine = pl.ds(pl.multiple_of(core * HALF, 16), HALF)
    own_copies = []

    def step_line(index):
        part = PARTS[index]
        kind, unit = part
        landing = pair_s if kind == "s" else pair_t
        started[index].wait_recv()
        if kind == "s":
            low = ws_in[unit, mine].astype(F32)
            high = landing[unit].astype(F32)
            first = jnp.where(core == 0, low, high)
            second = jnp.where(core == 0, high, low)
            stage_s[unit, 0] = jnp.concatenate([first, second], axis=1).astype(BF16)
            staged = stage_s.at[unit]
        else:
            low = wt_in[unit, mine].astype(F32)
            high = landing[unit].astype(F32)
            first = jnp.where(core == 0, low, high)
            second = jnp.where(core == 0, high, low)
            for tau in range(3):
                lanes = slice(64 * tau, 64 * tau + 64)
                stage_t[unit, tau, 0] = jnp.concatenate(
                    [first[:, lanes], second[:, lanes]], axis=1
                ).astype(BF16)
            staged = stage_t.at[unit]
        target = area(part, core, chip, line, 1)
        for step in (1, 2, 3):
            send(
                remote(
                    staged,
                    target,
                    line_send.at[index, step - 1],
                    line_recv.at[index, step - 1],
                    line_peer(at, step),
                )
            )
        own = pltpu.make_async_copy(staged, target, own_sem.at[4 + index])
        own.start()
        own_copies.append(own)

    def step_plane(index):
        part = PARTS[index]
        for step in (1, 2, 3):
            origin = area(part, core, chip, lax.rem(line + 4 - step, 4), 1)
            remote(
                origin,
                origin,
                line_send.at[index, step - 1],
                line_recv.at[index, step - 1],
                line_peer(at, step),
            ).wait_recv()
        own_copies[index].wait()
        held = area(part, core, chip, 0, 4)
        for way, name in enumerate(("x", "y")):
            send(
                remote(held, held, plane_send.at[index, way], plane_recv.at[index, way], at[name])
            )
        send(remote(held, held, core_send.at[index, 0], core_recv.at[index, 0], at["pair"]))

    def step_diag(index):
        part = PARTS[index]
        for way, (name, other, first) in enumerate((("x", "y", 0), ("y", "x", 2))):
            held = area(part, core, at["chip_" + name], 0, 4)
            remote(
                held, held, plane_send.at[index, way], plane_recv.at[index, way], at[name]
            ).wait_recv()
            half = area(part, core, at["chip_" + name], first, 2)
            send(
                remote(half, half, diag_send.at[index, way], diag_recv.at[index, way], at[other])
            )
            send(
                remote(
                    held, held, core_send.at[index, 1 + way], core_recv.at[index, 1 + way], at["pair"]
                )
            )

    def step_core(index):
        part = PARTS[index]
        for way, (other, first) in enumerate((("y", 0), ("x", 2))):
            half = area(part, core, at["chip_d"], first, 2)
            remote(
                half, half, diag_send.at[index, way], diag_recv.at[index, way], at[other]
            ).wait_recv()
        held = area(part, core, at["chip_d"], 0, 4)
        send(remote(held, held, core_send.at[index, 3], core_recv.at[index, 3], at["pair"]))

    def step_end(index):
        part = PARTS[index]
        for slot, name in enumerate(("chip", "chip_x", "chip_y", "chip_d")):
            held = area(part, 1 - core, at[name], 0, 4)
            remote(
                held, held, core_send.at[index, slot], core_recv.at[index, slot], at["pair"]
            ).wait_recv()

    step_line(0)
    feat_own = acts(0, feat_in, feat_out, ROWS)
    step_line(1)
    for step in (1, 2, 3):
        send(
            remote(
                par_in,
                par_out.at[line],
                act_send.at[2, step - 1],
                act_recv.at[2, step - 1],
                line_peer(at, step),
            )
        )
    par_own = pltpu.make_async_copy(par_in, par_out.at[line], own_sem.at[2])
    par_own.start()
    step_line(2)
    cot_own = acts(1, cot_in, cot_out, ROWS)
    step_line(3)
    step_plane(0)
    step_plane(1)
    step_diag(0)
    step_plane(2)
    step_diag(1)
    step_core(0)
    step_end(0)
    step_plane(3)
    step_diag(2)
    step_core(1)
    step_end(1)
    step_diag(3)
    step_core(2)
    step_end(2)
    step_core(3)
    step_end(3)
    acts_wait(0, feat_in, feat_out, ROWS)
    acts_wait(1, cot_in, cot_out, ROWS)
    for step in (1, 2, 3):
        remote(
            par_in,
            par_out.at[lax.rem(line + 4 - step, 4)],
            act_send.at[2, step - 1],
            act_recv.at[2, step - 1],
            line_peer(at, step),
        ).wait_recv()
    for own in (feat_own, cot_own, par_own):
        own.wait()
    for copy in started:
        copy.wait_send()


def rows_of(pixel):
    return pl.ds(pl.multiple_of(pixel * SLOTS, SLOTS), SLOTS)


def slope_of(values):
    sigmoid = jax.nn.sigmoid(values)
    return sigmoid * (1.0 + values * (1.0 - sigmoid))


def block_kernel(
    ws,
    wt,
    feat_in,
    cot_in,
    shuffle,
    mask_in,
    mid_in,
    out_in,
    block_out,
    input_out,
    grad_s,
    grad_t,
    mid_grad,
    out_grad,
    a_pad,
    s_ref,
    u_ref,
    t_ref,
    side,
    feat_ref,
    skip_ref,
    wide,
    ds_pad,
    thin,
    d_ref,
    w_buf,
    wt_buf,
    g_buf,
    land_mid,
    land_mid_two,
    land_out,
    land_out_two,
    w_sem,
    wt_sem,
    g_sem,
    one_send,
    one_recv,
    two_send,
    two_recv,
):
    at = place()
    dp, line = at["dp"], at["line"]

    def ring_peer(step):
        return (lax.rem(dp + step, 8), line)

    greet([ring_peer(step) for step in range(1, 8)] + [line_peer(at, step) for step in (1, 2, 3)])

    mask_mid = mask_in[...]
    mask_out = mask_in[:, :BLOCK_C]
    slot_rows = lax.broadcasted_iota(jnp.int32, (SLOTS, BLOCK_C), 0)
    has_before = (slot_rows >= 4).astype(F32)
    has_after = (slot_rows < 12).astype(F32)

    def fetch_w(unit, tap, slot):
        lanes = pl.ds(pl.multiple_of(tap * BLOCK_C, 128), BLOCK_C)
        return pltpu.make_async_copy(ws.at[unit, :, lanes], w_buf.at[slot], w_sem.at[slot])

    def fetch_wt(unit):
        return pltpu.make_async_copy(wt.at[unit], wt_buf, wt_sem.at[0])

    def over_taps(unit, use):
        fetch_w(unit, 0, 0).start()

        def body(tap, carry):
            slot = lax.rem(tap, 2)

            @pl.when(tap < 8)
            def _():
                fetch_w(unit, tap + 1, 1 - slot).start()

            fetch_w(unit, tap, slot).wait()
            use(tap, slot)
            return carry

        lax.fori_loop(0, 9, body, 0)

    def over_pixels(body, carry):
        return lax.fori_loop(0, HW, body, carry)

    def exchange(land, land_two, index, sem_index, count, payload, combine):
        for row, value in enumerate(payload):
            land[index, dp, row : row + 1, :] = value
        sent = []
        for step in range(1, 8):
            here = land.at[index, dp, pl.ds(0, count)]
            copy = remote(
                here,
                here,
                one_send.at[sem_index, step - 1],
                one_recv.at[sem_index, step - 1],
                ring_peer(step),
            )
            copy.start()
            sent.append(copy)
        for step in range(1, 8):
            there = land.at[index, lax.rem(dp + 8 - step, 8), pl.ds(0, count)]
            remote(
                there,
                there,
                one_send.at[sem_index, step - 1],
                one_recv.at[sem_index, step - 1],
                ring_peer(step),
            ).wait_recv()
        for copy in sent:
            copy.wait_send()
        merged = combine([land[index, source] for source in range(8)])
        for row, value in enumerate(merged):
            land_two[index, line, row : row + 1, :] = value
        sent = []
        for step in (1, 2, 3):
            here = land_two.at[index, line, pl.ds(0, count)]
            copy = remote(
                here,
                here,
                two_send.at[sem_index, step - 1],
                two_recv.at[sem_index, step - 1],
                line_peer(at, step),
            )
            copy.start()
            sent.append(copy)
        for step in (1, 2, 3):
            there = land_two.at[index, lax.rem(line + 4 - step, 4), pl.ds(0, count)]
            remote(
                there,
                there,
                two_send.at[sem_index, step - 1],
                two_recv.at[sem_index, step - 1],
                line_peer(at, step),
            ).wait_recv()
        for copy in sent:
            copy.wait_send()
        return combine([land_two[index, source] for source in range(4)])

    def combine_moments(blocks):
        total = sum(block[2:3] for block in blocks)
        mean = sum(block[2:3] * block[0:1] for block in blocks) / total
        spread = sum(
            block[1:2] + block[2:3] * (block[0:1] - mean) * (block[0:1] - mean) for block in blocks
        )
        return [mean, spread, total]

    def combine_sums(blocks):
        return [sum(block[0:1] for block in blocks), sum(block[1:2] for block in blocks)]

    def moments(values, mask, land, land_two, index, sem_index):
        width = mask.shape[1]
        zero = jnp.zeros((SLOTS, width), F32)
        local = HW * jnp.sum(mask, axis=0, keepdims=True)
        added = over_pixels(lambda p, acc: acc + values[rows_of(p), :], zero)
        mean = jnp.sum(added * mask, axis=0, keepdims=True) / local

        def squares(p, acc):
            centered = values[rows_of(p), :] - mean
            return acc + centered * centered

        spread = jnp.sum(over_pixels(squares, zero) * mask, axis=0, keepdims=True)
        mean, spread, total = exchange(
            land, land_two, index, sem_index, 4, [mean, spread, local, local], combine_moments_four
        )
        return mean, lax.rsqrt(spread / total + EPS_NORM), total

    def combine_moments_four(blocks):
        mean, spread, total = combine_moments(blocks)
        return [mean, spread, total]

    for unit in range(2):
        a_pad[unit] = jnp.zeros(a_pad.shape[1:], BF16)
    ds_pad[...] = jnp.zeros(ds_pad.shape, BF16)
    fetch_wt(0).start()
    permute = shuffle[...]
    feat_ref[...] = lax.dot_general(permute, feat_in[...], NN, preferred_element_type=F32).astype(
        BF16
    )

    def fill(p, carry):
        a_pad[0, 1 + p // SIDE, 1 + p % SIDE] = feat_ref[rows_of(p), :]
        return carry

    over_pixels(fill, 0)

    def window(unit, tap):
        return a_pad[unit, pl.ds(tap // 3, SIDE), pl.ds(tap % 3, SIDE)].reshape(ROWS, BLOCK_C)

    stats_mid = []
    stats_out = []
    for unit in range(2):
        gain, bias = mid_in[2 * unit : 2 * unit + 1], mid_in[2 * unit + 1 : 2 * unit + 2]

        def conv(tap, slot):
            value = lax.dot_general(
                window(unit, tap), w_buf[slot], NT, preferred_element_type=F32
            )

            @pl.when(tap == 0)
            def _():
                s_ref[unit] = value

            @pl.when(tap > 0)
            def _():
                s_ref[unit] = s_ref[unit] + value

        over_taps(unit, conv)
        mean, inverse, total = moments(
            s_ref.at[unit], mask_mid, land_mid, land_mid_two, unit, 2 * unit
        )
        stats_mid.append((inverse, total))

        def mid_act(p, carry):
            rows = rows_of(p)
            standard = (s_ref[unit, rows, :] - mean) * inverse
            s_ref[unit, rows, :] = standard
            normed = standard * gain + bias
            u_ref[unit, rows, :] = (jax.nn.sigmoid(normed) * normed * mask_mid).astype(BF16)
            return carry

        over_pixels(mid_act, 0)
        fetch_wt(unit).wait()
        t_ref[unit] = lax.dot_general(u_ref[unit], wt_buf[1], NN, preferred_element_type=F32)
        side[0] = lax.dot_general(u_ref[unit], wt_buf[0], NN, preferred_element_type=F32)
        side[1] = lax.dot_general(u_ref[unit], wt_buf[2], NN, preferred_element_type=F32)
        if unit == 0:
            fetch_wt(1).start()

        def frames(p, carry):
            rows = rows_of(p)
            t_ref[unit, rows, :] = (
                t_ref[unit, rows, :]
                + pltpu.roll(side[0, rows, :], 4, 0) * has_before
                + pltpu.roll(side[1, rows, :], 12, 0) * has_after
            )
            return carry

        over_pixels(frames, 0)
        mean, inverse, total = moments(
            t_ref.at[unit], mask_out, land_out, land_out_two, unit, 2 * unit + 1
        )
        stats_out.append((inverse, total))
        gain, bias = out_in[2 * unit : 2 * unit + 1], out_in[2 * unit + 1 : 2 * unit + 2]
        if unit == 0:

            def out_act(p, carry):
                rows = rows_of(p)
                standard = (t_ref[0, rows, :] - mean) * inverse
                t_ref[0, rows, :] = standard
                normed = standard * gain + bias
                hidden = jax.nn.sigmoid(normed) * normed * mask_out
                a_pad[1, 1 + p // SIDE, 1 + p % SIDE] = hidden.astype(BF16)
                return carry

            over_pixels(out_act, 0)
        else:
            side[0] = lax.dot_general(permute, cot_in[...], NN, preferred_element_type=F32)

            def end_act(p, carry):
                rows = rows_of(p)
                standard = (t_ref[1, rows, :] - mean) * inverse
                t_ref[1, rows, :] = standard
                pre = standard * gain + bias + feat_ref[rows, :].astype(F32)
                sigmoid = jax.nn.sigmoid(pre)
                thin[rows, :] = (pre * sigmoid * mask_out).astype(BF16)
                slope = sigmoid * (1.0 + pre * (1.0 - sigmoid))
                skip = side[0, rows, :] * mask_out * slope
                skip_ref[rows, :] = skip
                side[1, rows, :] = skip
                return carry

            over_pixels(end_act, 0)
            block_out[...] = lax.dot_general(
                permute, thin[...], TN, preferred_element_type=F32
            ).astype(BF16)

    zero_mid = jnp.zeros((SLOTS, MID_C), F32)
    zero_out = jnp.zeros((SLOTS, BLOCK_C), F32)

    def put_grad(target, slot):
        return pltpu.make_async_copy(g_buf.at[slot], target, g_sem.at[slot])

    for unit in (1, 0):
        gain = out_in[2 * unit : 2 * unit + 1]
        inverse, total = stats_out[unit]

        def out_sums(p, carry):
            rows = rows_of(p)
            grad = side[1, rows, :]
            return (carry[0] + grad, carry[1] + grad * t_ref[unit, rows, :])

        bias_acc, gain_acc = over_pixels(out_sums, (zero_out, zero_out))
        sums = [
            jnp.sum(bias_acc, axis=0, keepdims=True),
            jnp.sum(gain_acc, axis=0, keepdims=True),
        ]
        grad_bias, grad_gain = exchange(
            land_out, land_out_two, 2 + unit, 5 + 2 * unit, 2, sums, combine_sums
        )
        out_grad[2 * unit : 2 * unit + 1, :] = grad_gain
        out_grad[2 * unit + 1 : 2 * unit + 2, :] = grad_bias
        scale = gain * inverse
        bias_part, gain_part = grad_bias / total, grad_gain / total

        def out_back(p, carry):
            rows = rows_of(p)
            value = (
                mask_out
                * scale
                * (side[1, rows, :] - bias_part - t_ref[unit, rows, :] * gain_part)
            )
            d_ref[1, rows, :] = value.astype(BF16)
            d_ref[0, rows, :] = (pltpu.roll(value, 12, 0) * has_after).astype(BF16)
            d_ref[2, rows, :] = (pltpu.roll(value, 4, 0) * has_before).astype(BF16)
            return carry

        over_pixels(out_back, 0)
        if unit == 0:
            fetch_wt(0).wait()

        for tau in range(3):
            slot = tau % 2
            if tau == 2:
                put_grad(grad_t.at[unit, 0], slot).wait()
            g_buf[slot] = lax.dot_general(
                u_ref[unit], d_ref[tau], TN, preferred_element_type=F32
            ).astype(BF16)
            put_grad(grad_t.at[unit, tau], slot).start()
            value = lax.dot_general(d_ref[tau], wt_buf[tau], NT, preferred_element_type=F32)
            wide[...] = value if tau == 0 else wide[...] + value
        put_grad(grad_t.at[unit, 1], 1).wait()
        put_grad(grad_t.at[unit, 2], 0).wait()
        if unit == 1:
            fetch_wt(0).start()

        gain, bias = mid_in[2 * unit : 2 * unit + 1], mid_in[2 * unit + 1 : 2 * unit + 2]
        inverse, total = stats_mid[unit]

        def mid_sums(p, carry):
            rows = rows_of(p)
            standard = s_ref[unit, rows, :]
            grad = mask_mid * slope_of(standard * gain + bias) * wide[rows, :]
            wide[rows, :] = grad
            return (carry[0] + grad, carry[1] + grad * standard)

        bias_acc, gain_acc = over_pixels(mid_sums, (zero_mid, zero_mid))
        sums = [
            jnp.sum(bias_acc, axis=0, keepdims=True),
            jnp.sum(gain_acc, axis=0, keepdims=True),
        ]
        grad_bias, grad_gain = exchange(
            land_mid, land_mid_two, 2 + unit, 4 + 2 * unit, 2, sums, combine_sums
        )
        mid_grad[2 * unit : 2 * unit + 1, :] = grad_gain
        mid_grad[2 * unit + 1 : 2 * unit + 2, :] = grad_bias
        scale = gain * inverse
        bias_part, gain_part = grad_bias / total, grad_gain / total

        def mid_back(p, carry):
            rows = rows_of(p)
            value = (
                mask_mid
                * scale
                * (wide[rows, :] - bias_part - s_ref[unit, rows, :] * gain_part)
            )
            ds_pad[1 + p // SIDE, 1 + p % SIDE] = value.astype(BF16)
            return carry

        over_pixels(mid_back, 0)

        def grad_lanes(tap):
            return grad_s.at[unit, :, pl.ds(pl.multiple_of(tap * BLOCK_C, 128), BLOCK_C)]

        def back(tap, slot):
            @pl.when(tap >= 2)
            def _():
                put_grad(grad_lanes(tap - 2), slot).wait()

            inner = ds_pad[1 : 1 + SIDE, 1 : 1 + SIDE].reshape(ROWS, MID_C)
            g_buf[slot] = lax.dot_general(
                inner, window(unit, tap), TN, preferred_element_type=F32
            ).astype(BF16)
            put_grad(grad_lanes(tap), slot).start()
            moved = ds_pad[pl.ds(2 - tap // 3, SIDE), pl.ds(2 - tap % 3, SIDE)].reshape(ROWS, MID_C)
            value = lax.dot_general(moved, w_buf[slot], NN, preferred_element_type=F32)

            @pl.when(tap == 0)
            def _():
                side[0] = value

            @pl.when(tap > 0)
            def _():
                side[0] = side[0] + value

        over_taps(unit, back)
        put_grad(grad_lanes(7), 1).wait()
        put_grad(grad_lanes(8), 0).wait()
        if unit == 1:
            gain, bias = out_in[0:1], out_in[1:2]

            def hidden_back(p, carry):
                rows = rows_of(p)
                slope = slope_of(t_ref[0, rows, :] * gain + bias)
                side[1, rows, :] = mask_out * slope * side[0, rows, :]
                return carry

            over_pixels(hidden_back, 0)

    thin[...] = (side[0] + skip_ref[...]).astype(BF16)
    input_out[...] = lax.dot_general(permute, thin[...], TN, preferred_element_type=F32).astype(
        BF16
    )


def scatter_kernel(
    grad_s,
    grad_t,
    block_in,
    input_in,
    sum_s,
    sum_t,
    block_out,
    input_out,
    own_s,
    own_t,
    land_s,
    land_t,
    one_s,
    one_t,
    two_s,
    two_t,
    part_s,
    part_t,
    line_s,
    line_t,
    fin_s,
    fin_t,
    act_send,
    act_recv,
    core_send,
    core_recv,
    one_send,
    one_recv,
    two_send,
    two_recv,
    line_send,
    line_recv,
    fin_send,
    fin_recv,
    own_sem,
):
    at = place()
    line, core, chip = at["line"], at["core"], at["chip"]
    greet([at["pair"], at["x"], at["y"]] + [line_peer(at, step) for step in (1, 2, 3)])
    started = []

    def send(copy):
        copy.start()
        started.append(copy)

    def pick(part, small, large):
        return large if part[0] == "s" else small

    def grads(part, half):
        if part[0] == "s":
            return grad_s.at[part[1], :, half]
        return grad_t.at[part[1], :, :, half]

    def lanes_of(part, owner):
        width = pick(part, CHIP_T, CHIP_S)
        return pl.ds(pl.multiple_of(owner * width, 128), width)

    def cut(part, owner, first, count):
        ref = pick(part, own_t, own_s)
        lanes = lanes_of(part, owner)
        if part[0] == "s":
            return ref.at[part[1], pl.ds(first, count), :, lanes]
        return ref.at[part[1], :, pl.ds(first, count), :, lanes]

    def some(ref, part, first, count):
        if part[0] == "s":
            return ref.at[part[1], pl.ds(first, count)]
        return ref.at[part[1], :, pl.ds(first, count)]

    own_copies = []
    for index, part in enumerate(PARTS):
        landing = pick(part, land_t, land_s).at[part[1]]
        send(
            remote(
                grads(part, 1 - core),
                landing,
                core_send.at[index],
                core_recv.at[index],
                at["pair"],
            )
        )
        own = pltpu.make_async_copy(
            grads(part, core), pick(part, own_t, own_s).at[part[1]], own_sem.at[index]
        )
        own.start()
        own_copies.append(own)
    act_copies = []
    lanes_line = pl.ds(pl.multiple_of(line * 128, 128), 128)
    rows_line = pl.ds(pl.multiple_of(line * ROWS, 16), ROWS)
    for row, (source, target) in enumerate(((block_in, block_out), (input_in, input_out))):
        for step in (1, 2, 3):
            peer = line_peer(at, step)
            send(
                remote(
                    source.at[:, pl.ds(pl.multiple_of(peer[1] * 128, 128), 128)],
                    target.at[rows_line],
                    act_send.at[row, step - 1],
                    act_recv.at[row, step - 1],
                    peer,
                )
            )
        own = pltpu.make_async_copy(
            source.at[:, lanes_line], target.at[rows_line], own_sem.at[4 + row]
        )
        own.start()
        act_copies.append(own)

    def add_into(target, source, shape):
        outer = int(np.prod(shape[:-2]))
        step = 16 if shape[-1] > 2048 else HALF
        per = HALF // step

        def body(index, carry):
            place_in = lax.div(index, per)
            rows = pl.ds(pl.multiple_of(lax.rem(index, per) * step, 16), step)
            if len(shape) == 3:
                where = (place_in, rows)
            else:
                where = (lax.div(place_in, shape[1]), lax.rem(place_in, shape[1]), rows)
            target[where] = (target[where].astype(F32) + source[where].astype(F32)).astype(BF16)
            return carry

        lax.fori_loop(0, outer * per, body, 0)

    def step_one(index):
        part = PARTS[index]
        own_copies[index].wait()
        started[index].wait_recv()
        own, land = pick(part, own_t, own_s).at[part[1]], pick(part, land_t, land_s).at[part[1]]
        add_into(own, land, own.shape)
        ones, twos = pick(part, one_t, one_s), pick(part, two_t, two_s)
        for way, (name, first) in enumerate((("x", 0), ("y", 2))):
            send(
                remote(
                    cut(part, at["chip_d"], first, 2),
                    ones.at[part[1], way],
                    one_send.at[index, way],
                    one_recv.at[index, way],
                    at[name],
                )
            )
            send(
                remote(
                    cut(part, at["chip_" + name], first, 2),
                    some(twos.at[:, way], part, first, 2),
                    two_send.at[index, way, 0],
                    two_recv.at[index, way, 0],
                    at[name],
                )
            )

    def step_two(index):
        part = PARTS[index]
        ones, twos = pick(part, one_t, one_s), pick(part, two_t, two_s)
        for way, (name, other, first) in enumerate((("x", "y", 0), ("y", "x", 2))):
            landing = ones.at[part[1], way]
            remote(
                landing,
                landing,
                one_send.at[index, way],
                one_recv.at[index, way],
                at[name],
            ).wait_recv()
            target = cut(part, at["chip_" + other], first, 2)
            add_into(target, landing, target.shape)
            send(
                remote(
                    target,
                    some(twos.at[:, 1 - way], part, first, 2),
                    two_send.at[index, 1 - way, 1],
                    two_recv.at[index, 1 - way, 1],
                    at[other],
                )
            )

    def step_three(index):
        part = PARTS[index]
        unit = part[1]
        twos = pick(part, two_t, two_s)
        for way, (name, first) in enumerate((("x", 0), ("y", 2))):
            for turn, begin in enumerate((first, 2 - first)):
                landing = some(twos.at[:, way], part, begin, 2)
                remote(
                    landing,
                    landing,
                    two_send.at[index, way, turn],
                    two_recv.at[index, way, turn],
                    at[name],
                ).wait_recv()
        own = cut(part, chip, 0, 4)
        target = pick(part, part_t, part_s)

        def body(owner, carry):
            if part[0] == "s":
                target[unit, owner] = (
                    own[owner].astype(F32)
                    + twos[unit, 0, owner].astype(F32)
                    + twos[unit, 1, owner].astype(F32)
                ).astype(BF16)
            else:
                for tau in range(3):
                    target[unit, owner, tau] = (
                        own[tau, owner].astype(F32)
                        + twos[unit, 0, tau, owner].astype(F32)
                        + twos[unit, 1, tau, owner].astype(F32)
                    ).astype(BF16)
            return carry

        lax.fori_loop(0, 4, body, 0)
        lines = pick(part, line_t, line_s)
        for step in (1, 2, 3):
            peer = line_peer(at, step)
            send(
                remote(
                    target.at[unit, peer[1]],
                    lines.at[unit, step - 1],
                    line_send.at[index, step - 1],
                    line_recv.at[index, step - 1],
                    peer,
                )
            )

    fin_copies = [None] * 4

    def step_four(index):
        part = PARTS[index]
        unit = part[1]
        lines, target, fin = (
            pick(part, line_t, line_s),
            pick(part, part_t, part_s),
            pick(part, fin_t, fin_s),
        )
        for step in (1, 2, 3):
            landing = lines.at[unit, step - 1]
            remote(
                landing,
                landing,
                line_send.at[index, step - 1],
                line_recv.at[index, step - 1],
                line_peer(at, step),
            ).wait_recv()
        total = target[unit, line].astype(F32)
        for step in range(3):
            total = total + lines[unit, step].astype(F32)
        fin[unit, 0] = total
        copy = remote(
            fin.at[unit, 0], fin.at[unit, 1], fin_send.at[index], fin_recv.at[index], at["pair"]
        )
        send(copy)
        fin_copies[index] = copy

    def step_five(index):
        part = PARTS[index]
        unit = part[1]
        fin_copies[index].wait_recv()
        fin = pick(part, fin_t, fin_s)
        for which in range(2):
            half = core if which == 0 else 1 - core
            rows = pl.ds(pl.multiple_of(half * HALF, 16), HALF)
            if part[0] == "s":
                value = fin[unit, which]
                width = CHIP_S // 2
                sum_s[unit, rows, :] = jnp.where(core == 0, value[:, :width], value[:, width:])
            else:
                width = CHIP_T // 2
                for tau in range(3):
                    value = fin[unit, which, tau]
                    sum_t[unit, tau, rows, :] = jnp.where(
                        core == 0, value[:, :width], value[:, width:]
                    )

    order = (2, 3, 1, 0)
    step_one(order[0])
    step_one(order[1])
    step_two(order[0])
    step_one(order[2])
    step_two(order[1])
    step_one(order[3])
    step_three(order[0])
    step_two(order[2])
    step_three(order[1])
    step_two(order[3])
    step_four(order[0])
    step_three(order[2])
    step_four(order[1])
    step_three(order[3])
    step_five(order[0])
    step_five(order[1])
    step_four(order[2])
    step_five(order[2])
    step_four(order[3])
    step_five(order[3])
    for row, (source, target) in enumerate(((block_in, block_out), (input_in, input_out))):
        for step in (1, 2, 3):
            origin = lax.rem(line + 4 - step, 4)
            remote(
                source.at[:, lanes_line],
                target.at[pl.ds(pl.multiple_of(origin * ROWS, 16), ROWS)],
                act_send.at[row, step - 1],
                act_recv.at[row, step - 1],
                line_peer(at, step),
            ).wait_recv()
        act_copies[row].wait()
    for copy in started:
        copy.wait_send()


def spaces(text):
    return [pl.BlockSpec(memory_space=VMEM if mark == "v" else pl.ANY) for mark in text]


def dma(*shape):
    return pltpu.SemaphoreType.DMA(shape)


def params(number):
    return pltpu.CompilerParams(
        collective_id=number, has_side_effects=True, vmem_limit_bytes=GRANT
    )


def gather_all(ws, wt, feat, cot, par):
    return pl.pallas_call(
        gather_kernel,
        out_shape=[
            jax.ShapeDtypeStruct((2, 4, 2, HALF, TAPS_C), BF16),
            jax.ShapeDtypeStruct((2, 3, 4, 2, HALF, BLOCK_C), BF16),
            jax.ShapeDtypeStruct((ROWS, BLOCK_C), BF16),
            jax.ShapeDtypeStruct((ROWS, BLOCK_C), BF16),
            jax.ShapeDtypeStruct((4,) + par.shape, F32),
        ],
        in_specs=spaces("vvaav"),
        out_specs=spaces("aaaaa"),
        scratch_shapes=[
            VMEM((2, HALF, CHIP_S // 2), BF16),
            VMEM((2, HALF, 3 * CHIP_T // 2), BF16),
            VMEM((2, 1, HALF, CHIP_S), BF16),
            VMEM((2, 3, 1, HALF, CHIP_T), BF16),
            dma(4),
            dma(4),
            dma(3, 3),
            dma(3, 3),
            dma(4, 3),
            dma(4, 3),
            dma(4, 2),
            dma(4, 2),
            dma(4, 2),
            dma(4, 2),
            dma(4, 4),
            dma(4, 4),
            dma(8),
        ],
        compiler_params=params(0),
        name="gather_all",
    )(ws, wt, feat, cot, par)


def run_block(ws, wt, feat, cot, shuffle, mask, mid, out):
    return pl.pallas_call(
        block_kernel,
        out_shape=[
            jax.ShapeDtypeStruct((ROWS, BLOCK_C), BF16),
            jax.ShapeDtypeStruct((ROWS, BLOCK_C), BF16),
            jax.ShapeDtypeStruct((2, MID_C, TAPS_C), BF16),
            jax.ShapeDtypeStruct((2, 3, MID_C, BLOCK_C), BF16),
            jax.ShapeDtypeStruct((4, MID_C), F32),
            jax.ShapeDtypeStruct((4, BLOCK_C), F32),
        ],
        in_specs=spaces("aavvvvvv"),
        out_specs=spaces("vvaavv"),
        scratch_shapes=[
            VMEM((2, SIDE + 2, SIDE + 2, SLOTS, BLOCK_C), BF16),
            VMEM((2, ROWS, MID_C), F32),
            VMEM((2, ROWS, MID_C), BF16),
            VMEM((2, ROWS, BLOCK_C), F32),
            VMEM((2, ROWS, BLOCK_C), F32),
            VMEM((ROWS, BLOCK_C), BF16),
            VMEM((ROWS, BLOCK_C), F32),
            VMEM((ROWS, MID_C), F32),
            VMEM((SIDE + 2, SIDE + 2, SLOTS, MID_C), BF16),
            VMEM((ROWS, BLOCK_C), BF16),
            VMEM((3, ROWS, BLOCK_C), BF16),
            VMEM((2, MID_C, BLOCK_C), BF16),
            VMEM((3, MID_C, BLOCK_C), BF16),
            VMEM((2, MID_C, BLOCK_C), BF16),
            VMEM((4, 8, 8, MID_C), F32),
            VMEM((4, 4, 8, MID_C), F32),
            VMEM((4, 8, 8, BLOCK_C), F32),
            VMEM((4, 4, 8, BLOCK_C), F32),
            dma(2),
            dma(1),
            dma(2),
            dma(8, 7),
            dma(8, 7),
            dma(8, 3),
            dma(8, 3),
        ],
        compiler_params=params(1),
        name="run_block",
    )(ws, wt, feat, cot, shuffle, mask, mid, out)


def scatter_all(grad_s, grad_t, block, grad_in):
    return pl.pallas_call(
        scatter_kernel,
        out_shape=[
            jax.ShapeDtypeStruct((2, 2 * HALF, CHIP_S // 2), F32),
            jax.ShapeDtypeStruct((2, 3, 2 * HALF, CHIP_T // 2), F32),
            jax.ShapeDtypeStruct((4 * ROWS, 128), BF16),
            jax.ShapeDtypeStruct((4 * ROWS, 128), BF16),
        ],
        in_specs=spaces("aavv"),
        out_specs=spaces("vvaa"),
        scratch_shapes=[
            VMEM((2, 4, HALF, TAPS_C), BF16),
            VMEM((2, 3, 4, HALF, BLOCK_C), BF16),
            VMEM((2, 4, HALF, TAPS_C), BF16),
            VMEM((2, 3, 4, HALF, BLOCK_C), BF16),
            VMEM((2, 2, 2, HALF, CHIP_S), BF16),
            VMEM((2, 2, 3, 2, HALF, CHIP_T), BF16),
            VMEM((2, 2, 4, HALF, CHIP_S), BF16),
            VMEM((2, 2, 3, 4, HALF, CHIP_T), BF16),
            VMEM((2, 4, HALF, CHIP_S), BF16),
            VMEM((2, 4, 3, HALF, CHIP_T), BF16),
            VMEM((2, 3, HALF, CHIP_S), BF16),
            VMEM((2, 3, 3, HALF, CHIP_T), BF16),
            VMEM((2, 2, HALF, CHIP_S), F32),
            VMEM((2, 2, 3, HALF, CHIP_T), F32),
            dma(2, 3),
            dma(2, 3),
            dma(4),
            dma(4),
            dma(4, 2),
            dma(4, 2),
            dma(4, 2, 2),
            dma(4, 2, 2),
            dma(4, 3),
            dma(4, 3),
            dma(4),
            dma(4),
            dma(8),
        ],
        compiler_params=params(2),
        name="scatter_all",
    )(grad_s, grad_t, block, grad_in)


def shuffle_matrix():
    clip, frame, pixel = np.meshgrid(np.arange(4), np.arange(FRAMES), np.arange(HW), indexing="ij")
    source = (clip * FRAMES + frame) * HW + pixel
    target = pixel * SLOTS + frame * 4 + clip
    matrix = np.zeros((ROWS, ROWS), np.float32)
    matrix[target.reshape(-1), source.reshape(-1)] = 1.0
    return jnp.asarray(matrix, BF16)


def on_pairs(
    features,
    cotangent,
    clip_frames,
    spatial_master,
    spatial_first,
    spatial_second,
    temporal_master,
    temporal_first,
    temporal_second,
    mid_norm,
    mid_first,
    mid_second,
    out_norm,
    out_first,
    out_second,
):
    line = lax.axis_index("chan")
    ws_own = jnp.swapaxes(spatial_master, 1, 2).astype(BF16)
    wt_own = (
        jnp.swapaxes(temporal_master, 1, 2).reshape(2, 2 * HALF, 3 * CHIP_T // 2).astype(BF16)
    )
    norm_pack = jnp.pad(
        jnp.concatenate([mid_norm, out_norm], axis=1), ((0, 4), (0, 96))
    )
    ws, wt, feat, cot, norm_all = gather_all(
        ws_own, wt_own, features, cotangent.astype(BF16), norm_pack
    )
    width = mid_norm.shape[1]
    mid = jnp.swapaxes(norm_all[:, :4, :width], 0, 1).reshape(4, MID_C)
    out = jnp.swapaxes(norm_all[:, :4, width : width + 128], 0, 1).reshape(4, BLOCK_C)
    kept = clip_frames // 8
    kept_own = lax.dynamic_slice_in_dim(kept, line * 4, 4)
    frame_ids = jnp.arange(FRAMES, dtype=jnp.int32)
    mask = (frame_ids[:, None] < kept_own[None, :]).astype(F32).reshape(SLOTS, 1)
    mask = jnp.broadcast_to(mask, (SLOTS, MID_C))
    block, grad_in, grad_s, grad_t, mid_all, out_all = run_block(
        ws.reshape(2, MID_C, TAPS_C),
        wt.reshape(2, 3, MID_C, BLOCK_C),
        feat,
        cot,
        shuffle_matrix(),
        mask,
        mid,
        out,
    )
    sum_s, sum_t, block_rows, grad_rows = scatter_all(
        grad_s.reshape(2, 4, 2, HALF, TAPS_C),
        grad_t.reshape(2, 3, 4, 2, HALF, BLOCK_C),
        block,
        grad_in,
    )
    block_out = block_rows.astype(F32)
    clip_pool = (
        jnp.sum(block_out.reshape(-1, FRAMES * HW, block_out.shape[1]), axis=1)
        / (HW * kept.astype(F32))[:, None]
    )
    mid_grad = lax.dynamic_slice_in_dim(mid_all, line * width, width, axis=1)
    out_grad = lax.dynamic_slice_in_dim(out_all, line * 128, 128, axis=1)
    spatial = adam_update(
        spatial_master,
        spatial_first,
        spatial_second,
        jnp.swapaxes(sum_s, 1, 2),
        RATE_CONV,
        DECAY_CONV,
    )
    temporal = adam_update(
        temporal_master, temporal_first, temporal_second, sum_t, RATE_CONV, DECAY_CONV
    )
    mid_new = adam_update(mid_norm, mid_first, mid_second, mid_grad, RATE_NORM, 0.0)
    out_new = adam_update(out_norm, out_first, out_second, out_grad, RATE_NORM, 0.0)
    return (
        (block_out, clip_pool, grad_rows.astype(F32)) + spatial + temporal + mid_new + out_new
    )


def solution(mesh):
    in_specs = (
        P("dp", "chan"),
        P("dp", "chan"),
        P("dp"),
        P(None, "dp", "chan"),
        P(None, "dp", "chan"),
        P(None, "dp", "chan"),
        P(None, None, "chan", "dp"),
        P(None, None, "chan", "dp"),
        P(None, None, "chan", "dp"),
        P(None, "chan"),
        P(None, "chan"),
        P(None, "chan"),
        P(None, "chan"),
        P(None, "chan"),
        P(None, "chan"),
    )
    out_specs = (
        P("dp", "chan"),
        P("dp", "chan"),
        P("dp", "chan"),
        P(None, "dp", "chan"),
        P(None, "dp", "chan"),
        P(None, "dp", "chan"),
        P(None, None, "chan", "dp"),
        P(None, None, "chan", "dp"),
        P(None, None, "chan", "dp"),
        P(None, "chan"),
        P(None, "chan"),
        P(None, "chan"),
        P(None, "chan"),
        P(None, "chan"),
        P(None, "chan"),
    )
    body = on_pairs if mesh.shape["dp"] == 8 and mesh.shape["chan"] == 4 else on_device
    return jax.shard_map(
        body, mesh=mesh, in_specs=in_specs, out_specs=out_specs, check_vma=False
    )
```

```python
import jax
import jax.numpy as jnp
import numpy as np
from jax import lax
from jax.experimental import pallas as pl
from jax.experimental.pallas import tpu as pltpu
from jax.sharding import PartitionSpec as P

FRAMES = 4
SIDE = 7
STEP = 10
HW = 49


EPS_NORM = 1e-05
EPS_ADAM = 1e-08
BETA_ONE = 0.9
BETA_TWO = 0.95
RATE_CONV = 0.01
RATE_NORM = 0.8
DECAY_CONV = 0.05


def frame_mask(clip_frames):
    kept_frames = clip_frames // 8
    frame_ids = jnp.arange(FRAMES, dtype=jnp.int32)
    frame_grid = (frame_ids[None, :] < kept_frames[:, None]).astype(jnp.float32)
    return jnp.broadcast_to(frame_grid[:, :, None], (kept_frames.shape[0], FRAMES, HW)).reshape(
        -1, 1
    )


def silu_slope(values):
    sigmoid = jax.nn.sigmoid(values)
    return sigmoid * (1.0 + values * (1.0 - sigmoid))


def spatial_apply(inputs, tap_weights):
    channels = inputs.shape[1]
    padded = jnp.pad(inputs.reshape(-1, SIDE, SIDE, channels), ((0, 0), (1, 1), (1, 1), (0, 0)))
    summed = jnp.zeros((inputs.shape[0], tap_weights.shape[2]), jnp.float32)
    for tap_index in range(9):
        row_off, col_off = (tap_index // 3, tap_index % 3)
        window = padded[:, row_off : row_off + SIDE, col_off : col_off + SIDE].reshape(-1, channels)
        summed = summed + jnp.dot(
            window, tap_weights[tap_index], preferred_element_type=jnp.float32
        )
    return (summed, padded)


def spatial_grads(padded, tap_weights, grad_out):
    channels = padded.shape[3]
    weight_terms = []
    input_sum = jnp.zeros((padded.shape[0], SIDE, SIDE, channels), jnp.float32)
    for tap_index in range(9):
        row_off, col_off = (tap_index // 3, tap_index % 3)
        window = padded[:, row_off : row_off + SIDE, col_off : col_off + SIDE].reshape(-1, channels)
        weight_terms.append(
            lax.dot_general(
                window, grad_out, (((0,), (0,)), ((), ())), preferred_element_type=jnp.float32
            )
        )
        pulled = lax.dot_general(
            grad_out,
            tap_weights[tap_index],
            (((1,), (1,)), ((), ())),
            preferred_element_type=jnp.float32,
        )
        pulled = jnp.pad(pulled.reshape(-1, SIDE, SIDE, channels), ((0, 0), (1, 1), (1, 1), (0, 0)))
        input_sum = (
            input_sum
            + pulled[:, 2 - row_off : 2 - row_off + SIDE, 2 - col_off : 2 - col_off + SIDE]
        )
    return (jnp.stack(weight_terms).reshape(-1, grad_out.shape[1]), input_sum.reshape(-1, channels))


def temporal_apply(inputs, weight):
    frame_seq = inputs.reshape(-1, FRAMES, HW, inputs.shape[1])
    padded = jnp.pad(frame_seq, ((0, 0), (1, 1), (0, 0), (0, 0)))
    summed = jnp.zeros(frame_seq.shape[:3] + (weight.shape[2],), jnp.float32)
    for frame_off in range(3):
        summed = summed + jnp.einsum(
            "nfpm,mc->nfpc",
            padded[:, frame_off : frame_off + FRAMES],
            weight[frame_off],
            preferred_element_type=jnp.float32,
        )
    return (summed.reshape(inputs.shape[0], -1), padded)


def temporal_grads(padded, weight, grad_full):
    grad_seq = grad_full.reshape(-1, FRAMES, HW, grad_full.shape[1])
    grad_pad = jnp.pad(grad_seq, ((0, 0), (1, 1), (0, 0), (0, 0)))
    weight_terms = []
    input_sum = jnp.zeros(padded.shape[:1] + (FRAMES, HW, padded.shape[3]), jnp.float32)
    for frame_off in range(3):
        weight_terms.append(
            jnp.einsum(
                "nfpm,nfpc->mc",
                padded[:, frame_off : frame_off + FRAMES],
                grad_seq,
                preferred_element_type=jnp.float32,
            )
        )
        input_sum = input_sum + jnp.einsum(
            "nfpc,mc->nfpm",
            grad_pad[:, 2 - frame_off : 2 - frame_off + FRAMES],
            weight[frame_off],
            preferred_element_type=jnp.float32,
        )
    return (jnp.stack(weight_terms), input_sum.reshape(grad_full.shape[0], -1))


def normalize(values, validity, gain_row, bias_row):
    local_valid = jnp.sum(validity)
    total_valid, value_sums = lax.psum((local_valid, jnp.sum(values * validity, axis=0)), "dp")
    average = value_sums / total_valid
    centered = values - average
    variance = lax.psum(jnp.sum(validity * centered * centered, axis=0), "dp") / total_valid
    inverse = lax.rsqrt(variance + EPS_NORM)
    standard = centered * inverse
    return (standard * gain_row + bias_row, standard, inverse, total_valid)


def normalize_back(grad_normed, standard, inverse, gain_row, total_valid, validity):
    grad_bias, grad_gain = lax.psum(
        (
            jnp.sum(grad_normed * validity, axis=0),
            jnp.sum(grad_normed * standard * validity, axis=0),
        ),
        "dp",
    )
    grad_values = (
        validity
        * gain_row
        * inverse
        * (grad_normed - grad_bias / total_valid - standard * grad_gain / total_valid)
    )
    return (grad_values, grad_gain, grad_bias)


def adam_update(weight, moment_one, moment_two, grad_value, rate, decay):
    fresh_one = BETA_ONE * moment_one + (1.0 - BETA_ONE) * grad_value
    fresh_two = BETA_TWO * moment_two + (1.0 - BETA_TWO) * grad_value * grad_value
    scaled = (
        fresh_one
        / (1.0 - BETA_ONE**STEP)
        / (jnp.sqrt(fresh_two / (1.0 - BETA_TWO**STEP)) + EPS_ADAM)
    )
    return (weight - rate * (scaled + decay * weight), fresh_one, fresh_two)


def on_device(
    features,
    cotangent,
    clip_frames,
    spatial_master,
    spatial_first,
    spatial_second,
    temporal_master,
    temporal_first,
    temporal_second,
    mid_norm,
    mid_first,
    mid_second,
    out_norm,
    out_first,
    out_second,
):
    validity = frame_mask(clip_frames)
    spatial_all, temporal_all = (
        lax.all_gather(spatial_master.astype(jnp.bfloat16), "dp", axis=1, tiled=True),
        lax.all_gather(temporal_master.astype(jnp.bfloat16), "dp", axis=3, tiled=True),
    )
    channels = temporal_all.shape[3]
    spatial_taps = spatial_all.reshape(2, 9, channels, spatial_all.shape[2])
    residual = features.astype(jnp.float32)
    outgoing = features
    kept_state = []
    for unit_index in range(2):
        gathered = lax.all_gather(outgoing, "chan", axis=1, tiled=True)
        spatial_out, padded = spatial_apply(gathered, spatial_taps[unit_index])
        mid_normed, mid_standard, mid_inverse, total_valid = normalize(
            spatial_out, validity, mid_norm[2 * unit_index], mid_norm[2 * unit_index + 1]
        )
        temporal_in = (jax.nn.silu(mid_normed) * validity).astype(jnp.bfloat16)
        partial_value, frames_padded = temporal_apply(temporal_in, temporal_all[unit_index])
        temporal_out = lax.psum_scatter(
            partial_value.astype(jnp.bfloat16), "chan", scatter_dimension=1, tiled=True
        ).astype(jnp.float32)
        out_normed, out_standard, out_inverse, total_valid = normalize(
            temporal_out, validity, out_norm[2 * unit_index], out_norm[2 * unit_index + 1]
        )
        if unit_index == 0:
            pre_act = out_normed
            outgoing = (jax.nn.silu(pre_act) * validity).astype(jnp.bfloat16)
        else:
            pre_act = out_normed + residual
            block_out = jax.nn.silu(pre_act) * validity
        kept_state.append(
            (
                padded,
                mid_normed,
                mid_standard,
                mid_inverse,
                frames_padded,
                pre_act,
                out_standard,
                out_inverse,
            )
        )
    kept_frames = (clip_frames // 8).astype(jnp.float32)
    clip_pool = (
        jnp.sum(block_out.reshape(-1, FRAMES * HW, block_out.shape[1]), axis=1)
        / (HW * kept_frames)[:, None]
    )
    skip_grad = cotangent * validity * silu_slope(kept_state[1][5])
    grad_pre = skip_grad
    spatial_list = [None, None]
    temporal_list = [None, None]
    mid_rows = [None, None]
    out_rows = [None, None]
    grad_hidden = skip_grad
    for unit_index in (1, 0):
        (
            padded,
            mid_normed,
            mid_standard,
            mid_inverse,
            frames_padded,
            pre_act,
            out_standard,
            out_inverse,
        ) = kept_state[unit_index]
        if unit_index == 0:
            grad_pre = grad_hidden * validity * silu_slope(pre_act)
        grad_temporal, out_gain_grad, out_bias_grad = normalize_back(
            grad_pre, out_standard, out_inverse, out_norm[2 * unit_index], total_valid, validity
        )
        grad_full = lax.all_gather(grad_temporal.astype(jnp.bfloat16), "chan", axis=1, tiled=True)
        temporal_grad, grad_mid = temporal_grads(frames_padded, temporal_all[unit_index], grad_full)
        grad_mid_normed = grad_mid * validity * silu_slope(mid_normed)
        grad_spatial, mid_gain_grad, mid_bias_grad = normalize_back(
            grad_mid_normed,
            mid_standard,
            mid_inverse,
            mid_norm[2 * unit_index],
            total_valid,
            validity,
        )
        spatial_grad, grad_in_part = spatial_grads(
            padded, spatial_taps[unit_index], grad_spatial.astype(jnp.bfloat16)
        )
        grad_hidden = lax.psum_scatter(
            grad_in_part.astype(jnp.bfloat16), "chan", scatter_dimension=1, tiled=True
        ).astype(jnp.float32)
        spatial_list[unit_index] = spatial_grad
        temporal_list[unit_index] = temporal_grad
        mid_rows[unit_index] = (mid_gain_grad, mid_bias_grad)
        out_rows[unit_index] = (out_gain_grad, out_bias_grad)
    input_grad = grad_hidden + skip_grad
    spatial_sum, temporal_sum = (
        lax.psum_scatter(jnp.stack(spatial_list), "dp", scatter_dimension=1, tiled=True),
        lax.psum_scatter(jnp.stack(temporal_list), "dp", scatter_dimension=3, tiled=True),
    )
    mid_grad = jnp.stack([mid_rows[0][0], mid_rows[0][1], mid_rows[1][0], mid_rows[1][1]])
    out_grad = jnp.stack([out_rows[0][0], out_rows[0][1], out_rows[1][0], out_rows[1][1]])
    spatial_new, spatial_one, spatial_two = adam_update(
        spatial_master, spatial_first, spatial_second, spatial_sum, RATE_CONV, DECAY_CONV
    )
    temporal_new, temporal_one, temporal_two = adam_update(
        temporal_master, temporal_first, temporal_second, temporal_sum, RATE_CONV, DECAY_CONV
    )
    mid_new, mid_one, mid_two = adam_update(
        mid_norm, mid_first, mid_second, mid_grad, RATE_NORM, 0.0
    )
    out_new, out_one, out_two = adam_update(
        out_norm, out_first, out_second, out_grad, RATE_NORM, 0.0
    )
    return (
        block_out,
        clip_pool,
        input_grad,
        spatial_new,
        spatial_one,
        spatial_two,
        temporal_new,
        temporal_one,
        temporal_two,
        mid_new,
        mid_one,
        mid_two,
        out_new,
        out_one,
        out_two,
    )


F32 = jnp.float32
BF16 = jnp.bfloat16
MESH = pl.DeviceIdType.MESH
VMEM = pltpu.VMEM
NN = (((1,), (0,)), ((), ()))
NT = (((1,), (1,)), ((), ()))
TN = (((0,), (0,)), ((), ()))
BLOCK_C = 512
MID_C = 1152
THIRD = MID_C // 3
ROWS = 784
SLOTS = 16
SHUFFLE_C = 896
HALF = 144
SUB = 48
TAPS_C = 9 * BLOCK_C
CHIP_S = TAPS_C // 4
CHIP_T = BLOCK_C // 4
CHUNKS = (
    ("s", 0, 0, 1),
    ("s", 0, 1, 1),
    ("s", 0, 2, 1),
    ("t", 0, 0, 9),
    ("s", 1, 0, 1),
    ("s", 1, 1, 1),
    ("s", 1, 2, 1),
    ("t", 1, 0, 9),
)
N_CHUNKS = len(CHUNKS)
PARTS = (("s", 0), ("t", 0), ("s", 1), ("t", 1))
GRANT = 65000 * 1024


def place():
    dp = lax.axis_index("dp")
    line = lax.axis_index("chan")
    core = lax.rem(dp, 2)
    chip = lax.div(dp, 2)
    x_bit = lax.rem(chip, 2)
    y_bit = lax.div(chip, 2)
    return dict(
        dp=dp,
        line=line,
        core=core,
        chip=chip,
        chip_x=chip + 1 - 2 * x_bit,
        chip_y=chip + 2 - 4 * y_bit,
        chip_d=3 - chip,
        pair=(dp + 1 - 2 * core, line),
        x=(dp + 2 - 4 * x_bit, line),
        y=(dp + 4 - 8 * y_bit, line),
    )


def remote(source, target, send, recv, device):
    return pltpu.make_async_remote_copy(
        src_ref=source,
        dst_ref=target,
        send_sem=send,
        recv_sem=recv,
        device_id=device,
        device_id_type=MESH,
    )


def greet(devices):
    barrier = pltpu.get_barrier_semaphore()
    for device in devices:
        pl.semaphore_signal(barrier, inc=1, device_id=device, device_id_type=MESH)
    pl.semaphore_wait(barrier, len(devices))


def line_peer(at, step):
    return (at["dp"], lax.rem(at["line"] + step, 4))


def ring_peer(at, step):
    return (lax.rem(at["dp"] + step, 8), at["line"])


def greet_all(at):
    greet(
        [ring_peer(at, step) for step in range(1, 8)]
        + [line_peer(at, step) for step in (1, 2, 3)]
    )


def rows_of(pixel):
    return pl.ds(pl.multiple_of(pixel * SLOTS, SLOTS), SLOTS)


def slope_of(values):
    sigmoid = jax.nn.sigmoid(values)
    return sigmoid * (1.0 + values * (1.0 - sigmoid))


def over_pixels(body, carry):
    return lax.fori_loop(0, HW, body, carry)


def combine_moments(blocks):
    total = sum(block[2:3] for block in blocks)
    mean = sum(block[2:3] * block[0:1] for block in blocks) / total
    spread = sum(
        block[1:2] + block[2:3] * (block[0:1] - mean) * (block[0:1] - mean) for block in blocks
    )
    return [mean, spread, total]


def combine_sums(blocks):
    return [sum(block[0:1] for block in blocks), sum(block[1:2] for block in blocks)]


def exchange(at, land, land_two, index, sems, sem_index, count, payload, combine):
    dp, line = at["dp"], at["line"]
    one_send, one_recv, two_send, two_recv = sems
    for row, value in enumerate(payload):
        land[index, dp, row : row + 1, :] = value
    sent = []
    for step in range(1, 8):
        here = land.at[index, dp, pl.ds(0, count)]
        copy = remote(
            here,
            here,
            one_send.at[sem_index, step - 1],
            one_recv.at[sem_index, step - 1],
            ring_peer(at, step),
        )
        copy.start()
        sent.append(copy)
    for step in range(1, 8):
        there = land.at[index, lax.rem(dp + 8 - step, 8), pl.ds(0, count)]
        remote(
            there,
            there,
            one_send.at[sem_index, step - 1],
            one_recv.at[sem_index, step - 1],
            ring_peer(at, step),
        ).wait_recv()
    for copy in sent:
        copy.wait_send()
    merged = combine([land[index, source] for source in range(8)])
    for row, value in enumerate(merged):
        land_two[index, line, row : row + 1, :] = value
    sent = []
    for step in (1, 2, 3):
        here = land_two.at[index, line, pl.ds(0, count)]
        copy = remote(
            here,
            here,
            two_send.at[sem_index, step - 1],
            two_recv.at[sem_index, step - 1],
            line_peer(at, step),
        )
        copy.start()
        sent.append(copy)
    for step in (1, 2, 3):
        there = land_two.at[index, lax.rem(line + 4 - step, 4), pl.ds(0, count)]
        remote(
            there,
            there,
            two_send.at[sem_index, step - 1],
            two_recv.at[sem_index, step - 1],
            line_peer(at, step),
        ).wait_recv()
    for copy in sent:
        copy.wait_send()
    return combine([land_two[index, source] for source in range(4)])


def forward_kernel(
    ws_in,
    wt_in,
    feat_in,
    cot_in,
    par_in,
    shuffle,
    mask_in,
    ws_out,
    wt_out,
    par_out,
    block_out,
    a_out,
    s_out,
    u_out,
    t_out,
    skip_out,
    stat_mid,
    stat_out,
    pair_s,
    pair_t,
    stage_s,
    stage_t,
    feat_land,
    cot_land,
    par_land,
    a_pad,
    s_ref,
    x_ref,
    u_ref,
    t_ref,
    side,
    feat_ref,
    thin,
    w_buf,
    wt_buf,
    land_mid,
    land_mid_two,
    land_out,
    land_out_two,
    pair_send,
    pair_recv,
    act_send,
    act_recv,
    line_send,
    line_recv,
    plane_send,
    plane_recv,
    diag_send,
    diag_recv,
    core_send,
    core_recv,
    own_sem,
    chunk_sem,
    w_sem,
    wt_sem,
    save_sem,
    one_send,
    one_recv,
    two_send,
    two_recv,
):
    at = place()
    line, core, chip = at["line"], at["core"], at["chip"]
    sems = (one_send, one_recv, two_send, two_recv)
    greet_all(at)
    started = []

    def send(copy):
        copy.start()
        started.append(copy)
        return copy

    def area(chunk, owner_core, owner_chip, first, count):
        kind, unit, lead, leads = chunk
        ref, width = (ws_out, CHIP_S) if kind == "s" else (wt_out, CHIP_T)
        lanes = pl.ds(pl.multiple_of(owner_chip * width, 128), width)
        return ref.at[unit, pl.ds(lead, leads), pl.ds(first, count), owner_core, :, lanes]

    pairs = {}
    for index, (kind, unit) in enumerate(PARTS):
        theirs = pl.ds(pl.multiple_of((1 - core) * HALF, 16), HALF)
        source, landing = (ws_in, pair_s) if kind == "s" else (wt_in, pair_t)
        pairs[kind, unit] = send(
            remote(
                source.at[unit, theirs],
                landing.at[unit],
                pair_send.at[index],
                pair_recv.at[index],
                at["pair"],
            )
        )

    def acts(row, source, target):
        def cut(owner):
            return source.at[pl.ds(pl.multiple_of(owner * ROWS, 16), ROWS)]

        lanes = pl.ds(pl.multiple_of(line * 128, 128), 128)
        for step in (1, 2, 3):
            peer = line_peer(at, step)
            send(
                remote(
                    cut(peer[1]),
                    target.at[:, lanes],
                    act_send.at[row, step - 1],
                    act_recv.at[row, step - 1],
                    peer,
                )
            )
        own = pltpu.make_async_copy(cut(line), target.at[:, lanes], own_sem.at[row])
        own.start()
        return own

    def acts_wait(row, source, target, own):
        for step in (1, 2, 3):
            origin = lax.rem(line + 4 - step, 4)
            lanes = pl.ds(pl.multiple_of(origin * 128, 128), 128)
            remote(
                source.at[pl.ds(0, ROWS)],
                target.at[:, lanes],
                act_send.at[row, step - 1],
                act_recv.at[row, step - 1],
                line_peer(at, step),
            ).wait_recv()
        own.wait()

    mine = pl.ds(pl.multiple_of(core * HALF, 16), HALF)

    def merge(kind, unit):
        pairs[kind, unit].wait_recv()
        source, landing = (ws_in, pair_s) if kind == "s" else (wt_in, pair_t)
        low = source[unit, mine].astype(F32)
        high = landing[unit].astype(F32)
        first = jnp.where(core == 0, low, high)
        second = jnp.where(core == 0, high, low)
        if kind == "s":
            both = jnp.concatenate([first, second], axis=1).astype(BF16)
            stage_s[unit] = both.reshape(3, 1, SUB, CHIP_S)
        else:
            for tau in range(3):
                lanes = slice(64 * tau, 64 * tau + 64)
                both = jnp.concatenate([first[:, lanes], second[:, lanes]], axis=1).astype(BF16)
                stage_t[unit, 3 * tau : 3 * tau + 3] = both.reshape(3, 1, SUB, CHIP_T)

    own_copies = [None] * N_CHUNKS

    def step_line(index):
        chunk = CHUNKS[index]
        kind, unit, lead, leads = chunk
        if lead == 0:
            merge(kind, unit)
        staged = (stage_s if kind == "s" else stage_t).at[unit, pl.ds(lead, leads)]
        target = area(chunk, core, chip, line, 1)
        for step in (1, 3, 2):
            send(
                remote(
                    staged,
                    target,
                    line_send.at[index, step - 1],
                    line_recv.at[index, step - 1],
                    line_peer(at, step),
                )
            )
        own = pltpu.make_async_copy(staged, target, chunk_sem.at[index])
        own.start()
        own_copies[index] = own

    def step_plane(index):
        chunk = CHUNKS[index]
        for step in (1, 2, 3):
            origin = area(chunk, core, chip, lax.rem(line + 4 - step, 4), 1)
            remote(
                origin,
                origin,
                line_send.at[index, step - 1],
                line_recv.at[index, step - 1],
                line_peer(at, step),
            ).wait_recv()
        own_copies[index].wait()
        held = area(chunk, core, chip, 0, 4)
        for way, name in enumerate(("x", "y")):
            send(
                remote(held, held, plane_send.at[index, way], plane_recv.at[index, way], at[name])
            )
        send(remote(held, held, core_send.at[index, 0], core_recv.at[index, 0], at["pair"]))

    def step_diag(index):
        chunk = CHUNKS[index]
        for way, (name, other, first) in enumerate((("x", "y", 0), ("y", "x", 2))):
            held = area(chunk, core, at["chip_" + name], 0, 4)
            remote(
                held, held, plane_send.at[index, way], plane_recv.at[index, way], at[name]
            ).wait_recv()
            half = area(chunk, core, at["chip_" + name], first, 2)
            send(
                remote(half, half, diag_send.at[index, way], diag_recv.at[index, way], at[other])
            )
            send(
                remote(
                    held, held, core_send.at[index, 1 + way], core_recv.at[index, 1 + way], at["pair"]
                )
            )

    def step_core(index):
        chunk = CHUNKS[index]
        for way, (other, first) in enumerate((("y", 0), ("x", 2))):
            half = area(chunk, core, at["chip_d"], first, 2)
            remote(
                half, half, diag_send.at[index, way], diag_recv.at[index, way], at[other]
            ).wait_recv()
        held = area(chunk, core, at["chip_d"], 0, 4)
        send(remote(held, held, core_send.at[index, 3], core_recv.at[index, 3], at["pair"]))
        for slot, name in enumerate(("chip", "chip_x", "chip_y", "chip_d")):
            held = area(chunk, 1 - core, at[name], 0, 4)
            remote(
                held, held, core_send.at[index, slot], core_recv.at[index, slot], at["pair"]
            ).wait_recv()

    def fetch_w(unit, third, tap, slot):
        lanes = pl.ds(pl.multiple_of(tap * BLOCK_C, 128), BLOCK_C)
        return pltpu.make_async_copy(
            ws_out.at[unit, third, :, :, :, lanes], w_buf.at[slot], w_sem.at[slot]
        )

    def window(unit, tap):
        return a_pad[unit, pl.ds(tap // 3, SIDE), pl.ds(tap % 3, SIDE)].reshape(ROWS, BLOCK_C)

    def conv(unit, third):
        columns = slice(third * THIRD, (third + 1) * THIRD)
        fetch_w(unit, third, 0, 0).start()

        def body(tap, carry):
            slot = lax.rem(tap, 2)

            @pl.when(tap < 8)
            def _():
                fetch_w(unit, third, tap + 1, 1 - slot).start()

            fetch_w(unit, third, tap, slot).wait()
            value = lax.dot_general(
                window(unit, tap),
                w_buf[slot].reshape(THIRD, BLOCK_C),
                NT,
                preferred_element_type=F32,
            )

            @pl.when(tap == 0)
            def _():
                s_ref[:, columns] = value

            @pl.when(tap > 0)
            def _():
                s_ref[:, columns] = s_ref[:, columns] + value

            return carry

        lax.fori_loop(0, 9, body, 0)

    mask_mid = mask_in[...]
    mask_out = mask_in[:, :BLOCK_C]
    slot_rows = lax.broadcasted_iota(jnp.int32, (SLOTS, BLOCK_C), 0)
    has_before = (slot_rows >= 4).astype(F32)
    has_after = (slot_rows < 12).astype(F32)

    def moments(values, mask, land, land_two, index, sem_index):
        zero = jnp.zeros(mask.shape, F32)
        local = HW * jnp.sum(mask, axis=0, keepdims=True)
        added = over_pixels(lambda p, acc: acc + values[rows_of(p), :], zero)
        mean = jnp.sum(added * mask, axis=0, keepdims=True) / local

        def squares(p, acc):
            centered = values[rows_of(p), :] - mean
            return acc + centered * centered

        spread = jnp.sum(over_pixels(squares, zero) * mask, axis=0, keepdims=True)
        mean, spread, total = exchange(
            at, land, land_two, index, sems, sem_index, 4, [mean, spread, local], combine_moments
        )
        return mean, lax.rsqrt(spread / total + EPS_NORM), total

    saves = []

    def save(source, target):
        copy = pltpu.make_async_copy(source, target, save_sem.at[len(saves)])
        copy.start()
        saves.append(copy)

    def mid_norm_act(unit):
        gain = par_out[2 * unit : 2 * unit + 1]
        bias = par_out[2 * unit + 1 : 2 * unit + 2]
        mean, inverse, total = moments(
            s_ref, mask_mid, land_mid, land_mid_two, unit, 2 * unit
        )
        stat_mid[2 * unit : 2 * unit + 1] = inverse
        stat_mid[2 * unit + 1 : 2 * unit + 2] = total

        def mid_act(p, carry):
            rows = rows_of(p)
            standard = (s_ref[rows, :] - mean) * inverse
            x_ref[unit, rows, :] = standard.astype(BF16)
            normed = standard * gain + bias
            u_ref[unit, rows, :] = (jax.nn.sigmoid(normed) * normed * mask_mid).astype(BF16)
            return carry

        over_pixels(mid_act, 0)
        save(x_ref.at[unit], s_out.at[unit])
        save(u_ref.at[unit], u_out.at[unit])

    def temporal(unit):
        copy = pltpu.make_async_copy(wt_out.at[unit], wt_buf, wt_sem.at[0])
        copy.start()
        copy.wait()

        def weight(tau):
            return wt_buf[3 * tau : 3 * tau + 3].reshape(MID_C, BLOCK_C)

        t_ref[unit] = lax.dot_general(u_ref[unit], weight(1), NN, preferred_element_type=F32)
        side[0] = lax.dot_general(u_ref[unit], weight(0), NN, preferred_element_type=F32)
        side[1] = lax.dot_general(u_ref[unit], weight(2), NN, preferred_element_type=F32)

        def frames(p, carry):
            rows = rows_of(p)
            t_ref[unit, rows, :] = (
                t_ref[unit, rows, :]
                + pltpu.roll(side[0, rows, :], 4, 0) * has_before
                + pltpu.roll(side[1, rows, :], 12, 0) * has_after
            )
            return carry

        over_pixels(frames, 0)

    def out_stats(unit):
        mean, inverse, total = moments(
            t_ref.at[unit], mask_out, land_out, land_out_two, unit, 2 * unit + 1
        )
        stat_out[2 * unit : 2 * unit + 1] = inverse
        stat_out[2 * unit + 1 : 2 * unit + 2] = total
        gain = par_out[4 + 2 * unit : 5 + 2 * unit, :BLOCK_C]
        bias = par_out[5 + 2 * unit : 6 + 2 * unit, :BLOCK_C]
        return mean, inverse, gain, bias

    step_line(0)
    feat_own = acts(0, feat_in, feat_land)
    step_line(1)
    for step in (1, 2, 3):
        send(
            remote(
                par_in,
                par_land.at[line],
                act_send.at[2, step - 1],
                act_recv.at[2, step - 1],
                line_peer(at, step),
            )
        )
    par_own = pltpu.make_async_copy(par_in, par_land.at[line], own_sem.at[2])
    par_own.start()
    for unit in range(2):
        a_pad[unit] = jnp.zeros(a_pad.shape[1:], BF16)
    step_plane(0)
    step_line(2)
    step_line(3)
    permute = shuffle[:, :ROWS]
    acts_wait(0, feat_in, feat_land, feat_own)
    feat_ref[...] = lax.dot_general(permute, feat_land[...], NN, preferred_element_type=F32).astype(
        BF16
    )

    def fill(p, carry):
        a_pad[0, 1 + p // SIDE, 1 + p % SIDE] = feat_ref[rows_of(p), :]
        return carry

    over_pixels(fill, 0)
    save(a_pad.at[0], a_out.at[0])
    step_plane(1)
    step_diag(0)
    step_line(4)
    step_plane(2)
    step_core(0)
    conv(0, 0)
    step_diag(1)
    step_line(5)
    step_plane(3)
    step_core(1)
    conv(0, 1)
    step_diag(2)
    step_line(6)
    step_plane(4)
    step_core(2)
    conv(0, 2)
    for step in (1, 2, 3):
        remote(
            par_in,
            par_land.at[lax.rem(line + 4 - step, 4)],
            act_send.at[2, step - 1],
            act_recv.at[2, step - 1],
            line_peer(at, step),
        ).wait_recv()
    par_own.wait()
    par_out[...] = par_land[0] + par_land[1] + par_land[2] + par_land[3]
    step_diag(3)
    step_line(7)
    cot_own = acts(1, cot_in, cot_land)
    step_plane(5)
    mid_norm_act(0)
    step_diag(4)
    step_core(3)
    step_plane(6)
    temporal(0)
    mean, inverse, gain, bias = out_stats(0)
    step_diag(5)
    step_core(4)
    step_plane(7)

    def out_act(p, carry):
        rows = rows_of(p)
        standard = (t_ref[0, rows, :] - mean) * inverse
        t_ref[0, rows, :] = standard
        normed = standard * gain + bias
        hidden = jax.nn.sigmoid(normed) * normed * mask_out
        a_pad[1, 1 + p // SIDE, 1 + p % SIDE] = hidden.astype(BF16)
        return carry

    over_pixels(out_act, 0)
    save(t_ref.at[0], t_out.at[0])
    save(a_pad.at[1], a_out.at[1])
    conv(1, 0)
    step_diag(6)
    step_core(5)
    conv(1, 1)
    step_diag(7)
    step_core(6)
    conv(1, 2)
    mid_norm_act(1)
    acts_wait(1, cot_in, cot_land, cot_own)
    step_core(7)
    temporal(1)
    mean_one, inverse_one, gain_one, bias_one = out_stats(1)
    side[0] = lax.dot_general(permute, cot_land[...], NN, preferred_element_type=F32)

    def end_act(p, carry):
        rows = rows_of(p)
        standard = (t_ref[1, rows, :] - mean_one) * inverse_one
        t_ref[1, rows, :] = standard
        pre = standard * gain_one + bias_one + feat_ref[rows, :].astype(F32)
        sigmoid = jax.nn.sigmoid(pre)
        thin[rows, :] = (pre * sigmoid * mask_out).astype(BF16)
        slope = sigmoid * (1.0 + pre * (1.0 - sigmoid))
        cot_land[rows, :] = (side[0, rows, :] * mask_out * slope).astype(BF16)
        return carry

    over_pixels(end_act, 0)
    save(t_ref.at[1], t_out.at[1])
    save(cot_land, skip_out)
    block_out[...] = lax.dot_general(permute, thin[...], TN, preferred_element_type=F32).astype(
        BF16
    )
    for copy in saves:
        copy.wait()
    for copy in started:
        copy.wait_send()


def backward_kernel(
    ws,
    wt,
    a_in,
    s_in,
    u_in,
    t_in,
    skip_in,
    stat_mid,
    stat_out,
    par,
    mask_in,
    shuffle,
    block_in,
    sum_s,
    sum_t,
    mid_grad,
    out_grad,
    block_out,
    input_out,
    a_pad,
    s_ref,
    u_ref,
    t_ref,
    side,
    skip_ref,
    wide,
    ds_pad,
    d_ref,
    w_buf,
    land_mid,
    land_mid_two,
    land_out,
    land_out_two,
    g_s,
    g_t,
    land_s,
    land_t,
    one_s,
    one_t,
    two_s,
    two_t,
    line_s,
    line_t,
    fin_s,
    fin_t,
    load_sem,
    w_sem,
    ex_one_send,
    ex_one_recv,
    ex_two_send,
    ex_two_recv,
    act_send,
    act_recv,
    act_sem,
    pair_send,
    pair_recv,
    one_send,
    one_recv,
    two_send,
    two_recv,
    line_send,
    line_recv,
    fin_send,
    fin_recv,
):
    at = place()
    line, core, chip = at["line"], at["core"], at["chip"]
    sems = (ex_one_send, ex_one_recv, ex_two_send, ex_two_recv)

    def load(index, source, target):
        return pltpu.make_async_copy(source, target, load_sem.at[index])

    load_t = [load(0, t_in.at[unit], t_ref) for unit in range(2)]
    load_u = [load(1, u_in.at[unit], u_ref) for unit in range(2)]
    load_s = [load(2, s_in.at[unit], s_ref) for unit in range(2)]
    load_a = [load(3, a_in.at[unit], a_pad) for unit in range(2)]
    load_skip = load(4, skip_in, skip_ref)
    load_shuffle = load(5, shuffle, u_ref.at[:, pl.ds(0, SHUFFLE_C)])
    load_t[1].start()
    load_skip.start()
    load_u[1].start()
    load_s[1].start()
    load_a[1].start()
    greet_all(at)
    ds_pad[...] = jnp.zeros(ds_pad.shape, BF16)

    mask_mid = mask_in[...]
    mask_out = mask_in[:, :BLOCK_C]
    slot_rows = lax.broadcasted_iota(jnp.int32, (SLOTS, BLOCK_C), 0)
    has_before = (slot_rows >= 4).astype(F32)
    has_after = (slot_rows < 12).astype(F32)
    lanes_line = pl.ds(pl.multiple_of(line * 128, 128), 128)
    rows_line = pl.ds(pl.multiple_of(line * ROWS, 16), ROWS)

    act_copies = []

    def acts(row, source, target):
        for step in (1, 2, 3):
            peer = line_peer(at, step)
            copy = remote(
                source.at[:, pl.ds(pl.multiple_of(peer[1] * 128, 128), 128)],
                target.at[rows_line],
                act_send.at[row, step - 1],
                act_recv.at[row, step - 1],
                peer,
            )
            copy.start()
            act_copies.append(copy)
        own = pltpu.make_async_copy(source.at[:, lanes_line], target.at[rows_line], act_sem.at[row])
        own.start()
        return own

    def acts_wait(row, source, target, own):
        for step in (1, 2, 3):
            origin = lax.rem(line + 4 - step, 4)
            remote(
                source.at[:, lanes_line],
                target.at[pl.ds(pl.multiple_of(origin * ROWS, 16), ROWS)],
                act_send.at[row, step - 1],
                act_recv.at[row, step - 1],
                line_peer(at, step),
            ).wait_recv()
        own.wait()

    block_own = acts(0, block_in, block_out)

    flying = [[] for _ in CHUNKS]
    pair_copies = [None] * N_CHUNKS
    fin_copies = [None] * N_CHUNKS

    def launch(index, copy):
        copy.start()
        flying[index].append(copy)
        return copy

    def drain(index):
        for copy in flying[index]:
            copy.wait_send()
        flying[index] = []

    def grad_of(index):
        kind, _, lead, _ = CHUNKS[index]
        return g_s.at[lead] if kind == "s" else g_t

    def land_of(index):
        kind, _, lead, _ = CHUNKS[index]
        return land_s.at[lead] if kind == "s" else land_t

    def held(index, small, large):
        kind, unit, lead, _ = CHUNKS[index]
        return large.at[unit, lead] if kind == "s" else small.at[unit]

    def cut(index, owner, first, count):
        width = CHIP_S if CHUNKS[index][0] == "s" else CHIP_T
        lanes = pl.ds(pl.multiple_of(owner * width, 128), width)
        return grad_of(index).at[:, pl.ds(first, count), core, :, lanes]

    def add_into(target, source):
        leads, count, _, width = target.shape

        def body(turn, carry):
            if leads == 1 and width > 2048:
                where = (0, lax.div(turn, 3), pl.ds(pl.multiple_of(lax.rem(turn, 3) * 16, 16), 16))
            elif leads == 1:
                where = (0, turn)
            else:
                where = (turn,)
            target[where] = (target[where].astype(F32) + source[where].astype(F32)).astype(BF16)
            return carry

        turns = leads if leads > 1 else count * (3 if width > 2048 else 1)
        lax.fori_loop(0, turns, body, 0)

    def step_pair(index):
        pair_copies[index] = launch(
            index,
            remote(
                grad_of(index).at[:, :, 1 - core],
                land_of(index),
                pair_send.at[index],
                pair_recv.at[index],
                at["pair"],
            ),
        )

    def step_one(index):
        pair_copies[index].wait_recv()
        add_into(grad_of(index).at[:, :, core], land_of(index))
        ones, twos = held(index, one_t, one_s), held(index, two_t, two_s)
        for way, (name, first) in enumerate((("x", 0), ("y", 2))):
            launch(
                index,
                remote(
                    cut(index, at["chip_d"], first, 2),
                    ones.at[way],
                    one_send.at[index, way],
                    one_recv.at[index, way],
                    at[name],
                ),
            )
            launch(
                index,
                remote(
                    cut(index, at["chip_" + name], first, 2),
                    twos.at[way, :, pl.ds(first, 2)],
                    two_send.at[index, way, 0],
                    two_recv.at[index, way, 0],
                    at[name],
                ),
            )

    def step_two(index):
        ones, twos = held(index, one_t, one_s), held(index, two_t, two_s)
        for way, (name, other, first) in enumerate((("x", "y", 0), ("y", "x", 2))):
            landing = ones.at[way]
            remote(
                landing, landing, one_send.at[index, way], one_recv.at[index, way], at[name]
            ).wait_recv()
            target = cut(index, at["chip_" + other], first, 2)
            add_into(target, landing)
            launch(
                index,
                remote(
                    target,
                    twos.at[1 - way, :, pl.ds(first, 2)],
                    two_send.at[index, 1 - way, 1],
                    two_recv.at[index, 1 - way, 1],
                    at[other],
                ),
            )

    def step_three(index):
        twos = held(index, two_t, two_s)
        for way, (name, first) in enumerate((("x", 0), ("y", 2))):
            for turn, begin in enumerate((first, 2 - first)):
                landing = twos.at[way, :, pl.ds(begin, 2)]
                remote(
                    landing,
                    landing,
                    two_send.at[index, way, turn],
                    two_recv.at[index, way, turn],
                    at[name],
                ).wait_recv()
        own = cut(index, chip, 0, 4)
        leads = own.shape[0]

        def body(turn, carry):
            where = (0, turn) if leads == 1 else (turn,)
            own[where] = (
                own[where].astype(F32)
                + twos.at[0][where].astype(F32)
                + twos.at[1][where].astype(F32)
            ).astype(BF16)
            return carry

        lax.fori_loop(0, 4 if leads == 1 else leads, body, 0)
        lines = held(index, line_t, line_s)
        for step in (1, 3, 2):
            peer = line_peer(at, step)
            launch(
                index,
                remote(
                    cut(index, chip, peer[1], 1),
                    lines.at[step - 1],
                    line_send.at[index, step - 1],
                    line_recv.at[index, step - 1],
                    peer,
                ),
            )

    def step_four(index):
        lines, fin = held(index, line_t, line_s), held(index, fin_t, fin_s)
        for step in (1, 2, 3):
            landing = lines.at[step - 1]
            remote(
                landing,
                landing,
                line_send.at[index, step - 1],
                line_recv.at[index, step - 1],
                line_peer(at, step),
            ).wait_recv()
        total = cut(index, chip, line, 1)[...].astype(F32)
        for step in range(3):
            total = total + lines[step].astype(F32)
        fin[0] = total
        fin_copies[index] = launch(
            index,
            remote(fin.at[0], fin.at[1], fin_send.at[index], fin_recv.at[index], at["pair"]),
        )

    def step_five(index):
        kind, unit, lead, leads = CHUNKS[index]
        fin_copies[index].wait_recv()
        fin = held(index, fin_t, fin_s)
        for which in range(2):
            half = core if which == 0 else 1 - core
            if kind == "s":
                width = CHIP_S // 2
                rows = pl.ds(pl.multiple_of(half * HALF + SUB * lead, 16), SUB)
                value = fin[which, 0, 0]
                sum_s[unit, rows, :] = jnp.where(core == 0, value[:, :width], value[:, width:])
            else:
                width = CHIP_T // 2
                rows = pl.ds(pl.multiple_of(half * HALF, 16), HALF)
                for tau in range(3):
                    value = fin[which, 3 * tau : 3 * tau + 3].reshape(HALF, CHIP_T)
                    sum_t[unit, tau, rows, :] = jnp.where(
                        core == 0, value[:, :width], value[:, width:]
                    )

    def fetch_w(unit, tap, slot):
        lanes = pl.ds(pl.multiple_of(tap * BLOCK_C, 128), BLOCK_C)
        return pltpu.make_async_copy(ws.at[unit, :, lanes], w_buf.at[slot], w_sem.at[slot])

    def fetch_wt(unit, tau, slot):
        return pltpu.make_async_copy(wt.at[unit, tau], w_buf.at[slot], w_sem.at[slot])

    def window(tap):
        return a_pad[pl.ds(tap // 3, SIDE), pl.ds(tap % 3, SIDE)].reshape(ROWS, BLOCK_C)

    zero_mid = jnp.zeros((SLOTS, MID_C), F32)
    zero_out = jnp.zeros((SLOTS, BLOCK_C), F32)

    def out_norm_back(unit):
        grad_ref = skip_ref if unit == 1 else side
        gain = par[4 + 2 * unit : 5 + 2 * unit, :BLOCK_C]
        inverse = stat_out[2 * unit : 2 * unit + 1]
        total = stat_out[2 * unit + 1 : 2 * unit + 2]

        def out_sums(p, carry):
            rows = rows_of(p)
            grad = grad_ref[rows, :].astype(F32)
            return (carry[0] + grad, carry[1] + grad * t_ref[rows, :])

        bias_acc, gain_acc = over_pixels(out_sums, (zero_out, zero_out))
        sums = [
            jnp.sum(bias_acc, axis=0, keepdims=True),
            jnp.sum(gain_acc, axis=0, keepdims=True),
        ]
        grad_bias, grad_gain = exchange(
            at, land_out, land_out_two, unit, sems, 2 * unit, 2, sums, combine_sums
        )
        out_grad[2 * unit : 2 * unit + 1, :] = grad_gain
        out_grad[2 * unit + 1 : 2 * unit + 2, :] = grad_bias
        scale = gain * inverse
        bias_part, gain_part = grad_bias / total, grad_gain / total

        def out_back(p, carry):
            rows = rows_of(p)
            value = (
                mask_out
                * scale
                * (grad_ref[rows, :].astype(F32) - bias_part - t_ref[rows, :] * gain_part)
            )
            d_ref[1, rows, :] = value.astype(BF16)
            d_ref[0, rows, :] = (pltpu.roll(value, 12, 0) * has_after).astype(BF16)
            d_ref[2, rows, :] = (pltpu.roll(value, 4, 0) * has_before).astype(BF16)
            return carry

        over_pixels(out_back, 0)

    def temporal_grad():
        for tau in range(3):
            g_t[3 * tau : 3 * tau + 3] = (
                lax.dot_general(u_ref[...], d_ref[tau], TN, preferred_element_type=F32)
                .astype(BF16)
                .reshape(3, 4, 2, SUB, BLOCK_C)
            )

    def temporal_back(unit):
        for tau in range(3):
            slot = tau % 2
            if tau < 2:
                fetch_wt(unit, tau + 1, 1 - slot).start()
            fetch_wt(unit, tau, slot).wait()
            value = lax.dot_general(d_ref[tau], w_buf[slot], NT, preferred_element_type=F32)
            wide[...] = value if tau == 0 else wide[...] + value

    def mid_norm_back(unit):
        gain = par[2 * unit : 2 * unit + 1]
        bias = par[2 * unit + 1 : 2 * unit + 2]
        inverse = stat_mid[2 * unit : 2 * unit + 1]
        total = stat_mid[2 * unit + 1 : 2 * unit + 2]

        def mid_sums(p, carry):
            rows = rows_of(p)
            standard = s_ref[rows, :].astype(F32)
            grad = mask_mid * slope_of(standard * gain + bias) * wide[rows, :]
            wide[rows, :] = grad
            return (carry[0] + grad, carry[1] + grad * standard)

        bias_acc, gain_acc = over_pixels(mid_sums, (zero_mid, zero_mid))
        sums = [
            jnp.sum(bias_acc, axis=0, keepdims=True),
            jnp.sum(gain_acc, axis=0, keepdims=True),
        ]
        grad_bias, grad_gain = exchange(
            at, land_mid, land_mid_two, unit, sems, 2 * unit + 1, 2, sums, combine_sums
        )
        mid_grad[2 * unit : 2 * unit + 1, :] = grad_gain
        mid_grad[2 * unit + 1 : 2 * unit + 2, :] = grad_bias
        scale = gain * inverse
        bias_part, gain_part = grad_bias / total, grad_gain / total

        def mid_back(p, carry):
            rows = rows_of(p)
            value = (
                mask_mid
                * scale
                * (wide[rows, :] - bias_part - s_ref[rows, :].astype(F32) * gain_part)
            )
            ds_pad[1 + p // SIDE, 1 + p % SIDE] = value.astype(BF16)
            return carry

        over_pixels(mid_back, 0)

    def spatial_grad(third):
        columns = slice(third * THIRD, (third + 1) * THIRD)

        def body(tap, carry):
            inner = ds_pad[1 : 1 + SIDE, 1 : 1 + SIDE, :, columns].reshape(ROWS, THIRD)
            lanes = pl.ds(pl.multiple_of(tap * BLOCK_C, 128), BLOCK_C)
            g_s[third, 0, :, :, :, lanes] = (
                lax.dot_general(inner, window(tap), TN, preferred_element_type=F32)
                .astype(BF16)
                .reshape(4, 2, SUB, BLOCK_C)
            )
            return carry

        lax.fori_loop(0, 9, body, 0)

    def spatial_back(unit, first):
        if first == 0:
            fetch_w(unit, 0, 0).start()

        def body(tap, carry):
            slot = lax.rem(tap, 2)

            @pl.when(tap < 8)
            def _():
                fetch_w(unit, tap + 1, 1 - slot).start()

            fetch_w(unit, tap, slot).wait()
            moved = ds_pad[pl.ds(2 - tap // 3, SIDE), pl.ds(2 - tap % 3, SIDE)].reshape(ROWS, MID_C)
            value = lax.dot_general(moved, w_buf[slot], NN, preferred_element_type=F32)

            @pl.when(tap == 0)
            def _():
                side[...] = value

            @pl.when(tap > 0)
            def _():
                side[...] = side[...] + value

            return carry

        lax.fori_loop(first, first + 3, body, 0)

    a_0, b_0, c_0, t_0, a_1, b_1, c_1, t_1 = range(N_CHUNKS)

    load_t[1].wait()
    load_skip.wait()
    fetch_wt(1, 0, 0).start()
    out_norm_back(1)
    load_t[0].start()
    load_u[1].wait()
    temporal_grad()
    load_u[0].start()
    step_pair(t_1)
    temporal_back(1)
    step_one(t_1)
    load_s[1].wait()
    mid_norm_back(1)
    load_s[0].start()
    step_two(t_1)
    load_a[1].wait()
    spatial_grad(0)
    step_pair(a_1)
    step_three(t_1)
    spatial_grad(1)
    step_pair(b_1)
    step_one(a_1)
    spatial_grad(2)
    load_a[0].start()
    step_pair(c_1)
    step_one(b_1)
    step_two(a_1)
    step_four(t_1)
    spatial_back(1, 0)
    step_one(c_1)
    step_two(b_1)
    step_three(a_1)
    step_five(t_1)
    spatial_back(1, 3)
    step_two(c_1)
    step_four(a_1)
    spatial_back(1, 6)
    load_t[0].wait()
    gain, bias = par[4:5, :BLOCK_C], par[5:6, :BLOCK_C]

    def hidden_back(p, carry):
        rows = rows_of(p)
        slope = slope_of(t_ref[rows, :] * gain + bias)
        side[rows, :] = mask_out * slope * side[rows, :]
        return carry

    over_pixels(hidden_back, 0)
    fetch_wt(0, 0, 0).start()
    out_norm_back(0)
    step_three(b_1)
    step_five(a_1)
    drain(t_1)
    load_u[0].wait()
    temporal_grad()
    load_shuffle.start()
    step_pair(t_0)
    temporal_back(0)
    step_three(c_1)
    step_four(b_1)
    step_one(t_0)
    load_s[0].wait()
    mid_norm_back(0)
    step_two(t_0)
    step_five(b_1)
    step_four(c_1)
    load_a[0].wait()
    drain(a_1)
    spatial_grad(0)
    step_pair(a_0)
    step_five(c_1)
    drain(b_1)
    spatial_grad(1)
    step_pair(b_0)
    step_one(a_0)
    step_three(t_0)
    drain(c_1)
    spatial_grad(2)
    step_pair(c_0)
    step_one(b_0)
    step_two(a_0)
    step_four(t_0)
    spatial_back(0, 0)
    step_one(c_0)
    step_two(b_0)
    step_three(a_0)
    spatial_back(0, 3)
    step_two(c_0)
    step_five(t_0)
    spatial_back(0, 6)
    load_shuffle.wait()
    d_ref[0] = (side[...] + skip_ref[...].astype(F32)).astype(BF16)
    thin = d_ref.at[1]
    thin[...] = lax.dot_general(
        u_ref[:, :SHUFFLE_C], d_ref[0], TN, preferred_element_type=F32
    ).astype(BF16)[:ROWS]
    input_own = acts(1, thin, input_out)
    step_three(b_0)
    step_four(a_0)
    step_three(c_0)
    step_five(a_0)
    step_four(b_0)
    step_five(b_0)
    step_four(c_0)
    step_five(c_0)
    acts_wait(0, block_in, block_out, block_own)
    acts_wait(1, thin, input_out, input_own)
    for copy in act_copies:
        copy.wait_send()
    for index in (t_0, a_0, b_0, c_0):
        drain(index)


def spaces(text):
    return [pl.BlockSpec(memory_space=VMEM if mark == "v" else pl.ANY) for mark in text]


def dma(*shape):
    return pltpu.SemaphoreType.DMA(shape)


def params(number):
    return pltpu.CompilerParams(
        collective_id=number, has_side_effects=True, vmem_limit_bytes=GRANT
    )


def shaped(*shape, dtype=BF16):
    return jax.ShapeDtypeStruct(shape, dtype)


def run_forward(ws, wt, feat, cot, par, shuffle, mask):
    padded = (SIDE + 2, SIDE + 2, SLOTS, BLOCK_C)
    return pl.pallas_call(
        forward_kernel,
        out_shape=[
            shaped(2, 3, 4, 2, SUB, TAPS_C),
            shaped(2, 9, 4, 2, SUB, BLOCK_C),
            shaped(8, MID_C, dtype=F32),
            shaped(ROWS, BLOCK_C),
            shaped(2, *padded),
            shaped(2, ROWS, MID_C),
            shaped(2, ROWS, MID_C),
            shaped(2, ROWS, BLOCK_C, dtype=F32),
            shaped(ROWS, BLOCK_C),
            shaped(4, MID_C, dtype=F32),
            shaped(4, BLOCK_C, dtype=F32),
        ],
        in_specs=spaces("vvaavvv"),
        out_specs=spaces("aavvaaaaavv"),
        scratch_shapes=[
            VMEM((2, HALF, CHIP_S // 2), BF16),
            VMEM((2, HALF, 3 * CHIP_T // 2), BF16),
            VMEM((2, 3, 1, SUB, CHIP_S), BF16),
            VMEM((2, 9, 1, SUB, CHIP_T), BF16),
            VMEM((ROWS, BLOCK_C), BF16),
            VMEM((ROWS, BLOCK_C), BF16),
            VMEM((4, 8, MID_C), F32),
            VMEM((2,) + padded, BF16),
            VMEM((ROWS, MID_C), F32),
            VMEM((2, ROWS, MID_C), BF16),
            VMEM((2, ROWS, MID_C), BF16),
            VMEM((2, ROWS, BLOCK_C), F32),
            VMEM((2, ROWS, BLOCK_C), F32),
            VMEM((ROWS, BLOCK_C), BF16),
            VMEM((ROWS, BLOCK_C), BF16),
            VMEM((2, 4, 2, SUB, BLOCK_C), BF16),
            VMEM((9, 4, 2, SUB, BLOCK_C), BF16),
            VMEM((2, 8, 8, MID_C), F32),
            VMEM((2, 4, 8, MID_C), F32),
            VMEM((2, 8, 8, BLOCK_C), F32),
            VMEM((2, 4, 8, BLOCK_C), F32),
            dma(4),
            dma(4),
            dma(3, 3),
            dma(3, 3),
            dma(N_CHUNKS, 3),
            dma(N_CHUNKS, 3),
            dma(N_CHUNKS, 2),
            dma(N_CHUNKS, 2),
            dma(N_CHUNKS, 2),
            dma(N_CHUNKS, 2),
            dma(N_CHUNKS, 4),
            dma(N_CHUNKS, 4),
            dma(3),
            dma(N_CHUNKS),
            dma(2),
            dma(1),
            dma(10),
            dma(4, 7),
            dma(4, 7),
            dma(4, 3),
            dma(4, 3),
        ],
        compiler_params=params(0),
        name="forward",
    )(ws, wt, feat, cot, par, shuffle, mask)


def run_backward(*args):
    return pl.pallas_call(
        backward_kernel,
        out_shape=[
            shaped(2, 2 * HALF, CHIP_S // 2, dtype=F32),
            shaped(2, 3, 2 * HALF, CHIP_T // 2, dtype=F32),
            shaped(4, MID_C, dtype=F32),
            shaped(4, BLOCK_C, dtype=F32),
            shaped(4 * ROWS, 128),
            shaped(4 * ROWS, 128),
        ],
        in_specs=spaces("aaaaaaavvvvaa"),
        out_specs=spaces("vvvvaa"),
        scratch_shapes=[
            VMEM((SIDE + 2, SIDE + 2, SLOTS, BLOCK_C), BF16),
            VMEM((ROWS, MID_C), BF16),
            VMEM((ROWS, MID_C), BF16),
            VMEM((ROWS, BLOCK_C), F32),
            VMEM((ROWS, BLOCK_C), F32),
            VMEM((ROWS, BLOCK_C), BF16),
            VMEM((ROWS, MID_C), F32),
            VMEM((SIDE + 2, SIDE + 2, SLOTS, MID_C), BF16),
            VMEM((3, ROWS, BLOCK_C), BF16),
            VMEM((2, MID_C, BLOCK_C), BF16),
            VMEM((2, 8, 8, MID_C), F32),
            VMEM((2, 4, 8, MID_C), F32),
            VMEM((2, 8, 8, BLOCK_C), F32),
            VMEM((2, 4, 8, BLOCK_C), F32),
            VMEM((3, 1, 4, 2, SUB, TAPS_C), BF16),
            VMEM((9, 4, 2, SUB, BLOCK_C), BF16),
            VMEM((3, 1, 4, SUB, TAPS_C), BF16),
            VMEM((9, 4, SUB, BLOCK_C), BF16),
            VMEM((2, 3, 2, 1, 2, SUB, CHIP_S), BF16),
            VMEM((2, 2, 9, 2, SUB, CHIP_T), BF16),
            VMEM((2, 3, 2, 1, 4, SUB, CHIP_S), BF16),
            VMEM((2, 2, 9, 4, SUB, CHIP_T), BF16),
            VMEM((2, 3, 3, 1, 1, SUB, CHIP_S), BF16),
            VMEM((2, 3, 9, 1, SUB, CHIP_T), BF16),
            VMEM((2, 3, 2, 1, 1, SUB, CHIP_S), F32),
            VMEM((2, 2, 9, 1, SUB, CHIP_T), F32),
            dma(6),
            dma(2),
            dma(4, 7),
            dma(4, 7),
            dma(4, 3),
            dma(4, 3),
            dma(2, 3),
            dma(2, 3),
            dma(2),
            dma(N_CHUNKS),
            dma(N_CHUNKS),
            dma(N_CHUNKS, 2),
            dma(N_CHUNKS, 2),
            dma(N_CHUNKS, 2, 2),
            dma(N_CHUNKS, 2, 2),
            dma(N_CHUNKS, 3),
            dma(N_CHUNKS, 3),
            dma(N_CHUNKS),
            dma(N_CHUNKS),
        ],
        compiler_params=params(1),
        name="backward",
    )(*args)


def shuffle_matrix():
    clip, frame, pixel = np.meshgrid(np.arange(4), np.arange(FRAMES), np.arange(HW), indexing="ij")
    source = (clip * FRAMES + frame) * HW + pixel
    target = pixel * SLOTS + frame * 4 + clip
    matrix = np.zeros((ROWS, SHUFFLE_C), np.float32)
    matrix[target.reshape(-1), source.reshape(-1)] = 1.0
    return jnp.asarray(matrix, BF16)


def on_pairs(
    features,
    cotangent,
    clip_frames,
    spatial_master,
    spatial_first,
    spatial_second,
    temporal_master,
    temporal_first,
    temporal_second,
    mid_norm,
    mid_first,
    mid_second,
    out_norm,
    out_first,
    out_second,
):
    line = lax.axis_index("chan")
    ws_own = jnp.swapaxes(spatial_master, 1, 2).astype(BF16)
    wt_own = (
        jnp.swapaxes(temporal_master, 1, 2).reshape(2, 2 * HALF, 3 * CHIP_T // 2).astype(BF16)
    )
    here = (jnp.arange(4, dtype=jnp.int32) == line).astype(F32)
    mid_rows = jnp.swapaxes(mid_norm.reshape(4, 2, 3, SUB), 1, 2).reshape(4, 3, 1, 2 * SUB)
    mid_wide = (mid_rows * here[None, None, :, None]).reshape(4, MID_C)
    out_wide = (out_norm[:, None, :] * here[None, :, None]).reshape(4, BLOCK_C)
    par_own = jnp.concatenate([mid_wide, jnp.pad(out_wide, ((0, 0), (0, MID_C - BLOCK_C)))], axis=0)
    kept = clip_frames // 8
    kept_own = lax.dynamic_slice_in_dim(kept, line * 4, 4)
    frame_ids = jnp.arange(FRAMES, dtype=jnp.int32)
    mask = (frame_ids[:, None] < kept_own[None, :]).astype(F32).reshape(SLOTS, 1)
    mask = jnp.broadcast_to(mask, (SLOTS, MID_C))
    shuffle = shuffle_matrix()
    ws, wt, par, block, a_all, s_all, u_all, t_all, skip, stat_mid, stat_out = run_forward(
        ws_own, wt_own, features, cotangent.astype(BF16), par_own, shuffle, mask
    )
    sum_s, sum_t, mid_all, out_all, block_rows, grad_rows = run_backward(
        ws.reshape(2, MID_C, TAPS_C),
        wt.reshape(2, 3, MID_C, BLOCK_C),
        a_all,
        s_all,
        u_all,
        t_all,
        skip,
        stat_mid,
        stat_out,
        par,
        mask,
        shuffle,
        block,
    )
    block_out = block_rows.astype(F32)
    clip_pool = (
        jnp.sum(block_out.reshape(-1, FRAMES * HW, block_out.shape[1]), axis=1)
        / (HW * kept.astype(F32))[:, None]
    )
    mid_pick = lax.dynamic_index_in_dim(
        mid_all.reshape(4, 3, 4, 2, SUB), line, axis=2, keepdims=False
    )
    mid_grad = jnp.swapaxes(mid_pick, 1, 2).reshape(4, 2 * HALF)
    out_grad = lax.dynamic_slice_in_dim(out_all, line * 128, 128, axis=1)
    spatial = adam_update(
        spatial_master,
        spatial_first,
        spatial_second,
        jnp.swapaxes(sum_s, 1, 2),
        RATE_CONV,
        DECAY_CONV,
    )
    temporal = adam_update(
        temporal_master, temporal_first, temporal_second, sum_t, RATE_CONV, DECAY_CONV
    )
    mid_new = adam_update(mid_norm, mid_first, mid_second, mid_grad, RATE_NORM, 0.0)
    out_new = adam_update(out_norm, out_first, out_second, out_grad, RATE_NORM, 0.0)
    return (
        (block_out, clip_pool, grad_rows.astype(F32)) + spatial + temporal + mid_new + out_new
    )


def solution(mesh):
    in_specs = (
        P("dp", "chan"),
        P("dp", "chan"),
        P("dp"),
        P(None, "dp", "chan"),
        P(None, "dp", "chan"),
        P(None, "dp", "chan"),
        P(None, None, "chan", "dp"),
        P(None, None, "chan", "dp"),
        P(None, None, "chan", "dp"),
        P(None, "chan"),
        P(None, "chan"),
        P(None, "chan"),
        P(None, "chan"),
        P(None, "chan"),
        P(None, "chan"),
    )
    out_specs = (
        P("dp", "chan"),
        P("dp", "chan"),
        P("dp", "chan"),
        P(None, "dp", "chan"),
        P(None, "dp", "chan"),
        P(None, "dp", "chan"),
        P(None, None, "chan", "dp"),
        P(None, None, "chan", "dp"),
        P(None, None, "chan", "dp"),
        P(None, "chan"),
        P(None, "chan"),
        P(None, "chan"),
        P(None, "chan"),
        P(None, "chan"),
        P(None, "chan"),
    )
    body = on_pairs if mesh.shape["dp"] == 8 and mesh.shape["chan"] == 4 else on_device
    return jax.shard_map(
        body, mesh=mesh, in_specs=in_specs, out_specs=out_specs, check_vma=False
    )
```

```python
import jax
import jax.numpy as jnp
import numpy as np
from jax import lax
from jax.experimental import pallas as pl
from jax.experimental.pallas import tpu as pltpu
from jax.sharding import PartitionSpec as P

FRAMES = 4
SIDE = 7
STEP = 10
HW = 49


EPS_NORM = 1e-05
EPS_ADAM = 1e-08
BETA_ONE = 0.9
BETA_TWO = 0.95
RATE_CONV = 0.01
RATE_NORM = 0.8
DECAY_CONV = 0.05


def frame_mask(clip_frames):
    kept_frames = clip_frames // 8
    frame_ids = jnp.arange(FRAMES, dtype=jnp.int32)
    frame_grid = (frame_ids[None, :] < kept_frames[:, None]).astype(jnp.float32)
    return jnp.broadcast_to(frame_grid[:, :, None], (kept_frames.shape[0], FRAMES, HW)).reshape(
        -1, 1
    )


def silu_slope(values):
    sigmoid = jax.nn.sigmoid(values)
    return sigmoid * (1.0 + values * (1.0 - sigmoid))


def spatial_apply(inputs, tap_weights):
    channels = inputs.shape[1]
    padded = jnp.pad(inputs.reshape(-1, SIDE, SIDE, channels), ((0, 0), (1, 1), (1, 1), (0, 0)))
    summed = jnp.zeros((inputs.shape[0], tap_weights.shape[2]), jnp.float32)
    for tap_index in range(9):
        row_off, col_off = (tap_index // 3, tap_index % 3)
        window = padded[:, row_off : row_off + SIDE, col_off : col_off + SIDE].reshape(-1, channels)
        summed = summed + jnp.dot(
            window, tap_weights[tap_index], preferred_element_type=jnp.float32
        )
    return (summed, padded)


def spatial_grads(padded, tap_weights, grad_out):
    channels = padded.shape[3]
    weight_terms = []
    input_sum = jnp.zeros((padded.shape[0], SIDE, SIDE, channels), jnp.float32)
    for tap_index in range(9):
        row_off, col_off = (tap_index // 3, tap_index % 3)
        window = padded[:, row_off : row_off + SIDE, col_off : col_off + SIDE].reshape(-1, channels)
        weight_terms.append(
            lax.dot_general(
                window, grad_out, (((0,), (0,)), ((), ())), preferred_element_type=jnp.float32
            )
        )
        pulled = lax.dot_general(
            grad_out,
            tap_weights[tap_index],
            (((1,), (1,)), ((), ())),
            preferred_element_type=jnp.float32,
        )
        pulled = jnp.pad(pulled.reshape(-1, SIDE, SIDE, channels), ((0, 0), (1, 1), (1, 1), (0, 0)))
        input_sum = (
            input_sum
            + pulled[:, 2 - row_off : 2 - row_off + SIDE, 2 - col_off : 2 - col_off + SIDE]
        )
    return (jnp.stack(weight_terms).reshape(-1, grad_out.shape[1]), input_sum.reshape(-1, channels))


def temporal_apply(inputs, weight):
    frame_seq = inputs.reshape(-1, FRAMES, HW, inputs.shape[1])
    padded = jnp.pad(frame_seq, ((0, 0), (1, 1), (0, 0), (0, 0)))
    summed = jnp.zeros(frame_seq.shape[:3] + (weight.shape[2],), jnp.float32)
    for frame_off in range(3):
        summed = summed + jnp.einsum(
            "nfpm,mc->nfpc",
            padded[:, frame_off : frame_off + FRAMES],
            weight[frame_off],
            preferred_element_type=jnp.float32,
        )
    return (summed.reshape(inputs.shape[0], -1), padded)


def temporal_grads(padded, weight, grad_full):
    grad_seq = grad_full.reshape(-1, FRAMES, HW, grad_full.shape[1])
    grad_pad = jnp.pad(grad_seq, ((0, 0), (1, 1), (0, 0), (0, 0)))
    weight_terms = []
    input_sum = jnp.zeros(padded.shape[:1] + (FRAMES, HW, padded.shape[3]), jnp.float32)
    for frame_off in range(3):
        weight_terms.append(
            jnp.einsum(
                "nfpm,nfpc->mc",
                padded[:, frame_off : frame_off + FRAMES],
                grad_seq,
                preferred_element_type=jnp.float32,
            )
        )
        input_sum = input_sum + jnp.einsum(
            "nfpc,mc->nfpm",
            grad_pad[:, 2 - frame_off : 2 - frame_off + FRAMES],
            weight[frame_off],
            preferred_element_type=jnp.float32,
        )
    return (jnp.stack(weight_terms), input_sum.reshape(grad_full.shape[0], -1))


def normalize(values, validity, gain_row, bias_row):
    local_valid = jnp.sum(validity)
    total_valid, value_sums = lax.psum((local_valid, jnp.sum(values * validity, axis=0)), "dp")
    average = value_sums / total_valid
    centered = values - average
    variance = lax.psum(jnp.sum(validity * centered * centered, axis=0), "dp") / total_valid
    inverse = lax.rsqrt(variance + EPS_NORM)
    standard = centered * inverse
    return (standard * gain_row + bias_row, standard, inverse, total_valid)


def normalize_back(grad_normed, standard, inverse, gain_row, total_valid, validity):
    grad_bias, grad_gain = lax.psum(
        (
            jnp.sum(grad_normed * validity, axis=0),
            jnp.sum(grad_normed * standard * validity, axis=0),
        ),
        "dp",
    )
    grad_values = (
        validity
        * gain_row
        * inverse
        * (grad_normed - grad_bias / total_valid - standard * grad_gain / total_valid)
    )
    return (grad_values, grad_gain, grad_bias)


def adam_update(weight, moment_one, moment_two, grad_value, rate, decay):
    fresh_one = BETA_ONE * moment_one + (1.0 - BETA_ONE) * grad_value
    fresh_two = BETA_TWO * moment_two + (1.0 - BETA_TWO) * grad_value * grad_value
    scaled = (
        fresh_one
        / (1.0 - BETA_ONE**STEP)
        / (jnp.sqrt(fresh_two / (1.0 - BETA_TWO**STEP)) + EPS_ADAM)
    )
    return (weight - rate * (scaled + decay * weight), fresh_one, fresh_two)


def on_device(
    features,
    cotangent,
    clip_frames,
    spatial_master,
    spatial_first,
    spatial_second,
    temporal_master,
    temporal_first,
    temporal_second,
    mid_norm,
    mid_first,
    mid_second,
    out_norm,
    out_first,
    out_second,
):
    validity = frame_mask(clip_frames)
    spatial_all, temporal_all = (
        lax.all_gather(spatial_master.astype(jnp.bfloat16), "dp", axis=1, tiled=True),
        lax.all_gather(temporal_master.astype(jnp.bfloat16), "dp", axis=3, tiled=True),
    )
    channels = temporal_all.shape[3]
    spatial_taps = spatial_all.reshape(2, 9, channels, spatial_all.shape[2])
    residual = features.astype(jnp.float32)
    outgoing = features
    kept_state = []
    for unit_index in range(2):
        gathered = lax.all_gather(outgoing, "chan", axis=1, tiled=True)
        spatial_out, padded = spatial_apply(gathered, spatial_taps[unit_index])
        mid_normed, mid_standard, mid_inverse, total_valid = normalize(
            spatial_out, validity, mid_norm[2 * unit_index], mid_norm[2 * unit_index + 1]
        )
        temporal_in = (jax.nn.silu(mid_normed) * validity).astype(jnp.bfloat16)
        partial_value, frames_padded = temporal_apply(temporal_in, temporal_all[unit_index])
        temporal_out = lax.psum_scatter(
            partial_value.astype(jnp.bfloat16), "chan", scatter_dimension=1, tiled=True
        ).astype(jnp.float32)
        out_normed, out_standard, out_inverse, total_valid = normalize(
            temporal_out, validity, out_norm[2 * unit_index], out_norm[2 * unit_index + 1]
        )
        if unit_index == 0:
            pre_act = out_normed
            outgoing = (jax.nn.silu(pre_act) * validity).astype(jnp.bfloat16)
        else:
            pre_act = out_normed + residual
            block_out = jax.nn.silu(pre_act) * validity
        kept_state.append(
            (
                padded,
                mid_normed,
                mid_standard,
                mid_inverse,
                frames_padded,
                pre_act,
                out_standard,
                out_inverse,
            )
        )
    kept_frames = (clip_frames // 8).astype(jnp.float32)
    clip_pool = (
        jnp.sum(block_out.reshape(-1, FRAMES * HW, block_out.shape[1]), axis=1)
        / (HW * kept_frames)[:, None]
    )
    skip_grad = cotangent * validity * silu_slope(kept_state[1][5])
    grad_pre = skip_grad
    spatial_list = [None, None]
    temporal_list = [None, None]
    mid_rows = [None, None]
    out_rows = [None, None]
    grad_hidden = skip_grad
    for unit_index in (1, 0):
        (
            padded,
            mid_normed,
            mid_standard,
            mid_inverse,
            frames_padded,
            pre_act,
            out_standard,
            out_inverse,
        ) = kept_state[unit_index]
        if unit_index == 0:
            grad_pre = grad_hidden * validity * silu_slope(pre_act)
        grad_temporal, out_gain_grad, out_bias_grad = normalize_back(
            grad_pre, out_standard, out_inverse, out_norm[2 * unit_index], total_valid, validity
        )
        grad_full = lax.all_gather(grad_temporal.astype(jnp.bfloat16), "chan", axis=1, tiled=True)
        temporal_grad, grad_mid = temporal_grads(frames_padded, temporal_all[unit_index], grad_full)
        grad_mid_normed = grad_mid * validity * silu_slope(mid_normed)
        grad_spatial, mid_gain_grad, mid_bias_grad = normalize_back(
            grad_mid_normed,
            mid_standard,
            mid_inverse,
            mid_norm[2 * unit_index],
            total_valid,
            validity,
        )
        spatial_grad, grad_in_part = spatial_grads(
            padded, spatial_taps[unit_index], grad_spatial.astype(jnp.bfloat16)
        )
        grad_hidden = lax.psum_scatter(
            grad_in_part.astype(jnp.bfloat16), "chan", scatter_dimension=1, tiled=True
        ).astype(jnp.float32)
        spatial_list[unit_index] = spatial_grad
        temporal_list[unit_index] = temporal_grad
        mid_rows[unit_index] = (mid_gain_grad, mid_bias_grad)
        out_rows[unit_index] = (out_gain_grad, out_bias_grad)
    input_grad = grad_hidden + skip_grad
    spatial_sum, temporal_sum = (
        lax.psum_scatter(jnp.stack(spatial_list), "dp", scatter_dimension=1, tiled=True),
        lax.psum_scatter(jnp.stack(temporal_list), "dp", scatter_dimension=3, tiled=True),
    )
    mid_grad = jnp.stack([mid_rows[0][0], mid_rows[0][1], mid_rows[1][0], mid_rows[1][1]])
    out_grad = jnp.stack([out_rows[0][0], out_rows[0][1], out_rows[1][0], out_rows[1][1]])
    spatial_new, spatial_one, spatial_two = adam_update(
        spatial_master, spatial_first, spatial_second, spatial_sum, RATE_CONV, DECAY_CONV
    )
    temporal_new, temporal_one, temporal_two = adam_update(
        temporal_master, temporal_first, temporal_second, temporal_sum, RATE_CONV, DECAY_CONV
    )
    mid_new, mid_one, mid_two = adam_update(
        mid_norm, mid_first, mid_second, mid_grad, RATE_NORM, 0.0
    )
    out_new, out_one, out_two = adam_update(
        out_norm, out_first, out_second, out_grad, RATE_NORM, 0.0
    )
    return (
        block_out,
        clip_pool,
        input_grad,
        spatial_new,
        spatial_one,
        spatial_two,
        temporal_new,
        temporal_one,
        temporal_two,
        mid_new,
        mid_one,
        mid_two,
        out_new,
        out_one,
        out_two,
    )


F32 = jnp.float32
BF16 = jnp.bfloat16
MESH = pl.DeviceIdType.MESH
VMEM = pltpu.VMEM
NN = (((1,), (0,)), ((), ()))
NT = (((1,), (1,)), ((), ()))
TN = (((0,), (0,)), ((), ()))
BLOCK_C = 512
MID_C = 1152
THIRD = MID_C // 3
ROWS = 784
SLOTS = 16
SHUFFLE_C = 896
HALF = 144
SUB = 48
TAPS_C = 9 * BLOCK_C
CHIP_S = TAPS_C // 4
CHIP_T = BLOCK_C // 4
CHUNKS = (
    ("s", 0, 0, 1),
    ("s", 0, 1, 1),
    ("s", 0, 2, 1),
    ("t", 0, 0, 9),
    ("s", 1, 0, 1),
    ("s", 1, 1, 1),
    ("s", 1, 2, 1),
    ("t", 1, 0, 9),
)
N_CHUNKS = len(CHUNKS)
PARTS = (("s", 0), ("t", 0), ("s", 1), ("t", 1))
GRANT = 65000 * 1024


def place():
    dp = lax.axis_index("dp")
    line = lax.axis_index("chan")
    core = lax.rem(dp, 2)
    chip = lax.div(dp, 2)
    x_bit = lax.rem(chip, 2)
    y_bit = lax.div(chip, 2)
    return dict(
        dp=dp,
        line=line,
        core=core,
        chip=chip,
        chip_x=chip + 1 - 2 * x_bit,
        chip_y=chip + 2 - 4 * y_bit,
        chip_d=3 - chip,
        pair=(dp + 1 - 2 * core, line),
        x=(dp + 2 - 4 * x_bit, line),
        y=(dp + 4 - 8 * y_bit, line),
    )


def remote(source, target, send, recv, device):
    return pltpu.make_async_remote_copy(
        src_ref=source,
        dst_ref=target,
        send_sem=send,
        recv_sem=recv,
        device_id=device,
        device_id_type=MESH,
    )


def greet(devices):
    barrier = pltpu.get_barrier_semaphore()
    for device in devices:
        pl.semaphore_signal(barrier, inc=1, device_id=device, device_id_type=MESH)
    pl.semaphore_wait(barrier, len(devices))


def line_peer(at, step):
    return (at["dp"], lax.rem(at["line"] + step, 4))


def ring_peer(at, step):
    return (lax.rem(at["dp"] + step, 8), at["line"])


def greet_all(at):
    greet(
        [ring_peer(at, step) for step in range(1, 8)]
        + [line_peer(at, step) for step in (1, 2, 3)]
    )


def rows_of(pixel):
    return pl.ds(pl.multiple_of(pixel * SLOTS, SLOTS), SLOTS)


def slope_of(values):
    sigmoid = jax.nn.sigmoid(values)
    return sigmoid * (1.0 + values * (1.0 - sigmoid))


def over_pixels(body, carry):
    return lax.fori_loop(0, HW, body, carry, unroll=7)


def combine_moments(blocks):
    total = sum(block[2:3] for block in blocks)
    mean = sum(block[2:3] * block[0:1] for block in blocks) / total
    spread = sum(
        block[1:2] + block[2:3] * (block[0:1] - mean) * (block[0:1] - mean) for block in blocks
    )
    return [mean, spread, total]


def combine_sums(blocks):
    return [sum(block[0:1] for block in blocks), sum(block[1:2] for block in blocks)]


def exchange(
    at, land, land_two, index, sems, sem_index, count, payload, combine, hooks=(None, None)
):
    dp, line = at["dp"], at["line"]
    one_send, one_recv, two_send, two_recv = sems
    for row, value in enumerate(payload):
        land[index, dp, row : row + 1, :] = value
    sent = []
    for step in range(1, 8):
        here = land.at[index, dp, pl.ds(0, count)]
        copy = remote(
            here,
            here,
            one_send.at[sem_index, step - 1],
            one_recv.at[sem_index, step - 1],
            ring_peer(at, step),
        )
        copy.start()
        sent.append(copy)
    if hooks[0] is not None:
        hooks[0]()
    for step in range(1, 8):
        there = land.at[index, lax.rem(dp + 8 - step, 8), pl.ds(0, count)]
        remote(
            there,
            there,
            one_send.at[sem_index, step - 1],
            one_recv.at[sem_index, step - 1],
            ring_peer(at, step),
        ).wait_recv()
    for copy in sent:
        copy.wait_send()
    merged = combine([land[index, source] for source in range(8)])
    for row, value in enumerate(merged):
        land_two[index, line, row : row + 1, :] = value
    sent = []
    for step in (1, 2, 3):
        here = land_two.at[index, line, pl.ds(0, count)]
        copy = remote(
            here,
            here,
            two_send.at[sem_index, step - 1],
            two_recv.at[sem_index, step - 1],
            line_peer(at, step),
        )
        copy.start()
        sent.append(copy)
    if hooks[1] is not None:
        hooks[1]()
    for step in (1, 2, 3):
        there = land_two.at[index, lax.rem(line + 4 - step, 4), pl.ds(0, count)]
        remote(
            there,
            there,
            two_send.at[sem_index, step - 1],
            two_recv.at[sem_index, step - 1],
            line_peer(at, step),
        ).wait_recv()
    for copy in sent:
        copy.wait_send()
    return combine([land_two[index, source] for source in range(4)])


def forward_kernel(
    ws_in,
    wt_in,
    feat_in,
    cot_in,
    par_in,
    shuffle,
    mask_in,
    ws_out,
    wt_out,
    par_out,
    block_out,
    a_out,
    s_out,
    u_out,
    t_out,
    skip_out,
    stat_mid,
    stat_out,
    pair_s,
    pair_t,
    stage_s,
    stage_t,
    feat_land,
    cot_land,
    par_land,
    a_pad,
    s_ref,
    x_ref,
    u_ref,
    t_ref,
    side,
    feat_ref,
    thin,
    w_buf,
    wt_buf,
    land_mid,
    land_mid_two,
    land_out,
    land_out_two,
    pair_send,
    pair_recv,
    act_send,
    act_recv,
    line_send,
    line_recv,
    plane_send,
    plane_recv,
    diag_send,
    diag_recv,
    core_send,
    core_recv,
    own_sem,
    chunk_sem,
    w_sem,
    wt_sem,
    save_sem,
    one_send,
    one_recv,
    two_send,
    two_recv,
):
    at = place()
    line, core, chip = at["line"], at["core"], at["chip"]
    sems = (one_send, one_recv, two_send, two_recv)
    greet_all(at)
    started = []

    def send(copy):
        copy.start()
        started.append(copy)
        return copy

    def area(chunk, owner_core, owner_chip, first, count):
        kind, unit, lead, leads = chunk
        ref, width = (ws_out, CHIP_S) if kind == "s" else (wt_out, CHIP_T)
        lanes = pl.ds(pl.multiple_of(owner_chip * width, 128), width)
        return ref.at[unit, pl.ds(lead, leads), pl.ds(first, count), owner_core, :, lanes]

    pairs = {}
    for index, (kind, unit) in enumerate(PARTS):
        theirs = pl.ds(pl.multiple_of((1 - core) * HALF, 16), HALF)
        source, landing = (ws_in, pair_s) if kind == "s" else (wt_in, pair_t)
        pairs[kind, unit] = send(
            remote(
                source.at[unit, theirs],
                landing.at[unit],
                pair_send.at[index],
                pair_recv.at[index],
                at["pair"],
            )
        )

    def acts(row, source, target):
        def cut(owner):
            return source.at[pl.ds(pl.multiple_of(owner * ROWS, 16), ROWS)]

        lanes = pl.ds(pl.multiple_of(line * 128, 128), 128)
        for step in (1, 2, 3):
            peer = line_peer(at, step)
            send(
                remote(
                    cut(peer[1]),
                    target.at[:, lanes],
                    act_send.at[row, step - 1],
                    act_recv.at[row, step - 1],
                    peer,
                )
            )
        own = pltpu.make_async_copy(cut(line), target.at[:, lanes], own_sem.at[row])
        own.start()
        return own

    def acts_wait(row, source, target, own):
        for step in (1, 2, 3):
            origin = lax.rem(line + 4 - step, 4)
            lanes = pl.ds(pl.multiple_of(origin * 128, 128), 128)
            remote(
                source.at[pl.ds(0, ROWS)],
                target.at[:, lanes],
                act_send.at[row, step - 1],
                act_recv.at[row, step - 1],
                line_peer(at, step),
            ).wait_recv()
        own.wait()

    mine = pl.ds(pl.multiple_of(core * HALF, 16), HALF)

    def merge(kind, unit):
        pairs[kind, unit].wait_recv()
        source, landing = (ws_in, pair_s) if kind == "s" else (wt_in, pair_t)
        low = source[unit, mine].astype(F32)
        high = landing[unit].astype(F32)
        first = jnp.where(core == 0, low, high)
        second = jnp.where(core == 0, high, low)
        if kind == "s":
            both = jnp.concatenate([first, second], axis=1).astype(BF16)
            stage_s[unit] = both.reshape(3, 1, SUB, CHIP_S)
        else:
            for tau in range(3):
                lanes = slice(64 * tau, 64 * tau + 64)
                both = jnp.concatenate([first[:, lanes], second[:, lanes]], axis=1).astype(BF16)
                stage_t[unit, 3 * tau : 3 * tau + 3] = both.reshape(3, 1, SUB, CHIP_T)

    own_copies = [None] * N_CHUNKS

    def step_line(index):
        chunk = CHUNKS[index]
        kind, unit, lead, leads = chunk
        if lead == 0:
            merge(kind, unit)
        staged = (stage_s if kind == "s" else stage_t).at[unit, pl.ds(lead, leads)]
        target = area(chunk, core, chip, line, 1)
        for step in (1, 3, 2):
            send(
                remote(
                    staged,
                    target,
                    line_send.at[index, step - 1],
                    line_recv.at[index, step - 1],
                    line_peer(at, step),
                )
            )
        own = pltpu.make_async_copy(staged, target, chunk_sem.at[index])
        own.start()
        own_copies[index] = own

    def step_plane(index):
        chunk = CHUNKS[index]
        for step in (1, 2, 3):
            origin = area(chunk, core, chip, lax.rem(line + 4 - step, 4), 1)
            remote(
                origin,
                origin,
                line_send.at[index, step - 1],
                line_recv.at[index, step - 1],
                line_peer(at, step),
            ).wait_recv()
        own_copies[index].wait()
        held = area(chunk, core, chip, 0, 4)
        for way, name in enumerate(("x", "y")):
            send(
                remote(held, held, plane_send.at[index, way], plane_recv.at[index, way], at[name])
            )
        send(remote(held, held, core_send.at[index, 0], core_recv.at[index, 0], at["pair"]))

    def step_diag(index):
        chunk = CHUNKS[index]
        for way, (name, other, first) in enumerate((("x", "y", 0), ("y", "x", 2))):
            held = area(chunk, core, at["chip_" + name], 0, 4)
            remote(
                held, held, plane_send.at[index, way], plane_recv.at[index, way], at[name]
            ).wait_recv()
            half = area(chunk, core, at["chip_" + name], first, 2)
            send(
                remote(half, half, diag_send.at[index, way], diag_recv.at[index, way], at[other])
            )
            send(
                remote(
                    held, held, core_send.at[index, 1 + way], core_recv.at[index, 1 + way], at["pair"]
                )
            )

    def step_core(index):
        chunk = CHUNKS[index]
        for way, (other, first) in enumerate((("y", 0), ("x", 2))):
            half = area(chunk, core, at["chip_d"], first, 2)
            remote(
                half, half, diag_send.at[index, way], diag_recv.at[index, way], at[other]
            ).wait_recv()
        held = area(chunk, core, at["chip_d"], 0, 4)
        send(remote(held, held, core_send.at[index, 3], core_recv.at[index, 3], at["pair"]))

    def step_end(index):
        chunk = CHUNKS[index]
        for slot, name in enumerate(("chip", "chip_x", "chip_y", "chip_d")):
            held = area(chunk, 1 - core, at[name], 0, 4)
            remote(
                held, held, core_send.at[index, slot], core_recv.at[index, slot], at["pair"]
            ).wait_recv()
        kind, unit, lead, _ = chunk
        if kind == "s":
            fetch_w(unit, lead).start()
        else:
            fetch_wt(unit).start()

    def fetch_w(unit, third):
        slot = (3 * unit + third) % 2
        return pltpu.make_async_copy(ws_out.at[unit, third], w_buf.at[slot], w_sem.at[slot])

    def fetch_wt(unit):
        return pltpu.make_async_copy(wt_out.at[unit], wt_buf, wt_sem.at[0])

    def window(unit, tap):
        row, column = tap // 3, tap % 3
        return a_pad[unit, row : row + SIDE, column : column + SIDE].reshape(ROWS, BLOCK_C)

    def conv(unit, third):
        fetch_w(unit, third).wait()
        taps = jnp.concatenate([window(unit, tap) for tap in range(9)], axis=1)
        s_ref[:, third * THIRD : (third + 1) * THIRD] = lax.dot_general(
            taps,
            w_buf[(3 * unit + third) % 2].reshape(THIRD, TAPS_C),
            NT,
            preferred_element_type=F32,
        )

    mask_mid = mask_in[...]
    mask_out = mask_in[:, :BLOCK_C]
    slot_rows = lax.broadcasted_iota(jnp.int32, (SLOTS, BLOCK_C), 0)
    has_before = (slot_rows >= 4).astype(F32)
    has_after = (slot_rows < 12).astype(F32)

    def moments(values, mask, land, land_two, index, sem_index, hooks):
        zero = jnp.zeros(mask.shape, F32)
        local = HW * jnp.sum(mask, axis=0, keepdims=True)
        added = over_pixels(lambda p, acc: acc + values[rows_of(p), :], zero)
        mean = jnp.sum(added * mask, axis=0, keepdims=True) / local

        def squares(p, acc):
            centered = values[rows_of(p), :] - mean
            return acc + centered * centered

        spread = jnp.sum(over_pixels(squares, zero) * mask, axis=0, keepdims=True)
        mean, spread, total = exchange(
            at,
            land,
            land_two,
            index,
            sems,
            sem_index,
            4,
            [mean, spread, local],
            combine_moments,
            hooks,
        )
        return mean, lax.rsqrt(spread / total + EPS_NORM), total

    saves = []

    def save(source, target):
        copy = pltpu.make_async_copy(source, target, save_sem.at[len(saves)])
        copy.start()
        saves.append(copy)

    def mid_norm_act(unit, *hooks):
        gain = par_out[2 * unit : 2 * unit + 1]
        bias = par_out[2 * unit + 1 : 2 * unit + 2]
        mean, inverse, total = moments(
            s_ref, mask_mid, land_mid, land_mid_two, unit, 2 * unit, hooks
        )
        stat_mid[2 * unit : 2 * unit + 1] = inverse
        stat_mid[2 * unit + 1 : 2 * unit + 2] = total

        def mid_act(p, carry):
            rows = rows_of(p)
            standard = (s_ref[rows, :] - mean) * inverse
            x_ref[unit, rows, :] = standard.astype(BF16)
            normed = standard * gain + bias
            u_ref[unit, rows, :] = (jax.nn.sigmoid(normed) * normed * mask_mid).astype(BF16)
            return carry

        over_pixels(mid_act, 0)
        save(x_ref.at[unit], s_out.at[unit])
        save(u_ref.at[unit], u_out.at[unit])

    def temporal(unit):
        fetch_wt(unit).wait()

        def weight(tau):
            return wt_buf[3 * tau : 3 * tau + 3].reshape(MID_C, BLOCK_C)

        t_ref[unit] = lax.dot_general(u_ref[unit], weight(1), NN, preferred_element_type=F32)
        side[0] = lax.dot_general(u_ref[unit], weight(0), NN, preferred_element_type=F32)
        side[1] = lax.dot_general(u_ref[unit], weight(2), NN, preferred_element_type=F32)

        def frames(p, carry):
            rows = rows_of(p)
            t_ref[unit, rows, :] = (
                t_ref[unit, rows, :]
                + pltpu.roll(side[0, rows, :], 4, 0) * has_before
                + pltpu.roll(side[1, rows, :], 12, 0) * has_after
            )
            return carry

        over_pixels(frames, 0)

    def out_stats(unit, *hooks):
        mean, inverse, total = moments(
            t_ref.at[unit], mask_out, land_out, land_out_two, unit, 2 * unit + 1, hooks
        )
        stat_out[2 * unit : 2 * unit + 1] = inverse
        stat_out[2 * unit + 1 : 2 * unit + 2] = total
        gain = par_out[4 + 2 * unit : 5 + 2 * unit, :BLOCK_C]
        bias = par_out[5 + 2 * unit : 6 + 2 * unit, :BLOCK_C]
        return mean, inverse, gain, bias

    step_line(0)
    step_line(1)
    step_line(2)
    feat_own = acts(0, feat_in, feat_land)
    step_line(3)
    for step in (1, 2, 3):
        send(
            remote(
                par_in,
                par_land.at[line],
                act_send.at[2, step - 1],
                act_recv.at[2, step - 1],
                line_peer(at, step),
            )
        )
    par_own = pltpu.make_async_copy(par_in, par_land.at[line], own_sem.at[2])
    par_own.start()
    step_line(4)
    for unit in range(2):
        a_pad[unit] = jnp.zeros(a_pad.shape[1:], BF16)
    step_plane(0)
    step_plane(1)
    step_diag(0)
    step_plane(2)
    step_diag(1)
    step_core(0)
    permute = shuffle[:, :ROWS]
    acts_wait(0, feat_in, feat_land, feat_own)
    feat_ref[...] = lax.dot_general(permute, feat_land[...], NN, preferred_element_type=F32).astype(
        BF16
    )

    def fill(p, carry):
        a_pad[0, 1 + p // SIDE, 1 + p % SIDE] = feat_ref[rows_of(p), :]
        return carry

    over_pixels(fill, 0)
    save(a_pad.at[0], a_out.at[0])
    step_diag(2)
    step_end(0)
    conv(0, 0)
    step_core(1)
    step_end(1)
    conv(0, 1)
    step_plane(3)
    step_core(2)
    step_end(2)
    conv(0, 2)
    for step in (1, 2, 3):
        remote(
            par_in,
            par_land.at[lax.rem(line + 4 - step, 4)],
            act_send.at[2, step - 1],
            act_recv.at[2, step - 1],
            line_peer(at, step),
        ).wait_recv()
    par_own.wait()
    par_out[...] = par_land[0] + par_land[1] + par_land[2] + par_land[3]

    def hook_a():
        step_diag(3)
        step_plane(4)

    mid_norm_act(0, hook_a, lambda: step_line(5))
    step_core(3)
    step_end(3)
    temporal(0)
    cot_own = []

    def hook_b():
        step_diag(4)
        step_plane(5)

    def hook_c():
        step_line(6)
        step_line(7)
        cot_own.append(acts(1, cot_in, cot_land))

    mean, inverse, gain, bias = out_stats(0, hook_b, hook_c)

    def out_act(p, carry):
        rows = rows_of(p)
        standard = (t_ref[0, rows, :] - mean) * inverse
        t_ref[0, rows, :] = standard
        normed = standard * gain + bias
        hidden = jax.nn.sigmoid(normed) * normed * mask_out
        a_pad[1, 1 + p // SIDE, 1 + p % SIDE] = hidden.astype(BF16)
        return carry

    over_pixels(out_act, 0)
    save(t_ref.at[0], t_out.at[0])
    save(a_pad.at[1], a_out.at[1])
    step_core(4)
    step_end(4)
    conv(1, 0)
    step_diag(5)
    step_plane(6)
    step_core(5)
    step_end(5)
    conv(1, 1)
    step_diag(6)
    step_plane(7)
    step_core(6)
    step_end(6)
    conv(1, 2)
    mid_norm_act(1, lambda: step_diag(7), None)
    step_core(7)
    step_end(7)
    temporal(1)

    def hook_d():
        acts_wait(1, cot_in, cot_land, cot_own[0])
        side[0] = lax.dot_general(permute, cot_land[...], NN, preferred_element_type=F32)

    mean_one, inverse_one, gain_one, bias_one = out_stats(1, hook_d, None)

    def end_act(p, carry):
        rows = rows_of(p)
        standard = (t_ref[1, rows, :] - mean_one) * inverse_one
        t_ref[1, rows, :] = standard
        pre = standard * gain_one + bias_one + feat_ref[rows, :].astype(F32)
        sigmoid = jax.nn.sigmoid(pre)
        thin[rows, :] = (pre * sigmoid * mask_out).astype(BF16)
        slope = sigmoid * (1.0 + pre * (1.0 - sigmoid))
        cot_land[rows, :] = (side[0, rows, :] * mask_out * slope).astype(BF16)
        return carry

    over_pixels(end_act, 0)
    save(t_ref.at[1], t_out.at[1])
    save(cot_land, skip_out)
    block_out[...] = lax.dot_general(permute, thin[...], TN, preferred_element_type=F32).astype(
        BF16
    )
    for copy in saves:
        copy.wait()
    for copy in started:
        copy.wait_send()


def backward_kernel(
    ws,
    wt,
    a_in,
    s_in,
    u_in,
    t_in,
    skip_in,
    stat_mid,
    stat_out,
    par,
    mask_in,
    shuffle,
    block_in,
    sum_s,
    sum_t,
    mid_grad,
    out_grad,
    block_out,
    input_out,
    a_pad,
    s_ref,
    u_ref,
    t_ref,
    side,
    skip_ref,
    wide,
    ds_pad,
    d_ref,
    w_buf,
    land_mid,
    land_mid_two,
    land_out,
    land_out_two,
    g_s,
    g_t,
    land_s,
    land_t,
    one_s,
    one_t,
    two_s,
    two_t,
    line_s,
    line_t,
    fin_s,
    fin_t,
    load_sem,
    w_sem,
    ex_one_send,
    ex_one_recv,
    ex_two_send,
    ex_two_recv,
    act_send,
    act_recv,
    act_sem,
    pair_send,
    pair_recv,
    one_send,
    one_recv,
    two_send,
    two_recv,
    line_send,
    line_recv,
    fin_send,
    fin_recv,
):
    at = place()
    line, core, chip = at["line"], at["core"], at["chip"]
    sems = (ex_one_send, ex_one_recv, ex_two_send, ex_two_recv)

    def load(index, source, target):
        return pltpu.make_async_copy(source, target, load_sem.at[index])

    load_t = [load(0, t_in.at[unit], t_ref) for unit in range(2)]
    load_u = [load(1, u_in.at[unit], u_ref) for unit in range(2)]
    load_s = [load(2, s_in.at[unit], s_ref) for unit in range(2)]
    load_a = [load(3, a_in.at[unit], a_pad) for unit in range(2)]
    load_skip = load(4, skip_in, skip_ref)
    load_shuffle = load(5, shuffle, u_ref.at[:, pl.ds(0, SHUFFLE_C)])
    load_t[1].start()
    load_skip.start()
    load_u[1].start()
    load_s[1].start()
    load_a[1].start()
    greet_all(at)
    ds_pad[...] = jnp.zeros(ds_pad.shape, BF16)

    mask_mid = mask_in[...]
    mask_out = mask_in[:, :BLOCK_C]
    slot_rows = lax.broadcasted_iota(jnp.int32, (SLOTS, BLOCK_C), 0)
    has_before = (slot_rows >= 4).astype(F32)
    has_after = (slot_rows < 12).astype(F32)
    lanes_line = pl.ds(pl.multiple_of(line * 128, 128), 128)
    rows_line = pl.ds(pl.multiple_of(line * ROWS, 16), ROWS)

    act_copies = []

    def acts(row, source, target):
        for step in (1, 2, 3):
            peer = line_peer(at, step)
            copy = remote(
                source.at[:, pl.ds(pl.multiple_of(peer[1] * 128, 128), 128)],
                target.at[rows_line],
                act_send.at[row, step - 1],
                act_recv.at[row, step - 1],
                peer,
            )
            copy.start()
            act_copies.append(copy)
        own = pltpu.make_async_copy(source.at[:, lanes_line], target.at[rows_line], act_sem.at[row])
        own.start()
        return own

    def acts_wait(row, source, target, own):
        for step in (1, 2, 3):
            origin = lax.rem(line + 4 - step, 4)
            remote(
                source.at[:, lanes_line],
                target.at[pl.ds(pl.multiple_of(origin * ROWS, 16), ROWS)],
                act_send.at[row, step - 1],
                act_recv.at[row, step - 1],
                line_peer(at, step),
            ).wait_recv()
        own.wait()

    flying = [[] for _ in CHUNKS]
    pair_copies = [None] * N_CHUNKS
    fin_copies = [None] * N_CHUNKS

    def launch(index, copy):
        copy.start()
        flying[index].append(copy)
        return copy

    def drain(index):
        for copy in flying[index]:
            copy.wait_send()
        flying[index] = []

    def grad_of(index):
        kind, _, lead, _ = CHUNKS[index]
        return g_s.at[lead] if kind == "s" else g_t

    def land_of(index):
        kind, _, lead, _ = CHUNKS[index]
        return land_s.at[lead] if kind == "s" else land_t

    def held(index, small, large):
        kind, unit, lead, _ = CHUNKS[index]
        return large.at[unit, lead] if kind == "s" else small.at[unit]

    def cut(index, owner, first, count):
        width = CHIP_S if CHUNKS[index][0] == "s" else CHIP_T
        lanes = pl.ds(pl.multiple_of(owner * width, 128), width)
        return grad_of(index).at[:, pl.ds(first, count), core, :, lanes]

    def add_into(target, source):
        leads, count, _, width = target.shape

        def body(turn, carry):
            if leads == 1 and width > 2048:
                where = (0, lax.div(turn, 3), pl.ds(pl.multiple_of(lax.rem(turn, 3) * 16, 16), 16))
            elif leads == 1:
                where = (0, turn)
            else:
                where = (turn,)
            target[where] = (target[where].astype(F32) + source[where].astype(F32)).astype(BF16)
            return carry

        turns = leads if leads > 1 else count * (3 if width > 2048 else 1)
        lax.fori_loop(0, turns, body, 0)

    def step_pair(index):
        pair_copies[index] = launch(
            index,
            remote(
                grad_of(index).at[:, :, 1 - core],
                land_of(index),
                pair_send.at[index],
                pair_recv.at[index],
                at["pair"],
            ),
        )

    def step_one(index):
        pair_copies[index].wait_recv()
        add_into(grad_of(index).at[:, :, core], land_of(index))
        ones, twos = held(index, one_t, one_s), held(index, two_t, two_s)
        for way, (name, first) in enumerate((("x", 0), ("y", 2))):
            launch(
                index,
                remote(
                    cut(index, at["chip_d"], first, 2),
                    ones.at[way],
                    one_send.at[index, way],
                    one_recv.at[index, way],
                    at[name],
                ),
            )
            launch(
                index,
                remote(
                    cut(index, at["chip_" + name], first, 2),
                    twos.at[way, :, pl.ds(first, 2)],
                    two_send.at[index, way, 0],
                    two_recv.at[index, way, 0],
                    at[name],
                ),
            )

    def step_two(index):
        ones, twos = held(index, one_t, one_s), held(index, two_t, two_s)
        for way, (name, other, first) in enumerate((("x", "y", 0), ("y", "x", 2))):
            landing = ones.at[way]
            remote(
                landing, landing, one_send.at[index, way], one_recv.at[index, way], at[name]
            ).wait_recv()
            target = cut(index, at["chip_" + other], first, 2)
            add_into(target, landing)
            launch(
                index,
                remote(
                    target,
                    twos.at[1 - way, :, pl.ds(first, 2)],
                    two_send.at[index, 1 - way, 1],
                    two_recv.at[index, 1 - way, 1],
                    at[other],
                ),
            )

    def step_three(index):
        twos = held(index, two_t, two_s)
        for way, (name, first) in enumerate((("x", 0), ("y", 2))):
            for turn, begin in enumerate((first, 2 - first)):
                landing = twos.at[way, :, pl.ds(begin, 2)]
                remote(
                    landing,
                    landing,
                    two_send.at[index, way, turn],
                    two_recv.at[index, way, turn],
                    at[name],
                ).wait_recv()
        own = cut(index, chip, 0, 4)
        leads = own.shape[0]

        def body(turn, carry):
            where = (0, turn) if leads == 1 else (turn,)
            own[where] = (
                own[where].astype(F32)
                + twos.at[0][where].astype(F32)
                + twos.at[1][where].astype(F32)
            ).astype(BF16)
            return carry

        lax.fori_loop(0, 4 if leads == 1 else leads, body, 0)
        lines = held(index, line_t, line_s)
        for step in (1, 3, 2):
            peer = line_peer(at, step)
            launch(
                index,
                remote(
                    cut(index, chip, peer[1], 1),
                    lines.at[step - 1],
                    line_send.at[index, step - 1],
                    line_recv.at[index, step - 1],
                    peer,
                ),
            )

    def step_four(index):
        lines, fin = held(index, line_t, line_s), held(index, fin_t, fin_s)
        for step in (1, 2, 3):
            landing = lines.at[step - 1]
            remote(
                landing,
                landing,
                line_send.at[index, step - 1],
                line_recv.at[index, step - 1],
                line_peer(at, step),
            ).wait_recv()
        total = cut(index, chip, line, 1)[...].astype(F32)
        for step in range(3):
            total = total + lines[step].astype(F32)
        fin[0] = total
        fin_copies[index] = launch(
            index,
            remote(fin.at[0], fin.at[1], fin_send.at[index], fin_recv.at[index], at["pair"]),
        )

    def step_five(index):
        kind, unit, lead, leads = CHUNKS[index]
        fin_copies[index].wait_recv()
        fin = held(index, fin_t, fin_s)
        for which in range(2):
            half = core if which == 0 else 1 - core
            if kind == "s":
                width = CHIP_S // 2
                rows = pl.ds(pl.multiple_of(half * HALF + SUB * lead, 16), SUB)
                value = fin[which, 0, 0]
                sum_s[unit, rows, :] = jnp.where(core == 0, value[:, :width], value[:, width:])
            else:
                width = CHIP_T // 2
                rows = pl.ds(pl.multiple_of(half * HALF, 16), HALF)
                for tau in range(3):
                    value = fin[which, 3 * tau : 3 * tau + 3].reshape(HALF, CHIP_T)
                    sum_t[unit, tau, rows, :] = jnp.where(
                        core == 0, value[:, :width], value[:, width:]
                    )

    def fetch_w(unit, tap, slot):
        lanes = pl.ds(pl.multiple_of(tap * BLOCK_C, 128), BLOCK_C)
        return pltpu.make_async_copy(ws.at[unit, :, lanes], w_buf.at[slot], w_sem.at[slot])

    def fetch_wt(unit, tau, slot):
        return pltpu.make_async_copy(wt.at[unit, tau], w_buf.at[slot], w_sem.at[slot])

    def window(tap):
        return a_pad[pl.ds(tap // 3, SIDE), pl.ds(tap % 3, SIDE)].reshape(ROWS, BLOCK_C)

    zero_mid = jnp.zeros((SLOTS, MID_C), F32)
    zero_out = jnp.zeros((SLOTS, BLOCK_C), F32)

    def out_norm_back(unit, *hooks):
        grad_ref = skip_ref if unit == 1 else side
        gain = par[4 + 2 * unit : 5 + 2 * unit, :BLOCK_C]
        inverse = stat_out[2 * unit : 2 * unit + 1]
        total = stat_out[2 * unit + 1 : 2 * unit + 2]

        def out_sums(p, carry):
            rows = rows_of(p)
            grad = grad_ref[rows, :].astype(F32)
            return (carry[0] + grad, carry[1] + grad * t_ref[rows, :])

        bias_acc, gain_acc = over_pixels(out_sums, (zero_out, zero_out))
        sums = [
            jnp.sum(bias_acc, axis=0, keepdims=True),
            jnp.sum(gain_acc, axis=0, keepdims=True),
        ]
        grad_bias, grad_gain = exchange(
            at, land_out, land_out_two, unit, sems, 2 * unit, 2, sums, combine_sums, hooks
        )
        out_grad[2 * unit : 2 * unit + 1, :] = grad_gain
        out_grad[2 * unit + 1 : 2 * unit + 2, :] = grad_bias
        scale = gain * inverse
        bias_part, gain_part = grad_bias / total, grad_gain / total

        def out_back(p, carry):
            rows = rows_of(p)
            value = (
                mask_out
                * scale
                * (grad_ref[rows, :].astype(F32) - bias_part - t_ref[rows, :] * gain_part)
            )
            d_ref[1, rows, :] = value.astype(BF16)
            d_ref[0, rows, :] = (pltpu.roll(value, 12, 0) * has_after).astype(BF16)
            d_ref[2, rows, :] = (pltpu.roll(value, 4, 0) * has_before).astype(BF16)
            return carry

        over_pixels(out_back, 0)

    def temporal_grad():
        for tau in range(3):
            g_t[3 * tau : 3 * tau + 3] = (
                lax.dot_general(u_ref[...], d_ref[tau], TN, preferred_element_type=F32)
                .astype(BF16)
                .reshape(3, 4, 2, SUB, BLOCK_C)
            )

    def temporal_back(unit):
        for tau in range(3):
            slot = tau % 2
            if tau < 2:
                fetch_wt(unit, tau + 1, 1 - slot).start()
            fetch_wt(unit, tau, slot).wait()
            value = lax.dot_general(d_ref[tau], w_buf[slot], NT, preferred_element_type=F32)
            wide[...] = value if tau == 0 else wide[...] + value

    def mid_norm_back(unit, *hooks):
        gain = par[2 * unit : 2 * unit + 1]
        bias = par[2 * unit + 1 : 2 * unit + 2]
        inverse = stat_mid[2 * unit : 2 * unit + 1]
        total = stat_mid[2 * unit + 1 : 2 * unit + 2]

        def mid_sums(p, carry):
            rows = rows_of(p)
            standard = s_ref[rows, :].astype(F32)
            grad = mask_mid * slope_of(standard * gain + bias) * wide[rows, :]
            wide[rows, :] = grad
            return (carry[0] + grad, carry[1] + grad * standard)

        bias_acc, gain_acc = over_pixels(mid_sums, (zero_mid, zero_mid))
        sums = [
            jnp.sum(bias_acc, axis=0, keepdims=True),
            jnp.sum(gain_acc, axis=0, keepdims=True),
        ]
        grad_bias, grad_gain = exchange(
            at, land_mid, land_mid_two, unit, sems, 2 * unit + 1, 2, sums, combine_sums, hooks
        )
        mid_grad[2 * unit : 2 * unit + 1, :] = grad_gain
        mid_grad[2 * unit + 1 : 2 * unit + 2, :] = grad_bias
        scale = gain * inverse
        bias_part, gain_part = grad_bias / total, grad_gain / total

        def mid_back(p, carry):
            rows = rows_of(p)
            value = (
                mask_mid
                * scale
                * (wide[rows, :] - bias_part - s_ref[rows, :].astype(F32) * gain_part)
            )
            ds_pad[1 + p // SIDE, 1 + p % SIDE] = value.astype(BF16)
            return carry

        over_pixels(mid_back, 0)

    def spatial_grad(third):
        columns = slice(third * THIRD, (third + 1) * THIRD)

        def body(row, carry):
            inner = ds_pad[1 : 1 + SIDE, 1 : 1 + SIDE, :, columns].reshape(ROWS, THIRD)
            taps = jnp.concatenate([window(3 * row + column) for column in range(3)], axis=1)
            lanes = pl.ds(pl.multiple_of(row * 3 * BLOCK_C, 128), 3 * BLOCK_C)
            g_s[third, 0, :, :, :, lanes] = (
                lax.dot_general(inner, taps, TN, preferred_element_type=F32)
                .astype(BF16)
                .reshape(4, 2, SUB, 3 * BLOCK_C)
            )
            return carry

        lax.fori_loop(0, 3, body, 0)

    def spatial_back(unit, first):
        if first == 0:
            fetch_w(unit, 0, 0).start()

        def body(tap, carry):
            slot = lax.rem(tap, 2)

            @pl.when(tap < 8)
            def _():
                fetch_w(unit, tap + 1, 1 - slot).start()

            fetch_w(unit, tap, slot).wait()
            moved = ds_pad[pl.ds(2 - tap // 3, SIDE), pl.ds(2 - tap % 3, SIDE)].reshape(ROWS, MID_C)
            value = lax.dot_general(moved, w_buf[slot], NN, preferred_element_type=F32)

            @pl.when(tap == 0)
            def _():
                side[...] = value

            @pl.when(tap > 0)
            def _():
                side[...] = side[...] + value

            return carry

        lax.fori_loop(first, first + 3, body, 0)

    a_0, b_0, c_0, t_0, a_1, b_1, c_1, t_1 = range(N_CHUNKS)

    load_t[1].wait()
    load_skip.wait()
    fetch_wt(1, 0, 0).start()
    out_norm_back(1, None, None)
    load_t[0].start()
    load_u[1].wait()
    temporal_grad()
    load_u[0].start()
    step_pair(t_1)
    temporal_back(1)
    load_s[1].wait()
    own_acts = []
    mid_norm_back(
        1,
        lambda: step_one(t_1),
        lambda: own_acts.append(acts(0, block_in, block_out)),
    )
    load_s[0].start()
    load_a[1].wait()
    spatial_grad(0)
    step_pair(a_1)
    step_two(t_1)
    spatial_grad(1)
    step_pair(b_1)
    step_one(a_1)
    spatial_grad(2)
    load_a[0].start()
    step_pair(c_1)
    step_three(t_1)
    step_one(b_1)
    step_two(a_1)
    spatial_back(1, 0)
    step_four(t_1)
    spatial_back(1, 3)
    spatial_back(1, 6)
    load_t[0].wait()
    gain, bias = par[4:5, :BLOCK_C], par[5:6, :BLOCK_C]

    def hidden_back(p, carry):
        rows = rows_of(p)
        slope = slope_of(t_ref[rows, :] * gain + bias)
        side[rows, :] = mask_out * slope * side[rows, :]
        return carry

    over_pixels(hidden_back, 0)
    fetch_wt(0, 0, 0).start()

    def hook_a():
        step_one(c_1)
        step_two(b_1)

    out_norm_back(0, hook_a, lambda: step_three(a_1))
    drain(t_1)
    load_u[0].wait()
    temporal_grad()
    load_shuffle.start()
    step_pair(t_0)
    temporal_back(0)
    step_two(c_1)
    step_five(t_1)
    load_s[0].wait()
    mid_norm_back(0, lambda: step_one(t_0), lambda: step_three(b_1))
    load_a[0].wait()
    step_four(a_1)
    drain(a_1)
    spatial_grad(0)
    step_pair(a_0)
    step_two(t_0)
    step_three(c_1)
    step_five(a_1)
    step_four(b_1)
    spatial_back(0, 0)
    step_one(a_0)
    spatial_back(0, 3)
    spatial_back(0, 6)
    step_three(t_0)
    step_two(a_0)
    load_shuffle.wait()
    d_ref[0] = (side[...] + skip_ref[...].astype(F32)).astype(BF16)
    thin = d_ref.at[1]
    thin[...] = lax.dot_general(
        u_ref[:, :SHUFFLE_C], d_ref[0], TN, preferred_element_type=F32
    ).astype(BF16)[:ROWS]
    own_acts.append(acts(1, thin, input_out))
    drain(b_1)
    spatial_grad(1)
    step_pair(b_0)
    step_five(b_1)
    step_four(c_1)
    drain(c_1)
    spatial_grad(2)
    step_pair(c_0)
    step_one(b_0)
    step_three(a_0)
    step_five(c_1)
    step_four(t_0)
    step_one(c_0)
    step_two(b_0)
    step_five(t_0)
    step_two(c_0)
    step_four(a_0)
    step_three(b_0)
    step_five(a_0)
    step_three(c_0)
    step_four(b_0)
    step_five(b_0)
    step_four(c_0)
    step_five(c_0)
    acts_wait(0, block_in, block_out, own_acts[0])
    acts_wait(1, thin, input_out, own_acts[1])
    for copy in act_copies:
        copy.wait_send()
    for index in (t_0, a_0, b_0, c_0):
        drain(index)


def spaces(text):
    return [pl.BlockSpec(memory_space=VMEM if mark == "v" else pl.ANY) for mark in text]


def dma(*shape):
    return pltpu.SemaphoreType.DMA(shape)


def params(number):
    return pltpu.CompilerParams(
        collective_id=number, has_side_effects=True, vmem_limit_bytes=GRANT
    )


def shaped(*shape, dtype=BF16):
    return jax.ShapeDtypeStruct(shape, dtype)


def run_forward(ws, wt, feat, cot, par, shuffle, mask):
    padded = (SIDE + 2, SIDE + 2, SLOTS, BLOCK_C)
    return pl.pallas_call(
        forward_kernel,
        out_shape=[
            shaped(2, 3, 4, 2, SUB, TAPS_C),
            shaped(2, 9, 4, 2, SUB, BLOCK_C),
            shaped(8, MID_C, dtype=F32),
            shaped(ROWS, BLOCK_C),
            shaped(2, *padded),
            shaped(2, ROWS, MID_C),
            shaped(2, ROWS, MID_C),
            shaped(2, ROWS, BLOCK_C, dtype=F32),
            shaped(ROWS, BLOCK_C),
            shaped(4, MID_C, dtype=F32),
            shaped(4, BLOCK_C, dtype=F32),
        ],
        in_specs=spaces("vvaavvv"),
        out_specs=spaces("aavvaaaaavv"),
        scratch_shapes=[
            VMEM((2, HALF, CHIP_S // 2), BF16),
            VMEM((2, HALF, 3 * CHIP_T // 2), BF16),
            VMEM((2, 3, 1, SUB, CHIP_S), BF16),
            VMEM((2, 9, 1, SUB, CHIP_T), BF16),
            VMEM((ROWS, BLOCK_C), BF16),
            VMEM((ROWS, BLOCK_C), BF16),
            VMEM((4, 8, MID_C), F32),
            VMEM((2,) + padded, BF16),
            VMEM((ROWS, MID_C), F32),
            VMEM((2, ROWS, MID_C), BF16),
            VMEM((2, ROWS, MID_C), BF16),
            VMEM((2, ROWS, BLOCK_C), F32),
            VMEM((2, ROWS, BLOCK_C), F32),
            VMEM((ROWS, BLOCK_C), BF16),
            VMEM((ROWS, BLOCK_C), BF16),
            VMEM((2, 4, 2, SUB, TAPS_C), BF16),
            VMEM((9, 4, 2, SUB, BLOCK_C), BF16),
            VMEM((2, 8, 8, MID_C), F32),
            VMEM((2, 4, 8, MID_C), F32),
            VMEM((2, 8, 8, BLOCK_C), F32),
            VMEM((2, 4, 8, BLOCK_C), F32),
            dma(4),
            dma(4),
            dma(3, 3),
            dma(3, 3),
            dma(N_CHUNKS, 3),
            dma(N_CHUNKS, 3),
            dma(N_CHUNKS, 2),
            dma(N_CHUNKS, 2),
            dma(N_CHUNKS, 2),
            dma(N_CHUNKS, 2),
            dma(N_CHUNKS, 4),
            dma(N_CHUNKS, 4),
            dma(3),
            dma(N_CHUNKS),
            dma(2),
            dma(1),
            dma(10),
            dma(4, 7),
            dma(4, 7),
            dma(4, 3),
            dma(4, 3),
        ],
        compiler_params=params(0),
        name="forward",
    )(ws, wt, feat, cot, par, shuffle, mask)


def run_backward(*args):
    return pl.pallas_call(
        backward_kernel,
        out_shape=[
            shaped(2, 2 * HALF, CHIP_S // 2, dtype=F32),
            shaped(2, 3, 2 * HALF, CHIP_T // 2, dtype=F32),
            shaped(4, MID_C, dtype=F32),
            shaped(4, BLOCK_C, dtype=F32),
            shaped(4 * ROWS, 128),
            shaped(4 * ROWS, 128),
        ],
        in_specs=spaces("aaaaaaavvvvaa"),
        out_specs=spaces("vvvvaa"),
        scratch_shapes=[
            VMEM((SIDE + 2, SIDE + 2, SLOTS, BLOCK_C), BF16),
            VMEM((ROWS, MID_C), BF16),
            VMEM((ROWS, MID_C), BF16),
            VMEM((ROWS, BLOCK_C), F32),
            VMEM((ROWS, BLOCK_C), F32),
            VMEM((ROWS, BLOCK_C), BF16),
            VMEM((ROWS, MID_C), F32),
            VMEM((SIDE + 2, SIDE + 2, SLOTS, MID_C), BF16),
            VMEM((3, ROWS, BLOCK_C), BF16),
            VMEM((2, MID_C, BLOCK_C), BF16),
            VMEM((2, 8, 8, MID_C), F32),
            VMEM((2, 4, 8, MID_C), F32),
            VMEM((2, 8, 8, BLOCK_C), F32),
            VMEM((2, 4, 8, BLOCK_C), F32),
            VMEM((3, 1, 4, 2, SUB, TAPS_C), BF16),
            VMEM((9, 4, 2, SUB, BLOCK_C), BF16),
            VMEM((3, 1, 4, SUB, TAPS_C), BF16),
            VMEM((9, 4, SUB, BLOCK_C), BF16),
            VMEM((2, 3, 2, 1, 2, SUB, CHIP_S), BF16),
            VMEM((2, 2, 9, 2, SUB, CHIP_T), BF16),
            VMEM((2, 3, 2, 1, 4, SUB, CHIP_S), BF16),
            VMEM((2, 2, 9, 4, SUB, CHIP_T), BF16),
            VMEM((2, 3, 3, 1, 1, SUB, CHIP_S), BF16),
            VMEM((2, 3, 9, 1, SUB, CHIP_T), BF16),
            VMEM((2, 3, 2, 1, 1, SUB, CHIP_S), F32),
            VMEM((2, 2, 9, 1, SUB, CHIP_T), F32),
            dma(6),
            dma(2),
            dma(4, 7),
            dma(4, 7),
            dma(4, 3),
            dma(4, 3),
            dma(2, 3),
            dma(2, 3),
            dma(2),
            dma(N_CHUNKS),
            dma(N_CHUNKS),
            dma(N_CHUNKS, 2),
            dma(N_CHUNKS, 2),
            dma(N_CHUNKS, 2, 2),
            dma(N_CHUNKS, 2, 2),
            dma(N_CHUNKS, 3),
            dma(N_CHUNKS, 3),
            dma(N_CHUNKS),
            dma(N_CHUNKS),
        ],
        compiler_params=params(1),
        name="backward",
    )(*args)


def shuffle_matrix():
    clip, frame, pixel = np.meshgrid(np.arange(4), np.arange(FRAMES), np.arange(HW), indexing="ij")
    source = (clip * FRAMES + frame) * HW + pixel
    target = pixel * SLOTS + frame * 4 + clip
    matrix = np.zeros((ROWS, SHUFFLE_C), np.float32)
    matrix[target.reshape(-1), source.reshape(-1)] = 1.0
    return jnp.asarray(matrix, BF16)


def on_pairs(
    features,
    cotangent,
    clip_frames,
    spatial_master,
    spatial_first,
    spatial_second,
    temporal_master,
    temporal_first,
    temporal_second,
    mid_norm,
    mid_first,
    mid_second,
    out_norm,
    out_first,
    out_second,
):
    line = lax.axis_index("chan")
    ws_own = jnp.swapaxes(spatial_master, 1, 2).astype(BF16)
    wt_own = (
        jnp.swapaxes(temporal_master, 1, 2).reshape(2, 2 * HALF, 3 * CHIP_T // 2).astype(BF16)
    )
    here = (jnp.arange(4, dtype=jnp.int32) == line).astype(F32)
    mid_rows = jnp.swapaxes(mid_norm.reshape(4, 2, 3, SUB), 1, 2).reshape(4, 3, 1, 2 * SUB)
    mid_wide = (mid_rows * here[None, None, :, None]).reshape(4, MID_C)
    out_wide = (out_norm[:, None, :] * here[None, :, None]).reshape(4, BLOCK_C)
    par_own = jnp.concatenate([mid_wide, jnp.pad(out_wide, ((0, 0), (0, MID_C - BLOCK_C)))], axis=0)
    kept = clip_frames // 8
    kept_own = lax.dynamic_slice_in_dim(kept, line * 4, 4)
    frame_ids = jnp.arange(FRAMES, dtype=jnp.int32)
    mask = (frame_ids[:, None] < kept_own[None, :]).astype(F32).reshape(SLOTS, 1)
    mask = jnp.broadcast_to(mask, (SLOTS, MID_C))
    shuffle = shuffle_matrix()
    ws, wt, par, block, a_all, s_all, u_all, t_all, skip, stat_mid, stat_out = run_forward(
        ws_own, wt_own, features, cotangent.astype(BF16), par_own, shuffle, mask
    )
    sum_s, sum_t, mid_all, out_all, block_rows, grad_rows = run_backward(
        ws.reshape(2, MID_C, TAPS_C),
        wt.reshape(2, 3, MID_C, BLOCK_C),
        a_all,
        s_all,
        u_all,
        t_all,
        skip,
        stat_mid,
        stat_out,
        par,
        mask,
        shuffle,
        block,
    )
    block_out = block_rows.astype(F32)
    clip_pool = (
        jnp.sum(block_out.reshape(-1, FRAMES * HW, block_out.shape[1]), axis=1)
        / (HW * kept.astype(F32))[:, None]
    )
    mid_pick = lax.dynamic_index_in_dim(
        mid_all.reshape(4, 3, 4, 2, SUB), line, axis=2, keepdims=False
    )
    mid_grad = jnp.swapaxes(mid_pick, 1, 2).reshape(4, 2 * HALF)
    out_grad = lax.dynamic_slice_in_dim(out_all, line * 128, 128, axis=1)
    spatial = adam_update(
        spatial_master,
        spatial_first,
        spatial_second,
        jnp.swapaxes(sum_s, 1, 2),
        RATE_CONV,
        DECAY_CONV,
    )
    temporal = adam_update(
        temporal_master, temporal_first, temporal_second, sum_t, RATE_CONV, DECAY_CONV
    )
    mid_new = adam_update(mid_norm, mid_first, mid_second, mid_grad, RATE_NORM, 0.0)
    out_new = adam_update(out_norm, out_first, out_second, out_grad, RATE_NORM, 0.0)
    return (
        (block_out, clip_pool, grad_rows.astype(F32)) + spatial + temporal + mid_new + out_new
    )


def solution(mesh):
    in_specs = (
        P("dp", "chan"),
        P("dp", "chan"),
        P("dp"),
        P(None, "dp", "chan"),
        P(None, "dp", "chan"),
        P(None, "dp", "chan"),
        P(None, None, "chan", "dp"),
        P(None, None, "chan", "dp"),
        P(None, None, "chan", "dp"),
        P(None, "chan"),
        P(None, "chan"),
        P(None, "chan"),
        P(None, "chan"),
        P(None, "chan"),
        P(None, "chan"),
    )
    out_specs = (
        P("dp", "chan"),
        P("dp", "chan"),
        P("dp", "chan"),
        P(None, "dp", "chan"),
        P(None, "dp", "chan"),
        P(None, "dp", "chan"),
        P(None, None, "chan", "dp"),
        P(None, None, "chan", "dp"),
        P(None, None, "chan", "dp"),
        P(None, "chan"),
        P(None, "chan"),
        P(None, "chan"),
        P(None, "chan"),
        P(None, "chan"),
        P(None, "chan"),
    )
    body = on_pairs if mesh.shape["dp"] == 8 and mesh.shape["chan"] == 4 else on_device
    return jax.shard_map(
        body, mesh=mesh, in_specs=in_specs, out_specs=out_specs, check_vma=False
    )
```

```python
import jax
import jax.numpy as jnp
import numpy as np
from jax import lax
from jax.experimental import pallas as pl
from jax.experimental.pallas import tpu as pltpu
from jax.sharding import PartitionSpec as P

FRAMES = 4
SIDE = 7
STEP = 10
HW = 49


EPS_NORM = 1e-05
EPS_ADAM = 1e-08
BETA_ONE = 0.9
BETA_TWO = 0.95
RATE_CONV = 0.01
RATE_NORM = 0.8
DECAY_CONV = 0.05


def frame_mask(clip_frames):
    kept_frames = clip_frames // 8
    frame_ids = jnp.arange(FRAMES, dtype=jnp.int32)
    frame_grid = (frame_ids[None, :] < kept_frames[:, None]).astype(jnp.float32)
    return jnp.broadcast_to(frame_grid[:, :, None], (kept_frames.shape[0], FRAMES, HW)).reshape(
        -1, 1
    )


def silu_slope(values):
    sigmoid = jax.nn.sigmoid(values)
    return sigmoid * (1.0 + values * (1.0 - sigmoid))


def spatial_apply(inputs, tap_weights):
    channels = inputs.shape[1]
    padded = jnp.pad(inputs.reshape(-1, SIDE, SIDE, channels), ((0, 0), (1, 1), (1, 1), (0, 0)))
    summed = jnp.zeros((inputs.shape[0], tap_weights.shape[2]), jnp.float32)
    for tap_index in range(9):
        row_off, col_off = (tap_index // 3, tap_index % 3)
        window = padded[:, row_off : row_off + SIDE, col_off : col_off + SIDE].reshape(-1, channels)
        summed = summed + jnp.dot(
            window, tap_weights[tap_index], preferred_element_type=jnp.float32
        )
    return (summed, padded)


def spatial_grads(padded, tap_weights, grad_out):
    channels = padded.shape[3]
    weight_terms = []
    input_sum = jnp.zeros((padded.shape[0], SIDE, SIDE, channels), jnp.float32)
    for tap_index in range(9):
        row_off, col_off = (tap_index // 3, tap_index % 3)
        window = padded[:, row_off : row_off + SIDE, col_off : col_off + SIDE].reshape(-1, channels)
        weight_terms.append(
            lax.dot_general(
                window, grad_out, (((0,), (0,)), ((), ())), preferred_element_type=jnp.float32
            )
        )
        pulled = lax.dot_general(
            grad_out,
            tap_weights[tap_index],
            (((1,), (1,)), ((), ())),
            preferred_element_type=jnp.float32,
        )
        pulled = jnp.pad(pulled.reshape(-1, SIDE, SIDE, channels), ((0, 0), (1, 1), (1, 1), (0, 0)))
        input_sum = (
            input_sum
            + pulled[:, 2 - row_off : 2 - row_off + SIDE, 2 - col_off : 2 - col_off + SIDE]
        )
    return (jnp.stack(weight_terms).reshape(-1, grad_out.shape[1]), input_sum.reshape(-1, channels))


def temporal_apply(inputs, weight):
    frame_seq = inputs.reshape(-1, FRAMES, HW, inputs.shape[1])
    padded = jnp.pad(frame_seq, ((0, 0), (1, 1), (0, 0), (0, 0)))
    summed = jnp.zeros(frame_seq.shape[:3] + (weight.shape[2],), jnp.float32)
    for frame_off in range(3):
        summed = summed + jnp.einsum(
            "nfpm,mc->nfpc",
            padded[:, frame_off : frame_off + FRAMES],
            weight[frame_off],
            preferred_element_type=jnp.float32,
        )
    return (summed.reshape(inputs.shape[0], -1), padded)


def temporal_grads(padded, weight, grad_full):
    grad_seq = grad_full.reshape(-1, FRAMES, HW, grad_full.shape[1])
    grad_pad = jnp.pad(grad_seq, ((0, 0), (1, 1), (0, 0), (0, 0)))
    weight_terms = []
    input_sum = jnp.zeros(padded.shape[:1] + (FRAMES, HW, padded.shape[3]), jnp.float32)
    for frame_off in range(3):
        weight_terms.append(
            jnp.einsum(
                "nfpm,nfpc->mc",
                padded[:, frame_off : frame_off + FRAMES],
                grad_seq,
                preferred_element_type=jnp.float32,
            )
        )
        input_sum = input_sum + jnp.einsum(
            "nfpc,mc->nfpm",
            grad_pad[:, 2 - frame_off : 2 - frame_off + FRAMES],
            weight[frame_off],
            preferred_element_type=jnp.float32,
        )
    return (jnp.stack(weight_terms), input_sum.reshape(grad_full.shape[0], -1))


def normalize(values, validity, gain_row, bias_row):
    local_valid = jnp.sum(validity)
    total_valid, value_sums = lax.psum((local_valid, jnp.sum(values * validity, axis=0)), "dp")
    average = value_sums / total_valid
    centered = values - average
    variance = lax.psum(jnp.sum(validity * centered * centered, axis=0), "dp") / total_valid
    inverse = lax.rsqrt(variance + EPS_NORM)
    standard = centered * inverse
    return (standard * gain_row + bias_row, standard, inverse, total_valid)


def normalize_back(grad_normed, standard, inverse, gain_row, total_valid, validity):
    grad_bias, grad_gain = lax.psum(
        (
            jnp.sum(grad_normed * validity, axis=0),
            jnp.sum(grad_normed * standard * validity, axis=0),
        ),
        "dp",
    )
    grad_values = (
        validity
        * gain_row
        * inverse
        * (grad_normed - grad_bias / total_valid - standard * grad_gain / total_valid)
    )
    return (grad_values, grad_gain, grad_bias)


def adam_update(weight, moment_one, moment_two, grad_value, rate, decay):
    fresh_one = BETA_ONE * moment_one + (1.0 - BETA_ONE) * grad_value
    fresh_two = BETA_TWO * moment_two + (1.0 - BETA_TWO) * grad_value * grad_value
    scaled = (
        fresh_one
        / (1.0 - BETA_ONE**STEP)
        / (jnp.sqrt(fresh_two / (1.0 - BETA_TWO**STEP)) + EPS_ADAM)
    )
    return (weight - rate * (scaled + decay * weight), fresh_one, fresh_two)


def on_device(
    features,
    cotangent,
    clip_frames,
    spatial_master,
    spatial_first,
    spatial_second,
    temporal_master,
    temporal_first,
    temporal_second,
    mid_norm,
    mid_first,
    mid_second,
    out_norm,
    out_first,
    out_second,
):
    validity = frame_mask(clip_frames)
    spatial_all, temporal_all = (
        lax.all_gather(spatial_master.astype(jnp.bfloat16), "dp", axis=1, tiled=True),
        lax.all_gather(temporal_master.astype(jnp.bfloat16), "dp", axis=3, tiled=True),
    )
    channels = temporal_all.shape[3]
    spatial_taps = spatial_all.reshape(2, 9, channels, spatial_all.shape[2])
    residual = features.astype(jnp.float32)
    outgoing = features
    kept_state = []
    for unit_index in range(2):
        gathered = lax.all_gather(outgoing, "chan", axis=1, tiled=True)
        spatial_out, padded = spatial_apply(gathered, spatial_taps[unit_index])
        mid_normed, mid_standard, mid_inverse, total_valid = normalize(
            spatial_out, validity, mid_norm[2 * unit_index], mid_norm[2 * unit_index + 1]
        )
        temporal_in = (jax.nn.silu(mid_normed) * validity).astype(jnp.bfloat16)
        partial_value, frames_padded = temporal_apply(temporal_in, temporal_all[unit_index])
        temporal_out = lax.psum_scatter(
            partial_value.astype(jnp.bfloat16), "chan", scatter_dimension=1, tiled=True
        ).astype(jnp.float32)
        out_normed, out_standard, out_inverse, total_valid = normalize(
            temporal_out, validity, out_norm[2 * unit_index], out_norm[2 * unit_index + 1]
        )
        if unit_index == 0:
            pre_act = out_normed
            outgoing = (jax.nn.silu(pre_act) * validity).astype(jnp.bfloat16)
        else:
            pre_act = out_normed + residual
            block_out = jax.nn.silu(pre_act) * validity
        kept_state.append(
            (
                padded,
                mid_normed,
                mid_standard,
                mid_inverse,
                frames_padded,
                pre_act,
                out_standard,
                out_inverse,
            )
        )
    kept_frames = (clip_frames // 8).astype(jnp.float32)
    clip_pool = (
        jnp.sum(block_out.reshape(-1, FRAMES * HW, block_out.shape[1]), axis=1)
        / (HW * kept_frames)[:, None]
    )
    skip_grad = cotangent * validity * silu_slope(kept_state[1][5])
    grad_pre = skip_grad
    spatial_list = [None, None]
    temporal_list = [None, None]
    mid_rows = [None, None]
    out_rows = [None, None]
    grad_hidden = skip_grad
    for unit_index in (1, 0):
        (
            padded,
            mid_normed,
            mid_standard,
            mid_inverse,
            frames_padded,
            pre_act,
            out_standard,
            out_inverse,
        ) = kept_state[unit_index]
        if unit_index == 0:
            grad_pre = grad_hidden * validity * silu_slope(pre_act)
        grad_temporal, out_gain_grad, out_bias_grad = normalize_back(
            grad_pre, out_standard, out_inverse, out_norm[2 * unit_index], total_valid, validity
        )
        grad_full = lax.all_gather(grad_temporal.astype(jnp.bfloat16), "chan", axis=1, tiled=True)
        temporal_grad, grad_mid = temporal_grads(frames_padded, temporal_all[unit_index], grad_full)
        grad_mid_normed = grad_mid * validity * silu_slope(mid_normed)
        grad_spatial, mid_gain_grad, mid_bias_grad = normalize_back(
            grad_mid_normed,
            mid_standard,
            mid_inverse,
            mid_norm[2 * unit_index],
            total_valid,
            validity,
        )
        spatial_grad, grad_in_part = spatial_grads(
            padded, spatial_taps[unit_index], grad_spatial.astype(jnp.bfloat16)
        )
        grad_hidden = lax.psum_scatter(
            grad_in_part.astype(jnp.bfloat16), "chan", scatter_dimension=1, tiled=True
        ).astype(jnp.float32)
        spatial_list[unit_index] = spatial_grad
        temporal_list[unit_index] = temporal_grad
        mid_rows[unit_index] = (mid_gain_grad, mid_bias_grad)
        out_rows[unit_index] = (out_gain_grad, out_bias_grad)
    input_grad = grad_hidden + skip_grad
    spatial_sum, temporal_sum = (
        lax.psum_scatter(jnp.stack(spatial_list), "dp", scatter_dimension=1, tiled=True),
        lax.psum_scatter(jnp.stack(temporal_list), "dp", scatter_dimension=3, tiled=True),
    )
    mid_grad = jnp.stack([mid_rows[0][0], mid_rows[0][1], mid_rows[1][0], mid_rows[1][1]])
    out_grad = jnp.stack([out_rows[0][0], out_rows[0][1], out_rows[1][0], out_rows[1][1]])
    spatial_new, spatial_one, spatial_two = adam_update(
        spatial_master, spatial_first, spatial_second, spatial_sum, RATE_CONV, DECAY_CONV
    )
    temporal_new, temporal_one, temporal_two = adam_update(
        temporal_master, temporal_first, temporal_second, temporal_sum, RATE_CONV, DECAY_CONV
    )
    mid_new, mid_one, mid_two = adam_update(
        mid_norm, mid_first, mid_second, mid_grad, RATE_NORM, 0.0
    )
    out_new, out_one, out_two = adam_update(
        out_norm, out_first, out_second, out_grad, RATE_NORM, 0.0
    )
    return (
        block_out,
        clip_pool,
        input_grad,
        spatial_new,
        spatial_one,
        spatial_two,
        temporal_new,
        temporal_one,
        temporal_two,
        mid_new,
        mid_one,
        mid_two,
        out_new,
        out_one,
        out_two,
    )


F32 = jnp.float32
BF16 = jnp.bfloat16
MESH = pl.DeviceIdType.MESH
VMEM = pltpu.VMEM
NN = (((1,), (0,)), ((), ()))
NT = (((1,), (1,)), ((), ()))
TN = (((0,), (0,)), ((), ()))
BLOCK_C = 512
MID_C = 1152
THIRD = MID_C // 3
ROWS = 784
SLOTS = 16
SHUFFLE_C = 896
HALF = 144
SUB = 48
TAPS_C = 9 * BLOCK_C
CHIP_S = TAPS_C // 4
CHIP_T = BLOCK_C // 4
CHUNKS = (
    ("s", 0, 0, 1),
    ("s", 0, 1, 1),
    ("s", 0, 2, 1),
    ("t", 0, 0, 9),
    ("s", 1, 0, 1),
    ("s", 1, 1, 1),
    ("s", 1, 2, 1),
    ("t", 1, 0, 9),
)
N_CHUNKS = len(CHUNKS)
PARTS = (("s", 0), ("t", 0), ("s", 1), ("t", 1))
GRANT = 65000 * 1024


def place():
    dp = lax.axis_index("dp")
    line = lax.axis_index("chan")
    core = lax.rem(dp, 2)
    chip = lax.div(dp, 2)
    x_bit = lax.rem(chip, 2)
    y_bit = lax.div(chip, 2)
    return dict(
        dp=dp,
        line=line,
        core=core,
        chip=chip,
        chip_x=chip + 1 - 2 * x_bit,
        chip_y=chip + 2 - 4 * y_bit,
        chip_d=3 - chip,
        pair=(dp + 1 - 2 * core, line),
        x=(dp + 2 - 4 * x_bit, line),
        y=(dp + 4 - 8 * y_bit, line),
    )


def remote(source, target, send, recv, device):
    return pltpu.make_async_remote_copy(
        src_ref=source,
        dst_ref=target,
        send_sem=send,
        recv_sem=recv,
        device_id=device,
        device_id_type=MESH,
    )


def greet(devices):
    barrier = pltpu.get_barrier_semaphore()
    for device in devices:
        pl.semaphore_signal(barrier, inc=1, device_id=device, device_id_type=MESH)
    pl.semaphore_wait(barrier, len(devices))


def line_peer(at, step):
    return (at["dp"], lax.rem(at["line"] + step, 4))


def ring_peer(at, step):
    return (lax.rem(at["dp"] + step, 8), at["line"])


def greet_all(at):
    greet(
        [ring_peer(at, step) for step in range(1, 8)]
        + [line_peer(at, step) for step in (1, 2, 3)]
    )


def rows_of(pixel):
    return pl.ds(pl.multiple_of(pixel * SLOTS, SLOTS), SLOTS)


def slope_of(values):
    sigmoid = jax.nn.sigmoid(values)
    return sigmoid * (1.0 + values * (1.0 - sigmoid))


def over_pixels(body, carry):
    return lax.fori_loop(0, HW, body, carry, unroll=7)


def exchange(at, land, land_two, index, sems, sem_index, payload, combine, hooks=(None, None)):
    dp, line = at["dp"], at["line"]
    one_send, one_recv, two_send, two_recv = sems
    rows = pl.ds(0, 2)
    for row, value in enumerate(payload):
        land[index, dp, row : row + 1, :] = value
    sent = []
    for step in range(1, 8):
        here = land.at[index, dp, rows]
        copy = remote(
            here,
            here,
            one_send.at[sem_index, step - 1],
            one_recv.at[sem_index, step - 1],
            ring_peer(at, step),
        )
        copy.start()
        sent.append(copy)
    if hooks[0] is not None:
        hooks[0]()
    for step in range(1, 8):
        there = land.at[index, lax.rem(dp + 8 - step, 8), rows]
        remote(
            there,
            there,
            one_send.at[sem_index, step - 1],
            one_recv.at[sem_index, step - 1],
            ring_peer(at, step),
        ).wait_recv()
    merged = combine([land[index, source] for source in range(8)])
    for row, value in enumerate(merged):
        land_two[index, line, row : row + 1, :] = value
    for step in (1, 2, 3):
        here = land_two.at[index, line, rows]
        copy = remote(
            here,
            here,
            two_send.at[sem_index, step - 1],
            two_recv.at[sem_index, step - 1],
            line_peer(at, step),
        )
        copy.start()
        sent.append(copy)
    if hooks[1] is not None:
        hooks[1]()
    for step in (1, 2, 3):
        there = land_two.at[index, lax.rem(line + 4 - step, 4), rows]
        remote(
            there,
            there,
            two_send.at[sem_index, step - 1],
            two_recv.at[sem_index, step - 1],
            line_peer(at, step),
        ).wait_recv()
    merged = combine([land_two[index, source] for source in range(4)])
    for copy in sent:
        copy.wait_send()
    return merged


def combine_sums(blocks):
    total = sum(blocks[1:], blocks[0])
    return [total[0:1], total[1:2]]


def forward_kernel(
    ws_wide,
    wt_wide,
    feat_in,
    cot_wide,
    mid_own,
    out_own,
    frames_in,
    shuffle,
    ws_out,
    wt_out,
    par_out,
    mask_in,
    block_out,
    a_out,
    s_out,
    u_out,
    t_out,
    skip_out,
    stat_mid,
    stat_out,
    ws_in,
    wt_in,
    cot_raw,
    cot_in,
    par_in,
    pair_s,
    pair_t,
    stage_s,
    stage_t,
    feat_land,
    cot_land,
    par_land,
    a_pad,
    s_ref,
    x_ref,
    u_ref,
    t_ref,
    side,
    feat_ref,
    thin,
    w_buf,
    wt_buf,
    land_mid,
    land_mid_two,
    land_out,
    land_out_two,
    land_count,
    count_one,
    count_two,
    pair_send,
    pair_recv,
    act_send,
    act_recv,
    line_send,
    line_recv,
    plane_send,
    plane_recv,
    diag_send,
    diag_recv,
    core_send,
    core_recv,
    own_sem,
    chunk_sem,
    w_sem,
    wt_sem,
    save_sem,
    one_send,
    one_recv,
    two_send,
    two_recv,
):
    at = place()
    line, core, chip = at["line"], at["core"], at["chip"]
    sems = (one_send, one_recv, two_send, two_recv)
    cot_load = pltpu.make_async_copy(cot_wide, cot_raw, wt_sem.at[1])
    cot_load.start()
    for unit in range(2):
        ws_in[unit] = ws_wide[unit].astype(BF16)
        for tau in range(3):
            wt_in[unit, :, 64 * tau : 64 * tau + 64] = wt_wide[unit, tau].T.astype(BF16)
    pieces = []
    blank = jnp.zeros((4, THIRD - 2 * SUB), F32)
    for third in range(3):
        for half in range(2):
            first = half * HALF + third * SUB
            pieces.append(mid_own[:, first : first + SUB])
        pieces.append(blank)
    par_in[...] = jnp.zeros(par_in.shape, F32)
    wide_rows = jnp.concatenate(
        [jnp.concatenate(pieces, axis=1), jnp.zeros((4, MID_C), F32)], axis=0
    )
    par_in[0:4, :] = pltpu.roll(wide_rows, line * (2 * SUB), 1)[0:4]
    par_in[4:8, pl.ds(pl.multiple_of(line * 128, 128), 128)] = out_own[...]
    row_ids = lax.broadcasted_iota(jnp.int32, (SLOTS, MID_C), 0)
    mask = jnp.zeros((SLOTS, MID_C), F32)
    for clip in range(4):
        kept = lax.div(frames_in[4 * line + clip], 8)
        here = jnp.logical_and(row_ids % 4 == clip, row_ids // 4 < kept)
        mask = jnp.where(here, 1.0, mask)
    mask_in[...] = mask
    count_rows = lax.broadcasted_iota(jnp.int32, (8, 128), 0)
    count_tile = jnp.zeros((8, 128), F32)
    for owner in range(4):
        frames = lax.div(frames_in[4 * owner], 8)
        for clip in range(1, 4):
            frames = frames + lax.div(frames_in[4 * owner + clip], 8)
        count_tile = jnp.where(count_rows == owner, (HW * frames).astype(F32), count_tile)
    land_count[at["dp"]] = count_tile
    greet_all(at)
    started = []

    def send(copy):
        copy.start()
        started.append(copy)
        return copy

    def area(chunk, owner_core, owner_chip, first, count):
        kind, unit, lead, leads = chunk
        ref, width = (ws_out, CHIP_S) if kind == "s" else (wt_out, CHIP_T)
        lanes = pl.ds(pl.multiple_of(owner_chip * width, 128), width)
        return ref.at[unit, pl.ds(lead, leads), pl.ds(first, count), owner_core, :, lanes]

    pairs = {}
    for index, (kind, unit) in enumerate(PARTS):
        theirs = pl.ds(pl.multiple_of((1 - core) * HALF, 16), HALF)
        source, landing = (ws_in, pair_s) if kind == "s" else (wt_in, pair_t)
        pairs[kind, unit] = send(
            remote(
                source.at[unit, theirs],
                landing.at[unit],
                pair_send.at[index],
                pair_recv.at[index],
                at["pair"],
            )
        )

    def acts(row, source, target):
        def cut(owner):
            return source.at[pl.ds(pl.multiple_of(owner * ROWS, 16), ROWS)]

        lanes = pl.ds(pl.multiple_of(line * 128, 128), 128)
        for step in (1, 2, 3):
            peer = line_peer(at, step)
            send(
                remote(
                    cut(peer[1]),
                    target.at[:, lanes],
                    act_send.at[row, step - 1],
                    act_recv.at[row, step - 1],
                    peer,
                )
            )
        own = pltpu.make_async_copy(cut(line), target.at[:, lanes], own_sem.at[row])
        own.start()
        return own

    def acts_wait(row, source, target, own):
        for step in (1, 2, 3):
            origin = lax.rem(line + 4 - step, 4)
            lanes = pl.ds(pl.multiple_of(origin * 128, 128), 128)
            remote(
                source.at[pl.ds(0, ROWS)],
                target.at[:, lanes],
                act_send.at[row, step - 1],
                act_recv.at[row, step - 1],
                line_peer(at, step),
            ).wait_recv()
        own.wait()

    mine = pl.ds(pl.multiple_of(core * HALF, 16), HALF)

    def merge(kind, unit):
        pairs[kind, unit].wait_recv()
        source, landing = (ws_in, pair_s) if kind == "s" else (wt_in, pair_t)
        low = source[unit, mine].astype(F32)
        high = landing[unit].astype(F32)
        first = jnp.where(core == 0, low, high)
        second = jnp.where(core == 0, high, low)
        if kind == "s":
            both = jnp.concatenate([first, second], axis=1).astype(BF16)
            stage_s[unit] = both.reshape(3, 1, SUB, CHIP_S)
        else:
            for tau in range(3):
                lanes = slice(64 * tau, 64 * tau + 64)
                both = jnp.concatenate([first[:, lanes], second[:, lanes]], axis=1).astype(BF16)
                stage_t[unit, 3 * tau : 3 * tau + 3] = both.reshape(3, 1, SUB, CHIP_T)

    own_copies = [None] * N_CHUNKS

    def step_line(index):
        chunk = CHUNKS[index]
        kind, unit, lead, leads = chunk
        if lead == 0:
            merge(kind, unit)
        staged = (stage_s if kind == "s" else stage_t).at[unit, pl.ds(lead, leads)]
        target = area(chunk, core, chip, line, 1)
        for step in (1, 3, 2):
            send(
                remote(
                    staged,
                    target,
                    line_send.at[index, step - 1],
                    line_recv.at[index, step - 1],
                    line_peer(at, step),
                )
            )
        own = pltpu.make_async_copy(staged, target, chunk_sem.at[index])
        own.start()
        own_copies[index] = own

    def step_plane(index):
        chunk = CHUNKS[index]
        for step in (1, 2, 3):
            origin = area(chunk, core, chip, lax.rem(line + 4 - step, 4), 1)
            remote(
                origin,
                origin,
                line_send.at[index, step - 1],
                line_recv.at[index, step - 1],
                line_peer(at, step),
            ).wait_recv()
        own_copies[index].wait()
        for turn in range(2):
            for way, name in enumerate(("x", "y")):
                half = area(chunk, core, chip, 2 * (way ^ turn), 2)
                send(
                    remote(
                        half,
                        half,
                        plane_send.at[index, way, turn],
                        plane_recv.at[index, way, turn],
                        at[name],
                    )
                )
        held = area(chunk, core, chip, 0, 4)
        send(remote(held, held, core_send.at[index, 0], core_recv.at[index, 0], at["pair"]))

    def plane_wait(index, way, turn, name):
        half = area(CHUNKS[index], core, at["chip_" + name], 2 * (way ^ turn), 2)
        remote(
            half,
            half,
            plane_send.at[index, way, turn],
            plane_recv.at[index, way, turn],
            at[name],
        ).wait_recv()
        return half

    def step_diag(index):
        for way, (name, other) in enumerate((("x", "y"), ("y", "x"))):
            half = plane_wait(index, way, 0, name)
            send(
                remote(half, half, diag_send.at[index, way], diag_recv.at[index, way], at[other])
            )

    def step_core(index):
        chunk = CHUNKS[index]
        for way, name in enumerate(("x", "y")):
            plane_wait(index, way, 1, name)
            held = area(chunk, core, at["chip_" + name], 0, 4)
            send(
                remote(
                    held, held, core_send.at[index, 1 + way], core_recv.at[index, 1 + way], at["pair"]
                )
            )
        for way, (other, first) in enumerate((("y", 0), ("x", 2))):
            half = area(chunk, core, at["chip_d"], first, 2)
            remote(
                half, half, diag_send.at[index, way], diag_recv.at[index, way], at[other]
            ).wait_recv()
        held = area(chunk, core, at["chip_d"], 0, 4)
        send(remote(held, held, core_send.at[index, 3], core_recv.at[index, 3], at["pair"]))

    def step_end(index):
        chunk = CHUNKS[index]
        for slot, name in enumerate(("chip", "chip_x", "chip_y", "chip_d")):
            held = area(chunk, 1 - core, at[name], 0, 4)
            remote(
                held, held, core_send.at[index, slot], core_recv.at[index, slot], at["pair"]
            ).wait_recv()
        kind, unit, lead, _ = chunk
        if kind == "s":
            fetch_w(unit, lead).start()
        else:
            fetch_wt(unit).start()

    def fetch_w(unit, third):
        slot = (3 * unit + third) % 2
        return pltpu.make_async_copy(ws_out.at[unit, third], w_buf.at[slot], w_sem.at[slot])

    def fetch_wt(unit):
        return pltpu.make_async_copy(wt_out.at[unit], wt_buf, wt_sem.at[0])

    def window(unit, tap):
        row, column = tap // 3, tap % 3
        return a_pad[unit, row : row + SIDE, column : column + SIDE].reshape(ROWS, BLOCK_C)

    def conv(unit, third):
        fetch_w(unit, third).wait()
        taps = jnp.concatenate([window(unit, tap) for tap in range(9)], axis=1)
        s_ref[:, third * THIRD : (third + 1) * THIRD] = lax.dot_general(
            taps,
            w_buf[(3 * unit + third) % 2].reshape(THIRD, TAPS_C),
            NT,
            preferred_element_type=F32,
        )

    mask_mid = mask_in[...]
    mask_out = mask_in[:, :BLOCK_C]
    slot_rows = lax.broadcasted_iota(jnp.int32, (SLOTS, BLOCK_C), 0)
    has_before = (slot_rows >= 4).astype(F32)
    has_after = (slot_rows < 12).astype(F32)

    def moments(values, mask, land, land_two, index, sem_index, hooks):
        zero = jnp.zeros(mask.shape, F32)
        width = mask.shape[1]
        local = local_count[:, :width]
        added = over_pixels(lambda p, acc: acc + values[rows_of(p), :], zero)
        mean = jnp.sum(added * mask, axis=0, keepdims=True) / local

        def squares(p, acc):
            centered = values[rows_of(p), :] - mean
            return acc + centered * centered

        spread = jnp.sum(over_pixels(squares, zero) * mask, axis=0, keepdims=True)
        def combine(blocks):
            known = count_one if len(blocks) == 8 else count_two
            counts = [known[source, :, :width] for source in range(len(blocks))]
            pivot = blocks[0]
            drifts = [block - pivot for block in blocks[1:]]
            shift = sum(count * drift for count, drift in zip(counts[1:], drifts))[0:1]
            squared = sum(count * drift * drift for count, drift in zip(counts[1:], drifts))[0:1]
            inner = sum(blocks[1:], pivot)[1:2]
            total = sum(counts[1:], counts[0])[0:1]
            return [pivot[0:1] + shift / total, inner + squared - shift * shift / total]

        mean, spread = exchange(
            at, land, land_two, index, sems, sem_index, [mean, spread], combine, hooks
        )
        total = all_count[:, :width]
        return mean, lax.rsqrt(spread / total + EPS_NORM), total

    saves = []

    def save(source, target):
        copy = pltpu.make_async_copy(source, target, save_sem.at[len(saves)])
        copy.start()
        saves.append(copy)

    def mid_norm_act(unit, *hooks):
        gain = par_out[2 * unit : 2 * unit + 1]
        bias = par_out[2 * unit + 1 : 2 * unit + 2]
        mean, inverse, total = moments(
            s_ref, mask_mid, land_mid, land_mid_two, unit, 2 * unit, hooks
        )
        stat_mid[2 * unit : 2 * unit + 1] = inverse
        stat_mid[2 * unit + 1 : 2 * unit + 2] = total

        def mid_act(p, carry):
            rows = rows_of(p)
            standard = (s_ref[rows, :] - mean) * inverse
            x_ref[unit, rows, :] = standard.astype(BF16)
            normed = standard * gain + bias
            u_ref[unit, rows, :] = (jax.nn.sigmoid(normed) * normed * mask_mid).astype(BF16)
            return carry

        over_pixels(mid_act, 0)
        save(x_ref.at[unit], s_out.at[unit])
        save(u_ref.at[unit], u_out.at[unit])

    def temporal(unit):
        fetch_wt(unit).wait()

        def weight(tau):
            return wt_buf[3 * tau : 3 * tau + 3].reshape(MID_C, BLOCK_C)

        t_ref[unit] = lax.dot_general(u_ref[unit], weight(1), NN, preferred_element_type=F32)
        side[0] = lax.dot_general(u_ref[unit], weight(0), NN, preferred_element_type=F32)
        side[1] = lax.dot_general(u_ref[unit], weight(2), NN, preferred_element_type=F32)

        def frames(p, carry):
            rows = rows_of(p)
            t_ref[unit, rows, :] = (
                t_ref[unit, rows, :]
                + pltpu.roll(side[0, rows, :], 4, 0) * has_before
                + pltpu.roll(side[1, rows, :], 12, 0) * has_after
            )
            return carry

        over_pixels(frames, 0)

    def out_stats(unit, *hooks):
        mean, inverse, total = moments(
            t_ref.at[unit], mask_out, land_out, land_out_two, unit, 2 * unit + 1, hooks
        )
        stat_out[2 * unit : 2 * unit + 1] = inverse
        stat_out[2 * unit + 1 : 2 * unit + 2] = total
        gain = par_out[4 + 2 * unit : 5 + 2 * unit, :BLOCK_C]
        bias = par_out[5 + 2 * unit : 6 + 2 * unit, :BLOCK_C]
        return mean, inverse, gain, bias

    for step in range(1, 8):
        here = land_count.at[at["dp"]]
        send(
            remote(
                here,
                here,
                one_send.at[4, step - 1],
                one_recv.at[4, step - 1],
                ring_peer(at, step),
            )
        )
    step_line(0)
    for step in (1, 2, 3):
        send(
            remote(
                par_in,
                par_land.at[line],
                act_send.at[2, step - 1],
                act_recv.at[2, step - 1],
                line_peer(at, step),
            )
        )
    par_own = pltpu.make_async_copy(par_in, par_land.at[line], own_sem.at[2])
    par_own.start()
    step_line(1)
    for unit in range(2):
        a_pad[unit] = jnp.zeros(a_pad.shape[1:], BF16)
    step_plane(0)
    step_line(2)
    step_diag(0)
    step_plane(1)
    feat_own = acts(0, feat_in, feat_land)
    cot_load.wait()
    cot_in[...] = cot_raw[...].astype(BF16)
    for step in range(1, 8):
        there = land_count.at[lax.rem(at["dp"] + 8 - step, 8)]
        remote(
            there,
            there,
            one_send.at[4, step - 1],
            one_recv.at[4, step - 1],
            ring_peer(at, step),
        ).wait_recv()

    def widen(row, rows):
        return jnp.concatenate([jnp.broadcast_to(row, (rows, 128))] * (MID_C // 128), axis=1)

    def pick(tile):
        return jnp.sum(jnp.where(count_rows == line, tile, 0.0), axis=0, keepdims=True)

    sum_tile = land_count[0]
    for source in range(8):
        count_one[source] = widen(pick(land_count[source]), 8)
        if source > 0:
            sum_tile = sum_tile + land_count[source]
    for source in range(4):
        count_two[source] = widen(sum_tile[source : source + 1], 8)
    local_count = widen(pick(count_tile), 1)
    all_count = widen(jnp.sum(sum_tile[0:4], axis=0, keepdims=True), 1)
    step_plane(2)
    step_line(3)
    step_diag(1)
    step_core(0)
    step_end(0)
    permute = shuffle[:, :ROWS]
    acts_wait(0, feat_in, feat_land, feat_own)
    feat_ref[...] = lax.dot_general(permute, feat_land[...], NN, preferred_element_type=F32).astype(
        BF16
    )

    def fill(p, carry):
        a_pad[0, 1 + p // SIDE, 1 + p % SIDE] = feat_ref[rows_of(p), :]
        return carry

    over_pixels(fill, 0)
    save(a_pad.at[0], a_out.at[0])
    step_line(4)
    step_diag(2)
    conv(0, 0)
    step_core(1)
    step_end(1)
    conv(0, 1)
    step_plane(3)
    step_core(2)
    step_end(2)
    conv(0, 2)
    for step in (1, 2, 3):
        remote(
            par_in,
            par_land.at[lax.rem(line + 4 - step, 4)],
            act_send.at[2, step - 1],
            act_recv.at[2, step - 1],
            line_peer(at, step),
        ).wait_recv()
    par_own.wait()
    par_out[...] = par_land[0] + par_land[1] + par_land[2] + par_land[3]

    def hook_a():
        step_diag(3)
        step_plane(4)

    mid_norm_act(0, hook_a, lambda: step_line(5))
    step_core(3)
    step_end(3)
    temporal(0)
    cot_own = []

    def hook_b():
        step_diag(4)
        step_plane(5)

    def hook_c():
        step_line(6)
        step_line(7)
        cot_own.append(acts(1, cot_in, cot_land))

    mean, inverse, gain, bias = out_stats(0, hook_b, hook_c)

    def out_act(p, carry):
        rows = rows_of(p)
        standard = (t_ref[0, rows, :] - mean) * inverse
        t_ref[0, rows, :] = standard
        normed = standard * gain + bias
        hidden = jax.nn.sigmoid(normed) * normed * mask_out
        a_pad[1, 1 + p // SIDE, 1 + p % SIDE] = hidden.astype(BF16)
        return carry

    over_pixels(out_act, 0)
    save(t_ref.at[0], t_out.at[0])
    save(a_pad.at[1], a_out.at[1])
    step_core(4)
    step_end(4)
    conv(1, 0)
    step_diag(5)
    step_plane(6)
    step_core(5)
    step_end(5)
    conv(1, 1)
    step_diag(6)
    step_plane(7)
    step_core(6)
    step_end(6)
    conv(1, 2)
    mid_norm_act(1, lambda: step_diag(7), None)
    step_core(7)
    step_end(7)
    temporal(1)

    def hook_d():
        acts_wait(1, cot_in, cot_land, cot_own[0])
        side[0] = lax.dot_general(permute, cot_land[...], NN, preferred_element_type=F32)

    mean_one, inverse_one, gain_one, bias_one = out_stats(1, hook_d, None)

    def end_act(p, carry):
        rows = rows_of(p)
        standard = (t_ref[1, rows, :] - mean_one) * inverse_one
        t_ref[1, rows, :] = standard
        pre = standard * gain_one + bias_one + feat_ref[rows, :].astype(F32)
        sigmoid = jax.nn.sigmoid(pre)
        thin[rows, :] = (pre * sigmoid * mask_out).astype(BF16)
        slope = sigmoid * (1.0 + pre * (1.0 - sigmoid))
        cot_land[rows, :] = (side[0, rows, :] * mask_out * slope).astype(BF16)
        return carry

    over_pixels(end_act, 0)
    save(t_ref.at[1], t_out.at[1])
    save(cot_land, skip_out)
    block_out[...] = lax.dot_general(permute, thin[...], TN, preferred_element_type=F32).astype(
        BF16
    )
    for copy in saves:
        copy.wait()
    for copy in started:
        copy.wait_send()


def backward_kernel(
    ws,
    wt,
    a_in,
    s_in,
    u_in,
    t_in,
    skip_in,
    stat_mid,
    stat_out,
    par,
    mask_in,
    shuffle,
    block_in,
    sp_in,
    sm_in,
    sv_in,
    tp_in,
    tm_in,
    tv_in,
    sp_out,
    sm_out,
    sv_out,
    tp_out,
    tm_out,
    tv_out,
    mid_grad,
    out_grad,
    block_out,
    input_out,
    a_pad,
    s_ref,
    u_ref,
    t_ref,
    side,
    skip_ref,
    wide,
    ds_pad,
    d_ref,
    w_buf,
    land_mid,
    land_mid_two,
    land_out,
    land_out_two,
    g_s,
    g_t,
    land_s,
    land_t,
    one_s,
    one_t,
    two_s,
    two_t,
    line_s,
    line_t,
    fin_s,
    fin_t,
    adam_s,
    adam_t,
    load_sem,
    w_sem,
    ex_one_send,
    ex_one_recv,
    ex_two_send,
    ex_two_recv,
    act_send,
    act_recv,
    act_sem,
    pair_send,
    pair_recv,
    one_send,
    one_recv,
    two_send,
    two_recv,
    line_send,
    line_recv,
    fin_send,
    fin_recv,
    adam_load,
    adam_save,
):
    at = place()
    line, core, chip = at["line"], at["core"], at["chip"]
    sems = (ex_one_send, ex_one_recv, ex_two_send, ex_two_recv)

    def load(index, source, target):
        return pltpu.make_async_copy(source, target, load_sem.at[index])

    load_t = [load(0, t_in.at[unit], t_ref) for unit in range(2)]
    load_u = [load(1, u_in.at[unit], u_ref) for unit in range(2)]
    load_s = [load(2, s_in.at[unit], s_ref) for unit in range(2)]
    load_a = [load(3, a_in.at[unit], a_pad) for unit in range(2)]
    load_skip = load(4, skip_in, skip_ref)
    load_shuffle = load(5, shuffle, u_ref.at[:, pl.ds(0, SHUFFLE_C)])
    load_t[1].start()
    load_skip.start()
    load_u[1].start()
    load_s[1].start()
    load_a[1].start()
    greet_all(at)
    ds_pad[...] = jnp.zeros(ds_pad.shape, BF16)

    mask_mid = mask_in[...]
    mask_out = mask_in[:, :BLOCK_C]
    slot_rows = lax.broadcasted_iota(jnp.int32, (SLOTS, BLOCK_C), 0)
    has_before = (slot_rows >= 4).astype(F32)
    has_after = (slot_rows < 12).astype(F32)
    lanes_line = pl.ds(pl.multiple_of(line * 128, 128), 128)
    rows_line = pl.ds(pl.multiple_of(line * ROWS, 16), ROWS)

    act_copies = []

    def acts(row, source, target):
        for step in (1, 2, 3):
            peer = line_peer(at, step)
            copy = remote(
                source.at[:, pl.ds(pl.multiple_of(peer[1] * 128, 128), 128)],
                target.at[rows_line],
                act_send.at[row, step - 1],
                act_recv.at[row, step - 1],
                peer,
            )
            copy.start()
            act_copies.append(copy)
        own = pltpu.make_async_copy(source.at[:, lanes_line], target.at[rows_line], act_sem.at[row])
        own.start()
        return own

    def acts_wait(row, source, target, own):
        for step in (1, 2, 3):
            origin = lax.rem(line + 4 - step, 4)
            remote(
                source.at[:, lanes_line],
                target.at[pl.ds(pl.multiple_of(origin * ROWS, 16), ROWS)],
                act_send.at[row, step - 1],
                act_recv.at[row, step - 1],
                line_peer(at, step),
            ).wait_recv()
        own.wait()

    flying = [[] for _ in CHUNKS]
    pair_copies = [None] * N_CHUNKS
    fin_copies = [None] * N_CHUNKS

    def launch(index, copy):
        copy.start()
        flying[index].append(copy)
        return copy

    def drain(index):
        for copy in flying[index]:
            copy.wait_send()
        flying[index] = []

    def grad_of(index):
        kind, _, lead, _ = CHUNKS[index]
        return g_s.at[lead] if kind == "s" else g_t

    def land_of(index):
        kind, _, lead, _ = CHUNKS[index]
        return land_s.at[lead] if kind == "s" else land_t

    def held(index, small, large):
        kind, unit, lead, _ = CHUNKS[index]
        return large.at[unit, lead] if kind == "s" else small.at[unit]

    def cut(index, owner, first, count):
        width = CHIP_S if CHUNKS[index][0] == "s" else CHIP_T
        lanes = pl.ds(pl.multiple_of(owner * width, 128), width)
        return grad_of(index).at[:, pl.ds(first, count), core, :, lanes]

    def add_into(target, source):
        leads, count, _, width = target.shape

        def body(turn, carry):
            if leads == 1 and width > 2048:
                where = (0, lax.div(turn, 3), pl.ds(pl.multiple_of(lax.rem(turn, 3) * 16, 16), 16))
            elif leads == 1:
                where = (0, turn)
            else:
                where = (turn,)
            target[where] = (target[where].astype(F32) + source[where].astype(F32)).astype(BF16)
            return carry

        turns = leads if leads > 1 else count * (3 if width > 2048 else 1)
        lax.fori_loop(0, turns, body, 0)

    def step_pair(index):
        pair_copies[index] = launch(
            index,
            remote(
                grad_of(index).at[:, :, 1 - core],
                land_of(index),
                pair_send.at[index],
                pair_recv.at[index],
                at["pair"],
            ),
        )

    def step_one(index):
        pair_copies[index].wait_recv()
        add_into(grad_of(index).at[:, :, core], land_of(index))
        ones, twos = held(index, one_t, one_s), held(index, two_t, two_s)
        for way, (name, first) in enumerate((("x", 0), ("y", 2))):
            launch(
                index,
                remote(
                    cut(index, at["chip_d"], first, 2),
                    ones.at[way],
                    one_send.at[index, way],
                    one_recv.at[index, way],
                    at[name],
                ),
            )
            launch(
                index,
                remote(
                    cut(index, at["chip_" + name], first, 2),
                    twos.at[way, :, pl.ds(first, 2)],
                    two_send.at[index, way, 0],
                    two_recv.at[index, way, 0],
                    at[name],
                ),
            )

    def step_two(index):
        ones, twos = held(index, one_t, one_s), held(index, two_t, two_s)
        for way, (name, other, first) in enumerate((("x", "y", 0), ("y", "x", 2))):
            landing = ones.at[way]
            remote(
                landing, landing, one_send.at[index, way], one_recv.at[index, way], at[name]
            ).wait_recv()
            target = cut(index, at["chip_" + other], first, 2)
            add_into(target, landing)
            launch(
                index,
                remote(
                    target,
                    twos.at[1 - way, :, pl.ds(first, 2)],
                    two_send.at[index, 1 - way, 1],
                    two_recv.at[index, 1 - way, 1],
                    at[other],
                ),
            )

    def step_three(index):
        twos = held(index, two_t, two_s)
        for way, (name, first) in enumerate((("x", 0), ("y", 2))):
            for turn, begin in enumerate((first, 2 - first)):
                landing = twos.at[way, :, pl.ds(begin, 2)]
                remote(
                    landing,
                    landing,
                    two_send.at[index, way, turn],
                    two_recv.at[index, way, turn],
                    at[name],
                ).wait_recv()
        own = cut(index, chip, 0, 4)
        leads = own.shape[0]

        def body(turn, carry):
            where = (0, turn) if leads == 1 else (turn,)
            own[where] = (
                own[where].astype(F32)
                + twos.at[0][where].astype(F32)
                + twos.at[1][where].astype(F32)
            ).astype(BF16)
            return carry

        lax.fori_loop(0, 4 if leads == 1 else leads, body, 0)
        lines = held(index, line_t, line_s)
        for step in (1, 3, 2):
            peer = line_peer(at, step)
            launch(
                index,
                remote(
                    cut(index, chip, peer[1], 1),
                    lines.at[step - 1],
                    line_send.at[index, step - 1],
                    line_recv.at[index, step - 1],
                    peer,
                ),
            )

    def step_four(index):
        lines, fin = held(index, line_t, line_s), held(index, fin_t, fin_s)
        for step in (1, 2, 3):
            landing = lines.at[step - 1]
            remote(
                landing,
                landing,
                line_send.at[index, step - 1],
                line_recv.at[index, step - 1],
                line_peer(at, step),
            ).wait_recv()
        total = cut(index, chip, line, 1)[...].astype(F32)
        for step in range(3):
            total = total + lines[step].astype(F32)
        fin[0] = total
        fin_copies[index] = launch(
            index,
            remote(fin.at[0], fin.at[1], fin_send.at[index], fin_recv.at[index], at["pair"]),
        )

    adam_saves = {"s": [], "t": []}
    adam_loads = {}

    def adam_moves(index, load):
        kind, unit, lead, _ = CHUNKS[index]
        moves = []
        for which in range(2):
            if kind == "s":
                arrays = (sp_in, sm_in, sv_in) if load else (sp_out, sm_out, sv_out)
                half = core if which == 0 else 1 - core
                rows = pl.ds(pl.multiple_of(half * HALF + SUB * lead, 16), SUB)
                for array, ref in enumerate(arrays):
                    here, there = adam_s.at[array, which], ref.at[unit, rows]
                    moves.append((there, here) if load else (here, there))
            elif which == 0:
                arrays = (tp_in, tm_in, tv_in) if load else (tp_out, tm_out, tv_out)
                for array, ref in enumerate(arrays):
                    here, there = adam_t.at[array], ref.at[unit]
                    moves.append((there, here) if load else (here, there))
        sems = adam_load if load else adam_save
        row = 0 if kind == "s" else 1
        return [
            pltpu.make_async_copy(source, target, sems.at[row, number])
            for number, (source, target) in enumerate(moves)
        ]

    def adam_fetch(index):
        kind = CHUNKS[index][0]
        for copy in adam_saves[kind]:
            copy.wait()
        adam_saves[kind] = []
        adam_loads[index] = adam_moves(index, True)
        for copy in adam_loads[index]:
            copy.start()

    def step_five(index):
        kind, unit, lead, leads = CHUNKS[index]
        adam_fetch(index)
        fin_copies[index].wait_recv()
        fin = held(index, fin_t, fin_s)
        for copy in adam_loads[index]:
            copy.wait()
        if kind == "s":
            width = CHIP_S // 2
            for which in range(2):
                value = fin[which, 0, 0]
                grad = jnp.where(core == 0, value[:, :width], value[:, width:])
                fresh = adam_update(
                    adam_s[0, which],
                    adam_s[1, which],
                    adam_s[2, which],
                    grad,
                    RATE_CONV,
                    DECAY_CONV,
                )
                for array in range(3):
                    adam_s[array, which] = fresh[array]
        else:
            width = CHIP_T // 2
            for tau in range(3):
                both = [
                    fin[which, 3 * tau : 3 * tau + 3].reshape(HALF, CHIP_T) for which in range(2)
                ]
                first = jnp.where(core == 0, both[0], both[1])
                second = jnp.where(core == 0, both[1], both[0])
                turned = jnp.concatenate([first, second], axis=0).T
                grad = jnp.where(core == 0, turned[:width], turned[width:])
                fresh = adam_update(
                    adam_t[0, tau], adam_t[1, tau], adam_t[2, tau], grad, RATE_CONV, DECAY_CONV
                )
                for array in range(3):
                    adam_t[array, tau] = fresh[array]
        adam_saves[kind] = adam_moves(index, False)
        for copy in adam_saves[kind]:
            copy.start()

    def fetch_w(unit, tap, slot):
        lanes = pl.ds(pl.multiple_of(tap * BLOCK_C, 128), BLOCK_C)
        return pltpu.make_async_copy(ws.at[unit, :, lanes], w_buf.at[slot], w_sem.at[slot])

    def fetch_wt(unit, tau, slot):
        return pltpu.make_async_copy(wt.at[unit, tau], w_buf.at[slot], w_sem.at[slot])

    def window(tap):
        return a_pad[pl.ds(tap // 3, SIDE), pl.ds(tap % 3, SIDE)].reshape(ROWS, BLOCK_C)

    zero_mid = jnp.zeros((SLOTS, MID_C), F32)
    zero_out = jnp.zeros((SLOTS, BLOCK_C), F32)

    def out_norm_back(unit, *hooks):
        grad_ref = skip_ref if unit == 1 else side
        gain = par[4 + 2 * unit : 5 + 2 * unit, :BLOCK_C]
        inverse = stat_out[2 * unit : 2 * unit + 1]
        total = stat_out[2 * unit + 1 : 2 * unit + 2]

        def out_sums(p, carry):
            rows = rows_of(p)
            grad = grad_ref[rows, :].astype(F32)
            return (carry[0] + grad, carry[1] + grad * t_ref[rows, :])

        bias_acc, gain_acc = over_pixels(out_sums, (zero_out, zero_out))
        sums = [
            jnp.sum(bias_acc, axis=0, keepdims=True),
            jnp.sum(gain_acc, axis=0, keepdims=True),
        ]
        grad_bias, grad_gain = exchange(
            at, land_out, land_out_two, unit, sems, 2 * unit, sums, combine_sums, hooks
        )
        out_grad[2 * unit : 2 * unit + 1, :] = grad_gain
        out_grad[2 * unit + 1 : 2 * unit + 2, :] = grad_bias
        scale = gain * inverse
        bias_part, gain_part = grad_bias / total, grad_gain / total

        def out_back(p, carry):
            rows = rows_of(p)
            value = (
                mask_out
                * scale
                * (grad_ref[rows, :].astype(F32) - bias_part - t_ref[rows, :] * gain_part)
            )
            d_ref[1, rows, :] = value.astype(BF16)
            d_ref[0, rows, :] = (pltpu.roll(value, 12, 0) * has_after).astype(BF16)
            d_ref[2, rows, :] = (pltpu.roll(value, 4, 0) * has_before).astype(BF16)
            return carry

        over_pixels(out_back, 0)

    def temporal_grad():
        for tau in range(3):
            g_t[3 * tau : 3 * tau + 3] = (
                lax.dot_general(u_ref[...], d_ref[tau], TN, preferred_element_type=F32)
                .astype(BF16)
                .reshape(3, 4, 2, SUB, BLOCK_C)
            )

    def temporal_back(unit):
        for tau in range(3):
            slot = tau % 2
            if tau < 2:
                fetch_wt(unit, tau + 1, 1 - slot).start()
            fetch_wt(unit, tau, slot).wait()
            value = lax.dot_general(d_ref[tau], w_buf[slot], NT, preferred_element_type=F32)
            wide[...] = value if tau == 0 else wide[...] + value

    def mid_norm_back(unit, *hooks):
        gain = par[2 * unit : 2 * unit + 1]
        bias = par[2 * unit + 1 : 2 * unit + 2]
        inverse = stat_mid[2 * unit : 2 * unit + 1]
        total = stat_mid[2 * unit + 1 : 2 * unit + 2]

        def mid_sums(p, carry):
            rows = rows_of(p)
            standard = s_ref[rows, :].astype(F32)
            grad = mask_mid * slope_of(standard * gain + bias) * wide[rows, :]
            wide[rows, :] = grad
            return (carry[0] + grad, carry[1] + grad * standard)

        bias_acc, gain_acc = over_pixels(mid_sums, (zero_mid, zero_mid))
        sums = [
            jnp.sum(bias_acc, axis=0, keepdims=True),
            jnp.sum(gain_acc, axis=0, keepdims=True),
        ]
        grad_bias, grad_gain = exchange(
            at, land_mid, land_mid_two, unit, sems, 2 * unit + 1, sums, combine_sums, hooks
        )
        mid_grad[2 * unit : 2 * unit + 1, :] = grad_gain
        mid_grad[2 * unit + 1 : 2 * unit + 2, :] = grad_bias
        scale = gain * inverse
        bias_part, gain_part = grad_bias / total, grad_gain / total

        def mid_back(p, carry):
            rows = rows_of(p)
            value = (
                mask_mid
                * scale
                * (wide[rows, :] - bias_part - s_ref[rows, :].astype(F32) * gain_part)
            )
            ds_pad[1 + p // SIDE, 1 + p % SIDE] = value.astype(BF16)
            return carry

        over_pixels(mid_back, 0)

    def spatial_grad(third):
        columns = slice(third * THIRD, (third + 1) * THIRD)

        def body(row, carry):
            inner = ds_pad[1 : 1 + SIDE, 1 : 1 + SIDE, :, columns].reshape(ROWS, THIRD)
            taps = jnp.concatenate([window(3 * row + column) for column in range(3)], axis=1)
            lanes = pl.ds(pl.multiple_of(row * 3 * BLOCK_C, 128), 3 * BLOCK_C)
            g_s[third, 0, :, :, :, lanes] = (
                lax.dot_general(inner, taps, TN, preferred_element_type=F32)
                .astype(BF16)
                .reshape(4, 2, SUB, 3 * BLOCK_C)
            )
            return carry

        lax.fori_loop(0, 3, body, 0)

    def spatial_back(unit, first):
        if first == 0:
            fetch_w(unit, 0, 0).start()

        def body(tap, carry):
            slot = lax.rem(tap, 2)

            @pl.when(tap < 8)
            def _():
                fetch_w(unit, tap + 1, 1 - slot).start()

            fetch_w(unit, tap, slot).wait()
            moved = ds_pad[pl.ds(2 - tap // 3, SIDE), pl.ds(2 - tap % 3, SIDE)].reshape(ROWS, MID_C)
            value = lax.dot_general(moved, w_buf[slot], NN, preferred_element_type=F32)

            @pl.when(tap == 0)
            def _():
                side[...] = value

            @pl.when(tap > 0)
            def _():
                side[...] = side[...] + value

            return carry

        lax.fori_loop(first, first + 3, body, 0)

    a_0, b_0, c_0, t_0, a_1, b_1, c_1, t_1 = range(N_CHUNKS)

    load_t[1].wait()
    load_skip.wait()
    fetch_wt(1, 0, 0).start()
    out_norm_back(1, None, None)
    load_t[0].start()
    load_u[1].wait()
    temporal_grad()
    load_u[0].start()
    step_pair(t_1)
    temporal_back(1)
    load_s[1].wait()
    own_acts = []
    mid_norm_back(
        1,
        lambda: step_one(t_1),
        lambda: own_acts.append(acts(0, block_in, block_out)),
    )
    load_s[0].start()
    load_a[1].wait()
    spatial_grad(0)
    step_pair(a_1)
    step_two(t_1)
    spatial_grad(1)
    step_pair(b_1)
    step_one(a_1)
    spatial_grad(2)
    load_a[0].start()
    step_pair(c_1)
    step_three(t_1)
    step_one(b_1)
    step_two(a_1)
    spatial_back(1, 0)
    step_four(t_1)
    spatial_back(1, 3)
    spatial_back(1, 6)
    load_t[0].wait()
    gain, bias = par[4:5, :BLOCK_C], par[5:6, :BLOCK_C]

    def hidden_back(p, carry):
        rows = rows_of(p)
        slope = slope_of(t_ref[rows, :] * gain + bias)
        side[rows, :] = mask_out * slope * side[rows, :]
        return carry

    over_pixels(hidden_back, 0)
    fetch_wt(0, 0, 0).start()

    def hook_a():
        step_one(c_1)
        step_two(b_1)

    out_norm_back(0, hook_a, lambda: step_three(a_1))
    drain(t_1)
    load_u[0].wait()
    temporal_grad()
    load_shuffle.start()
    step_pair(t_0)
    temporal_back(0)
    step_two(c_1)
    step_five(t_1)
    load_s[0].wait()
    mid_norm_back(0, lambda: step_one(t_0), lambda: step_three(b_1))
    load_a[0].wait()
    step_four(a_1)
    drain(a_1)
    spatial_grad(0)
    step_pair(a_0)
    step_two(t_0)
    step_three(c_1)
    step_five(a_1)
    step_four(b_1)
    spatial_back(0, 0)
    step_one(a_0)
    spatial_back(0, 3)
    spatial_back(0, 6)
    step_three(t_0)
    step_two(a_0)
    load_shuffle.wait()
    d_ref[0] = (side[...] + skip_ref[...].astype(F32)).astype(BF16)
    thin = d_ref.at[1]
    thin[...] = lax.dot_general(
        u_ref[:, :SHUFFLE_C], d_ref[0], TN, preferred_element_type=F32
    ).astype(BF16)[:ROWS]
    own_acts.append(acts(1, thin, input_out))
    drain(b_1)
    spatial_grad(1)
    step_pair(b_0)
    step_five(b_1)
    step_four(c_1)
    drain(c_1)
    spatial_grad(2)
    step_pair(c_0)
    step_one(b_0)
    step_three(a_0)
    step_five(c_1)
    step_four(t_0)
    step_one(c_0)
    step_two(b_0)
    step_five(t_0)
    step_two(c_0)
    step_four(a_0)
    step_three(b_0)
    step_five(a_0)
    step_three(c_0)
    step_four(b_0)
    step_five(b_0)
    step_four(c_0)
    step_five(c_0)
    acts_wait(0, block_in, block_out, own_acts[0])
    acts_wait(1, thin, input_out, own_acts[1])
    for kind in ("s", "t"):
        for copy in adam_saves[kind]:
            copy.wait()
    for copy in act_copies:
        copy.wait_send()
    for index in (t_0, a_0, b_0, c_0):
        drain(index)


def spaces(text):
    kinds = {"v": VMEM, "a": pl.ANY, "s": pltpu.SMEM}
    return [pl.BlockSpec(memory_space=kinds[mark]) for mark in text]


def dma(*shape):
    return pltpu.SemaphoreType.DMA(shape)


def params(number):
    return pltpu.CompilerParams(
        collective_id=number, has_side_effects=True, vmem_limit_bytes=GRANT
    )


def shaped(*shape, dtype=BF16):
    return jax.ShapeDtypeStruct(shape, dtype)


def run_forward(*args):
    padded = (SIDE + 2, SIDE + 2, SLOTS, BLOCK_C)
    return pl.pallas_call(
        forward_kernel,
        out_shape=[
            shaped(2, 3, 4, 2, SUB, TAPS_C),
            shaped(2, 9, 4, 2, SUB, BLOCK_C),
            shaped(8, MID_C, dtype=F32),
            shaped(SLOTS, MID_C, dtype=F32),
            shaped(ROWS, BLOCK_C),
            shaped(2, *padded),
            shaped(2, ROWS, MID_C),
            shaped(2, ROWS, MID_C),
            shaped(2, ROWS, BLOCK_C, dtype=F32),
            shaped(ROWS, BLOCK_C),
            shaped(4, MID_C, dtype=F32),
            shaped(4, BLOCK_C, dtype=F32),
        ],
        in_specs=spaces("vvaavvsv"),
        out_specs=spaces("aavvvaaaaavv"),
        scratch_shapes=[
            VMEM((2, 2 * HALF, CHIP_S // 2), BF16),
            VMEM((2, 2 * HALF, 3 * CHIP_T // 2), BF16),
            VMEM((4 * ROWS, 128), F32),
            VMEM((4 * ROWS, 128), BF16),
            VMEM((8, MID_C), F32),
            VMEM((2, HALF, CHIP_S // 2), BF16),
            VMEM((2, HALF, 3 * CHIP_T // 2), BF16),
            VMEM((2, 3, 1, SUB, CHIP_S), BF16),
            VMEM((2, 9, 1, SUB, CHIP_T), BF16),
            VMEM((ROWS, BLOCK_C), BF16),
            VMEM((ROWS, BLOCK_C), BF16),
            VMEM((4, 8, MID_C), F32),
            VMEM((2,) + padded, BF16),
            VMEM((ROWS, MID_C), F32),
            VMEM((2, ROWS, MID_C), BF16),
            VMEM((2, ROWS, MID_C), BF16),
            VMEM((2, ROWS, BLOCK_C), F32),
            VMEM((2, ROWS, BLOCK_C), F32),
            VMEM((ROWS, BLOCK_C), BF16),
            VMEM((ROWS, BLOCK_C), BF16),
            VMEM((2, 4, 2, SUB, TAPS_C), BF16),
            VMEM((9, 4, 2, SUB, BLOCK_C), BF16),
            VMEM((2, 8, 8, MID_C), F32),
            VMEM((2, 4, 8, MID_C), F32),
            VMEM((2, 8, 8, BLOCK_C), F32),
            VMEM((2, 4, 8, BLOCK_C), F32),
            VMEM((8, 8, 128), F32),
            VMEM((8, 8, MID_C), F32),
            VMEM((4, 8, MID_C), F32),
            dma(4),
            dma(4),
            dma(3, 3),
            dma(3, 3),
            dma(N_CHUNKS, 3),
            dma(N_CHUNKS, 3),
            dma(N_CHUNKS, 2, 2),
            dma(N_CHUNKS, 2, 2),
            dma(N_CHUNKS, 2),
            dma(N_CHUNKS, 2),
            dma(N_CHUNKS, 4),
            dma(N_CHUNKS, 4),
            dma(3),
            dma(N_CHUNKS),
            dma(2),
            dma(2),
            dma(10),
            dma(5, 7),
            dma(5, 7),
            dma(5, 3),
            dma(5, 3),
        ],
        compiler_params=params(0),
        name="forward",
    )(*args)


def run_backward(*args):
    return pl.pallas_call(
        backward_kernel,
        out_shape=[
            *[shaped(2, 2 * HALF, CHIP_S // 2, dtype=F32)] * 3,
            *[shaped(2, 3, CHIP_T // 2, 2 * HALF, dtype=F32)] * 3,
            shaped(4, MID_C, dtype=F32),
            shaped(4, BLOCK_C, dtype=F32),
            shaped(4 * ROWS, 128),
            shaped(4 * ROWS, 128),
        ],
        in_specs=spaces("aaaaaaavvvvaaaaaaaa"),
        out_specs=spaces("aaaaaavvaa"),
        scratch_shapes=[
            VMEM((SIDE + 2, SIDE + 2, SLOTS, BLOCK_C), BF16),
            VMEM((ROWS, MID_C), BF16),
            VMEM((ROWS, MID_C), BF16),
            VMEM((ROWS, BLOCK_C), F32),
            VMEM((ROWS, BLOCK_C), F32),
            VMEM((ROWS, BLOCK_C), BF16),
            VMEM((ROWS, MID_C), F32),
            VMEM((SIDE + 2, SIDE + 2, SLOTS, MID_C), BF16),
            VMEM((3, ROWS, BLOCK_C), BF16),
            VMEM((2, MID_C, BLOCK_C), BF16),
            VMEM((2, 8, 8, MID_C), F32),
            VMEM((2, 4, 8, MID_C), F32),
            VMEM((2, 8, 8, BLOCK_C), F32),
            VMEM((2, 4, 8, BLOCK_C), F32),
            VMEM((3, 1, 4, 2, SUB, TAPS_C), BF16),
            VMEM((9, 4, 2, SUB, BLOCK_C), BF16),
            VMEM((3, 1, 4, SUB, TAPS_C), BF16),
            VMEM((9, 4, SUB, BLOCK_C), BF16),
            VMEM((2, 3, 2, 1, 2, SUB, CHIP_S), BF16),
            VMEM((2, 2, 9, 2, SUB, CHIP_T), BF16),
            VMEM((2, 3, 2, 1, 4, SUB, CHIP_S), BF16),
            VMEM((2, 2, 9, 4, SUB, CHIP_T), BF16),
            VMEM((2, 3, 3, 1, 1, SUB, CHIP_S), BF16),
            VMEM((2, 3, 9, 1, SUB, CHIP_T), BF16),
            VMEM((2, 3, 2, 1, 1, SUB, CHIP_S), F32),
            VMEM((2, 2, 9, 1, SUB, CHIP_T), F32),
            VMEM((3, 2, SUB, CHIP_S // 2), F32),
            VMEM((3, 3, CHIP_T // 2, 2 * HALF), F32),
            dma(6),
            dma(2),
            dma(4, 7),
            dma(4, 7),
            dma(4, 3),
            dma(4, 3),
            dma(2, 3),
            dma(2, 3),
            dma(2),
            dma(N_CHUNKS),
            dma(N_CHUNKS),
            dma(N_CHUNKS, 2),
            dma(N_CHUNKS, 2),
            dma(N_CHUNKS, 2, 2),
            dma(N_CHUNKS, 2, 2),
            dma(N_CHUNKS, 3),
            dma(N_CHUNKS, 3),
            dma(N_CHUNKS),
            dma(N_CHUNKS),
            dma(2, 6),
            dma(2, 6),
        ],
        compiler_params=params(1),
        name="backward",
    )(*args)


def finish_kernel(
    frames_in,
    mid_p,
    mid_m,
    mid_v,
    out_p,
    out_m,
    out_v,
    sp_in,
    sm_in,
    sv_in,
    tp_in,
    tm_in,
    tv_in,
    mid_all,
    out_all,
    block_in,
    grad_in,
    block_out,
    clip_pool,
    grad_out,
    mid_p_out,
    mid_m_out,
    mid_v_out,
    out_p_out,
    out_m_out,
    out_v_out,
    sp_out,
    sm_out,
    sv_out,
    tp_out,
    tm_out,
    tv_out,
    block_ref,
    grad_ref,
    block_wide,
    grad_wide,
    hold_s,
    hold_t,
    sems,
):
    line = lax.axis_index("chan")
    loads = [
        pltpu.make_async_copy(block_in, block_ref, sems.at[0]),
        pltpu.make_async_copy(grad_in, grad_ref, sems.at[1]),
    ]
    passing = (
        (sp_in, hold_s.at[0], sp_out),
        (sm_in, hold_s.at[1], sm_out),
        (sv_in, hold_s.at[2], sv_out),
        (tp_in, hold_t.at[0], tp_out),
        (tm_in, hold_t.at[1], tm_out),
        (tv_in, hold_t.at[2], tv_out),
    )
    gets = [
        pltpu.make_async_copy(source, held, sems.at[2 + number])
        for number, (source, held, _) in enumerate(passing)
    ]
    puts = [
        pltpu.make_async_copy(held, target, sems.at[10 + number])
        for number, (_, held, target) in enumerate(passing)
    ]
    for copy in loads + gets:
        copy.start()
    stores = [
        pltpu.make_async_copy(block_wide, block_out, sems.at[8]),
        pltpu.make_async_copy(grad_wide, grad_out, sems.at[9]),
    ]
    loads[0].wait()
    block_wide[...] = block_ref[...].astype(F32)
    stores[0].start()
    loads[1].wait()
    grad_wide[...] = grad_ref[...].astype(F32)
    stores[1].start()
    for get, put in zip(gets, puts):
        get.wait()
        put.start()
    size = FRAMES * HW
    for clip in range(clip_pool.shape[0]):
        total = jnp.sum(block_wide[clip * size : (clip + 1) * size, :], axis=0, keepdims=True)
        kept = lax.div(frames_in[clip], 8).astype(F32)
        clip_pool[clip : clip + 1, :] = total / (HW * kept)
    all_rows = jnp.concatenate([mid_all[...], jnp.zeros((4, MID_C), F32)], axis=0)
    turned = pltpu.roll(all_rows, lax.rem(MID_C - line * (2 * SUB), MID_C), 1)[0:4]
    grad = jnp.concatenate(
        [
            turned[:, third * THIRD + half * SUB : third * THIRD + (half + 1) * SUB]
            for half in range(2)
            for third in range(3)
        ],
        axis=1,
    )
    fresh = adam_update(mid_p[...], mid_m[...], mid_v[...], grad, RATE_NORM, 0.0)
    for ref, value in zip((mid_p_out, mid_m_out, mid_v_out), fresh):
        ref[...] = value
    grad = out_all[:, pl.ds(pl.multiple_of(line * 128, 128), 128)]
    fresh = adam_update(out_p[...], out_m[...], out_v[...], grad, RATE_NORM, 0.0)
    for ref, value in zip((out_p_out, out_m_out, out_v_out), fresh):
        ref[...] = value
    for copy in stores + puts:
        copy.wait()


def run_finish(frames, *args):
    convs = args[6:12]
    norms = args[:6]
    clips = frames.shape[0]
    return pl.pallas_call(
        finish_kernel,
        out_shape=[
            shaped(4 * ROWS, 128, dtype=F32),
            shaped(clips, 128, dtype=F32),
            shaped(4 * ROWS, 128, dtype=F32),
            *[shaped(*v.shape, dtype=F32) for v in norms],
            *[shaped(*v.shape, dtype=F32) for v in convs],
        ],
        in_specs=spaces("svvvvvvaaaaaavvaa"),
        out_specs=spaces("avavvvvvvaaaaaa"),
        scratch_shapes=[
            VMEM((4 * ROWS, 128), BF16),
            VMEM((4 * ROWS, 128), BF16),
            VMEM((4 * ROWS, 128), F32),
            VMEM((4 * ROWS, 128), F32),
            VMEM((3,) + convs[0].shape, F32),
            VMEM((3,) + convs[3].shape, F32),
            dma(16),
        ],
        compiler_params=pltpu.CompilerParams(vmem_limit_bytes=GRANT),
        name="finish",
    )(frames, *args)


def shuffle_matrix():
    clip, frame, pixel = np.meshgrid(np.arange(4), np.arange(FRAMES), np.arange(HW), indexing="ij")
    source = (clip * FRAMES + frame) * HW + pixel
    target = pixel * SLOTS + frame * 4 + clip
    matrix = np.zeros((ROWS, SHUFFLE_C), np.float32)
    matrix[target.reshape(-1), source.reshape(-1)] = 1.0
    return jnp.asarray(matrix, BF16)


def on_pairs(
    features,
    cotangent,
    clip_frames,
    spatial_master,
    spatial_first,
    spatial_second,
    temporal_master,
    temporal_first,
    temporal_second,
    mid_norm,
    mid_first,
    mid_second,
    out_norm,
    out_first,
    out_second,
):
    line = lax.axis_index("chan")
    spatial_own = [jnp.swapaxes(v, 1, 2) for v in (spatial_master, spatial_first, spatial_second)]
    temporal_own = [
        jnp.swapaxes(v, 2, 3) for v in (temporal_master, temporal_first, temporal_second)
    ]
    shuffle = shuffle_matrix()
    ws, wt, par, mask, block, a_all, s_all, u_all, t_all, skip, stat_mid, stat_out = run_forward(
        spatial_own[0],
        temporal_own[0],
        features,
        cotangent,
        mid_norm,
        out_norm,
        clip_frames,
        shuffle,
    )
    conv_new = run_backward(
        ws.reshape(2, MID_C, TAPS_C),
        wt.reshape(2, 3, MID_C, BLOCK_C),
        a_all,
        s_all,
        u_all,
        t_all,
        skip,
        stat_mid,
        stat_out,
        par,
        mask,
        shuffle,
        block,
        *spatial_own,
        *temporal_own,
    )
    block_out, clip_pool, grad_out, *rest = run_finish(
        clip_frames, mid_norm, mid_first, mid_second, out_norm, out_first, out_second, *conv_new
    )
    norms, convs = rest[:6], rest[6:]
    spatial = [jnp.swapaxes(v, 1, 2) for v in convs[:3]]
    temporal = [jnp.swapaxes(v, 2, 3) for v in convs[3:]]
    return (block_out, clip_pool, grad_out, *spatial, *temporal, *norms)


def solution(mesh):
    in_specs = (
        P("dp", "chan"),
        P("dp", "chan"),
        P("dp"),
        P(None, "dp", "chan"),
        P(None, "dp", "chan"),
        P(None, "dp", "chan"),
        P(None, None, "chan", "dp"),
        P(None, None, "chan", "dp"),
        P(None, None, "chan", "dp"),
        P(None, "chan"),
        P(None, "chan"),
        P(None, "chan"),
        P(None, "chan"),
        P(None, "chan"),
        P(None, "chan"),
    )
    out_specs = (
        P("dp", "chan"),
        P("dp", "chan"),
        P("dp", "chan"),
        P(None, "dp", "chan"),
        P(None, "dp", "chan"),
        P(None, "dp", "chan"),
        P(None, None, "chan", "dp"),
        P(None, None, "chan", "dp"),
        P(None, None, "chan", "dp"),
        P(None, "chan"),
        P(None, "chan"),
        P(None, "chan"),
        P(None, "chan"),
        P(None, "chan"),
        P(None, "chan"),
    )
    body = on_pairs if mesh.shape["dp"] == 8 and mesh.shape["chan"] == 4 else on_device
    return jax.shard_map(
        body, mesh=mesh, in_specs=in_specs, out_specs=out_specs, check_vma=False
    )
```

```python
import jax
import jax.numpy as jnp
import numpy as np
from jax import lax
from jax.experimental import pallas as pl
from jax.experimental.pallas import tpu as pltpu
from jax.sharding import PartitionSpec as P

FRAMES = 4
SIDE = 7
STEP = 10
HW = 49


EPS_NORM = 1e-05
EPS_ADAM = 1e-08
BETA_ONE = 0.9
BETA_TWO = 0.95
RATE_CONV = 0.01
RATE_NORM = 0.8
DECAY_CONV = 0.05


def frame_mask(clip_frames):
    kept_frames = clip_frames // 8
    frame_ids = jnp.arange(FRAMES, dtype=jnp.int32)
    frame_grid = (frame_ids[None, :] < kept_frames[:, None]).astype(jnp.float32)
    return jnp.broadcast_to(frame_grid[:, :, None], (kept_frames.shape[0], FRAMES, HW)).reshape(
        -1, 1
    )


def silu_slope(values):
    sigmoid = jax.nn.sigmoid(values)
    return sigmoid * (1.0 + values * (1.0 - sigmoid))


def spatial_apply(inputs, tap_weights):
    channels = inputs.shape[1]
    padded = jnp.pad(inputs.reshape(-1, SIDE, SIDE, channels), ((0, 0), (1, 1), (1, 1), (0, 0)))
    summed = jnp.zeros((inputs.shape[0], tap_weights.shape[2]), jnp.float32)
    for tap_index in range(9):
        row_off, col_off = (tap_index // 3, tap_index % 3)
        window = padded[:, row_off : row_off + SIDE, col_off : col_off + SIDE].reshape(-1, channels)
        summed = summed + jnp.dot(
            window, tap_weights[tap_index], preferred_element_type=jnp.float32
        )
    return (summed, padded)


def spatial_grads(padded, tap_weights, grad_out):
    channels = padded.shape[3]
    weight_terms = []
    input_sum = jnp.zeros((padded.shape[0], SIDE, SIDE, channels), jnp.float32)
    for tap_index in range(9):
        row_off, col_off = (tap_index // 3, tap_index % 3)
        window = padded[:, row_off : row_off + SIDE, col_off : col_off + SIDE].reshape(-1, channels)
        weight_terms.append(
            lax.dot_general(
                window, grad_out, (((0,), (0,)), ((), ())), preferred_element_type=jnp.float32
            )
        )
        pulled = lax.dot_general(
            grad_out,
            tap_weights[tap_index],
            (((1,), (1,)), ((), ())),
            preferred_element_type=jnp.float32,
        )
        pulled = jnp.pad(pulled.reshape(-1, SIDE, SIDE, channels), ((0, 0), (1, 1), (1, 1), (0, 0)))
        input_sum = (
            input_sum
            + pulled[:, 2 - row_off : 2 - row_off + SIDE, 2 - col_off : 2 - col_off + SIDE]
        )
    return (jnp.stack(weight_terms).reshape(-1, grad_out.shape[1]), input_sum.reshape(-1, channels))


def temporal_apply(inputs, weight):
    frame_seq = inputs.reshape(-1, FRAMES, HW, inputs.shape[1])
    padded = jnp.pad(frame_seq, ((0, 0), (1, 1), (0, 0), (0, 0)))
    summed = jnp.zeros(frame_seq.shape[:3] + (weight.shape[2],), jnp.float32)
    for frame_off in range(3):
        summed = summed + jnp.einsum(
            "nfpm,mc->nfpc",
            padded[:, frame_off : frame_off + FRAMES],
            weight[frame_off],
            preferred_element_type=jnp.float32,
        )
    return (summed.reshape(inputs.shape[0], -1), padded)


def temporal_grads(padded, weight, grad_full):
    grad_seq = grad_full.reshape(-1, FRAMES, HW, grad_full.shape[1])
    grad_pad = jnp.pad(grad_seq, ((0, 0), (1, 1), (0, 0), (0, 0)))
    weight_terms = []
    input_sum = jnp.zeros(padded.shape[:1] + (FRAMES, HW, padded.shape[3]), jnp.float32)
    for frame_off in range(3):
        weight_terms.append(
            jnp.einsum(
                "nfpm,nfpc->mc",
                padded[:, frame_off : frame_off + FRAMES],
                grad_seq,
                preferred_element_type=jnp.float32,
            )
        )
        input_sum = input_sum + jnp.einsum(
            "nfpc,mc->nfpm",
            grad_pad[:, 2 - frame_off : 2 - frame_off + FRAMES],
            weight[frame_off],
            preferred_element_type=jnp.float32,
        )
    return (jnp.stack(weight_terms), input_sum.reshape(grad_full.shape[0], -1))


def normalize(values, validity, gain_row, bias_row):
    local_valid = jnp.sum(validity)
    total_valid, value_sums = lax.psum((local_valid, jnp.sum(values * validity, axis=0)), "dp")
    average = value_sums / total_valid
    centered = values - average
    variance = lax.psum(jnp.sum(validity * centered * centered, axis=0), "dp") / total_valid
    inverse = lax.rsqrt(variance + EPS_NORM)
    standard = centered * inverse
    return (standard * gain_row + bias_row, standard, inverse, total_valid)


def normalize_back(grad_normed, standard, inverse, gain_row, total_valid, validity):
    grad_bias, grad_gain = lax.psum(
        (
            jnp.sum(grad_normed * validity, axis=0),
            jnp.sum(grad_normed * standard * validity, axis=0),
        ),
        "dp",
    )
    grad_values = (
        validity
        * gain_row
        * inverse
        * (grad_normed - grad_bias / total_valid - standard * grad_gain / total_valid)
    )
    return (grad_values, grad_gain, grad_bias)


def adam_update(weight, moment_one, moment_two, grad_value, rate, decay):
    fresh_one = BETA_ONE * moment_one + (1.0 - BETA_ONE) * grad_value
    fresh_two = BETA_TWO * moment_two + (1.0 - BETA_TWO) * grad_value * grad_value
    scaled = (
        fresh_one
        / (1.0 - BETA_ONE**STEP)
        / (jnp.sqrt(fresh_two / (1.0 - BETA_TWO**STEP)) + EPS_ADAM)
    )
    return (weight - rate * (scaled + decay * weight), fresh_one, fresh_two)


def on_device(
    features,
    cotangent,
    clip_frames,
    spatial_master,
    spatial_first,
    spatial_second,
    temporal_master,
    temporal_first,
    temporal_second,
    mid_norm,
    mid_first,
    mid_second,
    out_norm,
    out_first,
    out_second,
):
    validity = frame_mask(clip_frames)
    spatial_all, temporal_all = (
        lax.all_gather(spatial_master.astype(jnp.bfloat16), "dp", axis=1, tiled=True),
        lax.all_gather(temporal_master.astype(jnp.bfloat16), "dp", axis=3, tiled=True),
    )
    channels = temporal_all.shape[3]
    spatial_taps = spatial_all.reshape(2, 9, channels, spatial_all.shape[2])
    residual = features.astype(jnp.float32)
    outgoing = features
    kept_state = []
    for unit_index in range(2):
        gathered = lax.all_gather(outgoing, "chan", axis=1, tiled=True)
        spatial_out, padded = spatial_apply(gathered, spatial_taps[unit_index])
        mid_normed, mid_standard, mid_inverse, total_valid = normalize(
            spatial_out, validity, mid_norm[2 * unit_index], mid_norm[2 * unit_index + 1]
        )
        temporal_in = (jax.nn.silu(mid_normed) * validity).astype(jnp.bfloat16)
        partial_value, frames_padded = temporal_apply(temporal_in, temporal_all[unit_index])
        temporal_out = lax.psum_scatter(
            partial_value.astype(jnp.bfloat16), "chan", scatter_dimension=1, tiled=True
        ).astype(jnp.float32)
        out_normed, out_standard, out_inverse, total_valid = normalize(
            temporal_out, validity, out_norm[2 * unit_index], out_norm[2 * unit_index + 1]
        )
        if unit_index == 0:
            pre_act = out_normed
            outgoing = (jax.nn.silu(pre_act) * validity).astype(jnp.bfloat16)
        else:
            pre_act = out_normed + residual
            block_out = jax.nn.silu(pre_act) * validity
        kept_state.append(
            (
                padded,
                mid_normed,
                mid_standard,
                mid_inverse,
                frames_padded,
                pre_act,
                out_standard,
                out_inverse,
            )
        )
    kept_frames = (clip_frames // 8).astype(jnp.float32)
    clip_pool = (
        jnp.sum(block_out.reshape(-1, FRAMES * HW, block_out.shape[1]), axis=1)
        / (HW * kept_frames)[:, None]
    )
    skip_grad = cotangent * validity * silu_slope(kept_state[1][5])
    grad_pre = skip_grad
    spatial_list = [None, None]
    temporal_list = [None, None]
    mid_rows = [None, None]
    out_rows = [None, None]
    grad_hidden = skip_grad
    for unit_index in (1, 0):
        (
            padded,
            mid_normed,
            mid_standard,
            mid_inverse,
            frames_padded,
            pre_act,
            out_standard,
            out_inverse,
        ) = kept_state[unit_index]
        if unit_index == 0:
            grad_pre = grad_hidden * validity * silu_slope(pre_act)
        grad_temporal, out_gain_grad, out_bias_grad = normalize_back(
            grad_pre, out_standard, out_inverse, out_norm[2 * unit_index], total_valid, validity
        )
        grad_full = lax.all_gather(grad_temporal.astype(jnp.bfloat16), "chan", axis=1, tiled=True)
        temporal_grad, grad_mid = temporal_grads(frames_padded, temporal_all[unit_index], grad_full)
        grad_mid_normed = grad_mid * validity * silu_slope(mid_normed)
        grad_spatial, mid_gain_grad, mid_bias_grad = normalize_back(
            grad_mid_normed,
            mid_standard,
            mid_inverse,
            mid_norm[2 * unit_index],
            total_valid,
            validity,
        )
        spatial_grad, grad_in_part = spatial_grads(
            padded, spatial_taps[unit_index], grad_spatial.astype(jnp.bfloat16)
        )
        grad_hidden = lax.psum_scatter(
            grad_in_part.astype(jnp.bfloat16), "chan", scatter_dimension=1, tiled=True
        ).astype(jnp.float32)
        spatial_list[unit_index] = spatial_grad
        temporal_list[unit_index] = temporal_grad
        mid_rows[unit_index] = (mid_gain_grad, mid_bias_grad)
        out_rows[unit_index] = (out_gain_grad, out_bias_grad)
    input_grad = grad_hidden + skip_grad
    spatial_sum, temporal_sum = (
        lax.psum_scatter(jnp.stack(spatial_list), "dp", scatter_dimension=1, tiled=True),
        lax.psum_scatter(jnp.stack(temporal_list), "dp", scatter_dimension=3, tiled=True),
    )
    mid_grad = jnp.stack([mid_rows[0][0], mid_rows[0][1], mid_rows[1][0], mid_rows[1][1]])
    out_grad = jnp.stack([out_rows[0][0], out_rows[0][1], out_rows[1][0], out_rows[1][1]])
    spatial_new, spatial_one, spatial_two = adam_update(
        spatial_master, spatial_first, spatial_second, spatial_sum, RATE_CONV, DECAY_CONV
    )
    temporal_new, temporal_one, temporal_two = adam_update(
        temporal_master, temporal_first, temporal_second, temporal_sum, RATE_CONV, DECAY_CONV
    )
    mid_new, mid_one, mid_two = adam_update(
        mid_norm, mid_first, mid_second, mid_grad, RATE_NORM, 0.0
    )
    out_new, out_one, out_two = adam_update(
        out_norm, out_first, out_second, out_grad, RATE_NORM, 0.0
    )
    return (
        block_out,
        clip_pool,
        input_grad,
        spatial_new,
        spatial_one,
        spatial_two,
        temporal_new,
        temporal_one,
        temporal_two,
        mid_new,
        mid_one,
        mid_two,
        out_new,
        out_one,
        out_two,
    )


F32 = jnp.float32
BF16 = jnp.bfloat16
MESH = pl.DeviceIdType.MESH
VMEM = pltpu.VMEM
NN = (((1,), (0,)), ((), ()))
NT = (((1,), (1,)), ((), ()))
TN = (((0,), (0,)), ((), ()))
BLOCK_C = 512
MID_C = 1152
THIRD = MID_C // 3
ROWS = 784
SLOTS = 16
SHUFFLE_C = 896
HALF = 144
SUB = 48
TAPS_C = 9 * BLOCK_C
CHIP_S = TAPS_C // 4
CHIP_T = BLOCK_C // 4
CHUNKS = (
    ("s", 0, 0, 1),
    ("s", 0, 1, 1),
    ("s", 0, 2, 1),
    ("t", 0, 0, 9),
    ("s", 1, 0, 1),
    ("s", 1, 1, 1),
    ("s", 1, 2, 1),
    ("t", 1, 0, 9),
)
N_CHUNKS = len(CHUNKS)
NEAR = ("chip", "chip_x", "chip_y", "chip_d")
PARTS = (("s", 0), ("t", 0), ("s", 1), ("t", 1))
GRANT = 65000 * 1024


def place():
    dp = lax.axis_index("dp")
    line = lax.axis_index("chan")
    core = lax.rem(dp, 2)
    chip = lax.div(dp, 2)
    x_bit = lax.rem(chip, 2)
    y_bit = lax.div(chip, 2)
    return dict(
        dp=dp,
        line=line,
        core=core,
        chip=chip,
        chip_x=chip + 1 - 2 * x_bit,
        chip_y=chip + 2 - 4 * y_bit,
        chip_d=3 - chip,
        pair=(dp + 1 - 2 * core, line),
        x=(dp + 2 - 4 * x_bit, line),
        y=(dp + 4 - 8 * y_bit, line),
    )


def remote(source, target, send, recv, device):
    return pltpu.make_async_remote_copy(
        src_ref=source,
        dst_ref=target,
        send_sem=send,
        recv_sem=recv,
        device_id=device,
        device_id_type=MESH,
    )


def greet(devices):
    barrier = pltpu.get_barrier_semaphore()
    for device in devices:
        pl.semaphore_signal(barrier, inc=1, device_id=device, device_id_type=MESH)
    pl.semaphore_wait(barrier, len(devices))


def line_peer(at, step):
    return (at["dp"], lax.rem(at["line"] + step, 4))


def ring_peer(at, step):
    return (lax.rem(at["dp"] + step, 8), at["line"])


def greet_all(at):
    greet(
        [ring_peer(at, step) for step in range(1, 8)]
        + [line_peer(at, step) for step in (1, 2, 3)]
    )


def rows_of(pixel):
    return pl.ds(pl.multiple_of(pixel * SLOTS, SLOTS), SLOTS)


def slope_of(values):
    sigmoid = jax.nn.sigmoid(values)
    return sigmoid * (1.0 + values * (1.0 - sigmoid))


def over_pixels(body, carry):
    return lax.fori_loop(0, HW, body, carry, unroll=7)


def exchange(at, land, land_two, index, sems, sem_index, payload, combine, hooks=(None, None)):
    dp, line = at["dp"], at["line"]
    one_send, one_recv, two_send, two_recv = sems
    rows = pl.ds(0, 2)
    for row, value in enumerate(payload):
        land[index, dp, row : row + 1, :] = value
    sent = []
    for step in range(1, 8):
        here = land.at[index, dp, rows]
        copy = remote(
            here,
            here,
            one_send.at[sem_index, step - 1],
            one_recv.at[sem_index, step - 1],
            ring_peer(at, step),
        )
        copy.start()
        sent.append(copy)
    if hooks[0] is not None:
        hooks[0]()
    for step in range(1, 8):
        there = land.at[index, lax.rem(dp + 8 - step, 8), rows]
        remote(
            there,
            there,
            one_send.at[sem_index, step - 1],
            one_recv.at[sem_index, step - 1],
            ring_peer(at, step),
        ).wait_recv()
    merged = combine([land[index, source] for source in range(8)])
    for row, value in enumerate(merged):
        land_two[index, line, row : row + 1, :] = value
    for step in (1, 2, 3):
        here = land_two.at[index, line, rows]
        copy = remote(
            here,
            here,
            two_send.at[sem_index, step - 1],
            two_recv.at[sem_index, step - 1],
            line_peer(at, step),
        )
        copy.start()
        sent.append(copy)
    if hooks[1] is not None:
        hooks[1]()
    for step in (1, 2, 3):
        there = land_two.at[index, lax.rem(line + 4 - step, 4), rows]
        remote(
            there,
            there,
            two_send.at[sem_index, step - 1],
            two_recv.at[sem_index, step - 1],
            line_peer(at, step),
        ).wait_recv()
    merged = combine([land_two[index, source] for source in range(4)])
    for copy in sent:
        copy.wait_send()
    return merged


def combine_sums(blocks):
    total = sum(blocks[1:], blocks[0])
    return [total[0:1], total[1:2]]


def forward_kernel(
    ws_wide,
    wt_wide,
    feat_in,
    cot_wide,
    mid_own,
    out_own,
    frames_in,
    shuffle,
    ws_out,
    wt_out,
    par_out,
    mask_in,
    block_out,
    a_out,
    s_out,
    u_out,
    t_out,
    skip_out,
    stat_mid,
    stat_out,
    ws_in,
    wt_in,
    cot_raw,
    cot_in,
    par_in,
    pair_s,
    pair_t,
    stage_s,
    stage_t,
    feat_land,
    cot_land,
    par_land,
    a_pad,
    s_ref,
    x_ref,
    u_ref,
    t_ref,
    side,
    feat_ref,
    thin,
    w_buf,
    wt_buf,
    land_mid,
    land_mid_two,
    land_out,
    land_out_two,
    land_count,
    count_one,
    count_two,
    pair_send,
    pair_recv,
    act_send,
    act_recv,
    line_send,
    line_recv,
    plane_send,
    plane_recv,
    diag_send,
    diag_recv,
    core_send,
    core_recv,
    own_sem,
    chunk_sem,
    w_sem,
    wt_sem,
    save_sem,
    one_send,
    one_recv,
    two_send,
    two_recv,
):
    at = place()
    line, core, chip = at["line"], at["core"], at["chip"]
    sems = (one_send, one_recv, two_send, two_recv)
    cot_load = pltpu.make_async_copy(cot_wide, cot_raw, wt_sem.at[4])
    cot_load.start()
    for unit in range(2):
        ws_in[unit] = ws_wide[unit].astype(BF16)
        for tau in range(3):
            wt_in[unit, :, 64 * tau : 64 * tau + 64] = wt_wide[unit, tau].T.astype(BF16)
    pieces = []
    blank = jnp.zeros((4, THIRD - 2 * SUB), F32)
    for third in range(3):
        for half in range(2):
            first = half * HALF + third * SUB
            pieces.append(mid_own[:, first : first + SUB])
        pieces.append(blank)
    par_in[...] = jnp.zeros(par_in.shape, F32)
    wide_rows = jnp.concatenate(
        [jnp.concatenate(pieces, axis=1), jnp.zeros((4, MID_C), F32)], axis=0
    )
    par_in[0:4, :] = pltpu.roll(wide_rows, line * (2 * SUB), 1)[0:4]
    par_in[4:8, pl.ds(pl.multiple_of(line * 128, 128), 128)] = out_own[...]
    row_ids = lax.broadcasted_iota(jnp.int32, (SLOTS, MID_C), 0)
    mask = jnp.zeros((SLOTS, MID_C), F32)
    for clip in range(4):
        kept = lax.div(frames_in[4 * line + clip], 8)
        here = jnp.logical_and(row_ids % 4 == clip, row_ids // 4 < kept)
        mask = jnp.where(here, 1.0, mask)
    mask_in[...] = mask
    count_rows = lax.broadcasted_iota(jnp.int32, (8, 128), 0)
    count_tile = jnp.zeros((8, 128), F32)
    for owner in range(4):
        frames = lax.div(frames_in[4 * owner], 8)
        for clip in range(1, 4):
            frames = frames + lax.div(frames_in[4 * owner + clip], 8)
        count_tile = jnp.where(count_rows == owner, (HW * frames).astype(F32), count_tile)
    land_count[at["dp"]] = count_tile
    greet_all(at)
    started = []

    def send(copy):
        copy.start()
        started.append(copy)
        return copy

    def area(chunk, owner_core, owner_chip, first, count):
        kind, unit, lead, leads = chunk
        ref, width = (ws_out, CHIP_S) if kind == "s" else (wt_out, CHIP_T)
        lanes = pl.ds(pl.multiple_of(owner_chip * width, 128), width)
        return ref.at[unit, pl.ds(lead, leads), pl.ds(first, count), owner_core, :, lanes]

    pairs = {}
    for index, (kind, unit) in enumerate(PARTS):
        theirs = pl.ds(pl.multiple_of((1 - core) * HALF, 16), HALF)
        source, landing = (ws_in, pair_s) if kind == "s" else (wt_in, pair_t)
        pairs[kind, unit] = send(
            remote(
                source.at[unit, theirs],
                landing.at[unit],
                pair_send.at[index],
                pair_recv.at[index],
                at["pair"],
            )
        )

    def acts(row, source, target):
        def cut(owner):
            return source.at[pl.ds(pl.multiple_of(owner * ROWS, 16), ROWS)]

        lanes = pl.ds(pl.multiple_of(line * 128, 128), 128)
        for step in (1, 2, 3):
            peer = line_peer(at, step)
            send(
                remote(
                    cut(peer[1]),
                    target.at[:, lanes],
                    act_send.at[row, step - 1],
                    act_recv.at[row, step - 1],
                    peer,
                )
            )
        own = pltpu.make_async_copy(cut(line), target.at[:, lanes], own_sem.at[row])
        own.start()
        return own

    def acts_wait(row, source, target, own):
        for step in (1, 2, 3):
            origin = lax.rem(line + 4 - step, 4)
            lanes = pl.ds(pl.multiple_of(origin * 128, 128), 128)
            remote(
                source.at[pl.ds(0, ROWS)],
                target.at[:, lanes],
                act_send.at[row, step - 1],
                act_recv.at[row, step - 1],
                line_peer(at, step),
            ).wait_recv()
        own.wait()

    mine = pl.ds(pl.multiple_of(core * HALF, 16), HALF)

    def merge(kind, unit):
        pairs[kind, unit].wait_recv()
        source, landing = (ws_in, pair_s) if kind == "s" else (wt_in, pair_t)
        low = source[unit, mine].astype(F32)
        high = landing[unit].astype(F32)
        first = jnp.where(core == 0, low, high)
        second = jnp.where(core == 0, high, low)
        if kind == "s":
            both = jnp.concatenate([first, second], axis=1).astype(BF16)
            stage_s[unit] = both.reshape(3, 1, SUB, CHIP_S)
        else:
            for tau in range(3):
                lanes = slice(64 * tau, 64 * tau + 64)
                both = jnp.concatenate([first[:, lanes], second[:, lanes]], axis=1).astype(BF16)
                stage_t[unit, 3 * tau : 3 * tau + 3] = both.reshape(3, 1, SUB, CHIP_T)

    own_copies = [None] * N_CHUNKS

    def step_line(index):
        chunk = CHUNKS[index]
        kind, unit, lead, leads = chunk
        if lead == 0:
            merge(kind, unit)
        staged = (stage_s if kind == "s" else stage_t).at[unit, pl.ds(lead, leads)]
        target = area(chunk, core, chip, line, 1)
        for step in (1, 3, 2):
            send(
                remote(
                    staged,
                    target,
                    line_send.at[index, step - 1],
                    line_recv.at[index, step - 1],
                    line_peer(at, step),
                )
            )
        own = pltpu.make_async_copy(staged, target, chunk_sem.at[index])
        own.start()
        own_copies[index] = own

    def step_plane(index):
        chunk = CHUNKS[index]
        for step in (1, 2, 3):
            origin = area(chunk, core, chip, lax.rem(line + 4 - step, 4), 1)
            remote(
                origin,
                origin,
                line_send.at[index, step - 1],
                line_recv.at[index, step - 1],
                line_peer(at, step),
            ).wait_recv()
        own_copies[index].wait()
        for turn in range(2):
            for way, name in enumerate(("x", "y")):
                half = area(chunk, core, chip, 2 * (way ^ turn), 2)
                send(
                    remote(
                        half,
                        half,
                        plane_send.at[index, way, turn],
                        plane_recv.at[index, way, turn],
                        at[name],
                    )
                )
        held = area(chunk, core, chip, 0, 4)
        send(remote(held, held, core_send.at[index, 0], core_recv.at[index, 0], at["pair"]))

    def plane_wait(index, way, turn, name):
        half = area(CHUNKS[index], core, at["chip_" + name], 2 * (way ^ turn), 2)
        remote(
            half,
            half,
            plane_send.at[index, way, turn],
            plane_recv.at[index, way, turn],
            at[name],
        ).wait_recv()
        return half

    def step_diag(index):
        for way, (name, other) in enumerate((("x", "y"), ("y", "x"))):
            half = plane_wait(index, way, 0, name)
            send(
                remote(half, half, diag_send.at[index, way], diag_recv.at[index, way], at[other])
            )

    def step_core(index):
        chunk = CHUNKS[index]
        for way, name in enumerate(("x", "y")):
            plane_wait(index, way, 1, name)
            held = area(chunk, core, at["chip_" + name], 0, 4)
            send(
                remote(
                    held, held, core_send.at[index, 1 + way], core_recv.at[index, 1 + way], at["pair"]
                )
            )
        for slot, name in enumerate(NEAR[:3]):
            core_wait(index, slot, name)
        for way, (other, first) in enumerate((("y", 0), ("x", 2))):
            half = area(chunk, core, at["chip_d"], first, 2)
            remote(
                half, half, diag_send.at[index, way], diag_recv.at[index, way], at[other]
            ).wait_recv()
        held = area(chunk, core, at["chip_d"], 0, 4)
        send(remote(held, held, core_send.at[index, 3], core_recv.at[index, 3], at["pair"]))
        core_wait(index, 3, NEAR[3])

    def core_wait(index, slot, name):
        held = area(CHUNKS[index], 1 - core, at[name], 0, 4)
        remote(
            held, held, core_send.at[index, slot], core_recv.at[index, slot], at["pair"]
        ).wait_recv()
        fetch(index, slot, name).start()

    def fetch(index, slot, name):
        kind, unit, lead, _ = CHUNKS[index]
        if kind == "s":
            turn = (3 * unit + lead) % 2
            lanes = pl.ds(pl.multiple_of(at[name] * CHIP_S, 128), CHIP_S)
            return pltpu.make_async_copy(
                ws_out.at[unit, lead, :, :, :, lanes],
                w_buf.at[turn, :, :, :, lanes],
                w_sem.at[turn, slot],
            )
        lanes = pl.ds(pl.multiple_of(at[name] * CHIP_T, 128), CHIP_T)
        return pltpu.make_async_copy(
            wt_out.at[unit, :, :, :, :, lanes], wt_buf.at[:, :, :, :, lanes], wt_sem.at[slot]
        )

    def fetch_wait(index):
        for slot, name in enumerate(NEAR):
            fetch(index, slot, name).wait()

    def window(unit, tap):
        row, column = tap // 3, tap % 3
        return a_pad[unit, row : row + SIDE, column : column + SIDE].reshape(ROWS, BLOCK_C)

    def conv(unit, third):
        fetch_wait(4 * unit + third)
        taps = jnp.concatenate([window(unit, tap) for tap in range(9)], axis=1)
        s_ref[:, third * THIRD : (third + 1) * THIRD] = lax.dot_general(
            taps,
            w_buf[(3 * unit + third) % 2].reshape(THIRD, TAPS_C),
            NT,
            preferred_element_type=F32,
        )

    mask_mid = mask_in[...]
    mask_out = mask_in[:, :BLOCK_C]
    slot_rows = lax.broadcasted_iota(jnp.int32, (SLOTS, BLOCK_C), 0)
    has_before = (slot_rows >= 4).astype(F32)
    has_after = (slot_rows < 12).astype(F32)

    def moments(values, mask, land, land_two, index, sem_index, hooks):
        zero = jnp.zeros(mask.shape, F32)
        width = mask.shape[1]
        local = local_count[:, :width]
        added = over_pixels(lambda p, acc: acc + values[rows_of(p), :], zero)
        mean = jnp.sum(added * mask, axis=0, keepdims=True) / local

        def squares(p, acc):
            centered = values[rows_of(p), :] - mean
            return acc + centered * centered

        spread = jnp.sum(over_pixels(squares, zero) * mask, axis=0, keepdims=True)
        def combine(blocks):
            known = count_one if len(blocks) == 8 else count_two
            counts = [known[source, :, :width] for source in range(len(blocks))]
            pivot = blocks[0]
            drifts = [block - pivot for block in blocks[1:]]
            shift = sum(count * drift for count, drift in zip(counts[1:], drifts))[0:1]
            squared = sum(count * drift * drift for count, drift in zip(counts[1:], drifts))[0:1]
            inner = sum(blocks[1:], pivot)[1:2]
            total = sum(counts[1:], counts[0])[0:1]
            return [pivot[0:1] + shift / total, inner + squared - shift * shift / total]

        mean, spread = exchange(
            at, land, land_two, index, sems, sem_index, [mean, spread], combine, hooks
        )
        total = all_count[:, :width]
        return mean, lax.rsqrt(spread / total + EPS_NORM), total

    saves = []

    def save(source, target):
        copy = pltpu.make_async_copy(source, target, save_sem.at[len(saves)])
        copy.start()
        saves.append(copy)

    def mid_norm_act(unit, *hooks):
        gain = par_out[2 * unit : 2 * unit + 1]
        bias = par_out[2 * unit + 1 : 2 * unit + 2]
        mean, inverse, total = moments(
            s_ref, mask_mid, land_mid, land_mid_two, unit, 2 * unit, hooks
        )
        stat_mid[2 * unit : 2 * unit + 1] = inverse
        stat_mid[2 * unit + 1 : 2 * unit + 2] = total

        def mid_act(p, carry):
            rows = rows_of(p)
            standard = (s_ref[rows, :] - mean) * inverse
            x_ref[unit, rows, :] = standard.astype(BF16)
            normed = standard * gain + bias
            u_ref[unit, rows, :] = (jax.nn.sigmoid(normed) * normed * mask_mid).astype(BF16)
            return carry

        over_pixels(mid_act, 0)
        save(x_ref.at[unit], s_out.at[unit])
        save(u_ref.at[unit], u_out.at[unit])

    def temporal(unit):
        fetch_wait(4 * unit + 3)

        def weight(tau):
            return wt_buf[3 * tau : 3 * tau + 3].reshape(MID_C, BLOCK_C)

        t_ref[unit] = lax.dot_general(u_ref[unit], weight(1), NN, preferred_element_type=F32)
        side[0] = lax.dot_general(u_ref[unit], weight(0), NN, preferred_element_type=F32)
        side[1] = lax.dot_general(u_ref[unit], weight(2), NN, preferred_element_type=F32)

        def frames(p, carry):
            rows = rows_of(p)
            t_ref[unit, rows, :] = (
                t_ref[unit, rows, :]
                + pltpu.roll(side[0, rows, :], 4, 0) * has_before
                + pltpu.roll(side[1, rows, :], 12, 0) * has_after
            )
            return carry

        over_pixels(frames, 0)

    def out_stats(unit, *hooks):
        mean, inverse, total = moments(
            t_ref.at[unit], mask_out, land_out, land_out_two, unit, 2 * unit + 1, hooks
        )
        stat_out[2 * unit : 2 * unit + 1] = inverse
        stat_out[2 * unit + 1 : 2 * unit + 2] = total
        gain = par_out[4 + 2 * unit : 5 + 2 * unit, :BLOCK_C]
        bias = par_out[5 + 2 * unit : 6 + 2 * unit, :BLOCK_C]
        return mean, inverse, gain, bias

    for step in range(1, 8):
        here = land_count.at[at["dp"]]
        send(
            remote(
                here,
                here,
                one_send.at[4, step - 1],
                one_recv.at[4, step - 1],
                ring_peer(at, step),
            )
        )
    step_line(0)
    for step in (1, 2, 3):
        send(
            remote(
                par_in,
                par_land.at[line],
                act_send.at[2, step - 1],
                act_recv.at[2, step - 1],
                line_peer(at, step),
            )
        )
    par_own = pltpu.make_async_copy(par_in, par_land.at[line], own_sem.at[2])
    par_own.start()
    step_line(1)
    for unit in range(2):
        a_pad[unit] = jnp.zeros(a_pad.shape[1:], BF16)
    step_plane(0)
    step_line(2)
    step_diag(0)
    step_plane(1)
    feat_own = acts(0, feat_in, feat_land)
    cot_load.wait()
    cot_in[...] = cot_raw[...].astype(BF16)
    for step in range(1, 8):
        there = land_count.at[lax.rem(at["dp"] + 8 - step, 8)]
        remote(
            there,
            there,
            one_send.at[4, step - 1],
            one_recv.at[4, step - 1],
            ring_peer(at, step),
        ).wait_recv()

    def widen(row, rows):
        return jnp.concatenate([jnp.broadcast_to(row, (rows, 128))] * (MID_C // 128), axis=1)

    def pick(tile):
        return jnp.sum(jnp.where(count_rows == line, tile, 0.0), axis=0, keepdims=True)

    sum_tile = land_count[0]
    for source in range(8):
        count_one[source] = widen(pick(land_count[source]), 8)
        if source > 0:
            sum_tile = sum_tile + land_count[source]
    for source in range(4):
        count_two[source] = widen(sum_tile[source : source + 1], 8)
    local_count = widen(pick(count_tile), 1)
    all_count = widen(jnp.sum(sum_tile[0:4], axis=0, keepdims=True), 1)
    step_plane(2)
    step_line(3)
    step_diag(1)
    step_core(0)
    permute = shuffle[:, :ROWS]
    acts_wait(0, feat_in, feat_land, feat_own)
    feat_ref[...] = lax.dot_general(permute, feat_land[...], NN, preferred_element_type=F32).astype(
        BF16
    )

    def fill(p, carry):
        a_pad[0, 1 + p // SIDE, 1 + p % SIDE] = feat_ref[rows_of(p), :]
        return carry

    over_pixels(fill, 0)
    save(a_pad.at[0], a_out.at[0])
    step_line(4)
    step_diag(2)
    step_core(1)
    conv(0, 0)
    step_core(2)
    conv(0, 1)
    step_plane(3)
    conv(0, 2)
    for step in (1, 2, 3):
        remote(
            par_in,
            par_land.at[lax.rem(line + 4 - step, 4)],
            act_send.at[2, step - 1],
            act_recv.at[2, step - 1],
            line_peer(at, step),
        ).wait_recv()
    par_own.wait()
    par_out[...] = par_land[0] + par_land[1] + par_land[2] + par_land[3]

    def hook_a():
        step_diag(3)
        step_plane(4)

    def hook_e():
        step_line(5)
        step_core(3)

    mid_norm_act(0, hook_a, hook_e)
    temporal(0)
    cot_own = []

    def hook_b():
        step_diag(4)
        step_plane(5)

    def hook_c():
        step_line(6)
        step_line(7)
        cot_own.append(acts(1, cot_in, cot_land))
        step_core(4)

    mean, inverse, gain, bias = out_stats(0, hook_b, hook_c)

    def out_act(p, carry):
        rows = rows_of(p)
        standard = (t_ref[0, rows, :] - mean) * inverse
        t_ref[0, rows, :] = standard
        normed = standard * gain + bias
        hidden = jax.nn.sigmoid(normed) * normed * mask_out
        a_pad[1, 1 + p // SIDE, 1 + p % SIDE] = hidden.astype(BF16)
        return carry

    over_pixels(out_act, 0)
    save(t_ref.at[0], t_out.at[0])
    save(a_pad.at[1], a_out.at[1])
    conv(1, 0)
    step_diag(5)
    step_plane(6)
    step_core(5)
    conv(1, 1)
    step_diag(6)
    step_plane(7)
    step_core(6)
    conv(1, 2)
    mid_norm_act(1, lambda: step_diag(7), lambda: step_core(7))
    temporal(1)

    def hook_d():
        acts_wait(1, cot_in, cot_land, cot_own[0])
        side[0] = lax.dot_general(permute, cot_land[...], NN, preferred_element_type=F32)

    mean_one, inverse_one, gain_one, bias_one = out_stats(1, hook_d, None)

    def end_act(p, carry):
        rows = rows_of(p)
        standard = (t_ref[1, rows, :] - mean_one) * inverse_one
        t_ref[1, rows, :] = standard
        pre = standard * gain_one + bias_one + feat_ref[rows, :].astype(F32)
        sigmoid = jax.nn.sigmoid(pre)
        thin[rows, :] = (pre * sigmoid * mask_out).astype(BF16)
        slope = sigmoid * (1.0 + pre * (1.0 - sigmoid))
        cot_land[rows, :] = (side[0, rows, :] * mask_out * slope).astype(BF16)
        return carry

    over_pixels(end_act, 0)
    save(t_ref.at[1], t_out.at[1])
    save(cot_land, skip_out)
    block_out[...] = lax.dot_general(permute, thin[...], TN, preferred_element_type=F32).astype(
        BF16
    )
    for copy in saves:
        copy.wait()
    for copy in started:
        copy.wait_send()


def backward_kernel(
    ws,
    wt,
    a_in,
    s_in,
    u_in,
    t_in,
    skip_in,
    stat_mid,
    stat_out,
    par,
    mask_in,
    shuffle,
    block_in,
    sp_in,
    sm_in,
    sv_in,
    tp_in,
    tm_in,
    tv_in,
    sp_out,
    sm_out,
    sv_out,
    tp_out,
    tm_out,
    tv_out,
    mid_grad,
    out_grad,
    block_out,
    input_out,
    a_pad,
    s_ref,
    u_ref,
    t_ref,
    side,
    skip_ref,
    wide,
    ds_pad,
    d_ref,
    w_buf,
    land_mid,
    land_mid_two,
    land_out,
    land_out_two,
    g_s,
    g_t,
    land_s,
    land_t,
    one_s,
    one_t,
    two_s,
    two_t,
    line_s,
    line_t,
    fin_s,
    fin_t,
    adam_s,
    adam_t,
    load_sem,
    w_sem,
    ex_one_send,
    ex_one_recv,
    ex_two_send,
    ex_two_recv,
    act_send,
    act_recv,
    act_sem,
    pair_send,
    pair_recv,
    one_send,
    one_recv,
    two_send,
    two_recv,
    line_send,
    line_recv,
    fin_send,
    fin_recv,
    adam_load,
    adam_save,
):
    at = place()
    line, core, chip = at["line"], at["core"], at["chip"]
    sems = (ex_one_send, ex_one_recv, ex_two_send, ex_two_recv)

    def load(index, source, target):
        return pltpu.make_async_copy(source, target, load_sem.at[index])

    load_t = [load(0, t_in.at[unit], t_ref) for unit in range(2)]
    load_u = [load(1, u_in.at[unit], u_ref) for unit in range(2)]
    load_s = [load(2, s_in.at[unit], s_ref) for unit in range(2)]
    load_a = [load(3, a_in.at[unit], a_pad) for unit in range(2)]
    load_skip = load(4, skip_in, skip_ref)
    load_shuffle = load(5, shuffle, u_ref.at[:, pl.ds(0, SHUFFLE_C)])
    load_t[1].start()
    load_skip.start()
    load_u[1].start()
    load_s[1].start()
    load_a[1].start()
    greet_all(at)
    ds_pad[...] = jnp.zeros(ds_pad.shape, BF16)

    mask_mid = mask_in[...]
    mask_out = mask_in[:, :BLOCK_C]
    slot_rows = lax.broadcasted_iota(jnp.int32, (SLOTS, BLOCK_C), 0)
    has_before = (slot_rows >= 4).astype(F32)
    has_after = (slot_rows < 12).astype(F32)
    lanes_line = pl.ds(pl.multiple_of(line * 128, 128), 128)
    rows_line = pl.ds(pl.multiple_of(line * ROWS, 16), ROWS)

    act_copies = []

    def acts(row, source, target):
        for step in (1, 2, 3):
            peer = line_peer(at, step)
            copy = remote(
                source.at[:, pl.ds(pl.multiple_of(peer[1] * 128, 128), 128)],
                target.at[rows_line],
                act_send.at[row, step - 1],
                act_recv.at[row, step - 1],
                peer,
            )
            copy.start()
            act_copies.append(copy)
        own = pltpu.make_async_copy(source.at[:, lanes_line], target.at[rows_line], act_sem.at[row])
        own.start()
        return own

    def acts_wait(row, source, target, own):
        for step in (1, 2, 3):
            origin = lax.rem(line + 4 - step, 4)
            remote(
                source.at[:, lanes_line],
                target.at[pl.ds(pl.multiple_of(origin * ROWS, 16), ROWS)],
                act_send.at[row, step - 1],
                act_recv.at[row, step - 1],
                line_peer(at, step),
            ).wait_recv()
        own.wait()

    flying = [[] for _ in CHUNKS]
    pair_copies = [None] * N_CHUNKS
    fin_copies = [None] * N_CHUNKS

    def launch(index, copy):
        copy.start()
        flying[index].append(copy)
        return copy

    def drain(index):
        for copy in flying[index]:
            copy.wait_send()
        flying[index] = []

    def grad_of(index):
        kind, _, lead, _ = CHUNKS[index]
        return g_s.at[lead] if kind == "s" else g_t

    def land_of(index):
        kind, _, lead, _ = CHUNKS[index]
        return land_s.at[lead] if kind == "s" else land_t

    def held(index, small, large):
        kind, unit, lead, _ = CHUNKS[index]
        return large.at[unit, lead] if kind == "s" else small.at[unit]

    def cut(index, owner, first, count):
        width = CHIP_S if CHUNKS[index][0] == "s" else CHIP_T
        lanes = pl.ds(pl.multiple_of(owner * width, 128), width)
        return grad_of(index).at[:, pl.ds(first, count), core, :, lanes]

    def add_into(target, source):
        leads, count, _, width = target.shape

        def body(turn, carry):
            if leads == 1 and width > 2048:
                where = (0, lax.div(turn, 3), pl.ds(pl.multiple_of(lax.rem(turn, 3) * 16, 16), 16))
            elif leads == 1:
                where = (0, turn)
            else:
                where = (turn,)
            target[where] = (target[where].astype(F32) + source[where].astype(F32)).astype(BF16)
            return carry

        turns = leads if leads > 1 else count * (3 if width > 2048 else 1)
        lax.fori_loop(0, turns, body, 0)

    def step_pair(index):
        pair_copies[index] = launch(
            index,
            remote(
                grad_of(index).at[:, :, 1 - core],
                land_of(index),
                pair_send.at[index],
                pair_recv.at[index],
                at["pair"],
            ),
        )

    def step_one(index):
        pair_copies[index].wait_recv()
        add_into(grad_of(index).at[:, :, core], land_of(index))
        ones, twos = held(index, one_t, one_s), held(index, two_t, two_s)
        for way, (name, first) in enumerate((("x", 0), ("y", 2))):
            launch(
                index,
                remote(
                    cut(index, at["chip_d"], first, 2),
                    ones.at[way],
                    one_send.at[index, way],
                    one_recv.at[index, way],
                    at[name],
                ),
            )
            launch(
                index,
                remote(
                    cut(index, at["chip_" + name], first, 2),
                    twos.at[way, :, pl.ds(first, 2)],
                    two_send.at[index, way, 0],
                    two_recv.at[index, way, 0],
                    at[name],
                ),
            )

    def step_two(index):
        ones, twos = held(index, one_t, one_s), held(index, two_t, two_s)
        for way, (name, other, first) in enumerate((("x", "y", 0), ("y", "x", 2))):
            landing = ones.at[way]
            remote(
                landing, landing, one_send.at[index, way], one_recv.at[index, way], at[name]
            ).wait_recv()
            target = cut(index, at["chip_" + other], first, 2)
            add_into(target, landing)
            launch(
                index,
                remote(
                    target,
                    twos.at[1 - way, :, pl.ds(first, 2)],
                    two_send.at[index, 1 - way, 1],
                    two_recv.at[index, 1 - way, 1],
                    at[other],
                ),
            )

    def step_three(index):
        twos = held(index, two_t, two_s)
        for way, (name, first) in enumerate((("x", 0), ("y", 2))):
            for turn, begin in enumerate((first, 2 - first)):
                landing = twos.at[way, :, pl.ds(begin, 2)]
                remote(
                    landing,
                    landing,
                    two_send.at[index, way, turn],
                    two_recv.at[index, way, turn],
                    at[name],
                ).wait_recv()
        own = cut(index, chip, 0, 4)
        leads = own.shape[0]

        def body(turn, carry):
            where = (0, turn) if leads == 1 else (turn,)
            own[where] = (
                own[where].astype(F32)
                + twos.at[0][where].astype(F32)
                + twos.at[1][where].astype(F32)
            ).astype(BF16)
            return carry

        lax.fori_loop(0, 4 if leads == 1 else leads, body, 0)
        lines = held(index, line_t, line_s)
        for step in (1, 3, 2):
            peer = line_peer(at, step)
            launch(
                index,
                remote(
                    cut(index, chip, peer[1], 1),
                    lines.at[step - 1],
                    line_send.at[index, step - 1],
                    line_recv.at[index, step - 1],
                    peer,
                ),
            )

    def step_four(index):
        lines, fin = held(index, line_t, line_s), held(index, fin_t, fin_s)
        for step in (1, 2, 3):
            landing = lines.at[step - 1]
            remote(
                landing,
                landing,
                line_send.at[index, step - 1],
                line_recv.at[index, step - 1],
                line_peer(at, step),
            ).wait_recv()
        total = cut(index, chip, line, 1)[...].astype(F32)
        for step in range(3):
            total = total + lines[step].astype(F32)
        fin[0] = total
        fin_copies[index] = launch(
            index,
            remote(fin.at[0], fin.at[1], fin_send.at[index], fin_recv.at[index], at["pair"]),
        )

    adam_saves = {"s": [], "t": []}
    adam_loads = {}

    def adam_moves(index, load):
        kind, unit, lead, _ = CHUNKS[index]
        moves = []
        for which in range(2):
            if kind == "s":
                arrays = (sp_in, sm_in, sv_in) if load else (sp_out, sm_out, sv_out)
                half = core if which == 0 else 1 - core
                rows = pl.ds(pl.multiple_of(half * HALF + SUB * lead, 16), SUB)
                for array, ref in enumerate(arrays):
                    here, there = adam_s.at[array, which], ref.at[unit, rows]
                    moves.append((there, here) if load else (here, there))
            elif which == 0:
                arrays = (tp_in, tm_in, tv_in) if load else (tp_out, tm_out, tv_out)
                for array, ref in enumerate(arrays):
                    here, there = adam_t.at[array], ref.at[unit]
                    moves.append((there, here) if load else (here, there))
        sems = adam_load if load else adam_save
        row = 0 if kind == "s" else 1
        return [
            pltpu.make_async_copy(source, target, sems.at[row, number])
            for number, (source, target) in enumerate(moves)
        ]

    def adam_fetch(index):
        kind = CHUNKS[index][0]
        for copy in adam_saves[kind]:
            copy.wait()
        adam_saves[kind] = []
        adam_loads[index] = adam_moves(index, True)
        for copy in adam_loads[index]:
            copy.start()

    def step_five(index):
        kind, unit, lead, leads = CHUNKS[index]
        adam_fetch(index)
        fin_copies[index].wait_recv()
        fin = held(index, fin_t, fin_s)
        for copy in adam_loads[index]:
            copy.wait()
        if kind == "s":
            width = CHIP_S // 2
            for which in range(2):
                value = fin[which, 0, 0]
                grad = jnp.where(core == 0, value[:, :width], value[:, width:])
                fresh = adam_update(
                    adam_s[0, which],
                    adam_s[1, which],
                    adam_s[2, which],
                    grad,
                    RATE_CONV,
                    DECAY_CONV,
                )
                for array in range(3):
                    adam_s[array, which] = fresh[array]
        else:
            width = CHIP_T // 2
            for tau in range(3):
                both = [
                    fin[which, 3 * tau : 3 * tau + 3].reshape(HALF, CHIP_T) for which in range(2)
                ]
                first = jnp.where(core == 0, both[0], both[1])
                second = jnp.where(core == 0, both[1], both[0])
                turned = jnp.concatenate([first, second], axis=0).T
                grad = jnp.where(core == 0, turned[:width], turned[width:])
                fresh = adam_update(
                    adam_t[0, tau], adam_t[1, tau], adam_t[2, tau], grad, RATE_CONV, DECAY_CONV
                )
                for array in range(3):
                    adam_t[array, tau] = fresh[array]
        adam_saves[kind] = adam_moves(index, False)
        for copy in adam_saves[kind]:
            copy.start()

    def fetch_w(unit, tap, slot):
        lanes = pl.ds(pl.multiple_of(tap * BLOCK_C, 128), BLOCK_C)
        return pltpu.make_async_copy(ws.at[unit, :, lanes], w_buf.at[slot], w_sem.at[slot])

    def fetch_wt(unit, tau, slot):
        return pltpu.make_async_copy(wt.at[unit, tau], w_buf.at[slot], w_sem.at[slot])

    def window(tap):
        return a_pad[pl.ds(tap // 3, SIDE), pl.ds(tap % 3, SIDE)].reshape(ROWS, BLOCK_C)

    zero_mid = jnp.zeros((SLOTS, MID_C), F32)
    zero_out = jnp.zeros((SLOTS, BLOCK_C), F32)

    def out_norm_back(unit, *hooks):
        grad_ref = skip_ref if unit == 1 else side
        gain = par[4 + 2 * unit : 5 + 2 * unit, :BLOCK_C]
        inverse = stat_out[2 * unit : 2 * unit + 1]
        total = stat_out[2 * unit + 1 : 2 * unit + 2]

        def out_sums(p, carry):
            rows = rows_of(p)
            grad = grad_ref[rows, :].astype(F32)
            return (carry[0] + grad, carry[1] + grad * t_ref[rows, :])

        bias_acc, gain_acc = over_pixels(out_sums, (zero_out, zero_out))
        sums = [
            jnp.sum(bias_acc, axis=0, keepdims=True),
            jnp.sum(gain_acc, axis=0, keepdims=True),
        ]
        grad_bias, grad_gain = exchange(
            at, land_out, land_out_two, unit, sems, 2 * unit, sums, combine_sums, hooks
        )
        out_grad[2 * unit : 2 * unit + 1, :] = grad_gain
        out_grad[2 * unit + 1 : 2 * unit + 2, :] = grad_bias
        scale = gain * inverse
        bias_part, gain_part = grad_bias / total, grad_gain / total

        def out_back(p, carry):
            rows = rows_of(p)
            value = (
                mask_out
                * scale
                * (grad_ref[rows, :].astype(F32) - bias_part - t_ref[rows, :] * gain_part)
            )
            d_ref[1, rows, :] = value.astype(BF16)
            d_ref[0, rows, :] = (pltpu.roll(value, 12, 0) * has_after).astype(BF16)
            d_ref[2, rows, :] = (pltpu.roll(value, 4, 0) * has_before).astype(BF16)
            return carry

        over_pixels(out_back, 0)

    def temporal_grad():
        for tau in range(3):
            g_t[3 * tau : 3 * tau + 3] = (
                lax.dot_general(u_ref[...], d_ref[tau], TN, preferred_element_type=F32)
                .astype(BF16)
                .reshape(3, 4, 2, SUB, BLOCK_C)
            )

    def temporal_back(unit):
        for tau in range(3):
            slot = tau % 2
            if tau < 2:
                fetch_wt(unit, tau + 1, 1 - slot).start()
            fetch_wt(unit, tau, slot).wait()
            value = lax.dot_general(d_ref[tau], w_buf[slot], NT, preferred_element_type=F32)
            wide[...] = value if tau == 0 else wide[...] + value

    def mid_norm_back(unit, *hooks):
        gain = par[2 * unit : 2 * unit + 1]
        bias = par[2 * unit + 1 : 2 * unit + 2]
        inverse = stat_mid[2 * unit : 2 * unit + 1]
        total = stat_mid[2 * unit + 1 : 2 * unit + 2]

        def mid_sums(p, carry):
            rows = rows_of(p)
            standard = s_ref[rows, :].astype(F32)
            grad = mask_mid * slope_of(standard * gain + bias) * wide[rows, :]
            wide[rows, :] = grad
            return (carry[0] + grad, carry[1] + grad * standard)

        bias_acc, gain_acc = over_pixels(mid_sums, (zero_mid, zero_mid))
        sums = [
            jnp.sum(bias_acc, axis=0, keepdims=True),
            jnp.sum(gain_acc, axis=0, keepdims=True),
        ]
        grad_bias, grad_gain = exchange(
            at, land_mid, land_mid_two, unit, sems, 2 * unit + 1, sums, combine_sums, hooks
        )
        mid_grad[2 * unit : 2 * unit + 1, :] = grad_gain
        mid_grad[2 * unit + 1 : 2 * unit + 2, :] = grad_bias
        scale = gain * inverse
        bias_part, gain_part = grad_bias / total, grad_gain / total

        def mid_back(p, carry):
            rows = rows_of(p)
            value = (
                mask_mid
                * scale
                * (wide[rows, :] - bias_part - s_ref[rows, :].astype(F32) * gain_part)
            )
            ds_pad[1 + p // SIDE, 1 + p % SIDE] = value.astype(BF16)
            return carry

        over_pixels(mid_back, 0)

    def spatial_grad(third):
        columns = slice(third * THIRD, (third + 1) * THIRD)

        def body(row, carry):
            inner = ds_pad[1 : 1 + SIDE, 1 : 1 + SIDE, :, columns].reshape(ROWS, THIRD)
            taps = jnp.concatenate([window(3 * row + column) for column in range(3)], axis=1)
            lanes = pl.ds(pl.multiple_of(row * 3 * BLOCK_C, 128), 3 * BLOCK_C)
            g_s[third, 0, :, :, :, lanes] = (
                lax.dot_general(inner, taps, TN, preferred_element_type=F32)
                .astype(BF16)
                .reshape(4, 2, SUB, 3 * BLOCK_C)
            )
            return carry

        lax.fori_loop(0, 3, body, 0)

    def spatial_back(unit, first):
        if first == 0:
            fetch_w(unit, 0, 0).start()

        def body(tap, carry):
            slot = lax.rem(tap, 2)

            @pl.when(tap < 8)
            def _():
                fetch_w(unit, tap + 1, 1 - slot).start()

            fetch_w(unit, tap, slot).wait()
            moved = ds_pad[pl.ds(2 - tap // 3, SIDE), pl.ds(2 - tap % 3, SIDE)].reshape(ROWS, MID_C)
            value = lax.dot_general(moved, w_buf[slot], NN, preferred_element_type=F32)

            @pl.when(tap == 0)
            def _():
                side[...] = value

            @pl.when(tap > 0)
            def _():
                side[...] = side[...] + value

            return carry

        lax.fori_loop(first, first + 3, body, 0)

    a_0, b_0, c_0, t_0, a_1, b_1, c_1, t_1 = range(N_CHUNKS)

    load_t[1].wait()
    load_skip.wait()
    fetch_wt(1, 0, 0).start()
    out_norm_back(1, None, None)
    load_t[0].start()
    load_u[1].wait()
    temporal_grad()
    load_u[0].start()
    step_pair(t_1)
    temporal_back(1)
    load_s[1].wait()
    own_acts = []
    mid_norm_back(
        1,
        lambda: step_one(t_1),
        lambda: own_acts.append(acts(0, block_in, block_out)),
    )
    load_s[0].start()
    load_a[1].wait()
    spatial_grad(0)
    step_pair(a_1)
    step_two(t_1)
    spatial_grad(1)
    step_pair(b_1)
    step_one(a_1)
    spatial_grad(2)
    load_a[0].start()
    step_pair(c_1)
    step_three(t_1)
    step_one(b_1)
    step_two(a_1)
    spatial_back(1, 0)
    step_four(t_1)
    spatial_back(1, 3)
    spatial_back(1, 6)
    load_t[0].wait()
    gain, bias = par[4:5, :BLOCK_C], par[5:6, :BLOCK_C]

    def hidden_back(p, carry):
        rows = rows_of(p)
        slope = slope_of(t_ref[rows, :] * gain + bias)
        side[rows, :] = mask_out * slope * side[rows, :]
        return carry

    over_pixels(hidden_back, 0)
    fetch_wt(0, 0, 0).start()

    def hook_a():
        step_one(c_1)
        step_two(b_1)

    out_norm_back(0, hook_a, lambda: step_three(a_1))
    drain(t_1)
    load_u[0].wait()
    temporal_grad()
    load_shuffle.start()
    step_pair(t_0)
    temporal_back(0)
    step_two(c_1)
    step_five(t_1)
    load_s[0].wait()
    mid_norm_back(0, lambda: step_one(t_0), lambda: step_three(b_1))
    load_a[0].wait()
    step_four(a_1)
    drain(a_1)
    spatial_grad(0)
    step_pair(a_0)
    step_two(t_0)
    step_three(c_1)
    step_five(a_1)
    step_four(b_1)
    spatial_back(0, 0)
    step_one(a_0)
    spatial_back(0, 3)
    spatial_back(0, 6)
    step_three(t_0)
    step_two(a_0)
    load_shuffle.wait()
    d_ref[0] = (side[...] + skip_ref[...].astype(F32)).astype(BF16)
    thin = d_ref.at[1]
    thin[...] = lax.dot_general(
        u_ref[:, :SHUFFLE_C], d_ref[0], TN, preferred_element_type=F32
    ).astype(BF16)[:ROWS]
    own_acts.append(acts(1, thin, input_out))
    drain(b_1)
    spatial_grad(1)
    step_pair(b_0)
    step_five(b_1)
    step_four(c_1)
    drain(c_1)
    spatial_grad(2)
    step_pair(c_0)
    step_one(b_0)
    step_three(a_0)
    step_five(c_1)
    step_four(t_0)
    step_one(c_0)
    step_two(b_0)
    step_five(t_0)
    step_two(c_0)
    step_four(a_0)
    step_three(b_0)
    step_five(a_0)
    step_three(c_0)
    step_four(b_0)
    step_five(b_0)
    step_four(c_0)
    step_five(c_0)
    acts_wait(0, block_in, block_out, own_acts[0])
    acts_wait(1, thin, input_out, own_acts[1])
    for kind in ("s", "t"):
        for copy in adam_saves[kind]:
            copy.wait()
    for copy in act_copies:
        copy.wait_send()
    for index in (t_0, a_0, b_0, c_0):
        drain(index)


def spaces(text):
    kinds = {"v": VMEM, "a": pl.ANY, "s": pltpu.SMEM}
    return [pl.BlockSpec(memory_space=kinds[mark]) for mark in text]


def dma(*shape):
    return pltpu.SemaphoreType.DMA(shape)


def params(number):
    return pltpu.CompilerParams(
        collective_id=number, has_side_effects=True, vmem_limit_bytes=GRANT
    )


def shaped(*shape, dtype=BF16):
    return jax.ShapeDtypeStruct(shape, dtype)


def run_forward(*args):
    padded = (SIDE + 2, SIDE + 2, SLOTS, BLOCK_C)
    return pl.pallas_call(
        forward_kernel,
        out_shape=[
            shaped(2, 3, 4, 2, SUB, TAPS_C),
            shaped(2, 9, 4, 2, SUB, BLOCK_C),
            shaped(8, MID_C, dtype=F32),
            shaped(SLOTS, MID_C, dtype=F32),
            shaped(ROWS, BLOCK_C),
            shaped(2, *padded),
            shaped(2, ROWS, MID_C),
            shaped(2, ROWS, MID_C),
            shaped(2, ROWS, BLOCK_C, dtype=F32),
            shaped(ROWS, BLOCK_C),
            shaped(4, MID_C, dtype=F32),
            shaped(4, BLOCK_C, dtype=F32),
        ],
        in_specs=spaces("vvaavvsv"),
        out_specs=spaces("aavvvaaaaavv"),
        scratch_shapes=[
            VMEM((2, 2 * HALF, CHIP_S // 2), BF16),
            VMEM((2, 2 * HALF, 3 * CHIP_T // 2), BF16),
            VMEM((4 * ROWS, 128), F32),
            VMEM((4 * ROWS, 128), BF16),
            VMEM((8, MID_C), F32),
            VMEM((2, HALF, CHIP_S // 2), BF16),
            VMEM((2, HALF, 3 * CHIP_T // 2), BF16),
            VMEM((2, 3, 1, SUB, CHIP_S), BF16),
            VMEM((2, 9, 1, SUB, CHIP_T), BF16),
            VMEM((ROWS, BLOCK_C), BF16),
            VMEM((ROWS, BLOCK_C), BF16),
            VMEM((4, 8, MID_C), F32),
            VMEM((2,) + padded, BF16),
            VMEM((ROWS, MID_C), F32),
            VMEM((2, ROWS, MID_C), BF16),
            VMEM((2, ROWS, MID_C), BF16),
            VMEM((2, ROWS, BLOCK_C), F32),
            VMEM((2, ROWS, BLOCK_C), F32),
            VMEM((ROWS, BLOCK_C), BF16),
            VMEM((ROWS, BLOCK_C), BF16),
            VMEM((2, 4, 2, SUB, TAPS_C), BF16),
            VMEM((9, 4, 2, SUB, BLOCK_C), BF16),
            VMEM((2, 8, 8, MID_C), F32),
            VMEM((2, 4, 8, MID_C), F32),
            VMEM((2, 8, 8, BLOCK_C), F32),
            VMEM((2, 4, 8, BLOCK_C), F32),
            VMEM((8, 8, 128), F32),
            VMEM((8, 8, MID_C), F32),
            VMEM((4, 8, MID_C), F32),
            dma(4),
            dma(4),
            dma(3, 3),
            dma(3, 3),
            dma(N_CHUNKS, 3),
            dma(N_CHUNKS, 3),
            dma(N_CHUNKS, 2, 2),
            dma(N_CHUNKS, 2, 2),
            dma(N_CHUNKS, 2),
            dma(N_CHUNKS, 2),
            dma(N_CHUNKS, 4),
            dma(N_CHUNKS, 4),
            dma(3),
            dma(N_CHUNKS),
            dma(2, 4),
            dma(5),
            dma(10),
            dma(5, 7),
            dma(5, 7),
            dma(5, 3),
            dma(5, 3),
        ],
        compiler_params=params(0),
        name="forward",
    )(*args)


def run_backward(*args):
    return pl.pallas_call(
        backward_kernel,
        out_shape=[
            *[shaped(2, 2 * HALF, CHIP_S // 2, dtype=F32)] * 3,
            *[shaped(2, 3, CHIP_T // 2, 2 * HALF, dtype=F32)] * 3,
            shaped(4, MID_C, dtype=F32),
            shaped(4, BLOCK_C, dtype=F32),
            shaped(4 * ROWS, 128),
            shaped(4 * ROWS, 128),
        ],
        in_specs=spaces("aaaaaaavvvvaaaaaaaa"),
        out_specs=spaces("aaaaaavvaa"),
        scratch_shapes=[
            VMEM((SIDE + 2, SIDE + 2, SLOTS, BLOCK_C), BF16),
            VMEM((ROWS, MID_C), BF16),
            VMEM((ROWS, MID_C), BF16),
            VMEM((ROWS, BLOCK_C), F32),
            VMEM((ROWS, BLOCK_C), F32),
            VMEM((ROWS, BLOCK_C), BF16),
            VMEM((ROWS, MID_C), F32),
            VMEM((SIDE + 2, SIDE + 2, SLOTS, MID_C), BF16),
            VMEM((3, ROWS, BLOCK_C), BF16),
            VMEM((2, MID_C, BLOCK_C), BF16),
            VMEM((2, 8, 8, MID_C), F32),
            VMEM((2, 4, 8, MID_C), F32),
            VMEM((2, 8, 8, BLOCK_C), F32),
            VMEM((2, 4, 8, BLOCK_C), F32),
            VMEM((3, 1, 4, 2, SUB, TAPS_C), BF16),
            VMEM((9, 4, 2, SUB, BLOCK_C), BF16),
            VMEM((3, 1, 4, SUB, TAPS_C), BF16),
            VMEM((9, 4, SUB, BLOCK_C), BF16),
            VMEM((2, 3, 2, 1, 2, SUB, CHIP_S), BF16),
            VMEM((2, 2, 9, 2, SUB, CHIP_T), BF16),
            VMEM((2, 3, 2, 1, 4, SUB, CHIP_S), BF16),
            VMEM((2, 2, 9, 4, SUB, CHIP_T), BF16),
            VMEM((2, 3, 3, 1, 1, SUB, CHIP_S), BF16),
            VMEM((2, 3, 9, 1, SUB, CHIP_T), BF16),
            VMEM((2, 3, 2, 1, 1, SUB, CHIP_S), F32),
            VMEM((2, 2, 9, 1, SUB, CHIP_T), F32),
            VMEM((3, 2, SUB, CHIP_S // 2), F32),
            VMEM((3, 3, CHIP_T // 2, 2 * HALF), F32),
            dma(6),
            dma(2),
            dma(4, 7),
            dma(4, 7),
            dma(4, 3),
            dma(4, 3),
            dma(2, 3),
            dma(2, 3),
            dma(2),
            dma(N_CHUNKS),
            dma(N_CHUNKS),
            dma(N_CHUNKS, 2),
            dma(N_CHUNKS, 2),
            dma(N_CHUNKS, 2, 2),
            dma(N_CHUNKS, 2, 2),
            dma(N_CHUNKS, 3),
            dma(N_CHUNKS, 3),
            dma(N_CHUNKS),
            dma(N_CHUNKS),
            dma(2, 6),
            dma(2, 6),
        ],
        compiler_params=params(1),
        name="backward",
    )(*args)


def finish_kernel(
    frames_in,
    mid_p,
    mid_m,
    mid_v,
    out_p,
    out_m,
    out_v,
    sp_in,
    sm_in,
    sv_in,
    tp_in,
    tm_in,
    tv_in,
    mid_all,
    out_all,
    block_in,
    grad_in,
    block_out,
    clip_pool,
    grad_out,
    mid_p_out,
    mid_m_out,
    mid_v_out,
    out_p_out,
    out_m_out,
    out_v_out,
    sp_out,
    sm_out,
    sv_out,
    tp_out,
    tm_out,
    tv_out,
    block_ref,
    grad_ref,
    block_wide,
    grad_wide,
    hold_s,
    hold_t,
    sems,
):
    line = lax.axis_index("chan")
    loads = [
        pltpu.make_async_copy(block_in, block_ref, sems.at[0]),
        pltpu.make_async_copy(grad_in, grad_ref, sems.at[1]),
    ]
    passing = (
        (sp_in, hold_s.at[0], sp_out),
        (sm_in, hold_s.at[1], sm_out),
        (sv_in, hold_s.at[2], sv_out),
        (tp_in, hold_t.at[0], tp_out),
        (tm_in, hold_t.at[1], tm_out),
        (tv_in, hold_t.at[2], tv_out),
    )
    gets = [
        pltpu.make_async_copy(source, held, sems.at[2 + number])
        for number, (source, held, _) in enumerate(passing)
    ]
    puts = [
        pltpu.make_async_copy(held, target, sems.at[10 + number])
        for number, (_, held, target) in enumerate(passing)
    ]
    for copy in loads + gets:
        copy.start()
    stores = [
        pltpu.make_async_copy(block_wide, block_out, sems.at[8]),
        pltpu.make_async_copy(grad_wide, grad_out, sems.at[9]),
    ]
    loads[0].wait()
    block_wide[...] = block_ref[...].astype(F32)
    stores[0].start()
    loads[1].wait()
    grad_wide[...] = grad_ref[...].astype(F32)
    stores[1].start()
    for get, put in zip(gets, puts):
        get.wait()
        put.start()
    size = FRAMES * HW
    for clip in range(clip_pool.shape[0]):
        total = jnp.sum(block_wide[clip * size : (clip + 1) * size, :], axis=0, keepdims=True)
        kept = lax.div(frames_in[clip], 8).astype(F32)
        clip_pool[clip : clip + 1, :] = total / (HW * kept)
    all_rows = jnp.concatenate([mid_all[...], jnp.zeros((4, MID_C), F32)], axis=0)
    turned = pltpu.roll(all_rows, lax.rem(MID_C - line * (2 * SUB), MID_C), 1)[0:4]
    grad = jnp.concatenate(
        [
            turned[:, third * THIRD + half * SUB : third * THIRD + (half + 1) * SUB]
            for half in range(2)
            for third in range(3)
        ],
        axis=1,
    )
    fresh = adam_update(mid_p[...], mid_m[...], mid_v[...], grad, RATE_NORM, 0.0)
    for ref, value in zip((mid_p_out, mid_m_out, mid_v_out), fresh):
        ref[...] = value
    grad = out_all[:, pl.ds(pl.multiple_of(line * 128, 128), 128)]
    fresh = adam_update(out_p[...], out_m[...], out_v[...], grad, RATE_NORM, 0.0)
    for ref, value in zip((out_p_out, out_m_out, out_v_out), fresh):
        ref[...] = value
    for copy in stores + puts:
        copy.wait()


def run_finish(frames, *args):
    convs = args[6:12]
    norms = args[:6]
    clips = frames.shape[0]
    return pl.pallas_call(
        finish_kernel,
        out_shape=[
            shaped(4 * ROWS, 128, dtype=F32),
            shaped(clips, 128, dtype=F32),
            shaped(4 * ROWS, 128, dtype=F32),
            *[shaped(*v.shape, dtype=F32) for v in norms],
            *[shaped(*v.shape, dtype=F32) for v in convs],
        ],
        in_specs=spaces("svvvvvvaaaaaavvaa"),
        out_specs=spaces("avavvvvvvaaaaaa"),
        scratch_shapes=[
            VMEM((4 * ROWS, 128), BF16),
            VMEM((4 * ROWS, 128), BF16),
            VMEM((4 * ROWS, 128), F32),
            VMEM((4 * ROWS, 128), F32),
            VMEM((3,) + convs[0].shape, F32),
            VMEM((3,) + convs[3].shape, F32),
            dma(16),
        ],
        compiler_params=pltpu.CompilerParams(vmem_limit_bytes=GRANT),
        name="finish",
    )(frames, *args)


def shuffle_matrix():
    clip, frame, pixel = np.meshgrid(np.arange(4), np.arange(FRAMES), np.arange(HW), indexing="ij")
    source = (clip * FRAMES + frame) * HW + pixel
    target = pixel * SLOTS + frame * 4 + clip
    matrix = np.zeros((ROWS, SHUFFLE_C), np.float32)
    matrix[target.reshape(-1), source.reshape(-1)] = 1.0
    return jnp.asarray(matrix, BF16)


def on_pairs(
    features,
    cotangent,
    clip_frames,
    spatial_master,
    spatial_first,
    spatial_second,
    temporal_master,
    temporal_first,
    temporal_second,
    mid_norm,
    mid_first,
    mid_second,
    out_norm,
    out_first,
    out_second,
):
    line = lax.axis_index("chan")
    spatial_own = [jnp.swapaxes(v, 1, 2) for v in (spatial_master, spatial_first, spatial_second)]
    temporal_own = [
        jnp.swapaxes(v, 2, 3) for v in (temporal_master, temporal_first, temporal_second)
    ]
    shuffle = shuffle_matrix()
    ws, wt, par, mask, block, a_all, s_all, u_all, t_all, skip, stat_mid, stat_out = run_forward(
        spatial_own[0],
        temporal_own[0],
        features,
        cotangent,
        mid_norm,
        out_norm,
        clip_frames,
        shuffle,
    )
    conv_new = run_backward(
        ws.reshape(2, MID_C, TAPS_C),
        wt.reshape(2, 3, MID_C, BLOCK_C),
        a_all,
        s_all,
        u_all,
        t_all,
        skip,
        stat_mid,
        stat_out,
        par,
        mask,
        shuffle,
        block,
        *spatial_own,
        *temporal_own,
    )
    block_out, clip_pool, grad_out, *rest = run_finish(
        clip_frames, mid_norm, mid_first, mid_second, out_norm, out_first, out_second, *conv_new
    )
    norms, convs = rest[:6], rest[6:]
    spatial = [jnp.swapaxes(v, 1, 2) for v in convs[:3]]
    temporal = [jnp.swapaxes(v, 2, 3) for v in convs[3:]]
    return (block_out, clip_pool, grad_out, *spatial, *temporal, *norms)


def solution(mesh):
    in_specs = (
        P("dp", "chan"),
        P("dp", "chan"),
        P("dp"),
        P(None, "dp", "chan"),
        P(None, "dp", "chan"),
        P(None, "dp", "chan"),
        P(None, None, "chan", "dp"),
        P(None, None, "chan", "dp"),
        P(None, None, "chan", "dp"),
        P(None, "chan"),
        P(None, "chan"),
        P(None, "chan"),
        P(None, "chan"),
        P(None, "chan"),
        P(None, "chan"),
    )
    out_specs = (
        P("dp", "chan"),
        P("dp", "chan"),
        P("dp", "chan"),
        P(None, "dp", "chan"),
        P(None, "dp", "chan"),
        P(None, "dp", "chan"),
        P(None, None, "chan", "dp"),
        P(None, None, "chan", "dp"),
        P(None, None, "chan", "dp"),
        P(None, "chan"),
        P(None, "chan"),
        P(None, "chan"),
        P(None, "chan"),
        P(None, "chan"),
        P(None, "chan"),
    )
    body = on_pairs if mesh.shape["dp"] == 8 and mesh.shape["chan"] == 4 else on_device
    return jax.shard_map(
        body, mesh=mesh, in_specs=in_specs, out_specs=out_specs, check_vma=False
    )
```

```python
import jax
import jax.numpy as jnp
import numpy as np
from jax import lax
from jax.experimental import pallas as pl
from jax.experimental.pallas import tpu as pltpu
from jax.sharding import PartitionSpec as P

FRAMES = 4
SIDE = 7
STEP = 10
HW = 49


EPS_NORM = 1e-05
EPS_ADAM = 1e-08
BETA_ONE = 0.9
BETA_TWO = 0.95
RATE_CONV = 0.01
RATE_NORM = 0.8
DECAY_CONV = 0.05


def frame_mask(clip_frames):
    kept_frames = clip_frames // 8
    frame_ids = jnp.arange(FRAMES, dtype=jnp.int32)
    frame_grid = (frame_ids[None, :] < kept_frames[:, None]).astype(jnp.float32)
    return jnp.broadcast_to(frame_grid[:, :, None], (kept_frames.shape[0], FRAMES, HW)).reshape(
        -1, 1
    )


def silu_slope(values):
    sigmoid = jax.nn.sigmoid(values)
    return sigmoid * (1.0 + values * (1.0 - sigmoid))


def spatial_apply(inputs, tap_weights):
    channels = inputs.shape[1]
    padded = jnp.pad(inputs.reshape(-1, SIDE, SIDE, channels), ((0, 0), (1, 1), (1, 1), (0, 0)))
    summed = jnp.zeros((inputs.shape[0], tap_weights.shape[2]), jnp.float32)
    for tap_index in range(9):
        row_off, col_off = (tap_index // 3, tap_index % 3)
        window = padded[:, row_off : row_off + SIDE, col_off : col_off + SIDE].reshape(-1, channels)
        summed = summed + jnp.dot(
            window, tap_weights[tap_index], preferred_element_type=jnp.float32
        )
    return (summed, padded)


def spatial_grads(padded, tap_weights, grad_out):
    channels = padded.shape[3]
    weight_terms = []
    input_sum = jnp.zeros((padded.shape[0], SIDE, SIDE, channels), jnp.float32)
    for tap_index in range(9):
        row_off, col_off = (tap_index // 3, tap_index % 3)
        window = padded[:, row_off : row_off + SIDE, col_off : col_off + SIDE].reshape(-1, channels)
        weight_terms.append(
            lax.dot_general(
                window, grad_out, (((0,), (0,)), ((), ())), preferred_element_type=jnp.float32
            )
        )
        pulled = lax.dot_general(
            grad_out,
            tap_weights[tap_index],
            (((1,), (1,)), ((), ())),
            preferred_element_type=jnp.float32,
        )
        pulled = jnp.pad(pulled.reshape(-1, SIDE, SIDE, channels), ((0, 0), (1, 1), (1, 1), (0, 0)))
        input_sum = (
            input_sum
            + pulled[:, 2 - row_off : 2 - row_off + SIDE, 2 - col_off : 2 - col_off + SIDE]
        )
    return (jnp.stack(weight_terms).reshape(-1, grad_out.shape[1]), input_sum.reshape(-1, channels))


def temporal_apply(inputs, weight):
    frame_seq = inputs.reshape(-1, FRAMES, HW, inputs.shape[1])
    padded = jnp.pad(frame_seq, ((0, 0), (1, 1), (0, 0), (0, 0)))
    summed = jnp.zeros(frame_seq.shape[:3] + (weight.shape[2],), jnp.float32)
    for frame_off in range(3):
        summed = summed + jnp.einsum(
            "nfpm,mc->nfpc",
            padded[:, frame_off : frame_off + FRAMES],
            weight[frame_off],
            preferred_element_type=jnp.float32,
        )
    return (summed.reshape(inputs.shape[0], -1), padded)


def temporal_grads(padded, weight, grad_full):
    grad_seq = grad_full.reshape(-1, FRAMES, HW, grad_full.shape[1])
    grad_pad = jnp.pad(grad_seq, ((0, 0), (1, 1), (0, 0), (0, 0)))
    weight_terms = []
    input_sum = jnp.zeros(padded.shape[:1] + (FRAMES, HW, padded.shape[3]), jnp.float32)
    for frame_off in range(3):
        weight_terms.append(
            jnp.einsum(
                "nfpm,nfpc->mc",
                padded[:, frame_off : frame_off + FRAMES],
                grad_seq,
                preferred_element_type=jnp.float32,
            )
        )
        input_sum = input_sum + jnp.einsum(
            "nfpc,mc->nfpm",
            grad_pad[:, 2 - frame_off : 2 - frame_off + FRAMES],
            weight[frame_off],
            preferred_element_type=jnp.float32,
        )
    return (jnp.stack(weight_terms), input_sum.reshape(grad_full.shape[0], -1))


def normalize(values, validity, gain_row, bias_row):
    local_valid = jnp.sum(validity)
    total_valid, value_sums = lax.psum((local_valid, jnp.sum(values * validity, axis=0)), "dp")
    average = value_sums / total_valid
    centered = values - average
    variance = lax.psum(jnp.sum(validity * centered * centered, axis=0), "dp") / total_valid
    inverse = lax.rsqrt(variance + EPS_NORM)
    standard = centered * inverse
    return (standard * gain_row + bias_row, standard, inverse, total_valid)


def normalize_back(grad_normed, standard, inverse, gain_row, total_valid, validity):
    grad_bias, grad_gain = lax.psum(
        (
            jnp.sum(grad_normed * validity, axis=0),
            jnp.sum(grad_normed * standard * validity, axis=0),
        ),
        "dp",
    )
    grad_values = (
        validity
        * gain_row
        * inverse
        * (grad_normed - grad_bias / total_valid - standard * grad_gain / total_valid)
    )
    return (grad_values, grad_gain, grad_bias)


def adam_update(weight, moment_one, moment_two, grad_value, rate, decay):
    fresh_one = BETA_ONE * moment_one + (1.0 - BETA_ONE) * grad_value
    fresh_two = BETA_TWO * moment_two + (1.0 - BETA_TWO) * grad_value * grad_value
    scaled = (
        fresh_one
        / (1.0 - BETA_ONE**STEP)
        / (jnp.sqrt(fresh_two / (1.0 - BETA_TWO**STEP)) + EPS_ADAM)
    )
    return (weight - rate * (scaled + decay * weight), fresh_one, fresh_two)


def on_device(
    features,
    cotangent,
    clip_frames,
    spatial_master,
    spatial_first,
    spatial_second,
    temporal_master,
    temporal_first,
    temporal_second,
    mid_norm,
    mid_first,
    mid_second,
    out_norm,
    out_first,
    out_second,
):
    validity = frame_mask(clip_frames)
    spatial_all, temporal_all = (
        lax.all_gather(spatial_master.astype(jnp.bfloat16), "dp", axis=1, tiled=True),
        lax.all_gather(temporal_master.astype(jnp.bfloat16), "dp", axis=3, tiled=True),
    )
    channels = temporal_all.shape[3]
    spatial_taps = spatial_all.reshape(2, 9, channels, spatial_all.shape[2])
    residual = features.astype(jnp.float32)
    outgoing = features
    kept_state = []
    for unit_index in range(2):
        gathered = lax.all_gather(outgoing, "chan", axis=1, tiled=True)
        spatial_out, padded = spatial_apply(gathered, spatial_taps[unit_index])
        mid_normed, mid_standard, mid_inverse, total_valid = normalize(
            spatial_out, validity, mid_norm[2 * unit_index], mid_norm[2 * unit_index + 1]
        )
        temporal_in = (jax.nn.silu(mid_normed) * validity).astype(jnp.bfloat16)
        partial_value, frames_padded = temporal_apply(temporal_in, temporal_all[unit_index])
        temporal_out = lax.psum_scatter(
            partial_value.astype(jnp.bfloat16), "chan", scatter_dimension=1, tiled=True
        ).astype(jnp.float32)
        out_normed, out_standard, out_inverse, total_valid = normalize(
            temporal_out, validity, out_norm[2 * unit_index], out_norm[2 * unit_index + 1]
        )
        if unit_index == 0:
            pre_act = out_normed
            outgoing = (jax.nn.silu(pre_act) * validity).astype(jnp.bfloat16)
        else:
            pre_act = out_normed + residual
            block_out = jax.nn.silu(pre_act) * validity
        kept_state.append(
            (
                padded,
                mid_normed,
                mid_standard,
                mid_inverse,
                frames_padded,
                pre_act,
                out_standard,
                out_inverse,
            )
        )
    kept_frames = (clip_frames // 8).astype(jnp.float32)
    clip_pool = (
        jnp.sum(block_out.reshape(-1, FRAMES * HW, block_out.shape[1]), axis=1)
        / (HW * kept_frames)[:, None]
    )
    skip_grad = cotangent * validity * silu_slope(kept_state[1][5])
    grad_pre = skip_grad
    spatial_list = [None, None]
    temporal_list = [None, None]
    mid_rows = [None, None]
    out_rows = [None, None]
    grad_hidden = skip_grad
    for unit_index in (1, 0):
        (
            padded,
            mid_normed,
            mid_standard,
            mid_inverse,
            frames_padded,
            pre_act,
            out_standard,
            out_inverse,
        ) = kept_state[unit_index]
        if unit_index == 0:
            grad_pre = grad_hidden * validity * silu_slope(pre_act)
        grad_temporal, out_gain_grad, out_bias_grad = normalize_back(
            grad_pre, out_standard, out_inverse, out_norm[2 * unit_index], total_valid, validity
        )
        grad_full = lax.all_gather(grad_temporal.astype(jnp.bfloat16), "chan", axis=1, tiled=True)
        temporal_grad, grad_mid = temporal_grads(frames_padded, temporal_all[unit_index], grad_full)
        grad_mid_normed = grad_mid * validity * silu_slope(mid_normed)
        grad_spatial, mid_gain_grad, mid_bias_grad = normalize_back(
            grad_mid_normed,
            mid_standard,
            mid_inverse,
            mid_norm[2 * unit_index],
            total_valid,
            validity,
        )
        spatial_grad, grad_in_part = spatial_grads(
            padded, spatial_taps[unit_index], grad_spatial.astype(jnp.bfloat16)
        )
        grad_hidden = lax.psum_scatter(
            grad_in_part.astype(jnp.bfloat16), "chan", scatter_dimension=1, tiled=True
        ).astype(jnp.float32)
        spatial_list[unit_index] = spatial_grad
        temporal_list[unit_index] = temporal_grad
        mid_rows[unit_index] = (mid_gain_grad, mid_bias_grad)
        out_rows[unit_index] = (out_gain_grad, out_bias_grad)
    input_grad = grad_hidden + skip_grad
    spatial_sum, temporal_sum = (
        lax.psum_scatter(jnp.stack(spatial_list), "dp", scatter_dimension=1, tiled=True),
        lax.psum_scatter(jnp.stack(temporal_list), "dp", scatter_dimension=3, tiled=True),
    )
    mid_grad = jnp.stack([mid_rows[0][0], mid_rows[0][1], mid_rows[1][0], mid_rows[1][1]])
    out_grad = jnp.stack([out_rows[0][0], out_rows[0][1], out_rows[1][0], out_rows[1][1]])
    spatial_new, spatial_one, spatial_two = adam_update(
        spatial_master, spatial_first, spatial_second, spatial_sum, RATE_CONV, DECAY_CONV
    )
    temporal_new, temporal_one, temporal_two = adam_update(
        temporal_master, temporal_first, temporal_second, temporal_sum, RATE_CONV, DECAY_CONV
    )
    mid_new, mid_one, mid_two = adam_update(
        mid_norm, mid_first, mid_second, mid_grad, RATE_NORM, 0.0
    )
    out_new, out_one, out_two = adam_update(
        out_norm, out_first, out_second, out_grad, RATE_NORM, 0.0
    )
    return (
        block_out,
        clip_pool,
        input_grad,
        spatial_new,
        spatial_one,
        spatial_two,
        temporal_new,
        temporal_one,
        temporal_two,
        mid_new,
        mid_one,
        mid_two,
        out_new,
        out_one,
        out_two,
    )


F32 = jnp.float32
BF16 = jnp.bfloat16
MESH = pl.DeviceIdType.MESH
VMEM = pltpu.VMEM
NN = (((1,), (0,)), ((), ()))
NT = (((1,), (1,)), ((), ()))
TN = (((0,), (0,)), ((), ()))
BLOCK_C = 512
MID_C = 1152
THIRD = MID_C // 3
ROWS = 784
SLOTS = 16
SHUFFLE_C = 896
HALF = 144
SUB = 48
TAPS_C = 9 * BLOCK_C
CHIP_S = TAPS_C // 4
CHIP_T = BLOCK_C // 4
CHUNKS = (
    ("s", 0, 0, 1),
    ("s", 0, 1, 1),
    ("s", 0, 2, 1),
    ("t", 0, 0, 9),
    ("s", 1, 0, 1),
    ("s", 1, 1, 1),
    ("s", 1, 2, 1),
    ("t", 1, 0, 9),
)
N_CHUNKS = len(CHUNKS)
NEAR = ("chip", "chip_x", "chip_y", "chip_d")
PARTS = (("s", 0), ("t", 0), ("s", 1), ("t", 1))
GRANT = 65000 * 1024


def place():
    dp = lax.axis_index("dp")
    line = lax.axis_index("chan")
    core = lax.rem(dp, 2)
    chip = lax.div(dp, 2)
    x_bit = lax.rem(chip, 2)
    y_bit = lax.div(chip, 2)
    return dict(
        dp=dp,
        line=line,
        core=core,
        chip=chip,
        chip_x=chip + 1 - 2 * x_bit,
        chip_y=chip + 2 - 4 * y_bit,
        chip_d=3 - chip,
        pair=(dp + 1 - 2 * core, line),
        x=(dp + 2 - 4 * x_bit, line),
        y=(dp + 4 - 8 * y_bit, line),
    )


def remote(source, target, send, recv, device):
    return pltpu.make_async_remote_copy(
        src_ref=source,
        dst_ref=target,
        send_sem=send,
        recv_sem=recv,
        device_id=device,
        device_id_type=MESH,
    )


def greet(devices):
    barrier = pltpu.get_barrier_semaphore()
    for device in devices:
        pl.semaphore_signal(barrier, inc=1, device_id=device, device_id_type=MESH)
    pl.semaphore_wait(barrier, len(devices))


def line_peer(at, step):
    return (at["dp"], lax.rem(at["line"] + step, 4))


def ring_peer(at, step):
    return (lax.rem(at["dp"] + step, 8), at["line"])


def greet_all(at):
    greet(
        [ring_peer(at, step) for step in range(1, 8)]
        + [line_peer(at, step) for step in (1, 2, 3)]
    )


def rows_of(pixel):
    return pl.ds(pl.multiple_of(pixel * SLOTS, SLOTS), SLOTS)


def slope_of(values):
    sigmoid = jax.nn.sigmoid(values)
    return sigmoid * (1.0 + values * (1.0 - sigmoid))


def over_pixels(body, carry):
    return lax.fori_loop(0, HW, body, carry, unroll=7)


def exchange(at, land, land_two, index, sems, sem_index, payload, combine, hooks=(None, None)):
    dp, line = at["dp"], at["line"]
    one_send, one_recv, two_send, two_recv = sems
    rows = pl.ds(0, 2)
    for row, value in enumerate(payload):
        land[index, dp, row : row + 1, :] = value
    sent = []
    for step in range(1, 8):
        here = land.at[index, dp, rows]
        copy = remote(
            here,
            here,
            one_send.at[sem_index, step - 1],
            one_recv.at[sem_index, step - 1],
            ring_peer(at, step),
        )
        copy.start()
        sent.append(copy)
    if hooks[0] is not None:
        hooks[0]()
    for step in range(1, 8):
        there = land.at[index, lax.rem(dp + 8 - step, 8), rows]
        remote(
            there,
            there,
            one_send.at[sem_index, step - 1],
            one_recv.at[sem_index, step - 1],
            ring_peer(at, step),
        ).wait_recv()
    merged = combine([land[index, source] for source in range(8)])
    for row, value in enumerate(merged):
        land_two[index, line, row : row + 1, :] = value
    for step in (1, 2, 3):
        here = land_two.at[index, line, rows]
        copy = remote(
            here,
            here,
            two_send.at[sem_index, step - 1],
            two_recv.at[sem_index, step - 1],
            line_peer(at, step),
        )
        copy.start()
        sent.append(copy)
    if hooks[1] is not None:
        hooks[1]()
    for step in (1, 2, 3):
        there = land_two.at[index, lax.rem(line + 4 - step, 4), rows]
        remote(
            there,
            there,
            two_send.at[sem_index, step - 1],
            two_recv.at[sem_index, step - 1],
            line_peer(at, step),
        ).wait_recv()
    merged = combine([land_two[index, source] for source in range(4)])
    for copy in sent:
        copy.wait_send()
    return merged


def combine_sums(blocks):
    total = sum(blocks[1:], blocks[0])
    return [total[0:1], total[1:2]]


def forward_kernel(
    ws_wide,
    wt_wide,
    feat_in,
    cot_wide,
    mid_own,
    out_own,
    frames_in,
    shuffle,
    ws_out,
    wt_out,
    par_out,
    mask_in,
    block_out,
    a_out,
    s_out,
    u_out,
    t_out,
    skip_out,
    stat_mid,
    stat_out,
    ws_in,
    wt_in,
    cot_raw,
    cot_in,
    par_in,
    pair_s,
    pair_t,
    stage_s,
    stage_t,
    feat_land,
    cot_land,
    par_land,
    a_pad,
    s_ref,
    x_ref,
    u_ref,
    t_ref,
    side,
    feat_ref,
    thin,
    w_buf,
    wt_buf,
    land_mid,
    land_mid_two,
    land_out,
    land_out_two,
    land_count,
    count_one,
    count_two,
    pair_send,
    pair_recv,
    act_send,
    act_recv,
    line_send,
    line_recv,
    plane_send,
    plane_recv,
    diag_send,
    diag_recv,
    core_send,
    core_recv,
    own_sem,
    chunk_sem,
    w_sem,
    wt_sem,
    save_sem,
    one_send,
    one_recv,
    two_send,
    two_recv,
):
    at = place()
    line, core, chip = at["line"], at["core"], at["chip"]
    sems = (one_send, one_recv, two_send, two_recv)
    cot_load = pltpu.make_async_copy(cot_wide, cot_raw, wt_sem.at[4])
    cot_load.start()
    for unit in range(2):
        ws_in[unit] = ws_wide[unit].astype(BF16)
        for tau in range(3):
            wt_in[unit, :, 64 * tau : 64 * tau + 64] = wt_wide[unit, tau].T.astype(BF16)
    pieces = []
    blank = jnp.zeros((4, THIRD - 2 * SUB), F32)
    for third in range(3):
        for half in range(2):
            first = half * HALF + third * SUB
            pieces.append(mid_own[:, first : first + SUB])
        pieces.append(blank)
    par_in[...] = jnp.zeros(par_in.shape, F32)
    wide_rows = jnp.concatenate(
        [jnp.concatenate(pieces, axis=1), jnp.zeros((4, MID_C), F32)], axis=0
    )
    par_in[0:4, :] = pltpu.roll(wide_rows, line * (2 * SUB), 1)[0:4]
    par_in[4:8, pl.ds(pl.multiple_of(line * 128, 128), 128)] = out_own[...]
    row_ids = lax.broadcasted_iota(jnp.int32, (SLOTS, MID_C), 0)
    mask = jnp.zeros((SLOTS, MID_C), F32)
    for clip in range(4):
        kept = lax.div(frames_in[4 * line + clip], 8)
        here = jnp.logical_and(row_ids % 4 == clip, row_ids // 4 < kept)
        mask = jnp.where(here, 1.0, mask)
    mask_in[...] = mask
    count_rows = lax.broadcasted_iota(jnp.int32, (8, 128), 0)
    count_tile = jnp.zeros((8, 128), F32)
    for owner in range(4):
        frames = lax.div(frames_in[4 * owner], 8)
        for clip in range(1, 4):
            frames = frames + lax.div(frames_in[4 * owner + clip], 8)
        count_tile = jnp.where(count_rows == owner, (HW * frames).astype(F32), count_tile)
    land_count[at["dp"]] = count_tile
    greet_all(at)
    started = []

    def send(copy):
        copy.start()
        started.append(copy)
        return copy

    def area(chunk, owner_core, owner_chip, first, count):
        kind, unit, lead, leads = chunk
        ref, width = (ws_out, CHIP_S) if kind == "s" else (wt_out, CHIP_T)
        lanes = pl.ds(pl.multiple_of(owner_chip * width, 128), width)
        return ref.at[unit, pl.ds(lead, leads), pl.ds(first, count), owner_core, :, lanes]

    pairs = {}
    for index, (kind, unit) in enumerate(PARTS):
        theirs = pl.ds(pl.multiple_of((1 - core) * HALF, 16), HALF)
        source, landing = (ws_in, pair_s) if kind == "s" else (wt_in, pair_t)
        pairs[kind, unit] = send(
            remote(
                source.at[unit, theirs],
                landing.at[unit],
                pair_send.at[index],
                pair_recv.at[index],
                at["pair"],
            )
        )

    def acts(row, source, target):
        def cut(owner):
            return source.at[pl.ds(pl.multiple_of(owner * ROWS, 16), ROWS)]

        lanes = pl.ds(pl.multiple_of(line * 128, 128), 128)
        for step in (1, 2, 3):
            peer = line_peer(at, step)
            send(
                remote(
                    cut(peer[1]),
                    target.at[:, lanes],
                    act_send.at[row, step - 1],
                    act_recv.at[row, step - 1],
                    peer,
                )
            )
        own = pltpu.make_async_copy(cut(line), target.at[:, lanes], own_sem.at[row])
        own.start()
        return own

    def acts_wait(row, source, target, own):
        for step in (1, 2, 3):
            origin = lax.rem(line + 4 - step, 4)
            lanes = pl.ds(pl.multiple_of(origin * 128, 128), 128)
            remote(
                source.at[pl.ds(0, ROWS)],
                target.at[:, lanes],
                act_send.at[row, step - 1],
                act_recv.at[row, step - 1],
                line_peer(at, step),
            ).wait_recv()
        own.wait()

    mine = pl.ds(pl.multiple_of(core * HALF, 16), HALF)

    def merge(kind, unit):
        pairs[kind, unit].wait_recv()
        source, landing = (ws_in, pair_s) if kind == "s" else (wt_in, pair_t)
        low = source[unit, mine].astype(F32)
        high = landing[unit].astype(F32)
        first = jnp.where(core == 0, low, high)
        second = jnp.where(core == 0, high, low)
        if kind == "s":
            both = jnp.concatenate([first, second], axis=1).astype(BF16)
            stage_s[unit] = both.reshape(3, 1, SUB, CHIP_S)
        else:
            for tau in range(3):
                lanes = slice(64 * tau, 64 * tau + 64)
                both = jnp.concatenate([first[:, lanes], second[:, lanes]], axis=1).astype(BF16)
                stage_t[unit, 3 * tau : 3 * tau + 3] = both.reshape(3, 1, SUB, CHIP_T)

    own_copies = [None] * N_CHUNKS

    def step_line(index):
        chunk = CHUNKS[index]
        kind, unit, lead, leads = chunk
        if lead == 0:
            merge(kind, unit)
        staged = (stage_s if kind == "s" else stage_t).at[unit, pl.ds(lead, leads)]
        target = area(chunk, core, chip, line, 1)
        for step in (1, 3, 2):
            send(
                remote(
                    staged,
                    target,
                    line_send.at[index, step - 1],
                    line_recv.at[index, step - 1],
                    line_peer(at, step),
                )
            )
        own = pltpu.make_async_copy(staged, target, chunk_sem.at[index])
        own.start()
        own_copies[index] = own

    def step_plane(index):
        chunk = CHUNKS[index]
        for step in (1, 2, 3):
            origin = area(chunk, core, chip, lax.rem(line + 4 - step, 4), 1)
            remote(
                origin,
                origin,
                line_send.at[index, step - 1],
                line_recv.at[index, step - 1],
                line_peer(at, step),
            ).wait_recv()
        own_copies[index].wait()
        for turn in range(2):
            for way, name in enumerate(("x", "y")):
                half = area(chunk, core, chip, 2 * (way ^ turn), 2)
                send(
                    remote(
                        half,
                        half,
                        plane_send.at[index, way, turn],
                        plane_recv.at[index, way, turn],
                        at[name],
                    )
                )
        held = area(chunk, core, chip, 0, 4)
        send(remote(held, held, core_send.at[index, 0], core_recv.at[index, 0], at["pair"]))

    def plane_wait(index, way, turn, name):
        half = area(CHUNKS[index], core, at["chip_" + name], 2 * (way ^ turn), 2)
        remote(
            half,
            half,
            plane_send.at[index, way, turn],
            plane_recv.at[index, way, turn],
            at[name],
        ).wait_recv()
        return half

    def step_diag(index):
        for way, (name, other) in enumerate((("x", "y"), ("y", "x"))):
            half = plane_wait(index, way, 0, name)
            send(
                remote(half, half, diag_send.at[index, way], diag_recv.at[index, way], at[other])
            )

    def step_core(index):
        chunk = CHUNKS[index]
        for way, name in enumerate(("x", "y")):
            plane_wait(index, way, 1, name)
            held = area(chunk, core, at["chip_" + name], 0, 4)
            send(
                remote(
                    held, held, core_send.at[index, 1 + way], core_recv.at[index, 1 + way], at["pair"]
                )
            )
        for slot, name in enumerate(NEAR[:3]):
            core_wait(index, slot, name)
        for way, (other, first) in enumerate((("y", 0), ("x", 2))):
            half = area(chunk, core, at["chip_d"], first, 2)
            remote(
                half, half, diag_send.at[index, way], diag_recv.at[index, way], at[other]
            ).wait_recv()
        held = area(chunk, core, at["chip_d"], 0, 4)
        send(remote(held, held, core_send.at[index, 3], core_recv.at[index, 3], at["pair"]))
        core_wait(index, 3, NEAR[3])

    def core_wait(index, slot, name):
        held = area(CHUNKS[index], 1 - core, at[name], 0, 4)
        remote(
            held, held, core_send.at[index, slot], core_recv.at[index, slot], at["pair"]
        ).wait_recv()
        fetch(index, slot, name).start()

    def fetch(index, slot, name):
        kind, unit, lead, _ = CHUNKS[index]
        if kind == "s":
            turn = (3 * unit + lead) % 2
            lanes = pl.ds(pl.multiple_of(at[name] * CHIP_S, 128), CHIP_S)
            return pltpu.make_async_copy(
                ws_out.at[unit, lead, :, :, :, lanes],
                w_buf.at[turn, :, :, :, lanes],
                w_sem.at[turn, slot],
            )
        lanes = pl.ds(pl.multiple_of(at[name] * CHIP_T, 128), CHIP_T)
        return pltpu.make_async_copy(
            wt_out.at[unit, :, :, :, :, lanes], wt_buf.at[:, :, :, :, lanes], wt_sem.at[slot]
        )

    def fetch_wait(index):
        for slot, name in enumerate(NEAR):
            fetch(index, slot, name).wait()

    def window(unit, tap):
        row, column = tap // 3, tap % 3
        return a_pad[unit, row : row + SIDE, column : column + SIDE].reshape(ROWS, BLOCK_C)

    def conv(unit, third):
        fetch_wait(4 * unit + third)
        taps = jnp.concatenate([window(unit, tap) for tap in range(9)], axis=1)
        s_ref[:, third * THIRD : (third + 1) * THIRD] = lax.dot_general(
            taps,
            w_buf[(3 * unit + third) % 2].reshape(THIRD, TAPS_C),
            NT,
            preferred_element_type=F32,
        )

    mask_mid = mask_in[...]
    mask_out = mask_in[:, :BLOCK_C]
    slot_rows = lax.broadcasted_iota(jnp.int32, (SLOTS, BLOCK_C), 0)
    has_before = (slot_rows >= 4).astype(F32)
    has_after = (slot_rows < 12).astype(F32)

    def moments(values, mask, land, land_two, index, sem_index, hooks):
        zero = jnp.zeros(mask.shape, F32)
        width = mask.shape[1]
        local = local_count[:, :width]
        added = over_pixels(lambda p, acc: acc + values[rows_of(p), :], zero)
        mean = jnp.sum(added * mask, axis=0, keepdims=True) / local

        def squares(p, acc):
            centered = values[rows_of(p), :] - mean
            return acc + centered * centered

        spread = jnp.sum(over_pixels(squares, zero) * mask, axis=0, keepdims=True)
        def combine(blocks):
            known = count_one if len(blocks) == 8 else count_two
            counts = [known[source, :, :width] for source in range(len(blocks))]
            pivot = blocks[0]
            drifts = [block - pivot for block in blocks[1:]]
            shift = sum(count * drift for count, drift in zip(counts[1:], drifts))[0:1]
            squared = sum(count * drift * drift for count, drift in zip(counts[1:], drifts))[0:1]
            inner = sum(blocks[1:], pivot)[1:2]
            total = sum(counts[1:], counts[0])[0:1]
            return [pivot[0:1] + shift / total, inner + squared - shift * shift / total]

        mean, spread = exchange(
            at, land, land_two, index, sems, sem_index, [mean, spread], combine, hooks
        )
        total = all_count[:, :width]
        return mean, lax.rsqrt(spread / total + EPS_NORM), total

    saves = []

    def save(source, target):
        copy = pltpu.make_async_copy(source, target, save_sem.at[len(saves)])
        copy.start()
        saves.append(copy)

    def mid_norm_act(unit, *hooks):
        gain = par_out[2 * unit : 2 * unit + 1]
        bias = par_out[2 * unit + 1 : 2 * unit + 2]
        mean, inverse, total = moments(
            s_ref, mask_mid, land_mid, land_mid_two, unit, 2 * unit, hooks
        )
        stat_mid[2 * unit : 2 * unit + 1] = inverse
        stat_mid[2 * unit + 1 : 2 * unit + 2] = total

        def mid_act(p, carry):
            rows = rows_of(p)
            standard = (s_ref[rows, :] - mean) * inverse
            x_ref[unit, rows, :] = standard.astype(BF16)
            normed = standard * gain + bias
            u_ref[unit, rows, :] = (jax.nn.sigmoid(normed) * normed * mask_mid).astype(BF16)
            return carry

        over_pixels(mid_act, 0)
        save(x_ref.at[unit], s_out.at[unit])
        save(u_ref.at[unit], u_out.at[unit])

    def temporal(unit):
        fetch_wait(4 * unit + 3)

        def weight(tau):
            return wt_buf[3 * tau : 3 * tau + 3].reshape(MID_C, BLOCK_C)

        t_ref[unit] = lax.dot_general(u_ref[unit], weight(1), NN, preferred_element_type=F32)
        side[0] = lax.dot_general(u_ref[unit], weight(0), NN, preferred_element_type=F32)
        side[1] = lax.dot_general(u_ref[unit], weight(2), NN, preferred_element_type=F32)

        def frames(p, carry):
            rows = rows_of(p)
            t_ref[unit, rows, :] = (
                t_ref[unit, rows, :]
                + pltpu.roll(side[0, rows, :], 4, 0) * has_before
                + pltpu.roll(side[1, rows, :], 12, 0) * has_after
            )
            return carry

        over_pixels(frames, 0)

    def out_stats(unit, *hooks):
        mean, inverse, total = moments(
            t_ref.at[unit], mask_out, land_out, land_out_two, unit, 2 * unit + 1, hooks
        )
        stat_out[2 * unit : 2 * unit + 1] = inverse
        stat_out[2 * unit + 1 : 2 * unit + 2] = total
        gain = par_out[4 + 2 * unit : 5 + 2 * unit, :BLOCK_C]
        bias = par_out[5 + 2 * unit : 6 + 2 * unit, :BLOCK_C]
        return mean, inverse, gain, bias

    for step in range(1, 8):
        here = land_count.at[at["dp"]]
        send(
            remote(
                here,
                here,
                one_send.at[4, step - 1],
                one_recv.at[4, step - 1],
                ring_peer(at, step),
            )
        )
    step_line(0)
    for step in (1, 2, 3):
        send(
            remote(
                par_in,
                par_land.at[line],
                act_send.at[2, step - 1],
                act_recv.at[2, step - 1],
                line_peer(at, step),
            )
        )
    par_own = pltpu.make_async_copy(par_in, par_land.at[line], own_sem.at[2])
    par_own.start()
    step_line(1)
    for unit in range(2):
        a_pad[unit] = jnp.zeros(a_pad.shape[1:], BF16)
    step_plane(0)
    step_line(2)
    step_diag(0)
    step_plane(1)
    feat_own = acts(0, feat_in, feat_land)
    cot_load.wait()
    cot_in[...] = cot_raw[...].astype(BF16)
    for step in range(1, 8):
        there = land_count.at[lax.rem(at["dp"] + 8 - step, 8)]
        remote(
            there,
            there,
            one_send.at[4, step - 1],
            one_recv.at[4, step - 1],
            ring_peer(at, step),
        ).wait_recv()

    def widen(row, rows):
        return jnp.concatenate([jnp.broadcast_to(row, (rows, 128))] * (MID_C // 128), axis=1)

    def pick(tile):
        return jnp.sum(jnp.where(count_rows == line, tile, 0.0), axis=0, keepdims=True)

    sum_tile = land_count[0]
    for source in range(8):
        count_one[source] = widen(pick(land_count[source]), 8)
        if source > 0:
            sum_tile = sum_tile + land_count[source]
    for source in range(4):
        count_two[source] = widen(sum_tile[source : source + 1], 8)
    local_count = widen(pick(count_tile), 1)
    all_count = widen(jnp.sum(sum_tile[0:4], axis=0, keepdims=True), 1)
    step_plane(2)
    step_line(3)
    step_diag(1)
    step_core(0)
    permute = shuffle[:, :ROWS]
    acts_wait(0, feat_in, feat_land, feat_own)
    feat_ref[...] = lax.dot_general(permute, feat_land[...], NN, preferred_element_type=F32).astype(
        BF16
    )

    def fill(p, carry):
        a_pad[0, 1 + p // SIDE, 1 + p % SIDE] = feat_ref[rows_of(p), :]
        return carry

    over_pixels(fill, 0)
    save(a_pad.at[0], a_out.at[0])
    step_line(4)
    step_diag(2)
    step_core(1)
    conv(0, 0)
    step_core(2)
    step_plane(3)
    conv(0, 1)
    conv(0, 2)
    for step in (1, 2, 3):
        remote(
            par_in,
            par_land.at[lax.rem(line + 4 - step, 4)],
            act_send.at[2, step - 1],
            act_recv.at[2, step - 1],
            line_peer(at, step),
        ).wait_recv()
    par_own.wait()
    par_out[...] = par_land[0] + par_land[1] + par_land[2] + par_land[3]

    def hook_a():
        step_diag(3)
        step_plane(4)

    def hook_e():
        step_line(5)
        step_core(3)

    mid_norm_act(0, hook_a, hook_e)
    temporal(0)
    cot_own = []

    def hook_b():
        step_diag(4)
        step_plane(5)

    def hook_c():
        step_line(6)
        step_line(7)
        cot_own.append(acts(1, cot_in, cot_land))
        step_core(4)

    mean, inverse, gain, bias = out_stats(0, hook_b, hook_c)

    def out_act(p, carry):
        rows = rows_of(p)
        standard = (t_ref[0, rows, :] - mean) * inverse
        t_ref[0, rows, :] = standard
        normed = standard * gain + bias
        hidden = jax.nn.sigmoid(normed) * normed * mask_out
        a_pad[1, 1 + p // SIDE, 1 + p % SIDE] = hidden.astype(BF16)
        return carry

    over_pixels(out_act, 0)
    save(t_ref.at[0], t_out.at[0])
    save(a_pad.at[1], a_out.at[1])
    conv(1, 0)
    step_diag(5)
    step_plane(6)
    step_core(5)
    conv(1, 1)
    step_diag(6)
    step_plane(7)
    step_core(6)
    conv(1, 2)
    mid_norm_act(1, lambda: step_diag(7), lambda: step_core(7))
    temporal(1)

    def hook_d():
        acts_wait(1, cot_in, cot_land, cot_own[0])
        side[0] = lax.dot_general(permute, cot_land[...], NN, preferred_element_type=F32)

    mean_one, inverse_one, gain_one, bias_one = out_stats(1, hook_d, None)

    def end_act(p, carry):
        rows = rows_of(p)
        standard = (t_ref[1, rows, :] - mean_one) * inverse_one
        t_ref[1, rows, :] = standard
        pre = standard * gain_one + bias_one + feat_ref[rows, :].astype(F32)
        sigmoid = jax.nn.sigmoid(pre)
        thin[rows, :] = (pre * sigmoid * mask_out).astype(BF16)
        slope = sigmoid * (1.0 + pre * (1.0 - sigmoid))
        cot_land[rows, :] = (side[0, rows, :] * mask_out * slope).astype(BF16)
        return carry

    over_pixels(end_act, 0)
    save(t_ref.at[1], t_out.at[1])
    save(cot_land, skip_out)
    block_out[...] = lax.dot_general(permute, thin[...], TN, preferred_element_type=F32).astype(
        BF16
    )
    for copy in saves:
        copy.wait()
    for copy in started:
        copy.wait_send()


def backward_kernel(
    ws,
    wt,
    a_in,
    s_in,
    u_in,
    t_in,
    skip_in,
    stat_mid,
    stat_out,
    par,
    mask_in,
    shuffle,
    block_in,
    sp_in,
    sm_in,
    sv_in,
    tp_in,
    tm_in,
    tv_in,
    sp_out,
    sm_out,
    sv_out,
    tp_out,
    tm_out,
    tv_out,
    mid_grad,
    out_grad,
    block_out,
    input_out,
    a_pad,
    s_ref,
    u_ref,
    t_ref,
    side,
    skip_ref,
    wide,
    ds_pad,
    d_ref,
    w_buf,
    land_mid,
    land_mid_two,
    land_out,
    land_out_two,
    g_s,
    g_t,
    land_s,
    land_t,
    one_s,
    one_t,
    two_s,
    two_t,
    line_s,
    line_t,
    fin_s,
    fin_t,
    adam_s,
    adam_t,
    load_sem,
    w_sem,
    ex_one_send,
    ex_one_recv,
    ex_two_send,
    ex_two_recv,
    act_send,
    act_recv,
    act_sem,
    pair_send,
    pair_recv,
    one_send,
    one_recv,
    two_send,
    two_recv,
    line_send,
    line_recv,
    fin_send,
    fin_recv,
    adam_load,
    adam_save,
):
    at = place()
    line, core, chip = at["line"], at["core"], at["chip"]
    sems = (ex_one_send, ex_one_recv, ex_two_send, ex_two_recv)

    def load(index, source, target):
        return pltpu.make_async_copy(source, target, load_sem.at[index])

    load_t = [load(0, t_in.at[unit], t_ref) for unit in range(2)]
    load_u = [load(1, u_in.at[unit], u_ref) for unit in range(2)]
    load_s = [load(2, s_in.at[unit], s_ref) for unit in range(2)]
    load_a = [load(3, a_in.at[unit], a_pad) for unit in range(2)]
    load_skip = load(4, skip_in, skip_ref)
    load_shuffle = load(5, shuffle, u_ref.at[:, pl.ds(0, SHUFFLE_C)])
    load_t[1].start()
    load_skip.start()
    load_u[1].start()
    load_s[1].start()
    load_a[1].start()
    greet_all(at)
    ds_pad[...] = jnp.zeros(ds_pad.shape, BF16)

    mask_mid = mask_in[...]
    mask_out = mask_in[:, :BLOCK_C]
    slot_rows = lax.broadcasted_iota(jnp.int32, (SLOTS, BLOCK_C), 0)
    has_before = (slot_rows >= 4).astype(F32)
    has_after = (slot_rows < 12).astype(F32)
    lanes_line = pl.ds(pl.multiple_of(line * 128, 128), 128)
    rows_line = pl.ds(pl.multiple_of(line * ROWS, 16), ROWS)

    act_copies = []

    def acts(row, source, target):
        for step in (1, 2, 3):
            peer = line_peer(at, step)
            copy = remote(
                source.at[:, pl.ds(pl.multiple_of(peer[1] * 128, 128), 128)],
                target.at[rows_line],
                act_send.at[row, step - 1],
                act_recv.at[row, step - 1],
                peer,
            )
            copy.start()
            act_copies.append(copy)
        own = pltpu.make_async_copy(source.at[:, lanes_line], target.at[rows_line], act_sem.at[row])
        own.start()
        return own

    def acts_wait(row, source, target, own):
        for step in (1, 2, 3):
            origin = lax.rem(line + 4 - step, 4)
            remote(
                source.at[:, lanes_line],
                target.at[pl.ds(pl.multiple_of(origin * ROWS, 16), ROWS)],
                act_send.at[row, step - 1],
                act_recv.at[row, step - 1],
                line_peer(at, step),
            ).wait_recv()
        own.wait()

    flying = [[] for _ in CHUNKS]
    pair_copies = [None] * N_CHUNKS
    fin_copies = [None] * N_CHUNKS

    def launch(index, copy):
        copy.start()
        flying[index].append(copy)
        return copy

    def drain(index):
        for copy in flying[index]:
            copy.wait_send()
        flying[index] = []

    def grad_of(index):
        kind, _, lead, _ = CHUNKS[index]
        return g_s.at[lead] if kind == "s" else g_t

    def land_of(index):
        kind, _, lead, _ = CHUNKS[index]
        return land_s.at[lead] if kind == "s" else land_t

    def held(index, small, large):
        kind, unit, lead, _ = CHUNKS[index]
        return large.at[unit, lead] if kind == "s" else small.at[unit]

    def cut(index, owner, first, count):
        width = CHIP_S if CHUNKS[index][0] == "s" else CHIP_T
        lanes = pl.ds(pl.multiple_of(owner * width, 128), width)
        return grad_of(index).at[:, pl.ds(first, count), core, :, lanes]

    def add_into(target, source):
        leads, count, _, width = target.shape

        def body(turn, carry):
            if leads == 1 and width > 2048:
                where = (0, lax.div(turn, 3), pl.ds(pl.multiple_of(lax.rem(turn, 3) * 16, 16), 16))
            elif leads == 1:
                where = (0, turn)
            else:
                where = (turn,)
            target[where] = (target[where].astype(F32) + source[where].astype(F32)).astype(BF16)
            return carry

        turns = leads if leads > 1 else count * (3 if width > 2048 else 1)
        lax.fori_loop(0, turns, body, 0)

    def step_pair(index):
        pair_copies[index] = launch(
            index,
            remote(
                grad_of(index).at[:, :, 1 - core],
                land_of(index),
                pair_send.at[index],
                pair_recv.at[index],
                at["pair"],
            ),
        )

    def step_one(index):
        pair_copies[index].wait_recv()
        add_into(grad_of(index).at[:, :, core], land_of(index))
        ones, twos = held(index, one_t, one_s), held(index, two_t, two_s)
        for way, (name, first) in enumerate((("x", 0), ("y", 2))):
            launch(
                index,
                remote(
                    cut(index, at["chip_d"], first, 2),
                    ones.at[way],
                    one_send.at[index, way],
                    one_recv.at[index, way],
                    at[name],
                ),
            )
            launch(
                index,
                remote(
                    cut(index, at["chip_" + name], first, 2),
                    twos.at[way, :, pl.ds(first, 2)],
                    two_send.at[index, way, 0],
                    two_recv.at[index, way, 0],
                    at[name],
                ),
            )

    def step_two(index):
        ones, twos = held(index, one_t, one_s), held(index, two_t, two_s)
        for way, (name, other, first) in enumerate((("x", "y", 0), ("y", "x", 2))):
            landing = ones.at[way]
            remote(
                landing, landing, one_send.at[index, way], one_recv.at[index, way], at[name]
            ).wait_recv()
            target = cut(index, at["chip_" + other], first, 2)
            add_into(target, landing)
            launch(
                index,
                remote(
                    target,
                    twos.at[1 - way, :, pl.ds(first, 2)],
                    two_send.at[index, 1 - way, 1],
                    two_recv.at[index, 1 - way, 1],
                    at[other],
                ),
            )

    def step_three(index):
        twos = held(index, two_t, two_s)
        for way, (name, first) in enumerate((("x", 0), ("y", 2))):
            for turn, begin in enumerate((first, 2 - first)):
                landing = twos.at[way, :, pl.ds(begin, 2)]
                remote(
                    landing,
                    landing,
                    two_send.at[index, way, turn],
                    two_recv.at[index, way, turn],
                    at[name],
                ).wait_recv()
        own = cut(index, chip, 0, 4)
        leads = own.shape[0]

        def body(turn, carry):
            where = (0, turn) if leads == 1 else (turn,)
            own[where] = (
                own[where].astype(F32)
                + twos.at[0][where].astype(F32)
                + twos.at[1][where].astype(F32)
            ).astype(BF16)
            return carry

        lax.fori_loop(0, 4 if leads == 1 else leads, body, 0)
        lines = held(index, line_t, line_s)
        for step in (1, 3, 2):
            peer = line_peer(at, step)
            launch(
                index,
                remote(
                    cut(index, chip, peer[1], 1),
                    lines.at[step - 1],
                    line_send.at[index, step - 1],
                    line_recv.at[index, step - 1],
                    peer,
                ),
            )

    def step_four(index):
        lines, fin = held(index, line_t, line_s), held(index, fin_t, fin_s)
        for step in (1, 2, 3):
            landing = lines.at[step - 1]
            remote(
                landing,
                landing,
                line_send.at[index, step - 1],
                line_recv.at[index, step - 1],
                line_peer(at, step),
            ).wait_recv()
        total = cut(index, chip, line, 1)[...].astype(F32)
        for step in range(3):
            total = total + lines[step].astype(F32)
        fin[0] = total
        fin_copies[index] = launch(
            index,
            remote(fin.at[0], fin.at[1], fin_send.at[index], fin_recv.at[index], at["pair"]),
        )

    adam_saves = {"s": [], "t": []}
    adam_loads = {}

    def adam_moves(index, load):
        kind, unit, lead, _ = CHUNKS[index]
        moves = []
        for which in range(2):
            if kind == "s":
                arrays = (sp_in, sm_in, sv_in) if load else (sp_out, sm_out, sv_out)
                half = core if which == 0 else 1 - core
                rows = pl.ds(pl.multiple_of(half * HALF + SUB * lead, 16), SUB)
                for array, ref in enumerate(arrays):
                    here, there = adam_s.at[array, which], ref.at[unit, rows]
                    moves.append((there, here) if load else (here, there))
            elif which == 0:
                arrays = (tp_in, tm_in, tv_in) if load else (tp_out, tm_out, tv_out)
                for array, ref in enumerate(arrays):
                    here, there = adam_t.at[array], ref.at[unit]
                    moves.append((there, here) if load else (here, there))
        sems = adam_load if load else adam_save
        row = 0 if kind == "s" else 1
        return [
            pltpu.make_async_copy(source, target, sems.at[row, number])
            for number, (source, target) in enumerate(moves)
        ]

    def adam_fetch(index):
        kind = CHUNKS[index][0]
        for copy in adam_saves[kind]:
            copy.wait()
        adam_saves[kind] = []
        adam_loads[index] = adam_moves(index, True)
        for copy in adam_loads[index]:
            copy.start()

    def step_five(index):
        kind, unit, lead, leads = CHUNKS[index]
        adam_fetch(index)
        fin_copies[index].wait_recv()
        fin = held(index, fin_t, fin_s)
        for copy in adam_loads[index]:
            copy.wait()
        if kind == "s":
            width = CHIP_S // 2
            for which in range(2):
                value = fin[which, 0, 0]
                grad = jnp.where(core == 0, value[:, :width], value[:, width:])
                fresh = adam_update(
                    adam_s[0, which],
                    adam_s[1, which],
                    adam_s[2, which],
                    grad,
                    RATE_CONV,
                    DECAY_CONV,
                )
                for array in range(3):
                    adam_s[array, which] = fresh[array]
        else:
            width = CHIP_T // 2
            for tau in range(3):
                both = [
                    fin[which, 3 * tau : 3 * tau + 3].reshape(HALF, CHIP_T) for which in range(2)
                ]
                first = jnp.where(core == 0, both[0], both[1])
                second = jnp.where(core == 0, both[1], both[0])
                turned = jnp.concatenate([first, second], axis=0).T
                grad = jnp.where(core == 0, turned[:width], turned[width:])
                fresh = adam_update(
                    adam_t[0, tau], adam_t[1, tau], adam_t[2, tau], grad, RATE_CONV, DECAY_CONV
                )
                for array in range(3):
                    adam_t[array, tau] = fresh[array]
        adam_saves[kind] = adam_moves(index, False)
        for copy in adam_saves[kind]:
            copy.start()

    def fetch_w(unit, tap, slot):
        lanes = pl.ds(pl.multiple_of(tap * BLOCK_C, 128), BLOCK_C)
        return pltpu.make_async_copy(ws.at[unit, :, lanes], w_buf.at[slot], w_sem.at[slot])

    def fetch_wt(unit, tau, slot):
        return pltpu.make_async_copy(wt.at[unit, tau], w_buf.at[slot], w_sem.at[slot])

    def window(tap):
        return a_pad[pl.ds(tap // 3, SIDE), pl.ds(tap % 3, SIDE)].reshape(ROWS, BLOCK_C)

    zero_mid = jnp.zeros((SLOTS, MID_C), F32)
    zero_out = jnp.zeros((SLOTS, BLOCK_C), F32)

    def out_norm_back(unit, *hooks):
        grad_ref = skip_ref if unit == 1 else side
        gain = par[4 + 2 * unit : 5 + 2 * unit, :BLOCK_C]
        inverse = stat_out[2 * unit : 2 * unit + 1]
        total = stat_out[2 * unit + 1 : 2 * unit + 2]

        def out_sums(p, carry):
            rows = rows_of(p)
            grad = grad_ref[rows, :].astype(F32)
            return (carry[0] + grad, carry[1] + grad * t_ref[rows, :])

        bias_acc, gain_acc = over_pixels(out_sums, (zero_out, zero_out))
        sums = [
            jnp.sum(bias_acc, axis=0, keepdims=True),
            jnp.sum(gain_acc, axis=0, keepdims=True),
        ]
        grad_bias, grad_gain = exchange(
            at, land_out, land_out_two, unit, sems, 2 * unit, sums, combine_sums, hooks
        )
        out_grad[2 * unit : 2 * unit + 1, :] = grad_gain
        out_grad[2 * unit + 1 : 2 * unit + 2, :] = grad_bias
        scale = gain * inverse
        bias_part, gain_part = grad_bias / total, grad_gain / total

        def out_back(p, carry):
            rows = rows_of(p)
            value = (
                mask_out
                * scale
                * (grad_ref[rows, :].astype(F32) - bias_part - t_ref[rows, :] * gain_part)
            )
            d_ref[1, rows, :] = value.astype(BF16)
            d_ref[0, rows, :] = (pltpu.roll(value, 12, 0) * has_after).astype(BF16)
            d_ref[2, rows, :] = (pltpu.roll(value, 4, 0) * has_before).astype(BF16)
            return carry

        over_pixels(out_back, 0)

    def temporal_grad():
        for tau in range(3):
            g_t[3 * tau : 3 * tau + 3] = (
                lax.dot_general(u_ref[...], d_ref[tau], TN, preferred_element_type=F32)
                .astype(BF16)
                .reshape(3, 4, 2, SUB, BLOCK_C)
            )

    def temporal_back(unit):
        for tau in range(3):
            slot = tau % 2
            if tau < 2:
                fetch_wt(unit, tau + 1, 1 - slot).start()
            fetch_wt(unit, tau, slot).wait()
            value = lax.dot_general(d_ref[tau], w_buf[slot], NT, preferred_element_type=F32)
            wide[...] = value if tau == 0 else wide[...] + value

    def mid_norm_back(unit, *hooks):
        gain = par[2 * unit : 2 * unit + 1]
        bias = par[2 * unit + 1 : 2 * unit + 2]
        inverse = stat_mid[2 * unit : 2 * unit + 1]
        total = stat_mid[2 * unit + 1 : 2 * unit + 2]

        def mid_sums(p, carry):
            rows = rows_of(p)
            standard = s_ref[rows, :].astype(F32)
            grad = mask_mid * slope_of(standard * gain + bias) * wide[rows, :]
            wide[rows, :] = grad
            return (carry[0] + grad, carry[1] + grad * standard)

        bias_acc, gain_acc = over_pixels(mid_sums, (zero_mid, zero_mid))
        sums = [
            jnp.sum(bias_acc, axis=0, keepdims=True),
            jnp.sum(gain_acc, axis=0, keepdims=True),
        ]
        grad_bias, grad_gain = exchange(
            at, land_mid, land_mid_two, unit, sems, 2 * unit + 1, sums, combine_sums, hooks
        )
        mid_grad[2 * unit : 2 * unit + 1, :] = grad_gain
        mid_grad[2 * unit + 1 : 2 * unit + 2, :] = grad_bias
        scale = gain * inverse
        bias_part, gain_part = grad_bias / total, grad_gain / total

        def mid_back(p, carry):
            rows = rows_of(p)
            value = (
                mask_mid
                * scale
                * (wide[rows, :] - bias_part - s_ref[rows, :].astype(F32) * gain_part)
            )
            ds_pad[1 + p // SIDE, 1 + p % SIDE] = value.astype(BF16)
            return carry

        over_pixels(mid_back, 0)

    def spatial_grad(third):
        columns = slice(third * THIRD, (third + 1) * THIRD)

        def body(row, carry):
            inner = ds_pad[1 : 1 + SIDE, 1 : 1 + SIDE, :, columns].reshape(ROWS, THIRD)
            taps = jnp.concatenate([window(3 * row + column) for column in range(3)], axis=1)
            lanes = pl.ds(pl.multiple_of(row * 3 * BLOCK_C, 128), 3 * BLOCK_C)
            g_s[third, 0, :, :, :, lanes] = (
                lax.dot_general(inner, taps, TN, preferred_element_type=F32)
                .astype(BF16)
                .reshape(4, 2, SUB, 3 * BLOCK_C)
            )
            return carry

        lax.fori_loop(0, 3, body, 0)

    def spatial_back(unit, first):
        if first == 0:
            fetch_w(unit, 0, 0).start()

        def body(tap, carry):
            slot = lax.rem(tap, 2)

            @pl.when(tap < 8)
            def _():
                fetch_w(unit, tap + 1, 1 - slot).start()

            fetch_w(unit, tap, slot).wait()
            moved = ds_pad[pl.ds(2 - tap // 3, SIDE), pl.ds(2 - tap % 3, SIDE)].reshape(ROWS, MID_C)
            value = lax.dot_general(moved, w_buf[slot], NN, preferred_element_type=F32)

            @pl.when(tap == 0)
            def _():
                side[...] = value

            @pl.when(tap > 0)
            def _():
                side[...] = side[...] + value

            return carry

        lax.fori_loop(first, first + 3, body, 0)

    a_0, b_0, c_0, t_0, a_1, b_1, c_1, t_1 = range(N_CHUNKS)

    load_t[1].wait()
    load_skip.wait()
    fetch_wt(1, 0, 0).start()
    out_norm_back(1, None, None)
    load_t[0].start()
    load_u[1].wait()
    temporal_grad()
    load_u[0].start()
    step_pair(t_1)
    temporal_back(1)
    load_s[1].wait()
    own_acts = []
    mid_norm_back(
        1,
        lambda: step_one(t_1),
        lambda: own_acts.append(acts(0, block_in, block_out)),
    )
    load_s[0].start()
    load_a[1].wait()
    spatial_grad(0)
    step_pair(a_1)
    step_two(t_1)
    spatial_grad(1)
    step_pair(b_1)
    step_one(a_1)
    spatial_grad(2)
    load_a[0].start()
    step_pair(c_1)
    step_three(t_1)
    step_one(b_1)
    step_two(a_1)
    spatial_back(1, 0)
    step_four(t_1)
    spatial_back(1, 3)
    spatial_back(1, 6)
    load_t[0].wait()
    gain, bias = par[4:5, :BLOCK_C], par[5:6, :BLOCK_C]

    def hidden_back(p, carry):
        rows = rows_of(p)
        slope = slope_of(t_ref[rows, :] * gain + bias)
        side[rows, :] = mask_out * slope * side[rows, :]
        return carry

    over_pixels(hidden_back, 0)
    fetch_wt(0, 0, 0).start()

    def hook_a():
        step_one(c_1)
        step_two(b_1)

    out_norm_back(0, hook_a, lambda: step_three(a_1))
    drain(t_1)
    load_u[0].wait()
    temporal_grad()
    load_shuffle.start()
    step_pair(t_0)
    temporal_back(0)
    step_two(c_1)
    step_five(t_1)
    load_s[0].wait()
    mid_norm_back(0, lambda: step_one(t_0), lambda: step_three(b_1))
    load_a[0].wait()
    step_four(a_1)
    drain(a_1)
    spatial_grad(0)
    step_pair(a_0)
    step_two(t_0)
    step_three(c_1)
    step_five(a_1)
    step_four(b_1)
    spatial_back(0, 0)
    step_one(a_0)
    spatial_back(0, 3)
    spatial_back(0, 6)
    step_three(t_0)
    step_two(a_0)
    load_shuffle.wait()
    d_ref[0] = (side[...] + skip_ref[...].astype(F32)).astype(BF16)
    thin = d_ref.at[1]
    thin[...] = lax.dot_general(
        u_ref[:, :SHUFFLE_C], d_ref[0], TN, preferred_element_type=F32
    ).astype(BF16)[:ROWS]
    own_acts.append(acts(1, thin, input_out))
    drain(b_1)
    spatial_grad(1)
    step_pair(b_0)
    step_five(b_1)
    step_four(c_1)
    step_one(b_0)
    drain(c_1)
    spatial_grad(2)
    step_pair(c_0)
    step_three(a_0)
    step_five(c_1)
    step_four(t_0)
    step_one(c_0)
    step_two(b_0)
    step_five(t_0)
    step_two(c_0)
    step_four(a_0)
    step_three(b_0)
    step_five(a_0)
    step_three(c_0)
    step_four(b_0)
    step_five(b_0)
    step_four(c_0)
    step_five(c_0)
    acts_wait(0, block_in, block_out, own_acts[0])
    acts_wait(1, thin, input_out, own_acts[1])
    for kind in ("s", "t"):
        for copy in adam_saves[kind]:
            copy.wait()
    for copy in act_copies:
        copy.wait_send()
    for index in (t_0, a_0, b_0, c_0):
        drain(index)


def spaces(text):
    kinds = {"v": VMEM, "a": pl.ANY, "s": pltpu.SMEM}
    return [pl.BlockSpec(memory_space=kinds[mark]) for mark in text]


def dma(*shape):
    return pltpu.SemaphoreType.DMA(shape)


def params(number):
    return pltpu.CompilerParams(
        collective_id=number, has_side_effects=True, vmem_limit_bytes=GRANT
    )


def shaped(*shape, dtype=BF16):
    return jax.ShapeDtypeStruct(shape, dtype)


def run_forward(*args):
    padded = (SIDE + 2, SIDE + 2, SLOTS, BLOCK_C)
    return pl.pallas_call(
        forward_kernel,
        out_shape=[
            shaped(2, 3, 4, 2, SUB, TAPS_C),
            shaped(2, 9, 4, 2, SUB, BLOCK_C),
            shaped(8, MID_C, dtype=F32),
            shaped(SLOTS, MID_C, dtype=F32),
            shaped(ROWS, BLOCK_C),
            shaped(2, *padded),
            shaped(2, ROWS, MID_C),
            shaped(2, ROWS, MID_C),
            shaped(2, ROWS, BLOCK_C, dtype=F32),
            shaped(ROWS, BLOCK_C),
            shaped(4, MID_C, dtype=F32),
            shaped(4, BLOCK_C, dtype=F32),
        ],
        in_specs=spaces("vvaavvsv"),
        out_specs=spaces("aavvvaaaaavv"),
        scratch_shapes=[
            VMEM((2, 2 * HALF, CHIP_S // 2), BF16),
            VMEM((2, 2 * HALF, 3 * CHIP_T // 2), BF16),
            VMEM((4 * ROWS, 128), F32),
            VMEM((4 * ROWS, 128), BF16),
            VMEM((8, MID_C), F32),
            VMEM((2, HALF, CHIP_S // 2), BF16),
            VMEM((2, HALF, 3 * CHIP_T // 2), BF16),
            VMEM((2, 3, 1, SUB, CHIP_S), BF16),
            VMEM((2, 9, 1, SUB, CHIP_T), BF16),
            VMEM((ROWS, BLOCK_C), BF16),
            VMEM((ROWS, BLOCK_C), BF16),
            VMEM((4, 8, MID_C), F32),
            VMEM((2,) + padded, BF16),
            VMEM((ROWS, MID_C), F32),
            VMEM((2, ROWS, MID_C), BF16),
            VMEM((2, ROWS, MID_C), BF16),
            VMEM((2, ROWS, BLOCK_C), F32),
            VMEM((2, ROWS, BLOCK_C), F32),
            VMEM((ROWS, BLOCK_C), BF16),
            VMEM((ROWS, BLOCK_C), BF16),
            VMEM((2, 4, 2, SUB, TAPS_C), BF16),
            VMEM((9, 4, 2, SUB, BLOCK_C), BF16),
            VMEM((2, 8, 8, MID_C), F32),
            VMEM((2, 4, 8, MID_C), F32),
            VMEM((2, 8, 8, BLOCK_C), F32),
            VMEM((2, 4, 8, BLOCK_C), F32),
            VMEM((8, 8, 128), F32),
            VMEM((8, 8, MID_C), F32),
            VMEM((4, 8, MID_C), F32),
            dma(4),
            dma(4),
            dma(3, 3),
            dma(3, 3),
            dma(N_CHUNKS, 3),
            dma(N_CHUNKS, 3),
            dma(N_CHUNKS, 2, 2),
            dma(N_CHUNKS, 2, 2),
            dma(N_CHUNKS, 2),
            dma(N_CHUNKS, 2),
            dma(N_CHUNKS, 4),
            dma(N_CHUNKS, 4),
            dma(3),
            dma(N_CHUNKS),
            dma(2, 4),
            dma(5),
            dma(10),
            dma(5, 7),
            dma(5, 7),
            dma(5, 3),
            dma(5, 3),
        ],
        compiler_params=params(0),
        name="forward",
    )(*args)


def run_backward(*args):
    return pl.pallas_call(
        backward_kernel,
        out_shape=[
            *[shaped(2, 2 * HALF, CHIP_S // 2, dtype=F32)] * 3,
            *[shaped(2, 3, CHIP_T // 2, 2 * HALF, dtype=F32)] * 3,
            shaped(4, MID_C, dtype=F32),
            shaped(4, BLOCK_C, dtype=F32),
            shaped(4 * ROWS, 128),
            shaped(4 * ROWS, 128),
        ],
        in_specs=spaces("aaaaaaavvvvaaaaaaaa"),
        out_specs=spaces("aaaaaavvaa"),
        scratch_shapes=[
            VMEM((SIDE + 2, SIDE + 2, SLOTS, BLOCK_C), BF16),
            VMEM((ROWS, MID_C), BF16),
            VMEM((ROWS, MID_C), BF16),
            VMEM((ROWS, BLOCK_C), F32),
            VMEM((ROWS, BLOCK_C), F32),
            VMEM((ROWS, BLOCK_C), BF16),
            VMEM((ROWS, MID_C), F32),
            VMEM((SIDE + 2, SIDE + 2, SLOTS, MID_C), BF16),
            VMEM((3, ROWS, BLOCK_C), BF16),
            VMEM((2, MID_C, BLOCK_C), BF16),
            VMEM((2, 8, 8, MID_C), F32),
            VMEM((2, 4, 8, MID_C), F32),
            VMEM((2, 8, 8, BLOCK_C), F32),
            VMEM((2, 4, 8, BLOCK_C), F32),
            VMEM((3, 1, 4, 2, SUB, TAPS_C), BF16),
            VMEM((9, 4, 2, SUB, BLOCK_C), BF16),
            VMEM((3, 1, 4, SUB, TAPS_C), BF16),
            VMEM((9, 4, SUB, BLOCK_C), BF16),
            VMEM((2, 3, 2, 1, 2, SUB, CHIP_S), BF16),
            VMEM((2, 2, 9, 2, SUB, CHIP_T), BF16),
            VMEM((2, 3, 2, 1, 4, SUB, CHIP_S), BF16),
            VMEM((2, 2, 9, 4, SUB, CHIP_T), BF16),
            VMEM((2, 3, 3, 1, 1, SUB, CHIP_S), BF16),
            VMEM((2, 3, 9, 1, SUB, CHIP_T), BF16),
            VMEM((2, 3, 2, 1, 1, SUB, CHIP_S), F32),
            VMEM((2, 2, 9, 1, SUB, CHIP_T), F32),
            VMEM((3, 2, SUB, CHIP_S // 2), F32),
            VMEM((3, 3, CHIP_T // 2, 2 * HALF), F32),
            dma(6),
            dma(2),
            dma(4, 7),
            dma(4, 7),
            dma(4, 3),
            dma(4, 3),
            dma(2, 3),
            dma(2, 3),
            dma(2),
            dma(N_CHUNKS),
            dma(N_CHUNKS),
            dma(N_CHUNKS, 2),
            dma(N_CHUNKS, 2),
            dma(N_CHUNKS, 2, 2),
            dma(N_CHUNKS, 2, 2),
            dma(N_CHUNKS, 3),
            dma(N_CHUNKS, 3),
            dma(N_CHUNKS),
            dma(N_CHUNKS),
            dma(2, 6),
            dma(2, 6),
        ],
        compiler_params=params(1),
        name="backward",
    )(*args)


def finish_kernel(
    frames_in,
    mid_p,
    mid_m,
    mid_v,
    out_p,
    out_m,
    out_v,
    sp_in,
    sm_in,
    sv_in,
    tp_in,
    tm_in,
    tv_in,
    mid_all,
    out_all,
    block_in,
    grad_in,
    block_out,
    clip_pool,
    grad_out,
    mid_p_out,
    mid_m_out,
    mid_v_out,
    out_p_out,
    out_m_out,
    out_v_out,
    sp_out,
    sm_out,
    sv_out,
    tp_out,
    tm_out,
    tv_out,
    block_ref,
    grad_ref,
    block_wide,
    grad_wide,
    hold_s,
    hold_t,
    sems,
):
    line = lax.axis_index("chan")
    loads = [
        pltpu.make_async_copy(block_in, block_ref, sems.at[0]),
        pltpu.make_async_copy(grad_in, grad_ref, sems.at[1]),
    ]
    passing = (
        (sp_in, hold_s.at[0], sp_out),
        (sm_in, hold_s.at[1], sm_out),
        (sv_in, hold_s.at[2], sv_out),
        (tp_in, hold_t.at[0], tp_out),
        (tm_in, hold_t.at[1], tm_out),
        (tv_in, hold_t.at[2], tv_out),
    )
    gets = [
        pltpu.make_async_copy(source, held, sems.at[2 + number])
        for number, (source, held, _) in enumerate(passing)
    ]
    puts = [
        pltpu.make_async_copy(held, target, sems.at[10 + number])
        for number, (_, held, target) in enumerate(passing)
    ]
    for copy in loads + gets:
        copy.start()
    stores = [
        pltpu.make_async_copy(block_wide, block_out, sems.at[8]),
        pltpu.make_async_copy(grad_wide, grad_out, sems.at[9]),
    ]
    loads[0].wait()
    block_wide[...] = block_ref[...].astype(F32)
    stores[0].start()
    loads[1].wait()
    grad_wide[...] = grad_ref[...].astype(F32)
    stores[1].start()
    for get, put in zip(gets, puts):
        get.wait()
        put.start()
    size = FRAMES * HW
    for clip in range(clip_pool.shape[0]):
        total = jnp.sum(block_wide[clip * size : (clip + 1) * size, :], axis=0, keepdims=True)
        kept = lax.div(frames_in[clip], 8).astype(F32)
        clip_pool[clip : clip + 1, :] = total / (HW * kept)
    all_rows = jnp.concatenate([mid_all[...], jnp.zeros((4, MID_C), F32)], axis=0)
    turned = pltpu.roll(all_rows, lax.rem(MID_C - line * (2 * SUB), MID_C), 1)[0:4]
    grad = jnp.concatenate(
        [
            turned[:, third * THIRD + half * SUB : third * THIRD + (half + 1) * SUB]
            for half in range(2)
            for third in range(3)
        ],
        axis=1,
    )
    fresh = adam_update(mid_p[...], mid_m[...], mid_v[...], grad, RATE_NORM, 0.0)
    for ref, value in zip((mid_p_out, mid_m_out, mid_v_out), fresh):
        ref[...] = value
    grad = out_all[:, pl.ds(pl.multiple_of(line * 128, 128), 128)]
    fresh = adam_update(out_p[...], out_m[...], out_v[...], grad, RATE_NORM, 0.0)
    for ref, value in zip((out_p_out, out_m_out, out_v_out), fresh):
        ref[...] = value
    for copy in stores + puts:
        copy.wait()


def run_finish(frames, *args):
    convs = args[6:12]
    norms = args[:6]
    clips = frames.shape[0]
    return pl.pallas_call(
        finish_kernel,
        out_shape=[
            shaped(4 * ROWS, 128, dtype=F32),
            shaped(clips, 128, dtype=F32),
            shaped(4 * ROWS, 128, dtype=F32),
            *[shaped(*v.shape, dtype=F32) for v in norms],
            *[shaped(*v.shape, dtype=F32) for v in convs],
        ],
        in_specs=spaces("svvvvvvaaaaaavvaa"),
        out_specs=spaces("avavvvvvvaaaaaa"),
        scratch_shapes=[
            VMEM((4 * ROWS, 128), BF16),
            VMEM((4 * ROWS, 128), BF16),
            VMEM((4 * ROWS, 128), F32),
            VMEM((4 * ROWS, 128), F32),
            VMEM((3,) + convs[0].shape, F32),
            VMEM((3,) + convs[3].shape, F32),
            dma(16),
        ],
        compiler_params=pltpu.CompilerParams(vmem_limit_bytes=GRANT),
        name="finish",
    )(frames, *args)


def shuffle_matrix():
    clip, frame, pixel = np.meshgrid(np.arange(4), np.arange(FRAMES), np.arange(HW), indexing="ij")
    source = (clip * FRAMES + frame) * HW + pixel
    target = pixel * SLOTS + frame * 4 + clip
    matrix = np.zeros((ROWS, SHUFFLE_C), np.float32)
    matrix[target.reshape(-1), source.reshape(-1)] = 1.0
    return jnp.asarray(matrix, BF16)


def on_pairs(
    features,
    cotangent,
    clip_frames,
    spatial_master,
    spatial_first,
    spatial_second,
    temporal_master,
    temporal_first,
    temporal_second,
    mid_norm,
    mid_first,
    mid_second,
    out_norm,
    out_first,
    out_second,
):
    line = lax.axis_index("chan")
    spatial_own = [jnp.swapaxes(v, 1, 2) for v in (spatial_master, spatial_first, spatial_second)]
    temporal_own = [
        jnp.swapaxes(v, 2, 3) for v in (temporal_master, temporal_first, temporal_second)
    ]
    shuffle = shuffle_matrix()
    ws, wt, par, mask, block, a_all, s_all, u_all, t_all, skip, stat_mid, stat_out = run_forward(
        spatial_own[0],
        temporal_own[0],
        features,
        cotangent,
        mid_norm,
        out_norm,
        clip_frames,
        shuffle,
    )
    conv_new = run_backward(
        ws.reshape(2, MID_C, TAPS_C),
        wt.reshape(2, 3, MID_C, BLOCK_C),
        a_all,
        s_all,
        u_all,
        t_all,
        skip,
        stat_mid,
        stat_out,
        par,
        mask,
        shuffle,
        block,
        *spatial_own,
        *temporal_own,
    )
    block_out, clip_pool, grad_out, *rest = run_finish(
        clip_frames, mid_norm, mid_first, mid_second, out_norm, out_first, out_second, *conv_new
    )
    norms, convs = rest[:6], rest[6:]
    spatial = [jnp.swapaxes(v, 1, 2) for v in convs[:3]]
    temporal = [jnp.swapaxes(v, 2, 3) for v in convs[3:]]
    return (block_out, clip_pool, grad_out, *spatial, *temporal, *norms)


def solution(mesh):
    in_specs = (
        P("dp", "chan"),
        P("dp", "chan"),
        P("dp"),
        P(None, "dp", "chan"),
        P(None, "dp", "chan"),
        P(None, "dp", "chan"),
        P(None, None, "chan", "dp"),
        P(None, None, "chan", "dp"),
        P(None, None, "chan", "dp"),
        P(None, "chan"),
        P(None, "chan"),
        P(None, "chan"),
        P(None, "chan"),
        P(None, "chan"),
        P(None, "chan"),
    )
    out_specs = (
        P("dp", "chan"),
        P("dp", "chan"),
        P("dp", "chan"),
        P(None, "dp", "chan"),
        P(None, "dp", "chan"),
        P(None, "dp", "chan"),
        P(None, None, "chan", "dp"),
        P(None, None, "chan", "dp"),
        P(None, None, "chan", "dp"),
        P(None, "chan"),
        P(None, "chan"),
        P(None, "chan"),
        P(None, "chan"),
        P(None, "chan"),
        P(None, "chan"),
    )
    body = on_pairs if mesh.shape["dp"] == 8 and mesh.shape["chan"] == 4 else on_device
    return jax.shard_map(
        body, mesh=mesh, in_specs=in_specs, out_specs=out_specs, check_vma=False
    )
```

```python
import jax
import jax.numpy as jnp
import numpy as np
from jax import lax
from jax.experimental import pallas as pl
from jax.experimental.pallas import tpu as pltpu
from jax.sharding import PartitionSpec as P

FRAMES = 4
SIDE = 7
STEP = 10
HW = 49


EPS_NORM = 1e-05
EPS_ADAM = 1e-08
BETA_ONE = 0.9
BETA_TWO = 0.95
RATE_CONV = 0.01
RATE_NORM = 0.8
DECAY_CONV = 0.05


def frame_mask(clip_frames):
    kept_frames = clip_frames // 8
    frame_ids = jnp.arange(FRAMES, dtype=jnp.int32)
    frame_grid = (frame_ids[None, :] < kept_frames[:, None]).astype(jnp.float32)
    return jnp.broadcast_to(frame_grid[:, :, None], (kept_frames.shape[0], FRAMES, HW)).reshape(
        -1, 1
    )


def silu_slope(values):
    sigmoid = jax.nn.sigmoid(values)
    return sigmoid * (1.0 + values * (1.0 - sigmoid))


def spatial_apply(inputs, tap_weights):
    channels = inputs.shape[1]
    padded = jnp.pad(inputs.reshape(-1, SIDE, SIDE, channels), ((0, 0), (1, 1), (1, 1), (0, 0)))
    summed = jnp.zeros((inputs.shape[0], tap_weights.shape[2]), jnp.float32)
    for tap_index in range(9):
        row_off, col_off = (tap_index // 3, tap_index % 3)
        window = padded[:, row_off : row_off + SIDE, col_off : col_off + SIDE].reshape(-1, channels)
        summed = summed + jnp.dot(
            window, tap_weights[tap_index], preferred_element_type=jnp.float32
        )
    return (summed, padded)


def spatial_grads(padded, tap_weights, grad_out):
    channels = padded.shape[3]
    weight_terms = []
    input_sum = jnp.zeros((padded.shape[0], SIDE, SIDE, channels), jnp.float32)
    for tap_index in range(9):
        row_off, col_off = (tap_index // 3, tap_index % 3)
        window = padded[:, row_off : row_off + SIDE, col_off : col_off + SIDE].reshape(-1, channels)
        weight_terms.append(
            lax.dot_general(
                window, grad_out, (((0,), (0,)), ((), ())), preferred_element_type=jnp.float32
            )
        )
        pulled = lax.dot_general(
            grad_out,
            tap_weights[tap_index],
            (((1,), (1,)), ((), ())),
            preferred_element_type=jnp.float32,
        )
        pulled = jnp.pad(pulled.reshape(-1, SIDE, SIDE, channels), ((0, 0), (1, 1), (1, 1), (0, 0)))
        input_sum = (
            input_sum
            + pulled[:, 2 - row_off : 2 - row_off + SIDE, 2 - col_off : 2 - col_off + SIDE]
        )
    return (jnp.stack(weight_terms).reshape(-1, grad_out.shape[1]), input_sum.reshape(-1, channels))


def temporal_apply(inputs, weight):
    frame_seq = inputs.reshape(-1, FRAMES, HW, inputs.shape[1])
    padded = jnp.pad(frame_seq, ((0, 0), (1, 1), (0, 0), (0, 0)))
    summed = jnp.zeros(frame_seq.shape[:3] + (weight.shape[2],), jnp.float32)
    for frame_off in range(3):
        summed = summed + jnp.einsum(
            "nfpm,mc->nfpc",
            padded[:, frame_off : frame_off + FRAMES],
            weight[frame_off],
            preferred_element_type=jnp.float32,
        )
    return (summed.reshape(inputs.shape[0], -1), padded)


def temporal_grads(padded, weight, grad_full):
    grad_seq = grad_full.reshape(-1, FRAMES, HW, grad_full.shape[1])
    grad_pad = jnp.pad(grad_seq, ((0, 0), (1, 1), (0, 0), (0, 0)))
    weight_terms = []
    input_sum = jnp.zeros(padded.shape[:1] + (FRAMES, HW, padded.shape[3]), jnp.float32)
    for frame_off in range(3):
        weight_terms.append(
            jnp.einsum(
                "nfpm,nfpc->mc",
                padded[:, frame_off : frame_off + FRAMES],
                grad_seq,
                preferred_element_type=jnp.float32,
            )
        )
        input_sum = input_sum + jnp.einsum(
            "nfpc,mc->nfpm",
            grad_pad[:, 2 - frame_off : 2 - frame_off + FRAMES],
            weight[frame_off],
            preferred_element_type=jnp.float32,
        )
    return (jnp.stack(weight_terms), input_sum.reshape(grad_full.shape[0], -1))


def normalize(values, validity, gain_row, bias_row):
    local_valid = jnp.sum(validity)
    total_valid, value_sums = lax.psum((local_valid, jnp.sum(values * validity, axis=0)), "dp")
    average = value_sums / total_valid
    centered = values - average
    variance = lax.psum(jnp.sum(validity * centered * centered, axis=0), "dp") / total_valid
    inverse = lax.rsqrt(variance + EPS_NORM)
    standard = centered * inverse
    return (standard * gain_row + bias_row, standard, inverse, total_valid)


def normalize_back(grad_normed, standard, inverse, gain_row, total_valid, validity):
    grad_bias, grad_gain = lax.psum(
        (
            jnp.sum(grad_normed * validity, axis=0),
            jnp.sum(grad_normed * standard * validity, axis=0),
        ),
        "dp",
    )
    grad_values = (
        validity
        * gain_row
        * inverse
        * (grad_normed - grad_bias / total_valid - standard * grad_gain / total_valid)
    )
    return (grad_values, grad_gain, grad_bias)


def adam_update(weight, moment_one, moment_two, grad_value, rate, decay):
    fresh_one = BETA_ONE * moment_one + (1.0 - BETA_ONE) * grad_value
    fresh_two = BETA_TWO * moment_two + (1.0 - BETA_TWO) * grad_value * grad_value
    scaled = (
        fresh_one
        / (1.0 - BETA_ONE**STEP)
        / (jnp.sqrt(fresh_two / (1.0 - BETA_TWO**STEP)) + EPS_ADAM)
    )
    return (weight - rate * (scaled + decay * weight), fresh_one, fresh_two)


def on_device(
    features,
    cotangent,
    clip_frames,
    spatial_master,
    spatial_first,
    spatial_second,
    temporal_master,
    temporal_first,
    temporal_second,
    mid_norm,
    mid_first,
    mid_second,
    out_norm,
    out_first,
    out_second,
):
    validity = frame_mask(clip_frames)
    spatial_all, temporal_all = (
        lax.all_gather(spatial_master.astype(jnp.bfloat16), "dp", axis=1, tiled=True),
        lax.all_gather(temporal_master.astype(jnp.bfloat16), "dp", axis=3, tiled=True),
    )
    channels = temporal_all.shape[3]
    spatial_taps = spatial_all.reshape(2, 9, channels, spatial_all.shape[2])
    residual = features.astype(jnp.float32)
    outgoing = features
    kept_state = []
    for unit_index in range(2):
        gathered = lax.all_gather(outgoing, "chan", axis=1, tiled=True)
        spatial_out, padded = spatial_apply(gathered, spatial_taps[unit_index])
        mid_normed, mid_standard, mid_inverse, total_valid = normalize(
            spatial_out, validity, mid_norm[2 * unit_index], mid_norm[2 * unit_index + 1]
        )
        temporal_in = (jax.nn.silu(mid_normed) * validity).astype(jnp.bfloat16)
        partial_value, frames_padded = temporal_apply(temporal_in, temporal_all[unit_index])
        temporal_out = lax.psum_scatter(
            partial_value.astype(jnp.bfloat16), "chan", scatter_dimension=1, tiled=True
        ).astype(jnp.float32)
        out_normed, out_standard, out_inverse, total_valid = normalize(
            temporal_out, validity, out_norm[2 * unit_index], out_norm[2 * unit_index + 1]
        )
        if unit_index == 0:
            pre_act = out_normed
            outgoing = (jax.nn.silu(pre_act) * validity).astype(jnp.bfloat16)
        else:
            pre_act = out_normed + residual
            block_out = jax.nn.silu(pre_act) * validity
        kept_state.append(
            (
                padded,
                mid_normed,
                mid_standard,
                mid_inverse,
                frames_padded,
                pre_act,
                out_standard,
                out_inverse,
            )
        )
    kept_frames = (clip_frames // 8).astype(jnp.float32)
    clip_pool = (
        jnp.sum(block_out.reshape(-1, FRAMES * HW, block_out.shape[1]), axis=1)
        / (HW * kept_frames)[:, None]
    )
    skip_grad = cotangent * validity * silu_slope(kept_state[1][5])
    grad_pre = skip_grad
    spatial_list = [None, None]
    temporal_list = [None, None]
    mid_rows = [None, None]
    out_rows = [None, None]
    grad_hidden = skip_grad
    for unit_index in (1, 0):
        (
            padded,
            mid_normed,
            mid_standard,
            mid_inverse,
            frames_padded,
            pre_act,
            out_standard,
            out_inverse,
        ) = kept_state[unit_index]
        if unit_index == 0:
            grad_pre = grad_hidden * validity * silu_slope(pre_act)
        grad_temporal, out_gain_grad, out_bias_grad = normalize_back(
            grad_pre, out_standard, out_inverse, out_norm[2 * unit_index], total_valid, validity
        )
        grad_full = lax.all_gather(grad_temporal.astype(jnp.bfloat16), "chan", axis=1, tiled=True)
        temporal_grad, grad_mid = temporal_grads(frames_padded, temporal_all[unit_index], grad_full)
        grad_mid_normed = grad_mid * validity * silu_slope(mid_normed)
        grad_spatial, mid_gain_grad, mid_bias_grad = normalize_back(
            grad_mid_normed,
            mid_standard,
            mid_inverse,
            mid_norm[2 * unit_index],
            total_valid,
            validity,
        )
        spatial_grad, grad_in_part = spatial_grads(
            padded, spatial_taps[unit_index], grad_spatial.astype(jnp.bfloat16)
        )
        grad_hidden = lax.psum_scatter(
            grad_in_part.astype(jnp.bfloat16), "chan", scatter_dimension=1, tiled=True
        ).astype(jnp.float32)
        spatial_list[unit_index] = spatial_grad
        temporal_list[unit_index] = temporal_grad
        mid_rows[unit_index] = (mid_gain_grad, mid_bias_grad)
        out_rows[unit_index] = (out_gain_grad, out_bias_grad)
    input_grad = grad_hidden + skip_grad
    spatial_sum, temporal_sum = (
        lax.psum_scatter(jnp.stack(spatial_list), "dp", scatter_dimension=1, tiled=True),
        lax.psum_scatter(jnp.stack(temporal_list), "dp", scatter_dimension=3, tiled=True),
    )
    mid_grad = jnp.stack([mid_rows[0][0], mid_rows[0][1], mid_rows[1][0], mid_rows[1][1]])
    out_grad = jnp.stack([out_rows[0][0], out_rows[0][1], out_rows[1][0], out_rows[1][1]])
    spatial_new, spatial_one, spatial_two = adam_update(
        spatial_master, spatial_first, spatial_second, spatial_sum, RATE_CONV, DECAY_CONV
    )
    temporal_new, temporal_one, temporal_two = adam_update(
        temporal_master, temporal_first, temporal_second, temporal_sum, RATE_CONV, DECAY_CONV
    )
    mid_new, mid_one, mid_two = adam_update(
        mid_norm, mid_first, mid_second, mid_grad, RATE_NORM, 0.0
    )
    out_new, out_one, out_two = adam_update(
        out_norm, out_first, out_second, out_grad, RATE_NORM, 0.0
    )
    return (
        block_out,
        clip_pool,
        input_grad,
        spatial_new,
        spatial_one,
        spatial_two,
        temporal_new,
        temporal_one,
        temporal_two,
        mid_new,
        mid_one,
        mid_two,
        out_new,
        out_one,
        out_two,
    )


F32 = jnp.float32
BF16 = jnp.bfloat16
MESH = pl.DeviceIdType.MESH
VMEM = pltpu.VMEM
NN = (((1,), (0,)), ((), ()))
NT = (((1,), (1,)), ((), ()))
TN = (((0,), (0,)), ((), ()))
BLOCK_C = 512
MID_C = 1152
THIRD = MID_C // 3
ROWS = 784
SLOTS = 16
SHUFFLE_C = 896
HALF = 144
SUB = 48
TAPS_C = 9 * BLOCK_C
CHIP_S = TAPS_C // 4
CHIP_T = BLOCK_C // 4
CHUNKS = (
    ("s", 0, 0, 1),
    ("s", 0, 1, 1),
    ("s", 0, 2, 1),
    ("t", 0, 0, 9),
    ("s", 1, 0, 1),
    ("s", 1, 1, 1),
    ("s", 1, 2, 1),
    ("t", 1, 0, 9),
)
N_CHUNKS = len(CHUNKS)
NEAR = ("chip", "chip_x", "chip_y", "chip_d")
PARTS = (("s", 0), ("t", 0), ("s", 1), ("t", 1))
GRANT = 65000 * 1024


def place():
    dp = lax.axis_index("dp")
    line = lax.axis_index("chan")
    core = lax.rem(dp, 2)
    chip = lax.div(dp, 2)
    x_bit = lax.rem(chip, 2)
    y_bit = lax.div(chip, 2)
    return dict(
        dp=dp,
        line=line,
        core=core,
        chip=chip,
        chip_x=chip + 1 - 2 * x_bit,
        chip_y=chip + 2 - 4 * y_bit,
        chip_d=3 - chip,
        pair=(dp + 1 - 2 * core, line),
        x=(dp + 2 - 4 * x_bit, line),
        y=(dp + 4 - 8 * y_bit, line),
    )


def remote(source, target, send, recv, device):
    return pltpu.make_async_remote_copy(
        src_ref=source,
        dst_ref=target,
        send_sem=send,
        recv_sem=recv,
        device_id=device,
        device_id_type=MESH,
    )


def greet(devices):
    barrier = pltpu.get_barrier_semaphore()
    for device in devices:
        pl.semaphore_signal(barrier, inc=1, device_id=device, device_id_type=MESH)
    pl.semaphore_wait(barrier, len(devices))


def line_peer(at, step):
    return (at["dp"], lax.rem(at["line"] + step, 4))


def ring_peer(at, step):
    return (lax.rem(at["dp"] + step, 8), at["line"])


def greet_all(at):
    greet(
        [ring_peer(at, step) for step in range(1, 8)]
        + [line_peer(at, step) for step in (1, 2, 3)]
    )


def rows_of(pixel):
    return pl.ds(pl.multiple_of(pixel * SLOTS, SLOTS), SLOTS)


def slope_of(values):
    sigmoid = jax.nn.sigmoid(values)
    return sigmoid * (1.0 + values * (1.0 - sigmoid))


def over_pixels(body, carry):
    return lax.fori_loop(0, HW, body, carry, unroll=7)


def exchange(at, land, land_two, index, sems, sem_index, payload, combine, hooks=(None, None)):
    dp, line = at["dp"], at["line"]
    one_send, one_recv, two_send, two_recv = sems
    rows = pl.ds(0, 2)
    for row, value in enumerate(payload):
        land[index, dp, row : row + 1, :] = value
    sent = []
    for step in range(1, 8):
        here = land.at[index, dp, rows]
        copy = remote(
            here,
            here,
            one_send.at[sem_index, step - 1],
            one_recv.at[sem_index, step - 1],
            ring_peer(at, step),
        )
        copy.start()
        sent.append(copy)
    if hooks[0] is not None:
        hooks[0]()
    for step in range(1, 8):
        there = land.at[index, lax.rem(dp + 8 - step, 8), rows]
        remote(
            there,
            there,
            one_send.at[sem_index, step - 1],
            one_recv.at[sem_index, step - 1],
            ring_peer(at, step),
        ).wait_recv()
    merged = combine([land[index, source] for source in range(8)])
    for row, value in enumerate(merged):
        land_two[index, line, row : row + 1, :] = value
    for step in (1, 2, 3):
        here = land_two.at[index, line, rows]
        copy = remote(
            here,
            here,
            two_send.at[sem_index, step - 1],
            two_recv.at[sem_index, step - 1],
            line_peer(at, step),
        )
        copy.start()
        sent.append(copy)
    if hooks[1] is not None:
        hooks[1]()
    for step in (1, 2, 3):
        there = land_two.at[index, lax.rem(line + 4 - step, 4), rows]
        remote(
            there,
            there,
            two_send.at[sem_index, step - 1],
            two_recv.at[sem_index, step - 1],
            line_peer(at, step),
        ).wait_recv()
    merged = combine([land_two[index, source] for source in range(4)])
    for copy in sent:
        copy.wait_send()
    return merged


def combine_sums(blocks):
    total = sum(blocks[1:], blocks[0])
    return [total[0:1], total[1:2]]


def forward_kernel(
    ws_wide,
    wt_wide,
    feat_in,
    cot_wide,
    mid_own,
    out_own,
    frames_in,
    shuffle,
    ws_out,
    wt_out,
    par_out,
    mask_in,
    block_out,
    a_out,
    s_out,
    u_out,
    t_out,
    skip_out,
    stat_mid,
    stat_out,
    ws_in,
    wt_in,
    cot_raw,
    cot_in,
    par_in,
    pair_s,
    pair_t,
    stage_s,
    stage_t,
    feat_land,
    cot_land,
    par_land,
    a_pad,
    s_ref,
    x_ref,
    u_ref,
    t_ref,
    side,
    feat_ref,
    thin,
    w_buf,
    wt_buf,
    land_mid,
    land_mid_two,
    land_out,
    land_out_two,
    land_count,
    count_one,
    count_two,
    pair_send,
    pair_recv,
    act_send,
    act_recv,
    line_send,
    line_recv,
    plane_send,
    plane_recv,
    diag_send,
    diag_recv,
    core_send,
    core_recv,
    own_sem,
    chunk_sem,
    w_sem,
    wt_sem,
    save_sem,
    one_send,
    one_recv,
    two_send,
    two_recv,
):
    at = place()
    line, core, chip = at["line"], at["core"], at["chip"]
    sems = (one_send, one_recv, two_send, two_recv)
    cot_load = pltpu.make_async_copy(cot_wide, cot_raw, wt_sem.at[4])
    cot_load.start()
    for unit in range(2):
        ws_in[unit] = ws_wide[unit].astype(BF16)
        for tau in range(3):
            wt_in[unit, :, 64 * tau : 64 * tau + 64] = wt_wide[unit, tau].T.astype(BF16)
    pieces = []
    blank = jnp.zeros((4, THIRD - 2 * SUB), F32)
    for third in range(3):
        for half in range(2):
            first = half * HALF + third * SUB
            pieces.append(mid_own[:, first : first + SUB])
        pieces.append(blank)
    par_in[...] = jnp.zeros(par_in.shape, F32)
    wide_rows = jnp.concatenate(
        [jnp.concatenate(pieces, axis=1), jnp.zeros((4, MID_C), F32)], axis=0
    )
    par_in[0:4, :] = pltpu.roll(wide_rows, line * (2 * SUB), 1)[0:4]
    par_in[4:8, pl.ds(pl.multiple_of(line * 128, 128), 128)] = out_own[...]
    row_ids = lax.broadcasted_iota(jnp.int32, (SLOTS, MID_C), 0)
    mask = jnp.zeros((SLOTS, MID_C), F32)
    for clip in range(4):
        kept = lax.div(frames_in[4 * line + clip], 8)
        here = jnp.logical_and(row_ids % 4 == clip, row_ids // 4 < kept)
        mask = jnp.where(here, 1.0, mask)
    mask_in[...] = mask
    count_rows = lax.broadcasted_iota(jnp.int32, (8, 128), 0)
    count_tile = jnp.zeros((8, 128), F32)
    for owner in range(4):
        frames = lax.div(frames_in[4 * owner], 8)
        for clip in range(1, 4):
            frames = frames + lax.div(frames_in[4 * owner + clip], 8)
        count_tile = jnp.where(count_rows == owner, (HW * frames).astype(F32), count_tile)
    land_count[at["dp"]] = count_tile
    greet_all(at)
    started = []

    def send(copy):
        copy.start()
        started.append(copy)
        return copy

    def area(chunk, owner_core, owner_chip, first, count):
        kind, unit, lead, leads = chunk
        ref, width = (ws_out, CHIP_S) if kind == "s" else (wt_out, CHIP_T)
        lanes = pl.ds(pl.multiple_of(owner_chip * width, 128), width)
        return ref.at[unit, pl.ds(lead, leads), pl.ds(first, count), owner_core, :, lanes]

    pairs = {}
    for index, (kind, unit) in enumerate(PARTS):
        theirs = pl.ds(pl.multiple_of((1 - core) * HALF, 16), HALF)
        source, landing = (ws_in, pair_s) if kind == "s" else (wt_in, pair_t)
        pairs[kind, unit] = send(
            remote(
                source.at[unit, theirs],
                landing.at[unit],
                pair_send.at[index],
                pair_recv.at[index],
                at["pair"],
            )
        )

    def acts(row, source, target):
        def cut(owner):
            return source.at[pl.ds(pl.multiple_of(owner * ROWS, 16), ROWS)]

        lanes = pl.ds(pl.multiple_of(line * 128, 128), 128)
        for step in (1, 2, 3):
            peer = line_peer(at, step)
            send(
                remote(
                    cut(peer[1]),
                    target.at[:, lanes],
                    act_send.at[row, step - 1],
                    act_recv.at[row, step - 1],
                    peer,
                )
            )
        own = pltpu.make_async_copy(cut(line), target.at[:, lanes], own_sem.at[row])
        own.start()
        return own

    def acts_wait(row, source, target, own):
        for step in (1, 2, 3):
            origin = lax.rem(line + 4 - step, 4)
            lanes = pl.ds(pl.multiple_of(origin * 128, 128), 128)
            remote(
                source.at[pl.ds(0, ROWS)],
                target.at[:, lanes],
                act_send.at[row, step - 1],
                act_recv.at[row, step - 1],
                line_peer(at, step),
            ).wait_recv()
        own.wait()

    mine = pl.ds(pl.multiple_of(core * HALF, 16), HALF)

    def merge(kind, unit):
        pairs[kind, unit].wait_recv()
        source, landing = (ws_in, pair_s) if kind == "s" else (wt_in, pair_t)
        low = source[unit, mine].astype(F32)
        high = landing[unit].astype(F32)
        first = jnp.where(core == 0, low, high)
        second = jnp.where(core == 0, high, low)
        if kind == "s":
            both = jnp.concatenate([first, second], axis=1).astype(BF16)
            stage_s[unit] = both.reshape(3, 1, SUB, CHIP_S)
        else:
            for tau in range(3):
                lanes = slice(64 * tau, 64 * tau + 64)
                both = jnp.concatenate([first[:, lanes], second[:, lanes]], axis=1).astype(BF16)
                stage_t[unit, 3 * tau : 3 * tau + 3] = both.reshape(3, 1, SUB, CHIP_T)

    own_copies = [None] * N_CHUNKS

    def step_line(index):
        chunk = CHUNKS[index]
        kind, unit, lead, leads = chunk
        if lead == 0:
            merge(kind, unit)
        staged = (stage_s if kind == "s" else stage_t).at[unit, pl.ds(lead, leads)]
        target = area(chunk, core, chip, line, 1)
        for step in (1, 3, 2):
            send(
                remote(
                    staged,
                    target,
                    line_send.at[index, step - 1],
                    line_recv.at[index, step - 1],
                    line_peer(at, step),
                )
            )
        own = pltpu.make_async_copy(staged, target, chunk_sem.at[index])
        own.start()
        own_copies[index] = own

    def step_plane(index):
        chunk = CHUNKS[index]
        for step in (1, 2, 3):
            origin = area(chunk, core, chip, lax.rem(line + 4 - step, 4), 1)
            remote(
                origin,
                origin,
                line_send.at[index, step - 1],
                line_recv.at[index, step - 1],
                line_peer(at, step),
            ).wait_recv()
        own_copies[index].wait()
        for turn in range(2):
            for way, name in enumerate(("x", "y")):
                half = area(chunk, core, chip, 2 * (way ^ turn), 2)
                send(
                    remote(
                        half,
                        half,
                        plane_send.at[index, way, turn],
                        plane_recv.at[index, way, turn],
                        at[name],
                    )
                )
        held = area(chunk, core, chip, 0, 4)
        send(remote(held, held, core_send.at[index, 0], core_recv.at[index, 0], at["pair"]))

    def plane_wait(index, way, turn, name):
        half = area(CHUNKS[index], core, at["chip_" + name], 2 * (way ^ turn), 2)
        remote(
            half,
            half,
            plane_send.at[index, way, turn],
            plane_recv.at[index, way, turn],
            at[name],
        ).wait_recv()
        return half

    def step_diag(index):
        for way, (name, other) in enumerate((("x", "y"), ("y", "x"))):
            half = plane_wait(index, way, 0, name)
            send(
                remote(half, half, diag_send.at[index, way], diag_recv.at[index, way], at[other])
            )

    def step_core(index):
        chunk = CHUNKS[index]
        for way, name in enumerate(("x", "y")):
            plane_wait(index, way, 1, name)
            held = area(chunk, core, at["chip_" + name], 0, 4)
            send(
                remote(
                    held, held, core_send.at[index, 1 + way], core_recv.at[index, 1 + way], at["pair"]
                )
            )
        for slot, name in enumerate(NEAR[:3]):
            core_wait(index, slot, name)
        for way, (other, first) in enumerate((("y", 0), ("x", 2))):
            half = area(chunk, core, at["chip_d"], first, 2)
            remote(
                half, half, diag_send.at[index, way], diag_recv.at[index, way], at[other]
            ).wait_recv()
        held = area(chunk, core, at["chip_d"], 0, 4)
        send(remote(held, held, core_send.at[index, 3], core_recv.at[index, 3], at["pair"]))
        core_wait(index, 3, NEAR[3])

    def core_wait(index, slot, name):
        held = area(CHUNKS[index], 1 - core, at[name], 0, 4)
        remote(
            held, held, core_send.at[index, slot], core_recv.at[index, slot], at["pair"]
        ).wait_recv()
        fetch(index, slot, name).start()

    def fetch(index, slot, name):
        kind, unit, lead, _ = CHUNKS[index]
        if kind == "s":
            turn = (3 * unit + lead) % 2
            lanes = pl.ds(pl.multiple_of(at[name] * CHIP_S, 128), CHIP_S)
            return pltpu.make_async_copy(
                ws_out.at[unit, lead, :, :, :, lanes],
                w_buf.at[turn, :, :, :, lanes],
                w_sem.at[turn, slot],
            )
        lanes = pl.ds(pl.multiple_of(at[name] * CHIP_T, 128), CHIP_T)
        return pltpu.make_async_copy(
            wt_out.at[unit, :, :, :, :, lanes], wt_buf.at[:, :, :, :, lanes], wt_sem.at[slot]
        )

    def fetch_wait(index):
        for slot, name in enumerate(NEAR):
            fetch(index, slot, name).wait()

    def window(unit, tap):
        row, column = tap // 3, tap % 3
        return a_pad[unit, row : row + SIDE, column : column + SIDE].reshape(ROWS, BLOCK_C)

    def conv(unit, third):
        fetch_wait(4 * unit + third)
        taps = jnp.concatenate([window(unit, tap) for tap in range(9)], axis=1)
        s_ref[:, third * THIRD : (third + 1) * THIRD] = lax.dot_general(
            taps,
            w_buf[(3 * unit + third) % 2].reshape(THIRD, TAPS_C),
            NT,
            preferred_element_type=F32,
        )

    mask_mid = mask_in[...]
    mask_out = mask_in[:, :BLOCK_C]
    slot_rows = lax.broadcasted_iota(jnp.int32, (SLOTS, BLOCK_C), 0)
    has_before = (slot_rows >= 4).astype(F32)
    has_after = (slot_rows < 12).astype(F32)

    def moments(values, mask, land, land_two, index, sem_index, hooks):
        zero = jnp.zeros(mask.shape, F32)
        width = mask.shape[1]
        local = local_count[:, :width]
        added = over_pixels(lambda p, acc: acc + values[rows_of(p), :], zero)
        mean = jnp.sum(added * mask, axis=0, keepdims=True) / local

        def squares(p, acc):
            centered = values[rows_of(p), :] - mean
            return acc + centered * centered

        spread = jnp.sum(over_pixels(squares, zero) * mask, axis=0, keepdims=True)
        def combine(blocks):
            known = count_one if len(blocks) == 8 else count_two
            counts = [known[source, :, :width] for source in range(len(blocks))]
            pivot = blocks[0]
            drifts = [block - pivot for block in blocks[1:]]
            shift = sum(count * drift for count, drift in zip(counts[1:], drifts))[0:1]
            squared = sum(count * drift * drift for count, drift in zip(counts[1:], drifts))[0:1]
            inner = sum(blocks[1:], pivot)[1:2]
            total = sum(counts[1:], counts[0])[0:1]
            return [pivot[0:1] + shift / total, inner + squared - shift * shift / total]

        mean, spread = exchange(
            at, land, land_two, index, sems, sem_index, [mean, spread], combine, hooks
        )
        total = all_count[:, :width]
        return mean, lax.rsqrt(spread / total + EPS_NORM), total

    saves = []

    def save(source, target):
        copy = pltpu.make_async_copy(source, target, save_sem.at[len(saves)])
        copy.start()
        saves.append(copy)

    def mid_norm_act(unit, *hooks):
        gain = par_out[2 * unit : 2 * unit + 1]
        bias = par_out[2 * unit + 1 : 2 * unit + 2]
        mean, inverse, total = moments(
            s_ref, mask_mid, land_mid, land_mid_two, unit, 2 * unit, hooks
        )
        stat_mid[2 * unit : 2 * unit + 1] = inverse
        stat_mid[2 * unit + 1 : 2 * unit + 2] = total

        def mid_act(p, carry):
            rows = rows_of(p)
            standard = (s_ref[rows, :] - mean) * inverse
            x_ref[unit, rows, :] = standard.astype(BF16)
            normed = standard * gain + bias
            u_ref[unit, rows, :] = (jax.nn.sigmoid(normed) * normed * mask_mid).astype(BF16)
            return carry

        over_pixels(mid_act, 0)
        save(x_ref.at[unit], s_out.at[unit])
        save(u_ref.at[unit], u_out.at[unit])

    def temporal(unit):
        fetch_wait(4 * unit + 3)

        def weight(tau):
            return wt_buf[3 * tau : 3 * tau + 3].reshape(MID_C, BLOCK_C)

        t_ref[unit] = lax.dot_general(u_ref[unit], weight(1), NN, preferred_element_type=F32)
        side[0] = lax.dot_general(u_ref[unit], weight(0), NN, preferred_element_type=F32)
        side[1] = lax.dot_general(u_ref[unit], weight(2), NN, preferred_element_type=F32)

        def frames(p, carry):
            rows = rows_of(p)
            t_ref[unit, rows, :] = (
                t_ref[unit, rows, :]
                + pltpu.roll(side[0, rows, :], 4, 0) * has_before
                + pltpu.roll(side[1, rows, :], 12, 0) * has_after
            )
            return carry

        over_pixels(frames, 0)

    def out_stats(unit, *hooks):
        mean, inverse, total = moments(
            t_ref.at[unit], mask_out, land_out, land_out_two, unit, 2 * unit + 1, hooks
        )
        stat_out[2 * unit : 2 * unit + 1] = inverse
        stat_out[2 * unit + 1 : 2 * unit + 2] = total
        gain = par_out[4 + 2 * unit : 5 + 2 * unit, :BLOCK_C]
        bias = par_out[5 + 2 * unit : 6 + 2 * unit, :BLOCK_C]
        return mean, inverse, gain, bias

    for step in range(1, 8):
        here = land_count.at[at["dp"]]
        send(
            remote(
                here,
                here,
                one_send.at[4, step - 1],
                one_recv.at[4, step - 1],
                ring_peer(at, step),
            )
        )
    step_line(0)
    for step in (1, 2, 3):
        send(
            remote(
                par_in,
                par_land.at[line],
                act_send.at[2, step - 1],
                act_recv.at[2, step - 1],
                line_peer(at, step),
            )
        )
    par_own = pltpu.make_async_copy(par_in, par_land.at[line], own_sem.at[2])
    par_own.start()
    step_line(1)
    for unit in range(2):
        a_pad[unit] = jnp.zeros(a_pad.shape[1:], BF16)
    step_plane(0)
    step_line(2)
    step_diag(0)
    step_plane(1)
    feat_own = acts(0, feat_in, feat_land)
    cot_load.wait()
    cot_in[...] = cot_raw[...].astype(BF16)
    for step in range(1, 8):
        there = land_count.at[lax.rem(at["dp"] + 8 - step, 8)]
        remote(
            there,
            there,
            one_send.at[4, step - 1],
            one_recv.at[4, step - 1],
            ring_peer(at, step),
        ).wait_recv()

    def widen(row, rows):
        return jnp.concatenate([jnp.broadcast_to(row, (rows, 128))] * (MID_C // 128), axis=1)

    def pick(tile):
        return jnp.sum(jnp.where(count_rows == line, tile, 0.0), axis=0, keepdims=True)

    sum_tile = land_count[0]
    for source in range(8):
        count_one[source] = widen(pick(land_count[source]), 8)
        if source > 0:
            sum_tile = sum_tile + land_count[source]
    for source in range(4):
        count_two[source] = widen(sum_tile[source : source + 1], 8)
    local_count = widen(pick(count_tile), 1)
    all_count = widen(jnp.sum(sum_tile[0:4], axis=0, keepdims=True), 1)
    step_plane(2)
    step_line(3)
    step_diag(1)
    step_core(0)
    permute = shuffle[:, :ROWS]
    acts_wait(0, feat_in, feat_land, feat_own)
    feat_ref[...] = lax.dot_general(permute, feat_land[...], NN, preferred_element_type=F32).astype(
        BF16
    )

    def fill(p, carry):
        a_pad[0, 1 + p // SIDE, 1 + p % SIDE] = feat_ref[rows_of(p), :]
        return carry

    over_pixels(fill, 0)
    save(a_pad.at[0], a_out.at[0])
    step_line(4)
    step_diag(2)
    step_core(1)
    step_plane(3)
    conv(0, 0)
    step_core(2)
    conv(0, 1)
    conv(0, 2)
    for step in (1, 2, 3):
        remote(
            par_in,
            par_land.at[lax.rem(line + 4 - step, 4)],
            act_send.at[2, step - 1],
            act_recv.at[2, step - 1],
            line_peer(at, step),
        ).wait_recv()
    par_own.wait()
    par_out[...] = par_land[0] + par_land[1] + par_land[2] + par_land[3]

    def hook_a():
        step_diag(3)
        step_plane(4)

    def hook_e():
        step_line(5)
        step_core(3)

    mid_norm_act(0, hook_a, hook_e)
    temporal(0)
    cot_own = []

    def hook_b():
        step_diag(4)
        step_plane(5)

    def hook_c():
        step_line(6)
        step_line(7)
        cot_own.append(acts(1, cot_in, cot_land))
        step_core(4)

    mean, inverse, gain, bias = out_stats(0, hook_b, hook_c)

    def out_act(p, carry):
        rows = rows_of(p)
        standard = (t_ref[0, rows, :] - mean) * inverse
        t_ref[0, rows, :] = standard
        normed = standard * gain + bias
        hidden = jax.nn.sigmoid(normed) * normed * mask_out
        a_pad[1, 1 + p // SIDE, 1 + p % SIDE] = hidden.astype(BF16)
        return carry

    over_pixels(out_act, 0)
    save(t_ref.at[0], t_out.at[0])
    save(a_pad.at[1], a_out.at[1])
    conv(1, 0)
    step_diag(5)
    step_plane(6)
    step_core(5)
    conv(1, 1)
    step_diag(6)
    step_plane(7)
    step_core(6)
    conv(1, 2)
    mid_norm_act(1, lambda: step_diag(7), lambda: step_core(7))
    temporal(1)

    def hook_d():
        acts_wait(1, cot_in, cot_land, cot_own[0])
        side[0] = lax.dot_general(permute, cot_land[...], NN, preferred_element_type=F32)

    mean_one, inverse_one, gain_one, bias_one = out_stats(1, hook_d, None)

    def end_act(p, carry):
        rows = rows_of(p)
        standard = (t_ref[1, rows, :] - mean_one) * inverse_one
        t_ref[1, rows, :] = standard
        pre = standard * gain_one + bias_one + feat_ref[rows, :].astype(F32)
        sigmoid = jax.nn.sigmoid(pre)
        thin[rows, :] = (pre * sigmoid * mask_out).astype(BF16)
        slope = sigmoid * (1.0 + pre * (1.0 - sigmoid))
        cot_land[rows, :] = (side[0, rows, :] * mask_out * slope).astype(BF16)
        return carry

    over_pixels(end_act, 0)
    save(t_ref.at[1], t_out.at[1])
    save(cot_land, skip_out)
    block_out[...] = lax.dot_general(permute, thin[...], TN, preferred_element_type=F32).astype(
        BF16
    )
    for copy in saves:
        copy.wait()
    for copy in started:
        copy.wait_send()


def backward_kernel(
    ws,
    wt,
    a_in,
    s_in,
    u_in,
    t_in,
    skip_in,
    stat_mid,
    stat_out,
    par,
    mask_in,
    shuffle,
    block_in,
    sp_in,
    sm_in,
    sv_in,
    tp_in,
    tm_in,
    tv_in,
    sp_out,
    sm_out,
    sv_out,
    tp_out,
    tm_out,
    tv_out,
    mid_grad,
    out_grad,
    block_out,
    input_out,
    a_pad,
    s_ref,
    u_ref,
    t_ref,
    side,
    skip_ref,
    wide,
    ds_pad,
    d_ref,
    w_buf,
    land_mid,
    land_mid_two,
    land_out,
    land_out_two,
    g_s,
    g_t,
    land_s,
    land_t,
    one_s,
    one_t,
    two_s,
    two_t,
    line_s,
    line_t,
    fin_s,
    fin_t,
    adam_s,
    adam_t,
    load_sem,
    w_sem,
    ex_one_send,
    ex_one_recv,
    ex_two_send,
    ex_two_recv,
    act_send,
    act_recv,
    act_sem,
    pair_send,
    pair_recv,
    one_send,
    one_recv,
    two_send,
    two_recv,
    line_send,
    line_recv,
    fin_send,
    fin_recv,
    adam_load,
    adam_save,
):
    at = place()
    line, core, chip = at["line"], at["core"], at["chip"]
    sems = (ex_one_send, ex_one_recv, ex_two_send, ex_two_recv)

    def load(index, source, target):
        return pltpu.make_async_copy(source, target, load_sem.at[index])

    load_t = [load(0, t_in.at[unit], t_ref) for unit in range(2)]
    load_u = [load(1, u_in.at[unit], u_ref) for unit in range(2)]
    load_s = [load(2, s_in.at[unit], s_ref) for unit in range(2)]
    load_a = [load(3, a_in.at[unit], a_pad) for unit in range(2)]
    load_skip = load(4, skip_in, skip_ref)
    load_shuffle = load(5, shuffle, u_ref.at[:, pl.ds(0, SHUFFLE_C)])
    load_t[1].start()
    load_skip.start()
    load_u[1].start()
    load_s[1].start()
    load_a[1].start()
    greet_all(at)

    mask_mid = mask_in[...]
    mask_out = mask_in[:, :BLOCK_C]
    slot_rows = lax.broadcasted_iota(jnp.int32, (SLOTS, BLOCK_C), 0)
    has_before = (slot_rows >= 4).astype(F32)
    has_after = (slot_rows < 12).astype(F32)
    lanes_line = pl.ds(pl.multiple_of(line * 128, 128), 128)
    rows_line = pl.ds(pl.multiple_of(line * ROWS, 16), ROWS)

    act_copies = []

    def acts(row, source, target):
        for step in (1, 2, 3):
            peer = line_peer(at, step)
            copy = remote(
                source.at[:, pl.ds(pl.multiple_of(peer[1] * 128, 128), 128)],
                target.at[rows_line],
                act_send.at[row, step - 1],
                act_recv.at[row, step - 1],
                peer,
            )
            copy.start()
            act_copies.append(copy)
        own = pltpu.make_async_copy(source.at[:, lanes_line], target.at[rows_line], act_sem.at[row])
        own.start()
        return own

    def acts_wait(row, source, target, own):
        for step in (1, 2, 3):
            origin = lax.rem(line + 4 - step, 4)
            remote(
                source.at[:, lanes_line],
                target.at[pl.ds(pl.multiple_of(origin * ROWS, 16), ROWS)],
                act_send.at[row, step - 1],
                act_recv.at[row, step - 1],
                line_peer(at, step),
            ).wait_recv()
        own.wait()

    flying = [[] for _ in CHUNKS]
    pair_copies = [None] * N_CHUNKS
    fin_copies = [None] * N_CHUNKS

    def launch(index, copy):
        copy.start()
        flying[index].append(copy)
        return copy

    def drain(index):
        for copy in flying[index]:
            copy.wait_send()
        flying[index] = []

    def grad_of(index):
        kind, _, lead, _ = CHUNKS[index]
        return g_s.at[lead] if kind == "s" else g_t

    def land_of(index):
        kind, _, lead, _ = CHUNKS[index]
        return land_s.at[lead] if kind == "s" else land_t

    def held(index, small, large):
        kind, unit, lead, _ = CHUNKS[index]
        return large.at[unit, lead] if kind == "s" else small.at[unit]

    def cut(index, owner, first, count):
        width = CHIP_S if CHUNKS[index][0] == "s" else CHIP_T
        lanes = pl.ds(pl.multiple_of(owner * width, 128), width)
        return grad_of(index).at[:, pl.ds(first, count), core, :, lanes]

    def add_into(target, source):
        leads, count, _, width = target.shape

        def body(turn, carry):
            if leads == 1 and width > 2048:
                where = (0, lax.div(turn, 3), pl.ds(pl.multiple_of(lax.rem(turn, 3) * 16, 16), 16))
            elif leads == 1:
                where = (0, turn)
            else:
                where = (turn,)
            target[where] = (target[where].astype(F32) + source[where].astype(F32)).astype(BF16)
            return carry

        turns = leads if leads > 1 else count * (3 if width > 2048 else 1)
        lax.fori_loop(0, turns, body, 0)

    def step_pair(index):
        pair_copies[index] = launch(
            index,
            remote(
                grad_of(index).at[:, :, 1 - core],
                land_of(index),
                pair_send.at[index],
                pair_recv.at[index],
                at["pair"],
            ),
        )

    def step_one(index):
        pair_copies[index].wait_recv()
        add_into(grad_of(index).at[:, :, core], land_of(index))
        ones, twos = held(index, one_t, one_s), held(index, two_t, two_s)
        for way, (name, first) in enumerate((("x", 0), ("y", 2))):
            launch(
                index,
                remote(
                    cut(index, at["chip_d"], first, 2),
                    ones.at[way],
                    one_send.at[index, way],
                    one_recv.at[index, way],
                    at[name],
                ),
            )
            launch(
                index,
                remote(
                    cut(index, at["chip_" + name], first, 2),
                    twos.at[way, :, pl.ds(first, 2)],
                    two_send.at[index, way, 0],
                    two_recv.at[index, way, 0],
                    at[name],
                ),
            )

    def step_two(index):
        ones, twos = held(index, one_t, one_s), held(index, two_t, two_s)
        for way, (name, other, first) in enumerate((("x", "y", 0), ("y", "x", 2))):
            landing = ones.at[way]
            remote(
                landing, landing, one_send.at[index, way], one_recv.at[index, way], at[name]
            ).wait_recv()
            target = cut(index, at["chip_" + other], first, 2)
            add_into(target, landing)
            launch(
                index,
                remote(
                    target,
                    twos.at[1 - way, :, pl.ds(first, 2)],
                    two_send.at[index, 1 - way, 1],
                    two_recv.at[index, 1 - way, 1],
                    at[other],
                ),
            )

    def step_three(index):
        twos = held(index, two_t, two_s)
        for way, (name, first) in enumerate((("x", 0), ("y", 2))):
            for turn, begin in enumerate((first, 2 - first)):
                landing = twos.at[way, :, pl.ds(begin, 2)]
                remote(
                    landing,
                    landing,
                    two_send.at[index, way, turn],
                    two_recv.at[index, way, turn],
                    at[name],
                ).wait_recv()
        own = cut(index, chip, 0, 4)
        leads = own.shape[0]

        def body(turn, carry):
            where = (0, turn) if leads == 1 else (turn,)
            own[where] = (
                own[where].astype(F32)
                + twos.at[0][where].astype(F32)
                + twos.at[1][where].astype(F32)
            ).astype(BF16)
            return carry

        lax.fori_loop(0, 4 if leads == 1 else leads, body, 0)
        lines = held(index, line_t, line_s)
        for step in (1, 3, 2):
            peer = line_peer(at, step)
            launch(
                index,
                remote(
                    cut(index, chip, peer[1], 1),
                    lines.at[step - 1],
                    line_send.at[index, step - 1],
                    line_recv.at[index, step - 1],
                    peer,
                ),
            )

    def step_four(index):
        lines, fin = held(index, line_t, line_s), held(index, fin_t, fin_s)
        for step in (1, 2, 3):
            landing = lines.at[step - 1]
            remote(
                landing,
                landing,
                line_send.at[index, step - 1],
                line_recv.at[index, step - 1],
                line_peer(at, step),
            ).wait_recv()
        total = cut(index, chip, line, 1)[...].astype(F32)
        for step in range(3):
            total = total + lines[step].astype(F32)
        fin[0] = total
        fin_copies[index] = launch(
            index,
            remote(fin.at[0], fin.at[1], fin_send.at[index], fin_recv.at[index], at["pair"]),
        )

    adam_saves = {"s": [], "t": []}
    adam_loads = {}

    def adam_moves(index, load):
        kind, unit, lead, _ = CHUNKS[index]
        moves = []
        for which in range(2):
            if kind == "s":
                arrays = (sp_in, sm_in, sv_in) if load else (sp_out, sm_out, sv_out)
                half = core if which == 0 else 1 - core
                rows = pl.ds(pl.multiple_of(half * HALF + SUB * lead, 16), SUB)
                for array, ref in enumerate(arrays):
                    here, there = adam_s.at[array, which], ref.at[unit, rows]
                    moves.append((there, here) if load else (here, there))
            elif which == 0:
                arrays = (tp_in, tm_in, tv_in) if load else (tp_out, tm_out, tv_out)
                for array, ref in enumerate(arrays):
                    here, there = adam_t.at[array], ref.at[unit]
                    moves.append((there, here) if load else (here, there))
        sems = adam_load if load else adam_save
        row = 0 if kind == "s" else 1
        return [
            pltpu.make_async_copy(source, target, sems.at[row, number])
            for number, (source, target) in enumerate(moves)
        ]

    def adam_fetch(index):
        kind = CHUNKS[index][0]
        for copy in adam_saves[kind]:
            copy.wait()
        adam_saves[kind] = []
        adam_loads[index] = adam_moves(index, True)
        for copy in adam_loads[index]:
            copy.start()

    def step_five(index):
        kind, unit, lead, leads = CHUNKS[index]
        adam_fetch(index)
        fin_copies[index].wait_recv()
        fin = held(index, fin_t, fin_s)
        for copy in adam_loads[index]:
            copy.wait()
        if kind == "s":
            width = CHIP_S // 2
            for which in range(2):
                value = fin[which, 0, 0]
                grad = jnp.where(core == 0, value[:, :width], value[:, width:])
                fresh = adam_update(
                    adam_s[0, which],
                    adam_s[1, which],
                    adam_s[2, which],
                    grad,
                    RATE_CONV,
                    DECAY_CONV,
                )
                for array in range(3):
                    adam_s[array, which] = fresh[array]
        else:
            width = CHIP_T // 2
            for tau in range(3):
                both = [
                    fin[which, 3 * tau : 3 * tau + 3].reshape(HALF, CHIP_T) for which in range(2)
                ]
                first = jnp.where(core == 0, both[0], both[1])
                second = jnp.where(core == 0, both[1], both[0])
                turned = jnp.concatenate([first, second], axis=0).T
                grad = jnp.where(core == 0, turned[:width], turned[width:])
                fresh = adam_update(
                    adam_t[0, tau], adam_t[1, tau], adam_t[2, tau], grad, RATE_CONV, DECAY_CONV
                )
                for array in range(3):
                    adam_t[array, tau] = fresh[array]
        adam_saves[kind] = adam_moves(index, False)
        for copy in adam_saves[kind]:
            copy.start()

    def fetch_w(unit, tap, slot):
        lanes = pl.ds(pl.multiple_of(tap * BLOCK_C, 128), BLOCK_C)
        return pltpu.make_async_copy(ws.at[unit, :, lanes], w_buf.at[slot], w_sem.at[slot])

    def fetch_wt(unit, tau, slot):
        return pltpu.make_async_copy(wt.at[unit, tau], w_buf.at[slot], w_sem.at[slot])

    def window(tap):
        return a_pad[pl.ds(tap // 3, SIDE), pl.ds(tap % 3, SIDE)].reshape(ROWS, BLOCK_C)

    zero_mid = jnp.zeros((SLOTS, MID_C), F32)
    zero_out = jnp.zeros((SLOTS, BLOCK_C), F32)

    def out_norm_back(unit, *hooks):
        grad_ref = skip_ref if unit == 1 else side
        gain = par[4 + 2 * unit : 5 + 2 * unit, :BLOCK_C]
        inverse = stat_out[2 * unit : 2 * unit + 1]
        total = stat_out[2 * unit + 1 : 2 * unit + 2]

        def out_sums(p, carry):
            rows = rows_of(p)
            grad = grad_ref[rows, :].astype(F32)
            return (carry[0] + grad, carry[1] + grad * t_ref[rows, :])

        bias_acc, gain_acc = over_pixels(out_sums, (zero_out, zero_out))
        sums = [
            jnp.sum(bias_acc, axis=0, keepdims=True),
            jnp.sum(gain_acc, axis=0, keepdims=True),
        ]
        grad_bias, grad_gain = exchange(
            at, land_out, land_out_two, unit, sems, 2 * unit, sums, combine_sums, hooks
        )
        out_grad[2 * unit : 2 * unit + 1, :] = grad_gain
        out_grad[2 * unit + 1 : 2 * unit + 2, :] = grad_bias
        scale = gain * inverse
        bias_part, gain_part = grad_bias / total, grad_gain / total

        def out_back(p, carry):
            rows = rows_of(p)
            value = (
                mask_out
                * scale
                * (grad_ref[rows, :].astype(F32) - bias_part - t_ref[rows, :] * gain_part)
            )
            d_ref[1, rows, :] = value.astype(BF16)
            d_ref[0, rows, :] = (pltpu.roll(value, 12, 0) * has_after).astype(BF16)
            d_ref[2, rows, :] = (pltpu.roll(value, 4, 0) * has_before).astype(BF16)
            return carry

        over_pixels(out_back, 0)

    def temporal_grad():
        for tau in range(3):
            g_t[3 * tau : 3 * tau + 3] = (
                lax.dot_general(u_ref[...], d_ref[tau], TN, preferred_element_type=F32)
                .astype(BF16)
                .reshape(3, 4, 2, SUB, BLOCK_C)
            )

    def temporal_back(unit):
        for tau in range(3):
            slot = tau % 2
            if tau < 2:
                fetch_wt(unit, tau + 1, 1 - slot).start()
            fetch_wt(unit, tau, slot).wait()
            value = lax.dot_general(d_ref[tau], w_buf[slot], NT, preferred_element_type=F32)
            wide[...] = value if tau == 0 else wide[...] + value

    def mid_norm_back(unit, *hooks):
        gain = par[2 * unit : 2 * unit + 1]
        bias = par[2 * unit + 1 : 2 * unit + 2]
        inverse = stat_mid[2 * unit : 2 * unit + 1]
        total = stat_mid[2 * unit + 1 : 2 * unit + 2]

        def mid_sums(p, carry):
            rows = rows_of(p)
            standard = s_ref[rows, :].astype(F32)
            grad = mask_mid * slope_of(standard * gain + bias) * wide[rows, :]
            wide[rows, :] = grad
            return (carry[0] + grad, carry[1] + grad * standard)

        bias_acc, gain_acc = over_pixels(mid_sums, (zero_mid, zero_mid))
        sums = [
            jnp.sum(bias_acc, axis=0, keepdims=True),
            jnp.sum(gain_acc, axis=0, keepdims=True),
        ]
        grad_bias, grad_gain = exchange(
            at, land_mid, land_mid_two, unit, sems, 2 * unit + 1, sums, combine_sums, hooks
        )
        mid_grad[2 * unit : 2 * unit + 1, :] = grad_gain
        mid_grad[2 * unit + 1 : 2 * unit + 2, :] = grad_bias
        scale = gain * inverse
        bias_part, gain_part = grad_bias / total, grad_gain / total

        def mid_back(p, carry):
            rows = rows_of(p)
            value = (
                mask_mid
                * scale
                * (wide[rows, :] - bias_part - s_ref[rows, :].astype(F32) * gain_part)
            )
            ds_pad[1 + p // SIDE, 1 + p % SIDE] = value.astype(BF16)
            return carry

        over_pixels(mid_back, 0)

    def spatial_grad(third):
        columns = slice(third * THIRD, (third + 1) * THIRD)

        def body(row, carry):
            inner = ds_pad[1 : 1 + SIDE, 1 : 1 + SIDE, :, columns].reshape(ROWS, THIRD)
            taps = jnp.concatenate([window(3 * row + column) for column in range(3)], axis=1)
            lanes = pl.ds(pl.multiple_of(row * 3 * BLOCK_C, 128), 3 * BLOCK_C)
            g_s[third, 0, :, :, :, lanes] = (
                lax.dot_general(inner, taps, TN, preferred_element_type=F32)
                .astype(BF16)
                .reshape(4, 2, SUB, 3 * BLOCK_C)
            )
            return carry

        lax.fori_loop(0, 3, body, 0)

    def spatial_back(unit, first):
        if first == 0:
            fetch_w(unit, 0, 0).start()

        def body(tap, carry):
            slot = lax.rem(tap, 2)

            @pl.when(tap < 8)
            def _():
                fetch_w(unit, tap + 1, 1 - slot).start()

            fetch_w(unit, tap, slot).wait()
            moved = ds_pad[pl.ds(2 - tap // 3, SIDE), pl.ds(2 - tap % 3, SIDE)].reshape(ROWS, MID_C)
            value = lax.dot_general(moved, w_buf[slot], NN, preferred_element_type=F32)

            @pl.when(tap == 0)
            def _():
                side[...] = value

            @pl.when(tap > 0)
            def _():
                side[...] = side[...] + value

            return carry

        lax.fori_loop(first, first + 3, body, 0)

    a_0, b_0, c_0, t_0, a_1, b_1, c_1, t_1 = range(N_CHUNKS)

    load_t[1].wait()
    load_skip.wait()
    fetch_wt(1, 0, 0).start()

    def clear():
        ds_pad[...] = jnp.zeros(ds_pad.shape, BF16)

    out_norm_back(1, clear, None)
    load_t[0].start()
    load_u[1].wait()
    temporal_grad()
    load_u[0].start()
    step_pair(t_1)
    temporal_back(1)
    load_s[1].wait()
    own_acts = []
    mid_norm_back(
        1,
        lambda: step_one(t_1),
        lambda: own_acts.append(acts(0, block_in, block_out)),
    )
    load_s[0].start()
    load_a[1].wait()
    spatial_grad(0)
    step_pair(a_1)
    step_two(t_1)
    spatial_grad(1)
    step_pair(b_1)
    step_one(a_1)
    spatial_grad(2)
    load_a[0].start()
    step_pair(c_1)
    step_three(t_1)
    step_one(b_1)
    step_two(a_1)
    spatial_back(1, 0)
    step_four(t_1)
    spatial_back(1, 3)
    spatial_back(1, 6)
    load_t[0].wait()
    gain, bias = par[4:5, :BLOCK_C], par[5:6, :BLOCK_C]

    def hidden_back(p, carry):
        rows = rows_of(p)
        slope = slope_of(t_ref[rows, :] * gain + bias)
        side[rows, :] = mask_out * slope * side[rows, :]
        return carry

    over_pixels(hidden_back, 0)
    fetch_wt(0, 0, 0).start()

    def hook_a():
        step_one(c_1)
        step_two(b_1)

    out_norm_back(0, hook_a, lambda: step_three(a_1))
    drain(t_1)
    load_u[0].wait()
    temporal_grad()
    load_shuffle.start()
    step_pair(t_0)
    temporal_back(0)
    step_two(c_1)
    step_five(t_1)
    load_s[0].wait()
    mid_norm_back(0, lambda: step_one(t_0), lambda: step_three(b_1))
    load_a[0].wait()
    step_four(a_1)
    drain(a_1)
    spatial_grad(0)
    step_pair(a_0)
    step_two(t_0)
    step_three(c_1)
    step_five(a_1)
    step_four(b_1)
    spatial_back(0, 0)
    step_one(a_0)
    spatial_back(0, 3)
    spatial_back(0, 6)
    step_three(t_0)
    step_two(a_0)
    load_shuffle.wait()
    d_ref[0] = (side[...] + skip_ref[...].astype(F32)).astype(BF16)
    thin = d_ref.at[1]
    thin[...] = lax.dot_general(
        u_ref[:, :SHUFFLE_C], d_ref[0], TN, preferred_element_type=F32
    ).astype(BF16)[:ROWS]
    own_acts.append(acts(1, thin, input_out))
    drain(b_1)
    spatial_grad(1)
    step_pair(b_0)
    step_five(b_1)
    step_four(c_1)
    step_one(b_0)
    drain(c_1)
    spatial_grad(2)
    step_pair(c_0)
    step_three(a_0)
    step_five(c_1)
    step_four(t_0)
    step_one(c_0)
    step_two(b_0)
    step_five(t_0)
    step_two(c_0)
    step_four(a_0)
    step_three(b_0)
    step_five(a_0)
    step_three(c_0)
    step_four(b_0)
    step_five(b_0)
    step_four(c_0)
    step_five(c_0)
    acts_wait(0, block_in, block_out, own_acts[0])
    acts_wait(1, thin, input_out, own_acts[1])
    for kind in ("s", "t"):
        for copy in adam_saves[kind]:
            copy.wait()
    for copy in act_copies:
        copy.wait_send()
    for index in (t_0, a_0, b_0, c_0):
        drain(index)


def spaces(text):
    kinds = {"v": VMEM, "a": pl.ANY, "s": pltpu.SMEM}
    return [pl.BlockSpec(memory_space=kinds[mark]) for mark in text]


def dma(*shape):
    return pltpu.SemaphoreType.DMA(shape)


def params(number):
    return pltpu.CompilerParams(
        collective_id=number, has_side_effects=True, vmem_limit_bytes=GRANT
    )


def shaped(*shape, dtype=BF16):
    return jax.ShapeDtypeStruct(shape, dtype)


def run_forward(*args):
    padded = (SIDE + 2, SIDE + 2, SLOTS, BLOCK_C)
    return pl.pallas_call(
        forward_kernel,
        out_shape=[
            shaped(2, 3, 4, 2, SUB, TAPS_C),
            shaped(2, 9, 4, 2, SUB, BLOCK_C),
            shaped(8, MID_C, dtype=F32),
            shaped(SLOTS, MID_C, dtype=F32),
            shaped(ROWS, BLOCK_C),
            shaped(2, *padded),
            shaped(2, ROWS, MID_C),
            shaped(2, ROWS, MID_C),
            shaped(2, ROWS, BLOCK_C, dtype=F32),
            shaped(ROWS, BLOCK_C),
            shaped(4, MID_C, dtype=F32),
            shaped(4, BLOCK_C, dtype=F32),
        ],
        in_specs=spaces("vvaavvsv"),
        out_specs=spaces("aavvvaaaaavv"),
        scratch_shapes=[
            VMEM((2, 2 * HALF, CHIP_S // 2), BF16),
            VMEM((2, 2 * HALF, 3 * CHIP_T // 2), BF16),
            VMEM((4 * ROWS, 128), F32),
            VMEM((4 * ROWS, 128), BF16),
            VMEM((8, MID_C), F32),
            VMEM((2, HALF, CHIP_S // 2), BF16),
            VMEM((2, HALF, 3 * CHIP_T // 2), BF16),
            VMEM((2, 3, 1, SUB, CHIP_S), BF16),
            VMEM((2, 9, 1, SUB, CHIP_T), BF16),
            VMEM((ROWS, BLOCK_C), BF16),
            VMEM((ROWS, BLOCK_C), BF16),
            VMEM((4, 8, MID_C), F32),
            VMEM((2,) + padded, BF16),
            VMEM((ROWS, MID_C), F32),
            VMEM((2, ROWS, MID_C), BF16),
            VMEM((2, ROWS, MID_C), BF16),
            VMEM((2, ROWS, BLOCK_C), F32),
            VMEM((2, ROWS, BLOCK_C), F32),
            VMEM((ROWS, BLOCK_C), BF16),
            VMEM((ROWS, BLOCK_C), BF16),
            VMEM((2, 4, 2, SUB, TAPS_C), BF16),
            VMEM((9, 4, 2, SUB, BLOCK_C), BF16),
            VMEM((2, 8, 8, MID_C), F32),
            VMEM((2, 4, 8, MID_C), F32),
            VMEM((2, 8, 8, BLOCK_C), F32),
            VMEM((2, 4, 8, BLOCK_C), F32),
            VMEM((8, 8, 128), F32),
            VMEM((8, 8, MID_C), F32),
            VMEM((4, 8, MID_C), F32),
            dma(4),
            dma(4),
            dma(3, 3),
            dma(3, 3),
            dma(N_CHUNKS, 3),
            dma(N_CHUNKS, 3),
            dma(N_CHUNKS, 2, 2),
            dma(N_CHUNKS, 2, 2),
            dma(N_CHUNKS, 2),
            dma(N_CHUNKS, 2),
            dma(N_CHUNKS, 4),
            dma(N_CHUNKS, 4),
            dma(3),
            dma(N_CHUNKS),
            dma(2, 4),
            dma(5),
            dma(10),
            dma(5, 7),
            dma(5, 7),
            dma(5, 3),
            dma(5, 3),
        ],
        compiler_params=params(0),
        name="forward",
    )(*args)


def run_backward(*args):
    return pl.pallas_call(
        backward_kernel,
        out_shape=[
            *[shaped(2, 2 * HALF, CHIP_S // 2, dtype=F32)] * 3,
            *[shaped(2, 3, CHIP_T // 2, 2 * HALF, dtype=F32)] * 3,
            shaped(4, MID_C, dtype=F32),
            shaped(4, BLOCK_C, dtype=F32),
            shaped(4 * ROWS, 128),
            shaped(4 * ROWS, 128),
        ],
        in_specs=spaces("aaaaaaavvvvaaaaaaaa"),
        out_specs=spaces("aaaaaavvaa"),
        scratch_shapes=[
            VMEM((SIDE + 2, SIDE + 2, SLOTS, BLOCK_C), BF16),
            VMEM((ROWS, MID_C), BF16),
            VMEM((ROWS, MID_C), BF16),
            VMEM((ROWS, BLOCK_C), F32),
            VMEM((ROWS, BLOCK_C), F32),
            VMEM((ROWS, BLOCK_C), BF16),
            VMEM((ROWS, MID_C), F32),
            VMEM((SIDE + 2, SIDE + 2, SLOTS, MID_C), BF16),
            VMEM((3, ROWS, BLOCK_C), BF16),
            VMEM((2, MID_C, BLOCK_C), BF16),
            VMEM((2, 8, 8, MID_C), F32),
            VMEM((2, 4, 8, MID_C), F32),
            VMEM((2, 8, 8, BLOCK_C), F32),
            VMEM((2, 4, 8, BLOCK_C), F32),
            VMEM((3, 1, 4, 2, SUB, TAPS_C), BF16),
            VMEM((9, 4, 2, SUB, BLOCK_C), BF16),
            VMEM((3, 1, 4, SUB, TAPS_C), BF16),
            VMEM((9, 4, SUB, BLOCK_C), BF16),
            VMEM((2, 3, 2, 1, 2, SUB, CHIP_S), BF16),
            VMEM((2, 2, 9, 2, SUB, CHIP_T), BF16),
            VMEM((2, 3, 2, 1, 4, SUB, CHIP_S), BF16),
            VMEM((2, 2, 9, 4, SUB, CHIP_T), BF16),
            VMEM((2, 3, 3, 1, 1, SUB, CHIP_S), BF16),
            VMEM((2, 3, 9, 1, SUB, CHIP_T), BF16),
            VMEM((2, 3, 2, 1, 1, SUB, CHIP_S), F32),
            VMEM((2, 2, 9, 1, SUB, CHIP_T), F32),
            VMEM((3, 2, SUB, CHIP_S // 2), F32),
            VMEM((3, 3, CHIP_T // 2, 2 * HALF), F32),
            dma(6),
            dma(2),
            dma(4, 7),
            dma(4, 7),
            dma(4, 3),
            dma(4, 3),
            dma(2, 3),
            dma(2, 3),
            dma(2),
            dma(N_CHUNKS),
            dma(N_CHUNKS),
            dma(N_CHUNKS, 2),
            dma(N_CHUNKS, 2),
            dma(N_CHUNKS, 2, 2),
            dma(N_CHUNKS, 2, 2),
            dma(N_CHUNKS, 3),
            dma(N_CHUNKS, 3),
            dma(N_CHUNKS),
            dma(N_CHUNKS),
            dma(2, 6),
            dma(2, 6),
        ],
        compiler_params=params(1),
        name="backward",
    )(*args)


def finish_kernel(
    frames_in,
    mid_p,
    mid_m,
    mid_v,
    out_p,
    out_m,
    out_v,
    sp_in,
    sm_in,
    sv_in,
    tp_in,
    tm_in,
    tv_in,
    mid_all,
    out_all,
    block_in,
    grad_in,
    block_out,
    clip_pool,
    grad_out,
    mid_p_out,
    mid_m_out,
    mid_v_out,
    out_p_out,
    out_m_out,
    out_v_out,
    sp_out,
    sm_out,
    sv_out,
    tp_out,
    tm_out,
    tv_out,
    block_ref,
    grad_ref,
    block_wide,
    grad_wide,
    hold_s,
    hold_t,
    sems,
):
    line = lax.axis_index("chan")
    loads = [
        pltpu.make_async_copy(block_in, block_ref, sems.at[0]),
        pltpu.make_async_copy(grad_in, grad_ref, sems.at[1]),
    ]
    passing = (
        (sp_in, hold_s.at[0], sp_out),
        (sm_in, hold_s.at[1], sm_out),
        (sv_in, hold_s.at[2], sv_out),
        (tp_in, hold_t.at[0], tp_out),
        (tm_in, hold_t.at[1], tm_out),
        (tv_in, hold_t.at[2], tv_out),
    )
    gets = [
        pltpu.make_async_copy(source, held, sems.at[2 + number])
        for number, (source, held, _) in enumerate(passing)
    ]
    puts = [
        pltpu.make_async_copy(held, target, sems.at[10 + number])
        for number, (_, held, target) in enumerate(passing)
    ]
    for copy in loads + gets:
        copy.start()
    stores = [
        pltpu.make_async_copy(block_wide, block_out, sems.at[8]),
        pltpu.make_async_copy(grad_wide, grad_out, sems.at[9]),
    ]
    loads[0].wait()
    block_wide[...] = block_ref[...].astype(F32)
    stores[0].start()
    loads[1].wait()
    grad_wide[...] = grad_ref[...].astype(F32)
    stores[1].start()
    for get, put in zip(gets, puts):
        get.wait()
        put.start()
    size = FRAMES * HW
    for clip in range(clip_pool.shape[0]):
        total = jnp.sum(block_wide[clip * size : (clip + 1) * size, :], axis=0, keepdims=True)
        kept = lax.div(frames_in[clip], 8).astype(F32)
        clip_pool[clip : clip + 1, :] = total / (HW * kept)
    all_rows = jnp.concatenate([mid_all[...], jnp.zeros((4, MID_C), F32)], axis=0)
    turned = pltpu.roll(all_rows, lax.rem(MID_C - line * (2 * SUB), MID_C), 1)[0:4]
    grad = jnp.concatenate(
        [
            turned[:, third * THIRD + half * SUB : third * THIRD + (half + 1) * SUB]
            for half in range(2)
            for third in range(3)
        ],
        axis=1,
    )
    fresh = adam_update(mid_p[...], mid_m[...], mid_v[...], grad, RATE_NORM, 0.0)
    for ref, value in zip((mid_p_out, mid_m_out, mid_v_out), fresh):
        ref[...] = value
    grad = out_all[:, pl.ds(pl.multiple_of(line * 128, 128), 128)]
    fresh = adam_update(out_p[...], out_m[...], out_v[...], grad, RATE_NORM, 0.0)
    for ref, value in zip((out_p_out, out_m_out, out_v_out), fresh):
        ref[...] = value
    for copy in stores + puts:
        copy.wait()


def run_finish(frames, *args):
    convs = args[6:12]
    norms = args[:6]
    clips = frames.shape[0]
    return pl.pallas_call(
        finish_kernel,
        out_shape=[
            shaped(4 * ROWS, 128, dtype=F32),
            shaped(clips, 128, dtype=F32),
            shaped(4 * ROWS, 128, dtype=F32),
            *[shaped(*v.shape, dtype=F32) for v in norms],
            *[shaped(*v.shape, dtype=F32) for v in convs],
        ],
        in_specs=spaces("svvvvvvaaaaaavvaa"),
        out_specs=spaces("avavvvvvvaaaaaa"),
        scratch_shapes=[
            VMEM((4 * ROWS, 128), BF16),
            VMEM((4 * ROWS, 128), BF16),
            VMEM((4 * ROWS, 128), F32),
            VMEM((4 * ROWS, 128), F32),
            VMEM((3,) + convs[0].shape, F32),
            VMEM((3,) + convs[3].shape, F32),
            dma(16),
        ],
        compiler_params=pltpu.CompilerParams(vmem_limit_bytes=GRANT),
        name="finish",
    )(frames, *args)


def shuffle_matrix():
    clip, frame, pixel = np.meshgrid(np.arange(4), np.arange(FRAMES), np.arange(HW), indexing="ij")
    source = (clip * FRAMES + frame) * HW + pixel
    target = pixel * SLOTS + frame * 4 + clip
    matrix = np.zeros((ROWS, SHUFFLE_C), np.float32)
    matrix[target.reshape(-1), source.reshape(-1)] = 1.0
    return jnp.asarray(matrix, BF16)


def on_pairs(
    features,
    cotangent,
    clip_frames,
    spatial_master,
    spatial_first,
    spatial_second,
    temporal_master,
    temporal_first,
    temporal_second,
    mid_norm,
    mid_first,
    mid_second,
    out_norm,
    out_first,
    out_second,
):
    line = lax.axis_index("chan")
    spatial_own = [jnp.swapaxes(v, 1, 2) for v in (spatial_master, spatial_first, spatial_second)]
    temporal_own = [
        jnp.swapaxes(v, 2, 3) for v in (temporal_master, temporal_first, temporal_second)
    ]
    shuffle = shuffle_matrix()
    ws, wt, par, mask, block, a_all, s_all, u_all, t_all, skip, stat_mid, stat_out = run_forward(
        spatial_own[0],
        temporal_own[0],
        features,
        cotangent,
        mid_norm,
        out_norm,
        clip_frames,
        shuffle,
    )
    conv_new = run_backward(
        ws.reshape(2, MID_C, TAPS_C),
        wt.reshape(2, 3, MID_C, BLOCK_C),
        a_all,
        s_all,
        u_all,
        t_all,
        skip,
        stat_mid,
        stat_out,
        par,
        mask,
        shuffle,
        block,
        *spatial_own,
        *temporal_own,
    )
    block_out, clip_pool, grad_out, *rest = run_finish(
        clip_frames, mid_norm, mid_first, mid_second, out_norm, out_first, out_second, *conv_new
    )
    norms, convs = rest[:6], rest[6:]
    spatial = [jnp.swapaxes(v, 1, 2) for v in convs[:3]]
    temporal = [jnp.swapaxes(v, 2, 3) for v in convs[3:]]
    return (block_out, clip_pool, grad_out, *spatial, *temporal, *norms)


def solution(mesh):
    in_specs = (
        P("dp", "chan"),
        P("dp", "chan"),
        P("dp"),
        P(None, "dp", "chan"),
        P(None, "dp", "chan"),
        P(None, "dp", "chan"),
        P(None, None, "chan", "dp"),
        P(None, None, "chan", "dp"),
        P(None, None, "chan", "dp"),
        P(None, "chan"),
        P(None, "chan"),
        P(None, "chan"),
        P(None, "chan"),
        P(None, "chan"),
        P(None, "chan"),
    )
    out_specs = (
        P("dp", "chan"),
        P("dp", "chan"),
        P("dp", "chan"),
        P(None, "dp", "chan"),
        P(None, "dp", "chan"),
        P(None, "dp", "chan"),
        P(None, None, "chan", "dp"),
        P(None, None, "chan", "dp"),
        P(None, None, "chan", "dp"),
        P(None, "chan"),
        P(None, "chan"),
        P(None, "chan"),
        P(None, "chan"),
        P(None, "chan"),
        P(None, "chan"),
    )
    body = on_pairs if mesh.shape["dp"] == 8 and mesh.shape["chan"] == 4 else on_device
    return jax.shard_map(
        body, mesh=mesh, in_specs=in_specs, out_specs=out_specs, check_vma=False
    )
```
